32 devices in a mesh: rep: 8 (over y, x, core), shard: 4 (over z).
Axes of the slice: x: 2, y: 2, z: 4, core: 2. Of those that a mesh axis runs over, the one named last changes fastest.
Arguments:
- tokens: bfloat16 [8, 4, 784, 512], P('rep', 'shard'), may hold values from -6 to 6
- region: int32 [4, 784], P('shard'), may hold values from 0 to 2
- rel_index: int32 [392, 392], replicated, may hold values from 0 to 2534
- ln1_gain: bfloat16 [512], P('shard'), may hold values from 0.5 to 1.5
- ln1_shift: bfloat16 [512], P('shard'), may hold values from -1.75 to 1.75
- w_qkv: bfloat16 [512, 1536], P('shard'), may hold values from -0.25 to 0.25
- q_bias: bfloat16 [512], P('shard'), may hold values from -3 to 3
- v_bias: bfloat16 [512], P('shard'), may hold values from -1.75 to 1.75
- table: bfloat16 [2535, 16], P(None, 'shard'), may hold values from -6 to 6
- w_proj: bfloat16 [512, 512], P('shard'), may hold values from -3.5 to 3.5
- proj_bias: bfloat16 [512], P('shard'), may hold values from -1.75 to 1.75
- ln2_gain: bfloat16 [512], P('shard'), may hold values from 0.5 to 1.5
- ln2_shift: bfloat16 [512], P('shard'), may hold values from -1.75 to 1.75
- w_fc1: bfloat16 [512, 2048], P('shard'), may hold values from -0.25 to 0.25
- fc1_bias: bfloat16 [2048], P('shard'), may hold values from -3 to 3
- w_fc2: bfloat16 [2048, 512], P('shard'), may hold values from -0.1875 to 0.1875
- fc2_bias: bfloat16 [512], P('shard'), may hold values from -1.75 to 1.75
- cotangent: bfloat16 [8, 4, 784, 512], P('rep', 'shard'), may hold values from -6 to 6
Outputs:
- output: bfloat16 [8, 4, 784, 512], P('rep', 'shard')
- grad_tokens: float32 [8, 4, 784, 512], P('rep', 'shard')
- grad_ln1_gain: float32 [512], P('shard')
- grad_ln1_shift: float32 [512], P('shard')
- grad_w_qkv: float32 [512, 1536], P('shard')
- grad_q_bias: float32 [512], P('shard')
- grad_v_bias: float32 [512], P('shard')
- grad_table: float32 [2535, 16], P(None, 'shard')
- grad_w_proj: float32 [512, 512], P('shard')
- grad_proj_bias: float32 [512], P('shard')
- grad_ln2_gain: float32 [512], P('shard')
- grad_ln2_shift: float32 [512], P('shard')
- grad_w_fc1: float32 [512, 2048], P('shard')
- grad_fc1_bias: float32 [2048], P('shard')
- grad_w_fc2: float32 [2048, 512], P('shard')
- grad_fc2_bias: float32 [512], P('shard')
The draws below stay inside these ranges and needn't reach their ends.
All inputs are finite; a program needn't handle non-finite values.
Results may differ from the reference program's by a relative error of at most 0.015.
Values may be sent and summed in bfloat16 or wider, within the bound.
A program may use at most 256 MiB of HBM per device.

```python
import jax
import jax.numpy as jnp
from jax import lax

D = 512
HEADS = 16
HD = 32
FF = 2048
WT = 8
WH = 7
WW = 7
WIN = 392
BLOCK = 784
TABLE = 2535
CLIPS = 8
N_SHARD = 4


def with_ends(drawn, key, least, largest):
    index_at = [jax.random.randint(jax.random.fold_in(key, axis), (), 0, length) for axis, length in enumerate(drawn.shape)]
    longest = drawn.shape.index(max(drawn.shape))
    beside = index_at[:longest] + [(index_at[longest] + 1) % drawn.shape[longest]] + index_at[longest + 1:]
    return drawn.at[tuple(index_at)].set(least).at[tuple(beside)].set(largest)


def block_scale(stream_key, extent, shards, least, largest):
    factor_of, own = 1.0, jax.random.fold_in(stream_key, 6)
    for axis_at, parts in shards:
        steps = jnp.exp(jax.random.uniform(jax.random.fold_in(own, axis_at), (parts,), jnp.float32, least / len(shards), largest / len(shards)))
        factor_of = factor_of * jnp.repeat(steps, extent[axis_at] // parts).reshape([-1 if axis == axis_at else 1 for axis in range(len(extent))])
    return factor_of


def scatter_about(own_key, extent, scale, most, cuts=(), dtype=jnp.bfloat16):
    level = block_scale(own_key, extent, cuts, -0.22, 0.18) if cuts else 1.0
    values = jax.random.normal(own_key, extent, jnp.float32) * scale * level
    return jnp.minimum(jnp.maximum(values, -most), most).astype(dtype)


def setup_inputs(seed: int = 0) -> dict:
    key_list = jax.random.split(jax.random.key(seed), 19)
    tokens = scatter_about(key_list[0], (CLIPS, N_SHARD, BLOCK, D), 1.0, 6.0, ((0, 8), (1, 4)))
    region = with_ends(jax.random.randint(key_list[1], (N_SHARD, BLOCK), 0, 3), jax.random.fold_in(key_list[1], 1), 0, 2).astype(jnp.int32)
    rel_index = with_ends(jax.random.randint(key_list[2], (WIN, WIN), 0, TABLE), jax.random.fold_in(key_list[2], 1), 0, TABLE - 1).astype(jnp.int32)
    ln1_gain = jnp.clip(1.0 + 0.1 * jax.random.normal(key_list[3], (D,), jnp.float32), 0.5, 1.5).astype(jnp.bfloat16)
    ln1_shift = scatter_about(key_list[4], (D,), 0.3, 1.75, ((0, 4),))
    w_qkv = scatter_about(key_list[5], (D, 3 * D), D ** -0.5, 0.25, ((0, 4),))
    q_bias = scatter_about(key_list[6], (D,), 0.5, 3.0, ((0, 4),))
    v_bias = scatter_about(key_list[7], (D,), 0.3, 1.75, ((0, 4),))
    table = scatter_about(key_list[8], (TABLE, HEADS), 1.0, 6.0, ((1, 4),))
    w_proj = scatter_about(key_list[9], (D, D), (3 * D // WIN) ** -0.5, 3.5, ((0, 4),))
    proj_bias = scatter_about(key_list[10], (D,), 0.3, 1.75, ((0, 4),))
    ln2_gain = jnp.clip(1.0 + 0.1 * jax.random.normal(key_list[11], (D,), jnp.float32), 0.5, 1.5).astype(jnp.bfloat16)
    ln2_shift = scatter_about(key_list[12], (D,), 0.3, 1.75, ((0, 4),))
    w_fc1 = scatter_about(key_list[13], (D, FF), D ** -0.5, 0.25, ((0, 4),))
    fc1_bias = scatter_about(key_list[14], (FF,), 0.5, 3.0, ((0, 4),))
    w_fc2 = scatter_about(key_list[15], (FF, D), (FF // 2) ** -0.5, 0.1875, ((0, 4),))
    fc2_bias = scatter_about(key_list[16], (D,), 0.3, 1.75, ((0, 4),))
    cotangent = scatter_about(key_list[17], (CLIPS, N_SHARD, BLOCK, D), 1.0, 6.0, ((0, 8), (1, 4)))
    return {"tokens": tokens, "region": region, "rel_index": rel_index, "ln1_gain": ln1_gain, "ln1_shift": ln1_shift, "w_qkv": w_qkv, "q_bias": q_bias, "v_bias": v_bias, "table": table, "w_proj": w_proj, "proj_bias": proj_bias, "ln2_gain": ln2_gain, "ln2_shift": ln2_shift, "w_fc1": w_fc1, "fc1_bias": fc1_bias, "w_fc2": w_fc2, "fc2_bias": fc2_bias, "cotangent": cotangent}


@jax.custom_vjp
def low(v):
    return lax.optimization_barrier(v.astype(jnp.bfloat16)).astype(jnp.float32)

@jax.custom_vjp
def low_back(v):
    return v

def low_keep(v):
    return (low(v), None)

def low_pass(kept, grad):
    return (grad,)

def back_keep(v):
    return (v, None)

def back_low(kept, grad):
    return (low(grad),)
low.defvjp(low_keep, low_pass)
low_back.defvjp(back_keep, back_low)

def layer_norm(rows, gain, shift):
    centre = rows - lax.optimization_barrier(jnp.mean(rows, -1, keepdims=True))
    spread = lax.optimization_barrier(jnp.mean(centre * centre, -1, keepdims=True))
    return centre * lax.rsqrt(spread + 1e-05) * gain + shift

def to_grid(blocks, leading):
    rest = blocks.shape[3:]
    grid = blocks.reshape((leading, 2, 2, WT, WH, 2 * WW) + rest)
    grid = jnp.swapaxes(grid, 2, 3)
    return grid.reshape((leading, 2 * WT, 2 * WH, 2 * WW) + rest)

def from_grid(grid, leading):
    rest = grid.shape[4:]
    blocks = grid.reshape((leading, 2, WT, 2, WH, 2 * WW) + rest)
    blocks = jnp.swapaxes(blocks, 2, 3)
    return blocks.reshape((leading, 4, WT * WH * 2 * WW) + rest)

def window_heads(grid):
    split = grid.reshape(2, WT, 2, WH, 2, WW, HEADS, HD)
    return split.transpose(0, 2, 4, 6, 1, 3, 5, 7).reshape(8, HEADS, WIN, HD)

def window_ids(grid):
    split = grid.reshape(2, WT, 2, WH, 2, WW)
    return split.transpose(0, 2, 4, 1, 3, 5).reshape(8, WIN)

def grid_heads(windows):
    split = windows.reshape(2, 2, 2, HEADS, WT, WH, WW, HD)
    return split.transpose(0, 4, 1, 5, 2, 6, 3, 7).reshape(2 * WT, 2 * WH, 2 * WW, D)

def clip_forward(params, clip, labels, position):
    ln1_gain, ln1_shift, w_qkv, q_bias, v_bias, table, w_proj, proj_bias, ln2_gain, ln2_shift, w_fc1, fc1_bias, w_fc2, fc2_bias = params
    exact = lax.Precision.HIGHEST
    normed = layer_norm(clip, ln1_gain, ln1_shift)
    sent = low_back(low(normed))
    rolled = jnp.roll(sent, (-(WT // 2), -(WH // 2), -(WW // 2)), (0, 1, 2))
    flat = rolled.reshape(-1, D)
    mixed = jnp.dot(flat, w_qkv, precision=exact)
    queries = low_back(low(mixed[:, :D] + q_bias))
    keys = low_back(low(mixed[:, D:2 * D]))
    values = low_back(low(mixed[:, 2 * D:] + v_bias))
    shape = (2 * WT, 2 * WH, 2 * WW, HEADS, HD)
    query_win = window_heads(queries.reshape(shape))
    key_win = window_heads(keys.reshape(shape))
    value_win = window_heads(values.reshape(shape))
    scores = jnp.einsum('nhid,nhjd->nhij', query_win, key_win, precision=exact) * HD ** (-0.5) + position[None]
    allowed = labels[:, :, None] == labels[:, None, :]
    scores = low_back(jnp.where(allowed[:, None], scores, -1e+30))
    attend = jax.nn.softmax(scores, axis=-1)
    context = jnp.einsum('nhij,nhjd->nhid', low(attend), value_win, precision=exact)
    context = low_back(low(grid_heads(context)))
    unrolled = jnp.roll(context, (WT // 2, WH // 2, WW // 2), (0, 1, 2))
    branch = low_back(jnp.dot(unrolled.reshape(-1, D), w_proj, precision=exact) + proj_bias)
    middle = clip.reshape(-1, D) + branch
    normed_low = low(layer_norm(middle, ln2_gain, ln2_shift))
    hidden = low_back(jnp.dot(normed_low, w_fc1, precision=exact) + fc1_bias)
    active = low(jax.nn.gelu(hidden, approximate=False))
    result = middle + jnp.dot(active, w_fc2, precision=exact) + fc2_bias
    return result.reshape(2 * WT, 2 * WH, 2 * WW, D)

def reference(tokens, region, rel_index, ln1_gain, ln1_shift, w_qkv, q_bias, v_bias, table, w_proj, proj_bias, ln2_gain, ln2_shift, w_fc1, fc1_bias, w_fc2, fc2_bias, cotangent):
    params = tuple((w.astype(jnp.float32) for w in (ln1_gain, ln1_shift, w_qkv, q_bias, v_bias, table, w_proj, proj_bias, ln2_gain, ln2_shift, w_fc1, fc1_bias, w_fc2, fc2_bias)))
    grids = to_grid(tokens.astype(jnp.float32), CLIPS)
    labels = window_ids(to_grid(region[None], 1)[0])

    def forward(weights, inputs):
        position = jnp.transpose(weights[5][rel_index], (2, 0, 1))

        def one_clip(clip):
            return clip_forward(weights, clip, labels, position)
        return lax.map(jax.checkpoint(one_clip), inputs)
    result, pullback = jax.vjp(forward, params, grids)
    grad_params, grad_grids = pullback(to_grid(cotangent.astype(jnp.float32), CLIPS))
    output = from_grid(result, CLIPS).astype(jnp.bfloat16)
    grad_tokens = from_grid(grad_grids, CLIPS)
    return (output, grad_tokens, grad_params[0], grad_params[1], grad_params[2], grad_params[3], grad_params[4], grad_params[5], grad_params[6], grad_params[7], grad_params[8], grad_params[9], grad_params[10], grad_params[11], grad_params[12], grad_params[13])
```

```python
import functools

import jax
import jax.numpy as jnp
import numpy as np
from jax import lax
from jax.experimental import pallas as pl
from jax.experimental.pallas import tpu as pltpu
from jax.sharding import PartitionSpec as P

D = 512
HEADS = 16
HD = 32
WT = 8
WH = 7
WW = 7
WIN = 392
TABLE = 2535
PAD = 416
LANES = 512
GROUP = 4
CHUNKS = 20
SCALE = HD ** (-0.5)
NN = (((1,), (0,)), ((), ()))
NT = (((1,), (1,)), ((), ()))
TN = (((0,), (0,)), ((), ()))
VMEM_LIMIT = 60 * 2**20
f32 = jnp.float32
bf16 = jnp.bfloat16

PIECES = (
    ((0, 4), (0, 4), 112, 0),
    ((4, 8), (0, 4), 112, 112),
    ((0, 4), (4, 7), 96, 224),
    ((4, 8), (4, 7), 96, 320),
)


def send_matrix():
    matrix = np.zeros((2 * PAD, WT * WH * 2 * WW), np.float32)
    for window in range(2):
        for (t0, t1), (h0, h1), _, first in PIECES:
            row = window * PAD + first
            for t in range(t0, t1):
                for h in range(h0, h1):
                    for w in range(WW):
                        column = (window * WW + w + WW // 2) % (2 * WW)
                        source = ((t + 4) % WT * WH + (h + 3) % WH) * 2 * WW + column
                        matrix[row, source] = 1.0
                        row += 1
    return matrix


def pieces_of(array, axis, fill):
    shape = array.shape
    split = array.reshape(shape[:axis] + (WT, WH, WW) + shape[axis + 1 :])
    parts = []
    for (t0, t1), (h0, h1), padded, _ in PIECES:
        part = lax.slice_in_dim(lax.slice_in_dim(split, t0, t1, axis=axis), h0, h1, axis=axis + 1)
        length = (t1 - t0) * (h1 - h0) * WW
        part = part.reshape(shape[:axis] + (length,) + shape[axis + 1 :])
        widths = [(0, 0, 0)] * len(shape)
        widths[axis] = (0, padded - length, 0)
        parts.append(lax.pad(part, jnp.asarray(fill, array.dtype), widths))
    return jnp.concatenate(parts, axis)


def dot(a, b, dims=NN):
    return lax.dot_general(a, b, dims, preferred_element_type=f32)


def position_kernel(table_ref, rel_ref, out_ref):
    heads = table_ref.shape[1]

    def rows(step, carry):
        start = pl.multiple_of(step * 16, 16)
        for tile in range(LANES // 128):
            index = rel_ref[pl.ds(start, 16), tile * 128 : (tile + 1) * 128]
            halves = [(index[s : s + 8] & 127, index[s : s + 8] >> 7) for s in (0, 8)]
            found = [[None, None] for _ in range(heads)]
            for chunk in range(CHUNKS):
                for s, (low, high) in enumerate(halves):
                    here = high == chunk
                    for head in range(heads):
                        value = jnp.take_along_axis(table_ref[chunk, head], low, axis=1)
                        if chunk:
                            value = jnp.where(here, value, found[head][s])
                        found[head][s] = value
            for head in range(heads):
                out_ref[head, pl.ds(start, 16), tile * 128 : (tile + 1) * 128] = jnp.concatenate(
                    found[head], 0
                ).astype(bf16)
        return carry

    lax.fori_loop(0, PAD // 16, rows, 0)


def make_position(table, rel):
    heads = table.shape[1]
    chunks = jnp.pad(table.astype(f32).T, ((0, 0), (0, CHUNKS * 128 - TABLE)))
    chunks = chunks.reshape(heads, CHUNKS, 1, 128).transpose(1, 0, 2, 3)
    chunks = jnp.broadcast_to(chunks, (CHUNKS, heads, 8, 128))
    return pl.pallas_call(
        position_kernel,
        out_shape=jax.ShapeDtypeStruct((heads, PAD, LANES), bf16),
        in_specs=[pl.BlockSpec(memory_space=pltpu.VMEM)] * 2,
        out_specs=pl.BlockSpec(memory_space=pltpu.VMEM),
        compiler_params=pltpu.CompilerParams(vmem_limit_bytes=VMEM_LIMIT),
        name="position",
    )(chunks, rel)


def attend_kernel(q_ref, k_ref, v_ref, pos_ref, row_ref, column_ref, out_ref, attend_ref, mask):
    head_of = lax.broadcasted_iota(jnp.int32, (1, 128), 1) // HD
    none = jnp.zeros((), bf16)

    @pl.when(pl.program_id(0) == 0)
    def _():
        for window in range(2):
            same = column_ref[window] == row_ref[window, :, :PAD]
            mask[window] = jnp.where(same, 0.0, -1e30)

    def one(step, carry):
        window, head = step // GROUP, step % GROUP
        mine = head_of == head
        query = jnp.where(mine, q_ref[window], none)
        value = jnp.where(mine, v_ref[window], none)
        scores = dot(query, k_ref[window], NT) * SCALE + pos_ref[head, :, :PAD].astype(f32)
        scores = scores + mask[window]
        expo = jnp.exp(scores - jnp.max(scores, -1, keepdims=True))
        attend = (expo * (1.0 / jnp.sum(expo, -1, keepdims=True))).astype(bf16)
        attend_ref[window, head, :, :PAD] = attend
        out_ref[window] = jnp.where(mine, dot(attend, value).astype(bf16), out_ref[window])
        return carry

    lax.fori_loop(0, 2 * GROUP, one, 0)


def block_of(part):
    return pl.BlockSpec((2, PAD, 128), lambda g: (0, 0, g + GROUP * part))


def attend_forward(qkv, position, row_ids, column_ids):
    return pl.pallas_call(
        attend_kernel,
        grid=(HEADS // GROUP,),
        out_shape=(
            jax.ShapeDtypeStruct((2, PAD, D), bf16),
            jax.ShapeDtypeStruct((2, HEADS, PAD, LANES), bf16),
        ),
        in_specs=[
            block_of(0),
            block_of(1),
            block_of(2),
            pl.BlockSpec((GROUP, PAD, LANES), lambda g: (g, 0, 0)),
            pl.BlockSpec((2, 1, LANES), lambda g: (0, 0, 0)),
            pl.BlockSpec((2, PAD, 1), lambda g: (0, 0, 0)),
        ],
        out_specs=(block_of(0), pl.BlockSpec((2, GROUP, PAD, LANES), lambda g: (0, g, 0, 0))),
        scratch_shapes=[pltpu.VMEM((2, PAD, PAD), f32)],
        compiler_params=pltpu.CompilerParams(vmem_limit_bytes=VMEM_LIMIT),
        name="attend_forward",
    )(qkv, qkv, qkv, position, row_ids, column_ids)


def back_kernel(q_ref, k_ref, v_ref, g_ref, attend_ref, dq_ref, dk_ref, dv_ref, pair_ref, first):
    head_of = lax.broadcasted_iota(jnp.int32, (1, 128), 1) // HD
    none = jnp.zeros((), bf16)

    def one(head, carry):
        mine = head_of == head
        for window in range(2):
            query = jnp.where(mine, q_ref[window], none)
            key = jnp.where(mine, k_ref[window], none)
            grad = jnp.where(mine, g_ref[window], none)
            attend_low = attend_ref[window, head, :, :PAD]
            attend = attend_low.astype(f32)
            grad_attend = dot(grad, v_ref[window], NT)
            inner = jnp.sum(attend * grad_attend, -1, keepdims=True)
            grad_scores = (attend * (grad_attend - inner)).astype(bf16)
            if window == 0:
                first[...] = grad_scores.astype(f32)
            else:
                total = first[...] + grad_scores.astype(f32)
                for tile in range(LANES // 128):
                    part = total[:, tile * 128 : (tile + 1) * 128]
                    if part.shape[1] < 128:
                        rest = jnp.zeros((PAD, 128 - part.shape[1]), f32)
                        part = jnp.concatenate([part, rest], 1)
                    pair_ref[tile, pl.ds(head, PAD, stride=GROUP), :] = part
            for ref, value in (
                (dq_ref, dot(grad_scores, key) * SCALE),
                (dk_ref, dot(grad_scores, query, TN) * SCALE),
                (dv_ref, dot(attend_low, grad, TN)),
            ):
                ref[window] = jnp.where(mine, value.astype(bf16), ref[window])
        return carry

    lax.fori_loop(0, GROUP, one, 0)


def attend_backward(qkv, grad_context, attend):
    tiles = LANES // 128
    return pl.pallas_call(
        back_kernel,
        grid=(HEADS // GROUP,),
        out_shape=(jax.ShapeDtypeStruct((2, PAD, D), bf16),) * 3
        + (jax.ShapeDtypeStruct((HEADS // GROUP, tiles, PAD * GROUP, 128), f32),),
        in_specs=[
            block_of(0),
            block_of(1),
            block_of(2),
            block_of(0),
            pl.BlockSpec((2, GROUP, PAD, LANES), lambda g: (0, g, 0, 0)),
        ],
        out_specs=(block_of(0),) * 3
        + (pl.BlockSpec((None, tiles, PAD * GROUP, 128), lambda g: (g, 0, 0, 0)),),
        scratch_shapes=[pltpu.VMEM((PAD, PAD), f32)],
        compiler_params=pltpu.CompilerParams(vmem_limit_bytes=VMEM_LIMIT),
        name="attend_backward",
    )(qkv, qkv, qkv, grad_context, attend)


BATCH = 8
SPAN = 256


def table_kernel(pair_ref, rel_ref, out_ref):
    out_ref[...] = jnp.zeros_like(out_ref)
    spans = out_ref.shape[0] // HEADS
    low_of = lax.broadcasted_iota(jnp.int32, (SPAN, LANES), 0).astype(f32).astype(bf16)

    def add(step, carry):
        left, right = [], []
        for k in range(BATCH):
            row = step * BATCH + k
            index = rel_ref[pl.ds(row, 1), :]
            low = (index & (SPAN - 1)).astype(f32).astype(bf16)
            high = jnp.broadcast_to((index // SPAN).astype(f32).astype(bf16), (HEADS, LANES))
            pairs = jnp.concatenate(
                [
                    jnp.concatenate(
                        [pair_ref[g, t, pl.ds(row * GROUP, GROUP), :] for t in range(LANES // 128)], 1
                    )
                    for g in range(HEADS // GROUP)
                ],
                0,
            ).astype(bf16)
            none = jnp.zeros_like(pairs)
            left.append(
                jnp.concatenate(
                    [jnp.where(high == jnp.asarray(s, bf16), pairs, none) for s in range(spans)], 0
                )
            )
            hit = low_of == jnp.broadcast_to(low, (SPAN, LANES))
            right.append(jnp.where(hit, jnp.ones((), bf16), jnp.zeros((), bf16)))
        out_ref[...] += dot(jnp.concatenate(left, 1), jnp.concatenate(right, 1), NT)
        return carry

    lax.fori_loop(0, PAD // BATCH, add, 0)


def table_gradient(pairs, rel):
    spans = -(-TABLE // SPAN)
    total = pl.pallas_call(
        table_kernel,
        out_shape=jax.ShapeDtypeStruct((spans * HEADS, SPAN), f32),
        in_specs=[pl.BlockSpec(memory_space=pltpu.VMEM)] * 2,
        out_specs=pl.BlockSpec(memory_space=pltpu.VMEM),
        compiler_params=pltpu.CompilerParams(vmem_limit_bytes=VMEM_LIMIT),
        name="table_gradient",
    )(pairs, rel)
    total = total.reshape(spans, HEADS, SPAN).transpose(0, 2, 1)
    return total.reshape(spans * SPAN, HEADS)[:TABLE]


def exchange(x):
    parts = []
    for piece, (_, _, padded, first) in enumerate(PIECES):
        part = x[:, first : first + padded]
        if piece:
            across = (0, 2, 1, 3)[piece]
            pairs = [(i, i ^ across) for i in range(lax.axis_size("shard"))]
            part = lax.ppermute(part, "shard", pairs)
        parts.append(part)
    return jnp.concatenate(parts, 1)


def norm_forward(rows, gain, shift):
    centre = rows - jnp.mean(rows, -1, keepdims=True)
    inverse = lax.rsqrt(jnp.mean(centre * centre, -1, keepdims=True) + 1e-05)
    normal = centre * inverse
    return (normal * gain.astype(jnp.float32) + shift.astype(jnp.float32), normal, inverse)


def norm_backward(grad_out, normal, inverse, gain):
    scaled = grad_out * gain.astype(jnp.float32)
    inner = (
        scaled
        - jnp.mean(scaled, -1, keepdims=True)
        - normal * jnp.mean(scaled * normal, -1, keepdims=True)
    )
    return (inverse * inner, jnp.sum(grad_out * normal, 0), jnp.sum(grad_out, 0))


def shards(
    tokens,
    region,
    rel_index,
    ln1_gain,
    ln1_shift,
    w_qkv,
    q_bias,
    v_bias,
    table,
    w_proj,
    proj_bias,
    ln2_gain,
    ln2_shift,
    w_fc1,
    fc1_bias,
    w_fc2,
    fc2_bias,
    cotangent,
):
    inputs = tokens.reshape(-1, D).astype(jnp.float32)
    gain_one, shift_one, whole_qkv, bias_query, bias_value, whole_table, whole_proj, bias_proj = (
        lax.all_gather(ln1_gain, "shard", axis=0, tiled=True),
        lax.all_gather(ln1_shift, "shard", axis=0, tiled=True),
        lax.all_gather(w_qkv, "shard", axis=0, tiled=True),
        lax.all_gather(q_bias, "shard", axis=0, tiled=True),
        lax.all_gather(v_bias, "shard", axis=0, tiled=True),
        lax.all_gather(table, "shard", axis=1, tiled=True),
        lax.all_gather(w_proj, "shard", axis=0, tiled=True),
        lax.all_gather(proj_bias, "shard", axis=0, tiled=True),
    )
    order = jnp.asarray(send_matrix(), bf16)
    normed, normal_one, inverse_one = norm_forward(inputs, gain_one, shift_one)
    rolled = exchange(dot(order, normed.astype(bf16)).astype(bf16).reshape(2, PAD, D))
    rolled = rolled.reshape(2 * PAD, D)
    mixed = jnp.dot(rolled, whole_qkv, preferred_element_type=f32)
    bias_mixed = jnp.concatenate((bias_query, jnp.zeros_like(bias_query), bias_value))
    qkv = (mixed + bias_mixed.astype(f32)).astype(bf16).reshape(2, PAD, 3 * D)
    labels = region.reshape(WT, WH, 2, WW).transpose(2, 0, 1, 3).reshape(2, WIN)
    labels = pieces_of(labels, 1, -1)
    row_ids = jnp.pad(labels, ((0, 0), (0, LANES - PAD)), constant_values=-1)[:, None]
    rel = pieces_of(pieces_of(rel_index, 0, 0), 1, 0)
    rel = jnp.pad(rel, ((0, 0), (0, LANES - PAD)))
    position = make_position(whole_table, rel)
    contexts, attend = attend_forward(qkv, position, row_ids, labels[:, :, None])
    unrolled = dot(order, exchange(contexts).reshape(2 * PAD, D), TN).astype(bf16)
    middle = (
        inputs
        + jnp.dot(unrolled, whole_proj, preferred_element_type=jnp.float32)
        + bias_proj.astype(jnp.float32)
    )
    gain_two, shift_two, whole_fc1, bias_fc1, whole_fc2, bias_fc2 = (
        lax.all_gather(ln2_gain, "shard", axis=0, tiled=True),
        lax.all_gather(ln2_shift, "shard", axis=0, tiled=True),
        lax.all_gather(w_fc1, "shard", axis=0, tiled=True),
        lax.all_gather(fc1_bias, "shard", axis=0, tiled=True),
        lax.all_gather(w_fc2, "shard", axis=0, tiled=True),
        lax.all_gather(fc2_bias, "shard", axis=0, tiled=True),
    )
    normed_two, normal_two, inverse_two = norm_forward(middle, gain_two, shift_two)
    normed_low = normed_two.astype(jnp.bfloat16)
    hidden = jnp.dot(normed_low, whole_fc1, preferred_element_type=jnp.float32) + bias_fc1.astype(
        jnp.float32
    )
    active = jax.nn.gelu(hidden, approximate=False).astype(jnp.bfloat16)
    result = (
        middle
        + jnp.dot(active, whole_fc2, preferred_element_type=jnp.float32)
        + bias_fc2.astype(jnp.float32)
    )
    output = result.astype(jnp.bfloat16).reshape(tokens.shape)
    grad_out = cotangent.reshape(-1, D)
    grad_w_fc2 = jnp.einsum("rf,rd->fd", active, grad_out, preferred_element_type=jnp.float32)
    grad_fc2_bias = jnp.sum(grad_out.astype(jnp.float32), 0)
    slope = (
        0.5 * (1.0 + lax.erf(hidden * 0.7071067811865476))
        + hidden * jnp.exp(-0.5 * hidden * hidden) * 0.3989422804014327
    )
    grad_active = jnp.einsum("rd,fd->rf", grad_out, whole_fc2, preferred_element_type=jnp.float32)
    grad_hidden = (grad_active * slope).astype(jnp.bfloat16)
    grad_w_fc1 = jnp.einsum(
        "rd,rf->df", normed_low, grad_hidden, preferred_element_type=jnp.float32
    )
    grad_fc1_bias = jnp.sum(grad_hidden.astype(jnp.float32), 0)
    grad_normed_two = jnp.einsum(
        "rf,df->rd", grad_hidden, whole_fc1, preferred_element_type=jnp.float32
    )
    grad_inner_two, grad_ln2_gain, grad_ln2_shift = norm_backward(
        grad_normed_two, normal_two, inverse_two, gain_two
    )
    grad_middle = grad_out.astype(jnp.float32) + grad_inner_two
    part_a, part_b, part_c, part_d, part_e, part_f = (
        lax.psum_scatter(
            grad_ln2_gain.astype(jnp.bfloat16), "shard", scatter_dimension=0, tiled=True
        ).astype(jnp.float32),
        lax.psum_scatter(
            grad_ln2_shift.astype(jnp.bfloat16), "shard", scatter_dimension=0, tiled=True
        ).astype(jnp.float32),
        lax.psum_scatter(
            grad_w_fc1.astype(jnp.bfloat16), "shard", scatter_dimension=0, tiled=True
        ).astype(jnp.float32),
        lax.psum_scatter(
            grad_fc1_bias.astype(jnp.bfloat16), "shard", scatter_dimension=0, tiled=True
        ).astype(jnp.float32),
        lax.psum_scatter(
            grad_w_fc2.astype(jnp.bfloat16), "shard", scatter_dimension=0, tiled=True
        ).astype(jnp.float32),
        lax.psum_scatter(
            grad_fc2_bias.astype(jnp.bfloat16), "shard", scatter_dimension=0, tiled=True
        ).astype(jnp.float32),
    )
    grad_ln2_gain, grad_ln2_shift, grad_w_fc1, grad_fc1_bias, grad_w_fc2, grad_fc2_bias = lax.psum(
        (part_a, part_b, part_c, part_d, part_e, part_f), "rep"
    )
    grad_branch = grad_middle.astype(jnp.bfloat16)
    grad_w_proj = jnp.einsum("rd,re->de", unrolled, grad_branch, preferred_element_type=jnp.float32)
    grad_proj_bias = jnp.sum(grad_branch.astype(jnp.float32), 0)
    grad_unrolled = jnp.einsum(
        "re,de->rd", grad_branch, whole_proj, preferred_element_type=jnp.float32
    ).astype(jnp.bfloat16)
    grad_context = exchange(dot(order, grad_unrolled).astype(bf16).reshape(2, PAD, D))
    grad_queries, grad_keys, grad_values, pairs = attend_backward(qkv, grad_context, attend)
    grad_table = table_gradient(pairs, rel)
    grad_qkv = jnp.concatenate((grad_queries, grad_keys, grad_values), 2).reshape(2 * PAD, 3 * D)
    grad_w_qkv = jnp.einsum("rd,re->de", rolled, grad_qkv, preferred_element_type=jnp.float32)
    grad_q_bias = jnp.sum(grad_qkv[:, :D].astype(jnp.float32), 0)
    grad_v_bias = jnp.sum(grad_qkv[:, 2 * D :].astype(jnp.float32), 0)
    grad_rolled = jnp.einsum(
        "re,de->rd", grad_qkv, whole_qkv, preferred_element_type=jnp.float32
    ).astype(jnp.bfloat16)
    grad_normed = dot(order, exchange(grad_rolled.reshape(2, PAD, D)).reshape(2 * PAD, D), TN)
    grad_inner_one, grad_ln1_gain, grad_ln1_shift = norm_backward(
        grad_normed, normal_one, inverse_one, gain_one
    )
    grad_tokens = (grad_middle + grad_inner_one).reshape(tokens.shape)
    part_a, part_b, part_c, part_d, part_e, part_f, part_g, part_h = (
        lax.psum_scatter(
            grad_ln1_gain.astype(jnp.bfloat16), "shard", scatter_dimension=0, tiled=True
        ).astype(jnp.float32),
        lax.psum_scatter(
            grad_ln1_shift.astype(jnp.bfloat16), "shard", scatter_dimension=0, tiled=True
        ).astype(jnp.float32),
        lax.psum_scatter(
            grad_w_qkv.astype(jnp.bfloat16), "shard", scatter_dimension=0, tiled=True
        ).astype(jnp.float32),
        lax.psum_scatter(
            grad_q_bias.astype(jnp.bfloat16), "shard", scatter_dimension=0, tiled=True
        ).astype(jnp.float32),
        lax.psum_scatter(
            grad_v_bias.astype(jnp.bfloat16), "shard", scatter_dimension=0, tiled=True
        ).astype(jnp.float32),
        lax.psum_scatter(
            grad_table.astype(jnp.bfloat16), "shard", scatter_dimension=1, tiled=True
        ).astype(jnp.float32),
        lax.psum_scatter(
            grad_w_proj.astype(jnp.bfloat16), "shard", scatter_dimension=0, tiled=True
        ).astype(jnp.float32),
        lax.psum_scatter(
            grad_proj_bias.astype(jnp.bfloat16), "shard", scatter_dimension=0, tiled=True
        ).astype(jnp.float32),
    )
    (
        grad_ln1_gain,
        grad_ln1_shift,
        grad_w_qkv,
        grad_q_bias,
        grad_v_bias,
        grad_table,
        grad_w_proj,
        grad_proj_bias,
    ) = lax.psum((part_a, part_b, part_c, part_d, part_e, part_f, part_g, part_h), "rep")
    return (
        output,
        grad_tokens,
        grad_ln1_gain,
        grad_ln1_shift,
        grad_w_qkv,
        grad_q_bias,
        grad_v_bias,
        grad_table,
        grad_w_proj,
        grad_proj_bias,
        grad_ln2_gain,
        grad_ln2_shift,
        grad_w_fc1,
        grad_fc1_bias,
        grad_w_fc2,
        grad_fc2_bias,
    )


def solution(mesh):
    return jax.shard_map(
        shards,
        mesh=mesh,
        in_specs=(
            P("rep", "shard", None, None),
            P("shard", None),
            P(),
            P("shard"),
            P("shard"),
            P("shard", None),
            P("shard"),
            P("shard"),
            P(None, "shard"),
            P("shard", None),
            P("shard"),
            P("shard"),
            P("shard"),
            P("shard", None),
            P("shard"),
            P("shard", None),
            P("shard"),
            P("rep", "shard", None, None),
        ),
        out_specs=(
            P("rep", "shard", None, None),
            P("rep", "shard", None, None),
            P("shard"),
            P("shard"),
            P("shard", None),
            P("shard"),
            P("shard"),
            P(None, "shard"),
            P("shard", None),
            P("shard"),
            P("shard"),
            P("shard"),
            P("shard", None),
            P("shard"),
            P("shard", None),
            P("shard"),
        ),
        check_vma=False,
    )
```

```python
import functools

import jax
import jax.numpy as jnp
import numpy as np
from jax import lax
from jax.experimental import pallas as pl
from jax.experimental.pallas import tpu as pltpu
from jax.sharding import PartitionSpec as P

D = 512
HEADS = 16
HD = 32
WT = 8
WH = 7
WW = 7
WIN = 392
TABLE = 2535
PAD = 416
LANES = 512
GROUP = 4
CHUNKS = 20
SCALE = HD ** (-0.5)
NN = (((1,), (0,)), ((), ()))
NT = (((1,), (1,)), ((), ()))
TN = (((0,), (0,)), ((), ()))
VMEM_LIMIT = 60 * 2**20
f32 = jnp.float32
bf16 = jnp.bfloat16

PIECES = (
    ((0, 4), (0, 4), 112, 0),
    ((4, 8), (0, 4), 112, 112),
    ((0, 4), (4, 7), 96, 224),
    ((4, 8), (4, 7), 96, 320),
)


def send_matrix():
    matrix = np.zeros((2 * PAD, WT * WH * 2 * WW), np.float32)
    for window in range(2):
        for (t0, t1), (h0, h1), _, first in PIECES:
            row = window * PAD + first
            for t in range(t0, t1):
                for h in range(h0, h1):
                    for w in range(WW):
                        column = (window * WW + w + WW // 2) % (2 * WW)
                        source = ((t + 4) % WT * WH + (h + 3) % WH) * 2 * WW + column
                        matrix[row, source] = 1.0
                        row += 1
    return matrix


def spread_matrix():
    source = np.arange(WIN).reshape(WT, WH, WW)
    matrix = np.zeros((PAD, WIN), np.float32)
    for (t0, t1), (h0, h1), _, first in PIECES:
        tokens = source[t0:t1, h0:h1].reshape(-1)
        matrix[first + np.arange(tokens.size), tokens] = 1.0
    return matrix


def pieces_of(array, axis, fill):
    shape = array.shape
    split = array.reshape(shape[:axis] + (WT, WH, WW) + shape[axis + 1 :])
    parts = []
    for (t0, t1), (h0, h1), padded, _ in PIECES:
        part = lax.slice_in_dim(lax.slice_in_dim(split, t0, t1, axis=axis), h0, h1, axis=axis + 1)
        length = (t1 - t0) * (h1 - h0) * WW
        part = part.reshape(shape[:axis] + (length,) + shape[axis + 1 :])
        widths = [(0, 0, 0)] * len(shape)
        widths[axis] = (0, padded - length, 0)
        parts.append(lax.pad(part, jnp.asarray(fill, array.dtype), widths))
    return jnp.concatenate(parts, axis)


def dot(a, b, dims=NN):
    return lax.dot_general(a, b, dims, preferred_element_type=f32)


def block_of(part):
    return pl.BlockSpec((2, PAD, 128), lambda g: (0, 0, g + GROUP * part))


def back_kernel(q_ref, k_ref, v_ref, g_ref, attend_ref, dq_ref, dk_ref, dv_ref, pair_ref, first):
    head_of = lax.broadcasted_iota(jnp.int32, (1, 128), 1) // HD
    none = jnp.zeros((), bf16)

    def one(head, carry):
        mine = head_of == head
        for window in range(2):
            query = jnp.where(mine, q_ref[window], none)
            key = jnp.where(mine, k_ref[window], none)
            grad = jnp.where(mine, g_ref[window], none)
            attend_low = attend_ref[window, head, :, :PAD]
            attend = attend_low.astype(f32)
            grad_attend = dot(grad, v_ref[window], NT)
            inner = jnp.sum(attend * grad_attend, -1, keepdims=True)
            grad_scores = (attend * (grad_attend - inner)).astype(bf16)
            if window == 0:
                first[...] = grad_scores.astype(f32)
            else:
                total = first[...] + grad_scores.astype(f32)
                for tile in range(LANES // 128):
                    part = total[:, tile * 128 : (tile + 1) * 128]
                    if part.shape[1] < 128:
                        rest = jnp.zeros((PAD, 128 - part.shape[1]), f32)
                        part = jnp.concatenate([part, rest], 1)
                    pair_ref[tile, pl.ds(head, PAD, stride=GROUP), :] = part
            for ref, value in (
                (dq_ref, dot(grad_scores, key) * SCALE),
                (dk_ref, dot(grad_scores, query, TN) * SCALE),
                (dv_ref, dot(attend_low, grad, TN)),
            ):
                ref[window] = jnp.where(mine, value.astype(bf16), ref[window])
        return carry

    lax.fori_loop(0, GROUP, one, 0)


def attend_backward(qkv, grad_context, attend):
    tiles = LANES // 128
    return pl.pallas_call(
        back_kernel,
        grid=(HEADS // GROUP,),
        out_shape=(jax.ShapeDtypeStruct((2, PAD, D), bf16),) * 3
        + (jax.ShapeDtypeStruct((HEADS // GROUP, tiles, PAD * GROUP, 128), f32),),
        in_specs=[
            block_of(0),
            block_of(1),
            block_of(2),
            block_of(0),
            pl.BlockSpec((2, GROUP, PAD, LANES), lambda g: (0, g, 0, 0)),
        ],
        out_specs=(block_of(0),) * 3
        + (pl.BlockSpec((None, tiles, PAD * GROUP, 128), lambda g: (g, 0, 0, 0)),),
        scratch_shapes=[pltpu.VMEM((PAD, PAD), f32)],
        compiler_params=pltpu.CompilerParams(vmem_limit_bytes=VMEM_LIMIT),
        name="attend_backward",
    )(qkv, qkv, qkv, grad_context, attend)


BATCH = 8
SPAN = 256


def table_kernel(pair_ref, rel_ref, out_ref):
    out_ref[...] = jnp.zeros_like(out_ref)
    spans = out_ref.shape[0] // HEADS
    low_of = lax.broadcasted_iota(jnp.int32, (SPAN, LANES), 0).astype(f32).astype(bf16)

    def add(step, carry):
        left, right = [], []
        for k in range(BATCH):
            row = step * BATCH + k
            index = rel_ref[pl.ds(row, 1), :]
            low = (index & (SPAN - 1)).astype(f32).astype(bf16)
            high = jnp.broadcast_to((index // SPAN).astype(f32).astype(bf16), (HEADS, LANES))
            pairs = jnp.concatenate(
                [
                    jnp.concatenate(
                        [pair_ref[g, t, pl.ds(row * GROUP, GROUP), :] for t in range(LANES // 128)], 1
                    )
                    for g in range(HEADS // GROUP)
                ],
                0,
            ).astype(bf16)
            none = jnp.zeros_like(pairs)
            left.append(
                jnp.concatenate(
                    [jnp.where(high == jnp.asarray(s, bf16), pairs, none) for s in range(spans)], 0
                )
            )
            hit = low_of == jnp.broadcast_to(low, (SPAN, LANES))
            right.append(jnp.where(hit, jnp.ones((), bf16), jnp.zeros((), bf16)))
        out_ref[...] += dot(jnp.concatenate(left, 1), jnp.concatenate(right, 1), NT)
        return carry

    lax.fori_loop(0, PAD // BATCH, add, 0)


def table_gradient(pairs, rel):
    spans = -(-TABLE // SPAN)
    total = pl.pallas_call(
        table_kernel,
        out_shape=jax.ShapeDtypeStruct((spans * HEADS, SPAN), f32),
        in_specs=[pl.BlockSpec(memory_space=pltpu.VMEM)] * 2,
        out_specs=pl.BlockSpec(memory_space=pltpu.VMEM),
        compiler_params=pltpu.CompilerParams(vmem_limit_bytes=VMEM_LIMIT),
        name="table_gradient",
    )(pairs, rel)
    total = total.reshape(spans, HEADS, SPAN).transpose(0, 2, 1)
    return total.reshape(spans * SPAN, HEADS)[:TABLE]


def exchange(x):
    parts = []
    for piece, (_, _, padded, first) in enumerate(PIECES):
        part = x[:, first : first + padded]
        if piece:
            across = (0, 2, 1, 3)[piece]
            pairs = [(i, i ^ across) for i in range(lax.axis_size("shard"))]
            part = lax.ppermute(part, "shard", pairs)
        parts.append(part)
    return jnp.concatenate(parts, 1)


MESH = pl.DeviceIdType.MESH
PARTS = 8
FIRST_ROWS = tuple(first for _, _, _, first in PIECES)
LENGTHS = tuple(padded for _, _, padded, _ in PIECES)
ACROSS = (0, 2, 1, 3)
LN1_GAIN, LN1_SHIFT, Q_BIAS, V_BIAS, PROJ_BIAS, LN2_GAIN, LN2_SHIFT, FC2_BIAS, FC1_BIAS = range(9)
SMALL = 16


def place():
    rep, shard = lax.axis_index("rep"), lax.axis_index("shard")
    return rep, shard, lax.rem(rep, 2), lax.rem(rep // 2, 2), lax.rem(rep // 4, 2)


def flip(rep, bit):
    low = lax.rem(rep // (1 << bit), 2)
    return rep + (1 - 2 * low) * (1 << bit)


def remote(src, dst, send, recv, rep, shard):
    return pltpu.make_async_remote_copy(
        src_ref=src,
        dst_ref=dst,
        send_sem=send,
        recv_sem=recv,
        device_id={"rep": rep, "shard": shard},
        device_id_type=MESH,
    )


def greet(peers):
    barrier = pltpu.get_barrier_semaphore()
    for rep, shard in peers:
        pl.semaphore_signal(
            barrier, inc=1, device_id={"rep": rep, "shard": shard}, device_id_type=MESH
        )
    pl.semaphore_wait(barrier, len(peers))


def peers_of(rep, shard):
    return [(rep, lax.rem(shard + k, 4)) for k in (1, 2, 3)] + [
        (flip(rep, bit), shard) for bit in (0, 1, 2)
    ]


def quarter_across(shard, bits):
    low, high = lax.rem(shard, 2), shard // 2
    if bits & 1:
        low = 1 - low
    if bits & 2:
        high = 1 - high
    return high * 2 + low


def pieces_to(source, target, send, recv, rep, shard, window, columns=None):
    copies = []
    for piece in (1, 2, 3):
        rows = pl.ds(
            pl.multiple_of(window * PAD + FIRST_ROWS[piece], 16), LENGTHS[piece]
        )
        at = (rows,) if columns is None else (rows, columns)
        copies.append(
            remote(
                source.at[at],
                target.at[at],
                send(piece - 1),
                recv(piece - 1),
                rep,
                quarter_across(shard, ACROSS[piece]),
            )
        )
    return copies


def norm_rows(rows):
    centre = rows - jnp.mean(rows, -1, keepdims=True)
    inverse = lax.rsqrt(jnp.mean(centre * centre, -1, keepdims=True) + 1e-05)
    return centre * inverse, inverse


def small_row(ref, row):
    return jnp.concatenate([ref[s, row : row + 1, :] for s in range(4)], 1)


Z_PHASE, X_PHASE, Y_PHASE, CORE_PHASE = range(4)


def front_kernel(
    tokens,
    order,
    spread,
    small,
    table,
    row_ids,
    rel,
    qkv_part,
    proj_part,
    fc1_part,
    fc2_part,
    qkv_whole,
    proj_whole,
    fc1_whole,
    fc2_whole,
    small_out,
    rolled_out,
    mixed_out,
    attend_out,
    back_out,
    rel_out,
    small_all,
    table_all,
    table_wide,
    normed,
    outgoing,
    rolled,
    weights,
    mixed,
    index,
    bias,
    mask,
    attend,
    contexts,
    gather_send,
    gather_recv,
    small_send,
    small_recv,
    bias_send,
    bias_recv,
    piece_send,
    piece_recv,
    back_send,
    back_recv,
    local,
    attend_sem,
):
    rep, shard, core, x_bit, y_bit = place()
    greet(peers_of(rep, shard))
    parts = (qkv_part, proj_part, fc1_part, fc2_part)
    wholes = (qkv_whole, proj_whole, fc1_whole, fc2_whole)

    def gather(matrix, phase):
        copies = []
        for k in (1, 2, 3):
            at = lax.rem(shard + k, 4)
            whole = wholes[matrix]
            if phase == Z_PHASE:
                copies.append(
                    remote(
                        parts[matrix].at[y_bit, x_bit, core],
                        whole.at[shard, y_bit, x_bit, core],
                        gather_send.at[matrix, phase, k - 1],
                        gather_recv.at[matrix, phase, 3 - k],
                        rep,
                        at,
                    )
                )
                continue
            if phase == X_PHASE:
                block, partner = whole.at[at, y_bit, x_bit, core], flip(rep, 1)
            elif phase == Y_PHASE:
                block, partner = whole.at[at, y_bit, :, core], flip(rep, 2)
            else:
                block, partner = whole.at[at, :, :, core], flip(rep, 0)
            copies.append(
                remote(
                    block,
                    block,
                    gather_send.at[matrix, phase, k - 1],
                    gather_recv.at[matrix, phase, k - 1],
                    partner,
                    shard,
                )
            )
        return copies

    def start(matrix, phase):
        for copy in gather(matrix, phase):
            copy.start()

    def arrived(matrix, phase):
        for copy in gather(matrix, phase):
            copy.wait_recv()

    def small_copies():
        copies = []
        for k in (1, 2, 3):
            for n, ref in enumerate((table_all, small_all)):
                copies.append(
                    remote(
                        ref.at[shard],
                        ref.at[shard],
                        small_send.at[n, k - 1],
                        small_recv.at[n, 3 - k],
                        rep,
                        lax.rem(shard + k, 4),
                    )
                )
        return copies

    small_all[shard] = small[...]
    table_all[shard] = table[...]
    for copy in small_copies():
        copy.start()
    start(0, Z_PHASE)
    own = [
        pltpu.make_async_copy(parts[m], wholes[m].at[shard], local.at[m]) for m in range(4)
    ]
    for copy in own:
        copy.start()

    rel_index = rel[...]
    digits = (rel_index // 256).astype(f32).astype(bf16), (rel_index & 255).astype(f32).astype(bf16)
    moved = []
    for digit in digits:
        half = dot(spread[...], digit).astype(bf16)
        moved.append(dot(half, spread[...], NT).astype(jnp.int32))
    index[:, :PAD] = moved[0] * 256 + moved[1]
    index[:, PAD:] = jnp.zeros((PAD, LANES - PAD), jnp.int32)

    ids = lax.broadcasted_iota(jnp.int32, (8, LANES), 0)
    for window in range(2):
        kinds = jnp.where(row_ids[window] + 1 == ids, 1.0, 0.0).astype(bf16)[:, :PAD]
        mask[window] = (dot(kinds, kinds, TN) - 1.0) * 1e30

    for copy in small_copies():
        copy.wait_recv()

    gain, shift = small_row(small_all, LN1_GAIN), small_row(small_all, LN1_SHIFT)

    def norm_step(step, carry):
        rows = pl.ds(pl.multiple_of(step * 112, 16), 112)
        normal, _ = norm_rows(tokens[rows, :].astype(f32))
        normed[rows, :] = (normal * gain.astype(f32) + shift.astype(f32)).astype(bf16)
        return carry

    lax.fori_loop(0, 7, norm_step, 0)

    def order_step(step, carry):
        rows = pl.ds(pl.multiple_of(step * 208, 16), 208)
        outgoing[rows, :] = dot(order[rows, :], normed[...]).astype(bf16)
        return carry

    lax.fori_loop(0, 4, order_step, 0)

    def roll_copies(window):
        return pieces_to(
            outgoing,
            rolled,
            lambda n: piece_send.at[window, n],
            lambda n: piece_recv.at[window, n],
            rep,
            shard,
            window,
        )

    for window in range(2):
        for copy in roll_copies(window):
            copy.start()
        rows = slice(window * PAD, window * PAD + LENGTHS[0])
        rolled[rows, :] = outgoing[rows, :]
    for matrix in (1, 2, 3):
        start(matrix, Z_PHASE)

    for chunk in range(CHUNKS):
        for head in range(HEADS // 2):
            row = (head % 4) * CHUNKS + chunk
            table_wide[chunk, head] = jnp.broadcast_to(
                table_all[2 * core + head // 4, row : row + 1, :], (8, 128)
            )
    mine = core * (HEADS // 2)

    def bias_copy(rows, step):
        block = bias.at[pl.ds(mine, HEADS // 2), rows]
        return remote(block, block, bias_send.at[step], bias_recv.at[step], flip(rep, 0), shard)

    def on_the_way(step, table_of_steps):
        for when, actions in table_of_steps.items():

            @pl.when(step == when)
            def _():
                for action, matrix, phase in actions:
                    action(matrix, phase)

    def advance(matrix, phase):
        arrived(matrix, phase)
        if phase < CORE_PHASE:
            start(matrix, phase + 1)

    schedule = {
        4: [(advance, 0, Z_PHASE)],
        8: [(advance, 0, X_PHASE)],
        14: [(advance, 0, Y_PHASE)],
        16: [(advance, 1, Z_PHASE)],
        20: [(advance, 1, X_PHASE), (advance, 2, Z_PHASE)],
        24: [(advance, 3, Z_PHASE)],
    }
    later = {
        1: [(advance, 1, Y_PHASE)],
        4: [(advance, 2, X_PHASE)],
        8: [(advance, 3, X_PHASE)],
        14: [(advance, 2, Y_PHASE)],
        20: [(advance, 3, Y_PHASE)],
    }

    def bias_step(step, carry):
        on_the_way(step, schedule)
        rows = pl.ds(pl.multiple_of(step * 16, 16), 16)
        for tile in range(LANES // 128):
            lanes = slice(tile * 128, (tile + 1) * 128)
            here = index[rows, lanes]
            halves = [(here[s : s + 8] & 127, here[s : s + 8] >> 7) for s in (0, 8)]
            found = [[None, None] for _ in range(HEADS // 2)]
            for chunk in range(CHUNKS):
                for s, (low, high) in enumerate(halves):
                    hit = high == chunk
                    for head in range(HEADS // 2):
                        value = jnp.take_along_axis(table_wide[chunk, head], low, axis=1)
                        if chunk:
                            value = jnp.where(hit, value, found[head][s])
                        found[head][s] = value
            for head in range(HEADS // 2):
                bias[mine + head, rows, lanes] = jnp.concatenate(found[head], 0).astype(bf16)
        bias_copy(rows, step).start()
        return carry

    lax.fori_loop(0, PAD // 16, bias_step, 0)

    arrived(0, CORE_PHASE)
    own[0].wait()
    fetch = pltpu.make_async_copy(qkv_whole, weights, local.at[4])
    fetch.start()
    fetch.wait()
    q_bias, v_bias = small_row(small_all, Q_BIAS), small_row(small_all, V_BIAS)
    mixed_bias = jnp.concatenate([q_bias, jnp.zeros_like(q_bias), v_bias], 1).astype(f32)
    for window in range(2):
        for copy in roll_copies(window):
            copy.wait_recv()
        span = slice(window * PAD, (window + 1) * PAD)
        for part in range(3):
            lanes = slice(part * D, (part + 1) * D)
            got = dot(rolled[span, :], weights[...].reshape(D, 3 * D)[:, lanes])
            mixed[span, lanes] = (got + mixed_bias[:, lanes]).astype(bf16)
    keep = [
        pltpu.make_async_copy(rolled, rolled_out, local.at[4]),
        pltpu.make_async_copy(mixed, mixed_out, local.at[5]),
        pltpu.make_async_copy(index, rel_out, local.at[6]),
        pltpu.make_async_copy(small_all, small_out, local.at[7]),
    ]
    for copy in keep:
        copy.start()

    def bias_wait(step, carry):
        bias_copy(pl.ds(pl.multiple_of(step * 16, 16), 16), step).wait_recv()
        return carry

    lax.fori_loop(0, PAD // 16, bias_wait, 0)

    head_of = lax.broadcasted_iota(jnp.int32, (1, 128), 1) // HD
    none = jnp.zeros((), bf16)

    def attend_copy(step):
        window, head, slot = step // HEADS, lax.rem(step, HEADS), lax.rem(step, 2)
        return pltpu.make_async_copy(
            attend.at[slot], attend_out.at[window, head], attend_sem.at[slot]
        )

    def back_copies(step):
        window, group = step // HEADS, lax.rem(step // GROUP, HEADS // GROUP)
        lanes = pl.ds(pl.multiple_of(group * 128, 128), 128)
        return pieces_to(
            contexts,
            back_out,
            lambda n: back_send.at[window, group, n],
            lambda n: back_recv.at[window, group, n],
            rep,
            shard,
            window,
            lanes,
        )

    def attend_step(step, carry):
        on_the_way(step, later)
        window, head = step // HEADS, lax.rem(step, HEADS)
        group, member, slot = head // GROUP, lax.rem(head, GROUP), lax.rem(step, 2)
        rows = pl.ds(pl.multiple_of(window * PAD, 16), PAD)

        def lanes(part):
            return pl.ds(pl.multiple_of(part * D + group * 128, 128), 128)

        own_lanes = head_of == member
        query = jnp.where(own_lanes, mixed[rows, lanes(0)], none)
        value = jnp.where(own_lanes, mixed[rows, lanes(2)], none)
        scores = dot(query, mixed[rows, lanes(1)], NT) * SCALE + bias[head, :, :PAD].astype(f32)
        scores = scores + mask[window]
        expo = jnp.exp(scores - jnp.max(scores, -1, keepdims=True))
        weight = (expo * (1.0 / jnp.sum(expo, -1, keepdims=True))).astype(bf16)

        @pl.when(step >= 2)
        def _():
            attend_copy(step - 2).wait()

        attend[slot, :, :PAD] = weight
        attend_copy(step).start()
        result = dot(weight, value).astype(bf16)
        contexts[rows, lanes(0)] = jnp.where(own_lanes, result, contexts[rows, lanes(0)])

        @pl.when(member == GROUP - 1)
        def _():
            for copy in back_copies(step):
                copy.start()

        return carry

    lax.fori_loop(0, 2 * HEADS, attend_step, 0)

    stay = [
        pltpu.make_async_copy(
            contexts.at[pl.ds(w * PAD, LENGTHS[0])],
            back_out.at[pl.ds(w * PAD, LENGTHS[0])],
            local.at[8 + w],
        )
        for w in range(2)
    ]
    for copy in stay:
        copy.start()
    for matrix in (1, 2, 3):
        arrived(matrix, CORE_PHASE)
    attend_copy(2 * HEADS - 2).wait()
    attend_copy(2 * HEADS - 1).wait()

    def back_wait(step, carry):
        for copy in back_copies(step * GROUP):
            copy.wait()
        return carry

    lax.fori_loop(0, 2 * HEADS // GROUP, back_wait, 0)

    def bias_sent(step, carry):
        bias_copy(pl.ds(pl.multiple_of(step * 16, 16), 16), step).wait_send()
        return carry

    lax.fori_loop(0, PAD // 16, bias_sent, 0)
    for copy in small_copies():
        copy.wait_send()
    for window in range(2):
        for copy in roll_copies(window):
            copy.wait_send()
    for matrix in range(4):
        for phase in range(4):
            for copy in gather(matrix, phase):
                copy.wait_send()
    for copy in own[1:] + keep + stay:
        copy.wait()


def front(tokens, small, table, row_ids, rel_index, w_qkv, w_proj, w_fc1, w_fc2):
    anywhere, inside = pl.BlockSpec(memory_space=pl.ANY), pl.BlockSpec(memory_space=pltpu.VMEM)
    cut = (2, 2, 2)
    weights = [
        w.reshape(cut + (w.shape[0] // PARTS, w.shape[1])) for w in (w_qkv, w_proj, w_fc1, w_fc2)
    ]
    wholes = [jax.ShapeDtypeStruct((4,) + w.shape, bf16) for w in weights]
    dma = pltpu.SemaphoreType.DMA
    results = pl.pallas_call(
        front_kernel,
        out_shape=(
            *wholes,
            jax.ShapeDtypeStruct((4, SMALL, 128), bf16),
            jax.ShapeDtypeStruct((2 * PAD, D), bf16),
            jax.ShapeDtypeStruct((2 * PAD, 3 * D), bf16),
            jax.ShapeDtypeStruct((2, HEADS, PAD, LANES), bf16),
            jax.ShapeDtypeStruct((2 * PAD, D), bf16),
            jax.ShapeDtypeStruct((PAD, LANES), jnp.int32),
        ),
        in_specs=[inside] * 7 + [anywhere] * 4,
        out_specs=(anywhere,) * 10,
        scratch_shapes=[
            pltpu.VMEM((4, SMALL, 128), bf16),
            pltpu.VMEM((4, GROUP * CHUNKS, 128), f32),
            pltpu.VMEM((CHUNKS, HEADS // 2, 8, 128), f32),
            pltpu.VMEM(tokens.shape, bf16),
            pltpu.VMEM((2 * PAD, D), bf16),
            pltpu.VMEM((2 * PAD, D), bf16),
            pltpu.VMEM(wholes[0].shape, bf16),
            pltpu.VMEM((2 * PAD, 3 * D), bf16),
            pltpu.VMEM((PAD, LANES), jnp.int32),
            pltpu.VMEM((HEADS, PAD, LANES), bf16),
            pltpu.VMEM((2, PAD, PAD), f32),
            pltpu.VMEM((2, PAD, LANES), bf16),
            pltpu.VMEM((2 * PAD, D), bf16),
            dma((4, 4, 3)),
            dma((4, 4, 3)),
            dma((2, 3)),
            dma((2, 3)),
            dma((PAD // 16,)),
            dma((PAD // 16,)),
            dma((2, 3)),
            dma((2, 3)),
            dma((2, HEADS // GROUP, 3)),
            dma((2, HEADS // GROUP, 3)),
            dma((10,)),
            dma((2,)),
        ],
        compiler_params=pltpu.CompilerParams(
            vmem_limit_bytes=VMEM_LIMIT, collective_id=0, has_side_effects=True
        ),
        name="front",
    )(
        tokens,
        jnp.asarray(send_matrix(), bf16),
        jnp.asarray(spread_matrix(), bf16),
        small,
        table,
        row_ids,
        rel_index,
        *weights,
    )
    whole = [w.reshape(-1, w.shape[-1]) for w in results[:4]]
    return (*whole, *results[4:])


def norm_forward(rows, gain, shift):
    centre = rows - jnp.mean(rows, -1, keepdims=True)
    inverse = lax.rsqrt(jnp.mean(centre * centre, -1, keepdims=True) + 1e-05)
    normal = centre * inverse
    return (normal * gain.astype(jnp.float32) + shift.astype(jnp.float32), normal, inverse)


def norm_backward(grad_out, normal, inverse, gain):
    scaled = grad_out * gain.astype(jnp.float32)
    inner = (
        scaled
        - jnp.mean(scaled, -1, keepdims=True)
        - normal * jnp.mean(scaled * normal, -1, keepdims=True)
    )
    return (inverse * inner, jnp.sum(grad_out * normal, 0), jnp.sum(grad_out, 0))


def shards(
    tokens,
    region,
    rel_index,
    ln1_gain,
    ln1_shift,
    w_qkv,
    q_bias,
    v_bias,
    table,
    w_proj,
    proj_bias,
    ln2_gain,
    ln2_shift,
    w_fc1,
    fc1_bias,
    w_fc2,
    fc2_bias,
    cotangent,
):
    inputs = tokens.reshape(-1, D).astype(jnp.float32)
    small = jnp.concatenate(
        (ln1_gain, ln1_shift, q_bias, v_bias, proj_bias, ln2_gain, ln2_shift, fc2_bias, fc1_bias)
    ).reshape(-1, 128)
    small = jnp.pad(small, ((0, SMALL - small.shape[0]), (0, 0)))
    chunks = jnp.pad(table.astype(f32).T, ((0, 0), (0, CHUNKS * 128 - TABLE)))
    labels = region.reshape(WT, WH, 2, WW).transpose(2, 0, 1, 3).reshape(2, WIN)
    labels = pieces_of(labels, 1, -1)
    row_ids = jnp.pad(labels, ((0, 0), (0, LANES - PAD)), constant_values=-1)[:, None]
    (
        whole_qkv,
        whole_proj,
        whole_fc1,
        whole_fc2,
        small,
        rolled,
        qkv,
        attend,
        contexts,
        rel,
    ) = front(
        tokens.reshape(-1, D),
        small,
        chunks.reshape(-1, 128),
        row_ids,
        rel_index,
        w_qkv,
        w_proj,
        w_fc1,
        w_fc2,
    )
    qkv = qkv.reshape(2, PAD, 3 * D)
    gain_one, bias_proj = small[:, LN1_GAIN].reshape(-1), small[:, PROJ_BIAS].reshape(-1)
    gain_two, shift_two = small[:, LN2_GAIN].reshape(-1), small[:, LN2_SHIFT].reshape(-1)
    bias_fc2 = small[:, FC2_BIAS].reshape(-1)
    bias_fc1 = small[:, FC1_BIAS : FC1_BIAS + 4].reshape(-1)
    order = jnp.asarray(send_matrix(), bf16)
    normal_one, inverse_one = norm_rows(inputs)
    unrolled = dot(order, contexts, TN).astype(bf16)
    middle = (
        inputs
        + jnp.dot(unrolled, whole_proj, preferred_element_type=jnp.float32)
        + bias_proj.astype(jnp.float32)
    )
    normed_two, normal_two, inverse_two = norm_forward(middle, gain_two, shift_two)
    normed_low = normed_two.astype(jnp.bfloat16)
    hidden = jnp.dot(normed_low, whole_fc1, preferred_element_type=jnp.float32) + bias_fc1.astype(
        jnp.float32
    )
    active = jax.nn.gelu(hidden, approximate=False).astype(jnp.bfloat16)
    result = (
        middle
        + jnp.dot(active, whole_fc2, preferred_element_type=jnp.float32)
        + bias_fc2.astype(jnp.float32)
    )
    output = result.astype(jnp.bfloat16).reshape(tokens.shape)
    grad_out = cotangent.reshape(-1, D)
    grad_w_fc2 = jnp.einsum("rf,rd->fd", active, grad_out, preferred_element_type=jnp.float32)
    grad_fc2_bias = jnp.sum(grad_out.astype(jnp.float32), 0)
    slope = (
        0.5 * (1.0 + lax.erf(hidden * 0.7071067811865476))
        + hidden * jnp.exp(-0.5 * hidden * hidden) * 0.3989422804014327
    )
    grad_active = jnp.einsum("rd,fd->rf", grad_out, whole_fc2, preferred_element_type=jnp.float32)
    grad_hidden = (grad_active * slope).astype(jnp.bfloat16)
    grad_w_fc1 = jnp.einsum(
        "rd,rf->df", normed_low, grad_hidden, preferred_element_type=jnp.float32
    )
    grad_fc1_bias = jnp.sum(grad_hidden.astype(jnp.float32), 0)
    grad_normed_two = jnp.einsum(
        "rf,df->rd", grad_hidden, whole_fc1, preferred_element_type=jnp.float32
    )
    grad_inner_two, grad_ln2_gain, grad_ln2_shift = norm_backward(
        grad_normed_two, normal_two, inverse_two, gain_two
    )
    grad_middle = grad_out.astype(jnp.float32) + grad_inner_two
    part_a, part_b, part_c, part_d, part_e, part_f = (
        lax.psum_scatter(
            grad_ln2_gain.astype(jnp.bfloat16), "shard", scatter_dimension=0, tiled=True
        ).astype(jnp.float32),
        lax.psum_scatter(
            grad_ln2_shift.astype(jnp.bfloat16), "shard", scatter_dimension=0, tiled=True
        ).astype(jnp.float32),
        lax.psum_scatter(
            grad_w_fc1.astype(jnp.bfloat16), "shard", scatter_dimension=0, tiled=True
        ).astype(jnp.float32),
        lax.psum_scatter(
            grad_fc1_bias.astype(jnp.bfloat16), "shard", scatter_dimension=0, tiled=True
        ).astype(jnp.float32),
        lax.psum_scatter(
            grad_w_fc2.astype(jnp.bfloat16), "shard", scatter_dimension=0, tiled=True
        ).astype(jnp.float32),
        lax.psum_scatter(
            grad_fc2_bias.astype(jnp.bfloat16), "shard", scatter_dimension=0, tiled=True
        ).astype(jnp.float32),
    )
    grad_ln2_gain, grad_ln2_shift, grad_w_fc1, grad_fc1_bias, grad_w_fc2, grad_fc2_bias = lax.psum(
        (part_a, part_b, part_c, part_d, part_e, part_f), "rep"
    )
    grad_branch = grad_middle.astype(jnp.bfloat16)
    grad_w_proj = jnp.einsum("rd,re->de", unrolled, grad_branch, preferred_element_type=jnp.float32)
    grad_proj_bias = jnp.sum(grad_branch.astype(jnp.float32), 0)
    grad_unrolled = jnp.einsum(
        "re,de->rd", grad_branch, whole_proj, preferred_element_type=jnp.float32
    ).astype(jnp.bfloat16)
    grad_context = exchange(dot(order, grad_unrolled).astype(bf16).reshape(2, PAD, D))
    grad_queries, grad_keys, grad_values, pairs = attend_backward(qkv, grad_context, attend)
    grad_table = table_gradient(pairs, rel)
    grad_qkv = jnp.concatenate((grad_queries, grad_keys, grad_values), 2).reshape(2 * PAD, 3 * D)
    grad_w_qkv = jnp.einsum("rd,re->de", rolled, grad_qkv, preferred_element_type=jnp.float32)
    grad_q_bias = jnp.sum(grad_qkv[:, :D].astype(jnp.float32), 0)
    grad_v_bias = jnp.sum(grad_qkv[:, 2 * D :].astype(jnp.float32), 0)
    grad_rolled = jnp.einsum(
        "re,de->rd", grad_qkv, whole_qkv, preferred_element_type=jnp.float32
    ).astype(jnp.bfloat16)
    grad_normed = dot(order, exchange(grad_rolled.reshape(2, PAD, D)).reshape(2 * PAD, D), TN)
    grad_inner_one, grad_ln1_gain, grad_ln1_shift = norm_backward(
        grad_normed, normal_one, inverse_one, gain_one
    )
    grad_tokens = (grad_middle + grad_inner_one).reshape(tokens.shape)
    part_a, part_b, part_c, part_d, part_e, part_f, part_g, part_h = (
        lax.psum_scatter(
            grad_ln1_gain.astype(jnp.bfloat16), "shard", scatter_dimension=0, tiled=True
        ).astype(jnp.float32),
        lax.psum_scatter(
            grad_ln1_shift.astype(jnp.bfloat16), "shard", scatter_dimension=0, tiled=True
        ).astype(jnp.float32),
        lax.psum_scatter(
            grad_w_qkv.astype(jnp.bfloat16), "shard", scatter_dimension=0, tiled=True
        ).astype(jnp.float32),
        lax.psum_scatter(
            grad_q_bias.astype(jnp.bfloat16), "shard", scatter_dimension=0, tiled=True
        ).astype(jnp.float32),
        lax.psum_scatter(
            grad_v_bias.astype(jnp.bfloat16), "shard", scatter_dimension=0, tiled=True
        ).astype(jnp.float32),
        lax.psum_scatter(
            grad_table.astype(jnp.bfloat16), "shard", scatter_dimension=1, tiled=True
        ).astype(jnp.float32),
        lax.psum_scatter(
            grad_w_proj.astype(jnp.bfloat16), "shard", scatter_dimension=0, tiled=True
        ).astype(jnp.float32),
        lax.psum_scatter(
            grad_proj_bias.astype(jnp.bfloat16), "shard", scatter_dimension=0, tiled=True
        ).astype(jnp.float32),
    )
    (
        grad_ln1_gain,
        grad_ln1_shift,
        grad_w_qkv,
        grad_q_bias,
        grad_v_bias,
        grad_table,
        grad_w_proj,
        grad_proj_bias,
    ) = lax.psum((part_a, part_b, part_c, part_d, part_e, part_f, part_g, part_h), "rep")
    return (
        output,
        grad_tokens,
        grad_ln1_gain,
        grad_ln1_shift,
        grad_w_qkv,
        grad_q_bias,
        grad_v_bias,
        grad_table,
        grad_w_proj,
        grad_proj_bias,
        grad_ln2_gain,
        grad_ln2_shift,
        grad_w_fc1,
        grad_fc1_bias,
        grad_w_fc2,
        grad_fc2_bias,
    )


def solution(mesh):
    return jax.shard_map(
        shards,
        mesh=mesh,
        in_specs=(
            P("rep", "shard", None, None),
            P("shard", None),
            P(),
            P("shard"),
            P("shard"),
            P("shard", None),
            P("shard"),
            P("shard"),
            P(None, "shard"),
            P("shard", None),
            P("shard"),
            P("shard"),
            P("shard"),
            P("shard", None),
            P("shard"),
            P("shard", None),
            P("shard"),
            P("rep", "shard", None, None),
        ),
        out_specs=(
            P("rep", "shard", None, None),
            P("rep", "shard", None, None),
            P("shard"),
            P("shard"),
            P("shard", None),
            P("shard"),
            P("shard"),
            P(None, "shard"),
            P("shard", None),
            P("shard"),
            P("shard"),
            P("shard"),
            P("shard", None),
            P("shard"),
            P("shard", None),
            P("shard"),
        ),
        check_vma=False,
    )
```

```python
import functools

import jax
import jax.numpy as jnp
import numpy as np
from jax import lax
from jax.experimental import pallas as pl
from jax.experimental.pallas import tpu as pltpu
from jax.sharding import PartitionSpec as P

D = 512
HEADS = 16
HD = 32
WT = 8
WH = 7
WW = 7
WIN = 392
TABLE = 2535
PAD = 416
LANES = 512
GROUP = 4
CHUNKS = 20
SCALE = HD ** (-0.5)
NN = (((1,), (0,)), ((), ()))
NT = (((1,), (1,)), ((), ()))
TN = (((0,), (0,)), ((), ()))
VMEM_LIMIT = 60 * 2**20
f32 = jnp.float32
bf16 = jnp.bfloat16

PIECES = (
    ((0, 4), (0, 4), 112, 0),
    ((4, 8), (0, 4), 112, 112),
    ((0, 4), (4, 7), 96, 224),
    ((4, 8), (4, 7), 96, 320),
)


def send_matrix():
    matrix = np.zeros((2 * PAD, WT * WH * 2 * WW), np.float32)
    for window in range(2):
        for (t0, t1), (h0, h1), _, first in PIECES:
            row = window * PAD + first
            for t in range(t0, t1):
                for h in range(h0, h1):
                    for w in range(WW):
                        column = (window * WW + w + WW // 2) % (2 * WW)
                        source = ((t + 4) % WT * WH + (h + 3) % WH) * 2 * WW + column
                        matrix[row, source] = 1.0
                        row += 1
    return matrix


def spread_matrix():
    source = np.arange(WIN).reshape(WT, WH, WW)
    matrix = np.zeros((PAD, WIN), np.float32)
    for (t0, t1), (h0, h1), _, first in PIECES:
        tokens = source[t0:t1, h0:h1].reshape(-1)
        matrix[first + np.arange(tokens.size), tokens] = 1.0
    return matrix


def pieces_of(array, axis, fill):
    shape = array.shape
    split = array.reshape(shape[:axis] + (WT, WH, WW) + shape[axis + 1 :])
    parts = []
    for (t0, t1), (h0, h1), padded, _ in PIECES:
        part = lax.slice_in_dim(lax.slice_in_dim(split, t0, t1, axis=axis), h0, h1, axis=axis + 1)
        length = (t1 - t0) * (h1 - h0) * WW
        part = part.reshape(shape[:axis] + (length,) + shape[axis + 1 :])
        widths = [(0, 0, 0)] * len(shape)
        widths[axis] = (0, padded - length, 0)
        parts.append(lax.pad(part, jnp.asarray(fill, array.dtype), widths))
    return jnp.concatenate(parts, axis)


def dot(a, b, dims=NN):
    return lax.dot_general(a, b, dims, preferred_element_type=f32)


MESH = pl.DeviceIdType.MESH
PARTS = 8
FIRST_ROWS = tuple(first for _, _, _, first in PIECES)
LENGTHS = tuple(padded for _, _, padded, _ in PIECES)
ACROSS = (0, 2, 1, 3)
LN1_GAIN, LN1_SHIFT, Q_BIAS, V_BIAS, PROJ_BIAS, LN2_GAIN, LN2_SHIFT, FC2_BIAS, FC1_BIAS = range(9)
SMALL = 16


def place():
    rep, shard = lax.axis_index("rep"), lax.axis_index("shard")
    return rep, shard, lax.rem(rep, 2), lax.rem(rep // 2, 2), lax.rem(rep // 4, 2)


def flip(rep, bit):
    low = lax.rem(rep // (1 << bit), 2)
    return rep + (1 - 2 * low) * (1 << bit)


def remote(src, dst, send, recv, rep, shard):
    return pltpu.make_async_remote_copy(
        src_ref=src,
        dst_ref=dst,
        send_sem=send,
        recv_sem=recv,
        device_id={"rep": rep, "shard": shard},
        device_id_type=MESH,
    )


def greet(peers):
    barrier = pltpu.get_barrier_semaphore()
    for rep, shard in peers:
        pl.semaphore_signal(
            barrier, inc=1, device_id={"rep": rep, "shard": shard}, device_id_type=MESH
        )
    pl.semaphore_wait(barrier, len(peers))


def peers_of(rep, shard):
    return [(rep, lax.rem(shard + k, 4)) for k in (1, 2, 3)] + [
        (flip(rep, bit), shard) for bit in (0, 1, 2)
    ]


def quarter_across(shard, bits):
    low, high = lax.rem(shard, 2), shard // 2
    if bits & 1:
        low = 1 - low
    if bits & 2:
        high = 1 - high
    return high * 2 + low


def pieces_to(source, target, send, recv, rep, shard, window, columns=None):
    copies = []
    for piece in (1, 2, 3):
        rows = pl.ds(
            pl.multiple_of(window * PAD + FIRST_ROWS[piece], 16), LENGTHS[piece]
        )
        at = (rows,) if columns is None else (rows, columns)
        copies.append(
            remote(
                source.at[at],
                target.at[at],
                send(piece - 1),
                recv(piece - 1),
                rep,
                quarter_across(shard, ACROSS[piece]),
            )
        )
    return copies


def norm_rows(rows):
    centre = rows - jnp.mean(rows, -1, keepdims=True)
    inverse = lax.rsqrt(jnp.mean(centre * centre, -1, keepdims=True) + 1e-05)
    return centre * inverse, inverse


def small_row(ref, row):
    return jnp.concatenate([ref[s, row : row + 1, :] for s in range(4)], 1)


Z_PHASE, X_PHASE, Y_PHASE, CORE_PHASE = range(4)


def front_kernel(
    tokens,
    order,
    spread,
    small,
    table,
    row_ids,
    rel,
    qkv_part,
    proj_part,
    fc1_part,
    fc2_part,
    qkv_whole,
    proj_whole,
    fc1_whole,
    fc2_whole,
    small_out,
    rolled_out,
    mixed_out,
    attend_out,
    back_out,
    rel_out,
    small_all,
    table_all,
    table_wide,
    normed,
    outgoing,
    rolled,
    weights,
    mixed,
    index,
    bias,
    mask,
    attend,
    contexts,
    gather_send,
    gather_recv,
    small_send,
    small_recv,
    bias_send,
    bias_recv,
    piece_send,
    piece_recv,
    back_send,
    back_recv,
    local,
    attend_sem,
):
    rep, shard, core, x_bit, y_bit = place()
    greet(peers_of(rep, shard))
    parts = (qkv_part, proj_part, fc1_part, fc2_part)
    wholes = (qkv_whole, proj_whole, fc1_whole, fc2_whole)

    def gather(matrix, phase):
        copies = []
        for k in (1, 2, 3):
            at = lax.rem(shard + k, 4)
            whole = wholes[matrix]
            if phase == Z_PHASE:
                copies.append(
                    remote(
                        parts[matrix].at[y_bit, x_bit, core],
                        whole.at[shard, y_bit, x_bit, core],
                        gather_send.at[matrix, phase, k - 1],
                        gather_recv.at[matrix, phase, 3 - k],
                        rep,
                        at,
                    )
                )
                continue
            if phase == X_PHASE:
                block, partner = whole.at[at, y_bit, x_bit, core], flip(rep, 1)
            elif phase == Y_PHASE:
                block, partner = whole.at[at, y_bit, :, core], flip(rep, 2)
            else:
                block, partner = whole.at[at, :, :, core], flip(rep, 0)
            copies.append(
                remote(
                    block,
                    block,
                    gather_send.at[matrix, phase, k - 1],
                    gather_recv.at[matrix, phase, k - 1],
                    partner,
                    shard,
                )
            )
        return copies

    def start(matrix, phase):
        for copy in gather(matrix, phase):
            copy.start()

    def arrived(matrix, phase):
        for copy in gather(matrix, phase):
            copy.wait_recv()

    def small_copies():
        copies = []
        for k in (1, 2, 3):
            for n, ref in enumerate((table_all, small_all)):
                copies.append(
                    remote(
                        ref.at[shard],
                        ref.at[shard],
                        small_send.at[n, k - 1],
                        small_recv.at[n, 3 - k],
                        rep,
                        lax.rem(shard + k, 4),
                    )
                )
        return copies

    small_all[shard] = small[...]
    table_all[shard] = table[...]
    for copy in small_copies():
        copy.start()
    start(0, Z_PHASE)
    own = [
        pltpu.make_async_copy(parts[m], wholes[m].at[shard], local.at[m]) for m in range(4)
    ]
    for copy in own:
        copy.start()

    rel_index = rel[...]
    digits = (rel_index // 256).astype(f32).astype(bf16), (rel_index & 255).astype(f32).astype(bf16)
    moved = []
    for digit in digits:
        half = dot(spread[...], digit).astype(bf16)
        moved.append(dot(half, spread[...], NT).astype(jnp.int32))
    index[:, :PAD] = moved[0] * 256 + moved[1]
    index[:, PAD:] = jnp.zeros((PAD, LANES - PAD), jnp.int32)

    ids = lax.broadcasted_iota(jnp.int32, (8, LANES), 0)
    for window in range(2):
        kinds = jnp.where(row_ids[window] + 1 == ids, 1.0, 0.0).astype(bf16)[:, :PAD]
        mask[window] = (dot(kinds, kinds, TN) - 1.0) * 1e30

    for copy in small_copies():
        copy.wait_recv()

    gain, shift = small_row(small_all, LN1_GAIN), small_row(small_all, LN1_SHIFT)

    def norm_step(step, carry):
        rows = pl.ds(pl.multiple_of(step * 112, 16), 112)
        normal, _ = norm_rows(tokens[rows, :].astype(f32))
        normed[rows, :] = (normal * gain.astype(f32) + shift.astype(f32)).astype(bf16)
        return carry

    lax.fori_loop(0, 7, norm_step, 0)

    def order_step(step, carry):
        rows = pl.ds(pl.multiple_of(step * 208, 16), 208)
        outgoing[rows, :] = dot(order[rows, :], normed[...]).astype(bf16)
        return carry

    lax.fori_loop(0, 4, order_step, 0)

    def roll_copies(window):
        return pieces_to(
            outgoing,
            rolled,
            lambda n: piece_send.at[window, n],
            lambda n: piece_recv.at[window, n],
            rep,
            shard,
            window,
        )

    for window in range(2):
        for copy in roll_copies(window):
            copy.start()
        rows = slice(window * PAD, window * PAD + LENGTHS[0])
        rolled[rows, :] = outgoing[rows, :]
    for matrix in (1, 2, 3):
        start(matrix, Z_PHASE)

    for chunk in range(CHUNKS):
        for head in range(HEADS // 2):
            row = (head % 4) * CHUNKS + chunk
            table_wide[chunk, head] = jnp.broadcast_to(
                table_all[2 * core + head // 4, row : row + 1, :], (8, 128)
            )
    mine = core * (HEADS // 2)

    def bias_copy(rows, step):
        block = bias.at[pl.ds(mine, HEADS // 2), rows]
        return remote(block, block, bias_send.at[step], bias_recv.at[step], flip(rep, 0), shard)

    def on_the_way(step, table_of_steps):
        for when, actions in table_of_steps.items():

            @pl.when(step == when)
            def _():
                for action, matrix, phase in actions:
                    action(matrix, phase)

    def advance(matrix, phase):
        arrived(matrix, phase)
        if phase < CORE_PHASE:
            start(matrix, phase + 1)

    schedule = {
        4: [(advance, 0, Z_PHASE)],
        8: [(advance, 0, X_PHASE)],
        14: [(advance, 0, Y_PHASE)],
        16: [(advance, 1, Z_PHASE)],
        20: [(advance, 1, X_PHASE), (advance, 2, Z_PHASE)],
        24: [(advance, 3, Z_PHASE)],
    }
    later = {
        1: [(advance, 1, Y_PHASE)],
        4: [(advance, 2, X_PHASE)],
        8: [(advance, 3, X_PHASE)],
        14: [(advance, 2, Y_PHASE)],
        20: [(advance, 3, Y_PHASE)],
    }

    def bias_step(step, carry):
        on_the_way(step, schedule)
        rows = pl.ds(pl.multiple_of(step * 16, 16), 16)
        for tile in range(LANES // 128):
            lanes = slice(tile * 128, (tile + 1) * 128)
            here = index[rows, lanes]
            halves = [(here[s : s + 8] & 127, here[s : s + 8] >> 7) for s in (0, 8)]
            found = [[None, None] for _ in range(HEADS // 2)]
            for chunk in range(CHUNKS):
                for s, (low, high) in enumerate(halves):
                    hit = high == chunk
                    for head in range(HEADS // 2):
                        value = jnp.take_along_axis(table_wide[chunk, head], low, axis=1)
                        if chunk:
                            value = jnp.where(hit, value, found[head][s])
                        found[head][s] = value
            for head in range(HEADS // 2):
                bias[mine + head, rows, lanes] = jnp.concatenate(found[head], 0).astype(bf16)
        bias_copy(rows, step).start()
        return carry

    lax.fori_loop(0, PAD // 16, bias_step, 0)

    arrived(0, CORE_PHASE)
    own[0].wait()
    fetch = pltpu.make_async_copy(qkv_whole, weights, local.at[4])
    fetch.start()
    fetch.wait()
    q_bias, v_bias = small_row(small_all, Q_BIAS), small_row(small_all, V_BIAS)
    mixed_bias = jnp.concatenate([q_bias, jnp.zeros_like(q_bias), v_bias], 1).astype(f32)
    for window in range(2):
        for copy in roll_copies(window):
            copy.wait_recv()
        span = slice(window * PAD, (window + 1) * PAD)
        for part in range(3):
            lanes = slice(part * D, (part + 1) * D)
            got = dot(rolled[span, :], weights[...].reshape(D, 3 * D)[:, lanes])
            mixed[span, lanes] = (got + mixed_bias[:, lanes]).astype(bf16)
    keep = [
        pltpu.make_async_copy(rolled, rolled_out, local.at[4]),
        pltpu.make_async_copy(mixed, mixed_out, local.at[5]),
        pltpu.make_async_copy(index, rel_out, local.at[6]),
        pltpu.make_async_copy(small_all, small_out, local.at[7]),
    ]
    for copy in keep:
        copy.start()

    def bias_wait(step, carry):
        bias_copy(pl.ds(pl.multiple_of(step * 16, 16), 16), step).wait_recv()
        return carry

    lax.fori_loop(0, PAD // 16, bias_wait, 0)

    head_of = lax.broadcasted_iota(jnp.int32, (1, 128), 1) // HD
    none = jnp.zeros((), bf16)

    def attend_copy(step):
        window, head, slot = step // HEADS, lax.rem(step, HEADS), lax.rem(step, 2)
        return pltpu.make_async_copy(
            attend.at[slot], attend_out.at[window, head], attend_sem.at[slot]
        )

    def back_copies(step):
        window, group = step // HEADS, lax.rem(step // GROUP, HEADS // GROUP)
        lanes = pl.ds(pl.multiple_of(group * 128, 128), 128)
        return pieces_to(
            contexts,
            back_out,
            lambda n: back_send.at[window, group, n],
            lambda n: back_recv.at[window, group, n],
            rep,
            shard,
            window,
            lanes,
        )

    def attend_step(step, carry):
        on_the_way(step, later)
        window, head = step // HEADS, lax.rem(step, HEADS)
        group, member, slot = head // GROUP, lax.rem(head, GROUP), lax.rem(step, 2)
        rows = pl.ds(pl.multiple_of(window * PAD, 16), PAD)

        def lanes(part):
            return pl.ds(pl.multiple_of(part * D + group * 128, 128), 128)

        own_lanes = head_of == member
        query = jnp.where(own_lanes, mixed[rows, lanes(0)], none)
        value = jnp.where(own_lanes, mixed[rows, lanes(2)], none)
        scores = dot(query, mixed[rows, lanes(1)], NT) * SCALE + bias[head, :, :PAD].astype(f32)
        scores = scores + mask[window]
        expo = jnp.exp(scores - jnp.max(scores, -1, keepdims=True))
        weight = (expo * (1.0 / jnp.sum(expo, -1, keepdims=True))).astype(bf16)

        @pl.when(step >= 2)
        def _():
            attend_copy(step - 2).wait()

        attend[slot, :, :PAD] = weight
        attend_copy(step).start()
        result = dot(weight, value).astype(bf16)
        contexts[rows, lanes(0)] = jnp.where(own_lanes, result, contexts[rows, lanes(0)])

        @pl.when(member == GROUP - 1)
        def _():
            for copy in back_copies(step):
                copy.start()

        return carry

    lax.fori_loop(0, 2 * HEADS, attend_step, 0)

    stay = [
        pltpu.make_async_copy(
            contexts.at[pl.ds(w * PAD, LENGTHS[0])],
            back_out.at[pl.ds(w * PAD, LENGTHS[0])],
            local.at[8 + w],
        )
        for w in range(2)
    ]
    for copy in stay:
        copy.start()
    for matrix in (1, 2, 3):
        arrived(matrix, CORE_PHASE)
    attend_copy(2 * HEADS - 2).wait()
    attend_copy(2 * HEADS - 1).wait()

    def back_wait(step, carry):
        for copy in back_copies(step * GROUP):
            copy.wait()
        return carry

    lax.fori_loop(0, 2 * HEADS // GROUP, back_wait, 0)

    def bias_sent(step, carry):
        bias_copy(pl.ds(pl.multiple_of(step * 16, 16), 16), step).wait_send()
        return carry

    lax.fori_loop(0, PAD // 16, bias_sent, 0)
    for copy in small_copies():
        copy.wait_send()
    for window in range(2):
        for copy in roll_copies(window):
            copy.wait_send()
    for matrix in range(4):
        for phase in range(4):
            for copy in gather(matrix, phase):
                copy.wait_send()
    for copy in own[1:] + keep + stay:
        copy.wait()


def front(tokens, small, table, row_ids, rel_index, w_qkv, w_proj, w_fc1, w_fc2):
    anywhere, inside = pl.BlockSpec(memory_space=pl.ANY), pl.BlockSpec(memory_space=pltpu.VMEM)
    cut = (2, 2, 2)
    weights = [
        w.reshape(cut + (w.shape[0] // PARTS, w.shape[1])) for w in (w_qkv, w_proj, w_fc1, w_fc2)
    ]
    wholes = [jax.ShapeDtypeStruct((4,) + w.shape, bf16) for w in weights]
    dma = pltpu.SemaphoreType.DMA
    results = pl.pallas_call(
        front_kernel,
        out_shape=(
            *wholes,
            jax.ShapeDtypeStruct((4, SMALL, 128), bf16),
            jax.ShapeDtypeStruct((2 * PAD, D), bf16),
            jax.ShapeDtypeStruct((2 * PAD, 3 * D), bf16),
            jax.ShapeDtypeStruct((2, HEADS, PAD, LANES), bf16),
            jax.ShapeDtypeStruct((2 * PAD, D), bf16),
            jax.ShapeDtypeStruct((PAD, LANES), jnp.int32),
        ),
        in_specs=[inside] * 7 + [anywhere] * 4,
        out_specs=(anywhere,) * 10,
        scratch_shapes=[
            pltpu.VMEM((4, SMALL, 128), bf16),
            pltpu.VMEM((4, GROUP * CHUNKS, 128), f32),
            pltpu.VMEM((CHUNKS, HEADS // 2, 8, 128), f32),
            pltpu.VMEM(tokens.shape, bf16),
            pltpu.VMEM((2 * PAD, D), bf16),
            pltpu.VMEM((2 * PAD, D), bf16),
            pltpu.VMEM(wholes[0].shape, bf16),
            pltpu.VMEM((2 * PAD, 3 * D), bf16),
            pltpu.VMEM((PAD, LANES), jnp.int32),
            pltpu.VMEM((HEADS, PAD, LANES), bf16),
            pltpu.VMEM((2, PAD, PAD), f32),
            pltpu.VMEM((2, PAD, LANES), bf16),
            pltpu.VMEM((2 * PAD, D), bf16),
            dma((4, 4, 3)),
            dma((4, 4, 3)),
            dma((2, 3)),
            dma((2, 3)),
            dma((PAD // 16,)),
            dma((PAD // 16,)),
            dma((2, 3)),
            dma((2, 3)),
            dma((2, HEADS // GROUP, 3)),
            dma((2, HEADS // GROUP, 3)),
            dma((10,)),
            dma((2,)),
        ],
        compiler_params=pltpu.CompilerParams(
            vmem_limit_bytes=VMEM_LIMIT, collective_id=0, has_side_effects=True
        ),
        name="front",
    )(
        tokens,
        jnp.asarray(send_matrix(), bf16),
        jnp.asarray(spread_matrix(), bf16),
        small,
        table,
        row_ids,
        rel_index,
        *weights,
    )
    whole = [w.reshape(-1, w.shape[-1]) for w in results[:4]]
    return (*whole, *results[4:])


CORE_SUM, FIRST_SUM, SECOND_SUM, Z_SUM, SECOND_SHARE, FIRST_SHARE, CORE_SHARE = range(7)
SUMMED = ((16, 2048, True), (64, 512, False), (16, 512, True), (16, 768, True), (16, 768, False))
FC1, FC2, PROJ, QKV_A, QKV_B = range(5)
SPAN = 256
SPANS = -(-TABLE // SPAN)
BATCH = 8
HALF = PAD // 2
TILES = LANES // 128
SLAB = 2 * SPANS * GROUP + SMALL


def back_kernel(
    grad_unrolled,
    order,
    order_back,
    rolled,
    mixed,
    weights,
    rel,
    tokens,
    grad_middle,
    small_all,
    small_grads,
    attend_in,
    fc1_grad,
    fc2_grad,
    proj_grad,
    grad_tokens,
    fc1_out,
    fc2_out,
    proj_out,
    qkv_out_a,
    qkv_out_b,
    slab_out,
    outgoing,
    grad_context,
    attend,
    grads,
    grad_rolled,
    returned,
    pairs,
    pairs_out,
    pairs_in,
    qkv_grad_a,
    qkv_grad_b,
    table_sum,
    slab,
    slab_z,
    slab_rep,
    *rest,
):
    held = [rest[6 * m : 6 * m + 6] for m in range(5)]
    (
        sum_send,
        sum_recv,
        extra_send,
        extra_recv,
        piece_send,
        piece_recv,
        back_send,
        back_recv,
        attend_sem,
        pairs_send,
        pairs_recv,
        slab_send,
        slab_recv,
        local,
    ) = rest[30:]
    rep, shard, core, x_bit, y_bit = place()
    reps = lax.axis_size("rep")
    barrier = pltpu.get_barrier_semaphore()

    def hello(k, carry):
        pl.semaphore_signal(
            barrier,
            inc=1,
            device_id={"rep": lax.rem(rep + k, reps), "shard": shard},
            device_id_type=MESH,
        )
        return carry

    lax.fori_loop(1, reps, hello, 0)
    for k in (1, 2, 3):
        pl.semaphore_signal(
            barrier,
            inc=1,
            device_id={"rep": rep, "shard": lax.rem(shard + k, 4)},
            device_id_type=MESH,
        )
    pl.semaphore_wait(barrier, reps + 2)

    sources = (fc1_grad, fc2_grad, proj_grad, qkv_grad_a, qkv_grad_b)

    def axis_of(matrix, first):
        x_first = SUMMED[matrix][2]
        use_x = x_first == first
        return (1, x_bit) if use_x else (2, y_bit)

    def sum_copies(matrix, phase):
        from_core, kept, from_first, summed, from_z, shared = held[matrix]
        x_first = SUMMED[matrix][2]
        first_bit, first = axis_of(matrix, True)
        second_bit, second = axis_of(matrix, False)

        def one(src, dst, bit, n=0):
            return remote(
                src,
                dst,
                sum_send.at[matrix, phase, n],
                sum_recv.at[matrix, phase, n],
                flip(rep, bit),
                shard,
            )

        if phase == CORE_SUM:
            return [one(sources[matrix].at[:, :, :, 1 - core], from_core, 0)]
        if phase == FIRST_SUM:
            cut = kept.at[:, :, 1 - x_bit] if x_first else kept.at[:, 1 - y_bit]
            return [one(cut, from_first, first_bit)]
        if phase == SECOND_SUM:
            return [one(from_first.at[:, 1 - second], summed, second_bit)]
        if phase == Z_SUM:
            copies = []
            for k in (1, 2, 3):
                to = lax.rem(shard + k, 4)
                copies.append(
                    remote(
                        summed.at[to],
                        from_z.at[3 - k],
                        sum_send.at[matrix, phase, k - 1],
                        sum_recv.at[matrix, phase, 3 - k],
                        rep,
                        to,
                    )
                )
            return copies
        if phase == SECOND_SHARE:
            block = shared.at[y_bit, x_bit, core]
            return [one(block, block, second_bit)]
        if phase == FIRST_SHARE:
            block = shared.at[:, x_bit, core] if x_first else shared.at[y_bit, :, core]
            return [one(block, block, first_bit)]
        block = shared.at[:, :, core]
        return [one(block, block, 0)]

    def own_copy(matrix):
        return pltpu.make_async_copy(
            sources[matrix].at[:, :, :, core], held[matrix][1], local.at[matrix]
        )

    def extra_copy(matrix, bit):
        shared, from_z = held[matrix][5], held[matrix][4]
        return remote(
            shared.at[y_bit, x_bit, core],
            from_z.at[bit],
            extra_send.at[matrix, bit - 3],
            extra_recv.at[matrix, bit - 3],
            flip(rep, bit),
            shard,
        )

    def add(into, at, other, other_at):
        into[at] = (into[at].astype(f32) + other[other_at].astype(f32)).astype(bf16)

    def begin(matrix):
        own_copy(matrix).start()
        for copy in sum_copies(matrix, CORE_SUM):
            copy.start()

    def advance(matrix, phase):
        from_core, kept, from_first, summed, from_z, shared = held[matrix]
        x_first = SUMMED[matrix][2]
        _, second = axis_of(matrix, False)
        for copy in sum_copies(matrix, phase):
            copy.wait_recv()
        if phase == CORE_SUM:
            own_copy(matrix).wait()

            def step(n, carry):
                at = (n // 4, lax.rem(n // 2, 2), lax.rem(n, 2))
                add(kept, at, from_core, at)
                return carry

            lax.fori_loop(0, 16, step, 0)
        elif phase == FIRST_SUM:

            def step(n, carry):
                owner, other = n // 2, lax.rem(n, 2)
                at = (owner, other, x_bit) if x_first else (owner, y_bit, other)
                add(from_first, (owner, other), kept, at)
                return carry

            lax.fori_loop(0, 8, step, 0)
        elif phase == SECOND_SUM:

            def step(owner, carry):
                add(summed, (owner,), from_first, (owner, second))
                return carry

            lax.fori_loop(0, 4, step, 0)
        elif phase == Z_SUM:
            total = summed[shard].astype(f32)
            for n in range(3):
                total = total + from_z[n].astype(f32)
            shared[y_bit, x_bit, core] = total.astype(bf16)
            bit = 3
            while (1 << bit) < reps:
                copy = extra_copy(matrix, bit)
                copy.start()
                copy.wait()
                at = (y_bit, x_bit, core)
                add(shared, at, from_z, (bit,))
                bit += 1
        if phase < CORE_SHARE:
            for copy in sum_copies(matrix, phase + 1):
                copy.start()

    def on_the_way(step, table_of_steps):
        for when, actions in table_of_steps.items():

            @pl.when(step == when)
            def _():
                for matrix, phase in actions:
                    advance(matrix, phase)

    outgoing[...] = dot(order[...], grad_unrolled[...]).astype(bf16)

    def roll_copies(window):
        return pieces_to(
            outgoing,
            grad_context,
            lambda n: piece_send.at[window, n],
            lambda n: piece_recv.at[window, n],
            rep,
            shard,
            window,
        )

    for window in range(2):
        for copy in roll_copies(window):
            copy.start()
        rows = slice(window * PAD, window * PAD + LENGTHS[0])
        grad_context[rows, :] = outgoing[rows, :]
    for matrix in (FC1, FC2, PROJ):
        begin(matrix)

    head_of = lax.broadcasted_iota(jnp.int32, (1, 128), 1) // HD
    none = jnp.zeros((), bf16)

    def attend_copy(step):
        window, head, slot = step // HEADS, lax.rem(step, HEADS), lax.rem(step, 3)
        return pltpu.make_async_copy(
            attend_in.at[window, head], attend.at[slot], attend_sem.at[slot]
        )

    attend_copy(0).start()
    attend_copy(1).start()

    def return_copies(window):
        return pieces_to(
            grad_rolled,
            returned,
            lambda n: back_send.at[window, n],
            lambda n: back_recv.at[window, n],
            rep,
            shard,
            window,
        )

    def give_back(window):
        span = slice(window * PAD, (window + 1) * PAD)
        grad_rolled[span, :] = dot(grads[span, :], weights[...], NT).astype(bf16)
        for copy in return_copies(window):
            copy.start()
        rows = slice(window * PAD, window * PAD + LENGTHS[0])
        returned[rows, :] = grad_rolled[rows, :]

    first_schedule = {
        5: [(FC1, CORE_SUM)],
        7: [(FC2, CORE_SUM)],
        9: [(PROJ, CORE_SUM)],
        17: [(FC1, FIRST_SUM)],
        19: [(FC2, FIRST_SUM)],
        21: [(PROJ, FIRST_SUM)],
        25: [(FC1, SECOND_SUM)],
        27: [(FC2, SECOND_SUM)],
        29: [(PROJ, SECOND_SUM)],
    }
    second_schedule = {
        1: [(FC1, Z_SUM), (QKV_A, CORE_SUM), (QKV_B, CORE_SUM)],
        3: [(FC2, Z_SUM), (PROJ, Z_SUM)],
        5: [(FC1, SECOND_SHARE)],
        7: [(FC2, SECOND_SHARE), (PROJ, SECOND_SHARE), (QKV_A, FIRST_SUM), (QKV_B, FIRST_SUM)],
        9: [(FC1, FIRST_SHARE)],
        11: [(FC2, FIRST_SHARE), (PROJ, FIRST_SHARE), (QKV_A, SECOND_SUM), (QKV_B, SECOND_SUM)],
        15: [(QKV_A, Z_SUM), (QKV_B, Z_SUM), (FC1, CORE_SHARE)],
        18: [(QKV_A, SECOND_SHARE), (QKV_B, SECOND_SHARE), (FC2, CORE_SHARE), (PROJ, CORE_SHARE)],
        21: [(QKV_A, FIRST_SHARE), (QKV_B, FIRST_SHARE)],
    }

    for copy in roll_copies(0):
        copy.wait_recv()

    def head_step(step, carry):
        on_the_way(step, first_schedule)

        @pl.when(step == HEADS)
        def _():
            for copy in roll_copies(1):
                copy.wait_recv()
            give_back(0)

        @pl.when(step + 2 < 2 * HEADS)
        def _():
            attend_copy(step + 2).start()

        attend_copy(step).wait()
        window, head, slot = step // HEADS, lax.rem(step, HEADS), lax.rem(step, 3)
        group, member = head // GROUP, lax.rem(head, GROUP)
        rows = pl.ds(pl.multiple_of(window * PAD, 16), PAD)

        def lanes(part):
            return pl.ds(pl.multiple_of(part * D + group * 128, 128), 128)

        mine = head_of == member
        query = jnp.where(mine, mixed[rows, lanes(0)], none)
        key = jnp.where(mine, mixed[rows, lanes(1)], none)
        grad = jnp.where(mine, grad_context[rows, lanes(0)], none)
        weight_low = attend[slot, :, :PAD]
        weight = weight_low.astype(f32)
        grad_attend = dot(grad, mixed[rows, lanes(2)], NT)
        inner = jnp.sum(weight * grad_attend, -1, keepdims=True)
        grad_scores = (weight * (grad_attend - inner)).astype(bf16)
        wide = grad_scores.astype(f32)
        for tile in range(TILES):
            part = wide[:, tile * 128 : (tile + 1) * 128]
            if part.shape[1] < 128:
                part = jnp.concatenate([part, jnp.zeros((PAD, 128 - part.shape[1]), f32)], 1)
            at = (tile, pl.ds(head, PAD, stride=HEADS), slice(None))

            @pl.when(window == 0)
            def _():
                pairs[at] = part

            @pl.when(window == 1)
            def _():
                pairs[at] = pairs[at] + part

        for part, value in (
            (0, dot(grad_scores, key) * SCALE),
            (1, dot(grad_scores, query, TN) * SCALE),
            (2, dot(weight_low, grad, TN)),
        ):
            grads[rows, lanes(part)] = jnp.where(
                mine, value.astype(bf16), grads[rows, lanes(part)]
            )
        return carry

    lax.fori_loop(0, 2 * HEADS, head_step, 0)

    theirs = (1 - core) * (HALF * HEADS)
    piece_rows = HALF * HEADS // 4

    def round_step(step, carry):
        at = pl.ds(pl.multiple_of(step * piece_rows, 16), piece_rows)
        source = pl.ds(pl.multiple_of(theirs + step * piece_rows, 16), piece_rows)
        for tile in range(TILES):
            pairs_out[tile, at, :] = pairs[tile, source, :].astype(bf16)
        return carry

    lax.fori_loop(0, 4, round_step, 0)
    pairs_copy = remote(
        pairs_out, pairs_in, pairs_send.at[0], pairs_recv.at[0], flip(rep, 0), shard
    )
    pairs_copy.start()

    give_back(1)
    for n, ref in enumerate((qkv_grad_a, qkv_grad_b)):
        columns = slice(n * 768, (n + 1) * 768)
        got = dot(rolled[...], grads[:, columns], TN).astype(bf16)
        ref[...] = got.reshape(ref.shape)
        begin(QKV_A + n)

    low_of = lax.broadcasted_iota(jnp.int32, (SPAN, LANES), 0).astype(f32).astype(bf16)
    table_sum[...] = jnp.zeros_like(table_sum)
    pairs_copy.wait_recv()

    def table_step(step, carry):
        on_the_way(step, second_schedule)
        left, right = [], []
        for k in range(BATCH):
            row = step * BATCH + k
            there = core * HALF + row
            at = pl.ds(pl.multiple_of(there * HEADS, HEADS), HEADS)
            near = pl.ds(pl.multiple_of(row * HEADS, HEADS), HEADS)
            index = rel[pl.ds(there, 1), :]
            low = (index & (SPAN - 1)).astype(f32).astype(bf16)
            high = jnp.broadcast_to((index // SPAN).astype(f32).astype(bf16), (HEADS, LANES))
            total = jnp.concatenate(
                [pairs[t, at, :] + pairs_in[t, near, :].astype(f32) for t in range(TILES)], 1
            ).astype(bf16)
            nothing = jnp.zeros_like(total)
            left.append(
                jnp.concatenate(
                    [jnp.where(high == jnp.asarray(s, bf16), total, nothing) for s in range(SPANS)],
                    0,
                )
            )
            hit = low_of == jnp.broadcast_to(low, (SPAN, LANES))
            right.append(jnp.where(hit, jnp.ones((), bf16), jnp.zeros((), bf16)))
        table_sum[...] += dot(jnp.concatenate(left, 1), jnp.concatenate(right, 1), NT)
        return carry

    lax.fori_loop(0, HALF // BATCH, table_step, 0)

    for window in range(2):
        for copy in return_copies(window):
            copy.wait_recv()
    gain = small_row(small_all, LN1_GAIN).astype(f32)

    def norm_step(step, carry):
        gain_sum, shift_sum = carry
        rows = pl.ds(pl.multiple_of(step * 112, 16), 112)
        grad_out = dot(order_back[rows, :], returned[...])
        normal, inverse = norm_rows(tokens[rows, :].astype(f32))
        scaled = grad_out * gain
        inner = (
            scaled
            - jnp.mean(scaled, -1, keepdims=True)
            - normal * jnp.mean(scaled * normal, -1, keepdims=True)
        )
        grad_tokens[rows, :] = grad_middle[rows, :] + inverse * inner
        return (
            gain_sum + jnp.sum(grad_out * normal, 0, keepdims=True),
            shift_sum + jnp.sum(grad_out, 0, keepdims=True),
        )

    nought = jnp.zeros((1, D), f32)
    gain_sum, shift_sum = lax.fori_loop(0, 7, norm_step, (nought, nought))

    query_sum = jnp.sum(grads[:, :D].astype(f32), 0, keepdims=True)
    value_sum = jnp.sum(grads[:, 2 * D :].astype(f32), 0, keepdims=True)
    for owner in range(4):
        lanes = slice(owner * 128, (owner + 1) * 128)
        sums = jnp.concatenate(
            [table_sum[pl.ds(s * HEADS + GROUP * owner, GROUP), :] for s in range(SPANS)], 0
        )
        slab[owner, : SPANS * GROUP, :] = sums[:, :128]
        slab[owner, SPANS * GROUP : 2 * SPANS * GROUP, :] = sums[:, 128:]
        slab[owner, 2 * SPANS * GROUP :, :] = jnp.concatenate(
            [
                gain_sum[:, lanes],
                shift_sum[:, lanes],
                query_sum[:, lanes],
                value_sum[:, lanes],
                small_grads[owner, V_BIAS + 1 :, :],
            ],
            0,
        )

    def slab_copies():
        return [
            remote(
                slab.at[lax.rem(shard + k, 4)],
                slab_z.at[3 - k],
                slab_send.at[k - 1],
                slab_recv.at[3 - k],
                rep,
                lax.rem(shard + k, 4),
            )
            for k in (1, 2, 3)
        ]

    for copy in slab_copies():
        copy.start()

    for matrix in (QKV_A, QKV_B):
        advance(matrix, CORE_SHARE)
    for copy in slab_copies():
        copy.wait_recv()
    slab_rep[rep] = slab[shard] + (slab_z[0] + slab_z[1] + slab_z[2])

    def slab_share(k):
        return remote(
            slab_rep.at[rep],
            slab_rep.at[rep],
            slab_send.at[2 + k],
            slab_recv.at[2 + reps - k],
            lax.rem(rep + k, reps),
            shard,
        )

    def share_start(k, carry):
        slab_share(k).start()
        return carry

    lax.fori_loop(1, reps, share_start, 0)
    outs = (fc1_out, fc2_out, proj_out, qkv_out_a, qkv_out_b)
    results = [
        pltpu.make_async_copy(held[matrix][5], outs[matrix], local.at[5 + matrix])
        for matrix in range(5)
    ]
    for copy in results:
        copy.start()

    def share_wait(k, carry):
        slab_share(k).wait()
        return carry

    lax.fori_loop(1, reps, share_wait, 0)

    def slab_step(k, total):
        return total + slab_rep[k]

    slab_out[...] = lax.fori_loop(1, reps, slab_step, slab_rep[0])

    for copy in slab_copies():
        copy.wait_send()
    pairs_copy.wait_send()
    for window in range(2):
        for copy in roll_copies(window) + return_copies(window):
            copy.wait_send()
    for matrix in range(5):
        for phase in range(7):
            for copy in sum_copies(matrix, phase):
                copy.wait_send()
    for copy in results:
        copy.wait()


def back(
    grad_unrolled,
    rolled,
    mixed,
    weights,
    rel,
    tokens,
    grad_middle,
    small_all,
    small_grads,
    attend,
    fc1_grad,
    fc2_grad,
    proj_grad,
):
    anywhere, inside = pl.BlockSpec(memory_space=pl.ANY), pl.BlockSpec(memory_space=pltpu.VMEM)
    reps = lax.axis_size("rep")
    dma = pltpu.SemaphoreType.DMA
    order = send_matrix()
    extra = max(1, reps.bit_length() - 4)
    held = []
    for rows, columns, _ in SUMMED:
        held += [
            pltpu.VMEM((4, 2, 2, rows, columns), bf16),
            pltpu.VMEM((4, 2, 2, rows, columns), bf16),
            pltpu.VMEM((4, 2, rows, columns), bf16),
            pltpu.VMEM((4, rows, columns), bf16),
            pltpu.VMEM((3 + extra, rows, columns), bf16),
            pltpu.VMEM((2, 2, 2, rows, columns), bf16),
        ]
    return pl.pallas_call(
        back_kernel,
        out_shape=(
            jax.ShapeDtypeStruct(tokens.shape, f32),
            *[jax.ShapeDtypeStruct((2, 2, 2) + shape[:2], bf16) for shape in SUMMED],
            jax.ShapeDtypeStruct((SLAB, 128), f32),
        ),
        in_specs=[inside] * 11 + [anywhere] * 4,
        out_specs=(inside, *[anywhere] * 5, inside),
        scratch_shapes=[
            pltpu.VMEM((2 * PAD, D), bf16),
            pltpu.VMEM((2 * PAD, D), bf16),
            pltpu.VMEM((3, PAD, LANES), bf16),
            pltpu.VMEM((2 * PAD, 3 * D), bf16),
            pltpu.VMEM((2 * PAD, D), bf16),
            pltpu.VMEM((2 * PAD, D), bf16),
            pltpu.VMEM((TILES, PAD * HEADS, 128), f32),
            pltpu.VMEM((TILES, HALF * HEADS, 128), bf16),
            pltpu.VMEM((TILES, HALF * HEADS, 128), bf16),
            pltpu.VMEM((4, 2, 2, 2, 16, 768), bf16),
            pltpu.VMEM((4, 2, 2, 2, 16, 768), bf16),
            pltpu.VMEM((SPANS * HEADS, SPAN), f32),
            pltpu.VMEM((4, SLAB, 128), f32),
            pltpu.VMEM((3, SLAB, 128), f32),
            pltpu.VMEM((reps, SLAB, 128), f32),
            *held,
            dma((5, 7, 3)),
            dma((5, 7, 3)),
            dma((5, extra)),
            dma((5, extra)),
            dma((2, 3)),
            dma((2, 3)),
            dma((2, 3)),
            dma((2, 3)),
            dma((3,)),
            dma((1,)),
            dma((1,)),
            dma((3 + reps,)),
            dma((3 + reps,)),
            dma((10,)),
        ],
        compiler_params=pltpu.CompilerParams(
            vmem_limit_bytes=VMEM_LIMIT, collective_id=1, has_side_effects=True
        ),
        name="back",
    )(
        grad_unrolled,
        jnp.asarray(order, bf16),
        jnp.asarray(order.T, bf16),
        rolled,
        mixed,
        weights,
        rel,
        tokens,
        grad_middle,
        small_all,
        small_grads,
        attend,
        fc1_grad.reshape(4, 2, 2, 2, 16, 2048),
        fc2_grad.reshape(4, 2, 2, 2, 64, 512),
        proj_grad.reshape(4, 2, 2, 2, 16, 512),
    )


def norm_forward(rows, gain, shift):
    centre = rows - jnp.mean(rows, -1, keepdims=True)
    inverse = lax.rsqrt(jnp.mean(centre * centre, -1, keepdims=True) + 1e-05)
    normal = centre * inverse
    return (normal * gain.astype(jnp.float32) + shift.astype(jnp.float32), normal, inverse)


def norm_backward(grad_out, normal, inverse, gain):
    scaled = grad_out * gain.astype(jnp.float32)
    inner = (
        scaled
        - jnp.mean(scaled, -1, keepdims=True)
        - normal * jnp.mean(scaled * normal, -1, keepdims=True)
    )
    return (inverse * inner, jnp.sum(grad_out * normal, 0), jnp.sum(grad_out, 0))


def shards(
    tokens,
    region,
    rel_index,
    ln1_gain,
    ln1_shift,
    w_qkv,
    q_bias,
    v_bias,
    table,
    w_proj,
    proj_bias,
    ln2_gain,
    ln2_shift,
    w_fc1,
    fc1_bias,
    w_fc2,
    fc2_bias,
    cotangent,
):
    inputs = tokens.reshape(-1, D).astype(jnp.float32)
    small = jnp.concatenate(
        (ln1_gain, ln1_shift, q_bias, v_bias, proj_bias, ln2_gain, ln2_shift, fc2_bias, fc1_bias)
    ).reshape(-1, 128)
    small = jnp.pad(small, ((0, SMALL - small.shape[0]), (0, 0)))
    chunks = jnp.pad(table.astype(f32).T, ((0, 0), (0, CHUNKS * 128 - TABLE)))
    labels = region.reshape(WT, WH, 2, WW).transpose(2, 0, 1, 3).reshape(2, WIN)
    labels = pieces_of(labels, 1, -1)
    row_ids = jnp.pad(labels, ((0, 0), (0, LANES - PAD)), constant_values=-1)[:, None]
    (
        whole_qkv,
        whole_proj,
        whole_fc1,
        whole_fc2,
        small,
        rolled,
        qkv,
        attend,
        contexts,
        rel,
    ) = front(
        tokens.reshape(-1, D),
        small,
        chunks.reshape(-1, 128),
        row_ids,
        rel_index,
        w_qkv,
        w_proj,
        w_fc1,
        w_fc2,
    )
    gain_one, bias_proj = small[:, LN1_GAIN].reshape(-1), small[:, PROJ_BIAS].reshape(-1)
    gain_two, shift_two = small[:, LN2_GAIN].reshape(-1), small[:, LN2_SHIFT].reshape(-1)
    bias_fc2 = small[:, FC2_BIAS].reshape(-1)
    bias_fc1 = small[:, FC1_BIAS : FC1_BIAS + 4].reshape(-1)
    order = jnp.asarray(send_matrix(), bf16)
    unrolled = dot(order, contexts, TN).astype(bf16)
    middle = (
        inputs
        + jnp.dot(unrolled, whole_proj, preferred_element_type=jnp.float32)
        + bias_proj.astype(jnp.float32)
    )
    normed_two, normal_two, inverse_two = norm_forward(middle, gain_two, shift_two)
    normed_low = normed_two.astype(jnp.bfloat16)
    hidden = jnp.dot(normed_low, whole_fc1, preferred_element_type=jnp.float32) + bias_fc1.astype(
        jnp.float32
    )
    active = jax.nn.gelu(hidden, approximate=False).astype(jnp.bfloat16)
    result = (
        middle
        + jnp.dot(active, whole_fc2, preferred_element_type=jnp.float32)
        + bias_fc2.astype(jnp.float32)
    )
    output = result.astype(jnp.bfloat16).reshape(tokens.shape)
    grad_out = cotangent.reshape(-1, D)
    grad_w_fc2 = jnp.einsum("rf,rd->fd", active, grad_out, preferred_element_type=jnp.float32)
    grad_fc2_bias = jnp.sum(grad_out.astype(jnp.float32), 0)
    slope = (
        0.5 * (1.0 + lax.erf(hidden * 0.7071067811865476))
        + hidden * jnp.exp(-0.5 * hidden * hidden) * 0.3989422804014327
    )
    grad_active = jnp.einsum("rd,fd->rf", grad_out, whole_fc2, preferred_element_type=jnp.float32)
    grad_hidden = (grad_active * slope).astype(jnp.bfloat16)
    grad_w_fc1 = jnp.einsum(
        "rd,rf->df", normed_low, grad_hidden, preferred_element_type=jnp.float32
    )
    grad_fc1_bias = jnp.sum(grad_hidden.astype(jnp.float32), 0)
    grad_normed_two = jnp.einsum(
        "rf,df->rd", grad_hidden, whole_fc1, preferred_element_type=jnp.float32
    )
    grad_inner_two, grad_ln2_gain, grad_ln2_shift = norm_backward(
        grad_normed_two, normal_two, inverse_two, gain_two
    )
    grad_middle = grad_out.astype(jnp.float32) + grad_inner_two
    grad_branch = grad_middle.astype(jnp.bfloat16)
    grad_w_proj = jnp.einsum("rd,re->de", unrolled, grad_branch, preferred_element_type=jnp.float32)
    grad_proj_bias = jnp.sum(grad_branch.astype(jnp.float32), 0)
    grad_unrolled = jnp.einsum(
        "re,de->rd", grad_branch, whole_proj, preferred_element_type=jnp.float32
    ).astype(jnp.bfloat16)
    rows = [jnp.zeros((4, 128), f32)] * 4
    for gradient in (grad_proj_bias, grad_ln2_gain, grad_ln2_shift, grad_fc2_bias):
        rows.append(gradient.reshape(4, 128))
    small_grads = jnp.concatenate(
        [jnp.stack(rows, 1), grad_fc1_bias.reshape(4, 4, 128), jnp.zeros((4, 4, 128), f32)], 1
    )
    grad_tokens, grad_w_fc1, grad_w_fc2, grad_w_proj, grad_w_qkv_a, grad_w_qkv_b, slab = back(
        grad_unrolled,
        rolled,
        qkv,
        whole_qkv,
        rel,
        tokens.reshape(-1, D),
        grad_middle,
        small,
        small_grads,
        attend,
        grad_w_fc1.astype(bf16),
        grad_w_fc2.astype(bf16),
        grad_w_proj.astype(bf16),
    )
    grad_tokens = grad_tokens.reshape(tokens.shape)
    grad_w_fc1 = grad_w_fc1.astype(f32).reshape(w_fc1.shape)
    grad_w_fc2 = grad_w_fc2.astype(f32).reshape(w_fc2.shape)
    grad_w_proj = grad_w_proj.astype(f32).reshape(w_proj.shape)
    grad_w_qkv = jnp.concatenate((grad_w_qkv_a, grad_w_qkv_b), -1).astype(f32)
    grad_w_qkv = grad_w_qkv.reshape(w_qkv.shape)
    spans = slab[: 2 * SPANS * GROUP].reshape(2, SPANS, GROUP, 128).transpose(1, 0, 3, 2)
    grad_table = spans.reshape(SPANS * SPAN, GROUP)[:TABLE]
    vectors = slab[2 * SPANS * GROUP :]
    grad_ln1_gain, grad_ln1_shift = vectors[LN1_GAIN], vectors[LN1_SHIFT]
    grad_q_bias, grad_v_bias = vectors[Q_BIAS], vectors[V_BIAS]
    grad_proj_bias, grad_fc2_bias = vectors[PROJ_BIAS], vectors[FC2_BIAS]
    grad_ln2_gain, grad_ln2_shift = vectors[LN2_GAIN], vectors[LN2_SHIFT]
    grad_fc1_bias = vectors[FC1_BIAS : FC1_BIAS + 4].reshape(-1)
    return (
        output,
        grad_tokens,
        grad_ln1_gain,
        grad_ln1_shift,
        grad_w_qkv,
        grad_q_bias,
        grad_v_bias,
        grad_table,
        grad_w_proj,
        grad_proj_bias,
        grad_ln2_gain,
        grad_ln2_shift,
        grad_w_fc1,
        grad_fc1_bias,
        grad_w_fc2,
        grad_fc2_bias,
    )


def solution(mesh):
    return jax.shard_map(
        shards,
        mesh=mesh,
        in_specs=(
            P("rep", "shard", None, None),
            P("shard", None),
            P(),
            P("shard"),
            P("shard"),
            P("shard", None),
            P("shard"),
            P("shard"),
            P(None, "shard"),
            P("shard", None),
            P("shard"),
            P("shard"),
            P("shard"),
            P("shard", None),
            P("shard"),
            P("shard", None),
            P("shard"),
            P("rep", "shard", None, None),
        ),
        out_specs=(
            P("rep", "shard", None, None),
            P("rep", "shard", None, None),
            P("shard"),
            P("shard"),
            P("shard", None),
            P("shard"),
            P("shard"),
            P(None, "shard"),
            P("shard", None),
            P("shard"),
            P("shard"),
            P("shard"),
            P("shard", None),
            P("shard"),
            P("shard", None),
            P("shard"),
        ),
        check_vma=False,
    )
```

```python
import functools

import jax
import jax.numpy as jnp
import numpy as np
from jax import lax
from jax.experimental import pallas as pl
from jax.experimental.pallas import tpu as pltpu
from jax.sharding import PartitionSpec as P

D = 512
HEADS = 16
HD = 32
WT = 8
WH = 7
WW = 7
WIN = 392
TABLE = 2535
PAD = 416
LANES = 512
GROUP = 4
CHUNKS = 20
SCALE = HD ** (-0.5)
NN = (((1,), (0,)), ((), ()))
NT = (((1,), (1,)), ((), ()))
TN = (((0,), (0,)), ((), ()))
VMEM_LIMIT = 60 * 2**20
f32 = jnp.float32
bf16 = jnp.bfloat16

PIECES = (
    ((0, 4), (0, 4), 112, 0),
    ((4, 8), (0, 4), 112, 112),
    ((0, 4), (4, 7), 96, 224),
    ((4, 8), (4, 7), 96, 320),
)


def send_matrix():
    matrix = np.zeros((2 * PAD, WT * WH * 2 * WW), np.float32)
    for window in range(2):
        for (t0, t1), (h0, h1), _, first in PIECES:
            row = window * PAD + first
            for t in range(t0, t1):
                for h in range(h0, h1):
                    for w in range(WW):
                        column = (window * WW + w + WW // 2) % (2 * WW)
                        source = ((t + 4) % WT * WH + (h + 3) % WH) * 2 * WW + column
                        matrix[row, source] = 1.0
                        row += 1
    return matrix


def spread_matrix():
    source = np.arange(WIN).reshape(WT, WH, WW)
    matrix = np.zeros((PAD, WIN), np.float32)
    for (t0, t1), (h0, h1), _, first in PIECES:
        tokens = source[t0:t1, h0:h1].reshape(-1)
        matrix[first + np.arange(tokens.size), tokens] = 1.0
    return matrix


def pieces_of(array, axis, fill):
    shape = array.shape
    split = array.reshape(shape[:axis] + (WT, WH, WW) + shape[axis + 1 :])
    parts = []
    for (t0, t1), (h0, h1), padded, _ in PIECES:
        part = lax.slice_in_dim(lax.slice_in_dim(split, t0, t1, axis=axis), h0, h1, axis=axis + 1)
        length = (t1 - t0) * (h1 - h0) * WW
        part = part.reshape(shape[:axis] + (length,) + shape[axis + 1 :])
        widths = [(0, 0, 0)] * len(shape)
        widths[axis] = (0, padded - length, 0)
        parts.append(lax.pad(part, jnp.asarray(fill, array.dtype), widths))
    return jnp.concatenate(parts, axis)


def dot(a, b, dims=NN):
    return lax.dot_general(a, b, dims, preferred_element_type=f32)


MESH = pl.DeviceIdType.MESH
PARTS = 8
FIRST_ROWS = tuple(first for _, _, _, first in PIECES)
LENGTHS = tuple(padded for _, _, padded, _ in PIECES)
ACROSS = (0, 2, 1, 3)
LN1_GAIN, LN1_SHIFT, Q_BIAS, V_BIAS, PROJ_BIAS, LN2_GAIN, LN2_SHIFT, FC2_BIAS, FC1_BIAS = range(9)
SMALL = 16


def place():
    rep, shard = lax.axis_index("rep"), lax.axis_index("shard")
    return rep, shard, lax.rem(rep, 2), lax.rem(rep // 2, 2), lax.rem(rep // 4, 2)


def flip(rep, bit):
    low = lax.rem(rep // (1 << bit), 2)
    return rep + (1 - 2 * low) * (1 << bit)


def remote(src, dst, send, recv, rep, shard):
    return pltpu.make_async_remote_copy(
        src_ref=src,
        dst_ref=dst,
        send_sem=send,
        recv_sem=recv,
        device_id={"rep": rep, "shard": shard},
        device_id_type=MESH,
    )


def greet(peers):
    barrier = pltpu.get_barrier_semaphore()
    for rep, shard in peers:
        pl.semaphore_signal(
            barrier, inc=1, device_id={"rep": rep, "shard": shard}, device_id_type=MESH
        )
    pl.semaphore_wait(barrier, len(peers))


def peers_of(rep, shard):
    return [(rep, lax.rem(shard + k, 4)) for k in (1, 2, 3)] + [
        (flip(rep, bit), shard) for bit in (0, 1, 2)
    ]


def quarter_across(shard, bits):
    low, high = lax.rem(shard, 2), shard // 2
    if bits & 1:
        low = 1 - low
    if bits & 2:
        high = 1 - high
    return high * 2 + low


def pieces_to(source, target, send, recv, rep, shard, window, columns=None):
    copies = []
    for piece in (1, 2, 3):
        rows = pl.ds(
            pl.multiple_of(window * PAD + FIRST_ROWS[piece], 16), LENGTHS[piece]
        )
        at = (rows,) if columns is None else (rows, columns)
        copies.append(
            remote(
                source.at[at],
                target.at[at],
                send(piece - 1),
                recv(piece - 1),
                rep,
                quarter_across(shard, ACROSS[piece]),
            )
        )
    return copies


def norm_rows(rows):
    centre = rows - jnp.mean(rows, -1, keepdims=True)
    inverse = lax.rsqrt(jnp.mean(centre * centre, -1, keepdims=True) + 1e-05)
    return centre * inverse, inverse


def small_row(ref, row):
    return jnp.concatenate([ref[s, row : row + 1, :] for s in range(4)], 1)


Z_PHASE, FIRST_PHASE, SECOND_PHASE, CORE_PHASE = range(4)
X_FIRST = (True, False, False, True)


def front_kernel(
    tokens,
    order,
    spread,
    small,
    table,
    row_ids,
    rel,
    qkv_part,
    proj_part,
    fc1_part,
    fc2_part,
    qkv_whole,
    proj_whole,
    fc1_whole,
    fc2_whole,
    small_out,
    rolled_out,
    mixed_out,
    attend_out,
    back_out,
    rel_out,
    small_all,
    table_all,
    table_wide,
    outgoing,
    arriving,
    rolled,
    weights,
    mixed,
    index,
    bias,
    mask,
    attend,
    contexts,
    gather_send,
    gather_recv,
    small_send,
    small_recv,
    bias_send,
    bias_recv,
    piece_send,
    piece_recv,
    back_send,
    back_recv,
    local,
    attend_sem,
):
    rep, shard, core, x_bit, y_bit = place()
    greet(peers_of(rep, shard))
    parts = (qkv_part, proj_part, fc1_part, fc2_part)
    wholes = (qkv_whole, proj_whole, fc1_whole, fc2_whole)

    def gather(matrix, phase):
        copies = []
        for k in (1, 2, 3):
            at = lax.rem(shard + k, 4)
            whole = wholes[matrix]
            if phase == Z_PHASE:
                copies.append(
                    remote(
                        parts[matrix].at[y_bit, x_bit, core],
                        whole.at[shard, y_bit, x_bit, core],
                        gather_send.at[matrix, phase, k - 1],
                        gather_recv.at[matrix, phase, 3 - k],
                        rep,
                        at,
                    )
                )
                continue
            x_first = X_FIRST[matrix]
            if phase == FIRST_PHASE:
                block, partner = whole.at[at, y_bit, x_bit, core], flip(rep, 1 if x_first else 2)
            elif phase == SECOND_PHASE and x_first:
                block, partner = whole.at[at, y_bit, :, core], flip(rep, 2)
            elif phase == SECOND_PHASE:
                block, partner = whole.at[at, :, x_bit, core], flip(rep, 1)
            else:
                block, partner = whole.at[at, :, :, core], flip(rep, 0)
            copies.append(
                remote(
                    block,
                    block,
                    gather_send.at[matrix, phase, k - 1],
                    gather_recv.at[matrix, phase, k - 1],
                    partner,
                    shard,
                )
            )
        return copies

    def start(matrix, phase):
        for copy in gather(matrix, phase):
            copy.start()

    def arrived(matrix, phase):
        for copy in gather(matrix, phase):
            copy.wait_recv()

    def small_copies():
        copies = []
        for k in (1, 2, 3):
            for n, ref in enumerate((table_all, small_all)):
                copies.append(
                    remote(
                        ref.at[shard],
                        ref.at[shard],
                        small_send.at[n, k - 1],
                        small_recv.at[n, 3 - k],
                        rep,
                        lax.rem(shard + k, 4),
                    )
                )
        return copies

    small_all[shard] = small[...]
    table_all[shard] = table[...]
    for copy in small_copies():
        copy.start()
    start(0, Z_PHASE)
    own = [
        pltpu.make_async_copy(parts[m], wholes[m].at[shard], local.at[m]) for m in range(4)
    ]
    for copy in own:
        copy.start()

    outgoing[...] = dot(order[...], tokens[...]).astype(bf16)

    def roll_copies(window):
        return pieces_to(
            outgoing,
            arriving,
            lambda n: piece_send.at[window, n],
            lambda n: piece_recv.at[window, n],
            rep,
            shard,
            window,
        )

    for window in range(2):
        for copy in roll_copies(window):
            copy.start()
        rows = slice(window * PAD, window * PAD + LENGTHS[0])
        arriving[rows, :] = outgoing[rows, :]

    rel_index = rel[...]
    digits = (rel_index // 256).astype(f32).astype(bf16), (rel_index & 255).astype(f32).astype(bf16)
    moved = []
    for digit in digits:
        half = dot(spread[...], digit).astype(bf16)
        moved.append(dot(half, spread[...], NT).astype(jnp.int32))
    index[:, :PAD] = moved[0] * 256 + moved[1]
    index[:, PAD:] = jnp.zeros((PAD, LANES - PAD), jnp.int32)

    ids = lax.broadcasted_iota(jnp.int32, (8, LANES), 0)
    for window in range(2):
        kinds = jnp.where(row_ids[window] + 1 == ids, 1.0, 0.0).astype(bf16)[:, :PAD]
        mask[window] = (dot(kinds, kinds, TN) - 1.0) * 1e30

    for copy in small_copies():
        copy.wait_recv()

    for chunk in range(CHUNKS):
        for head in range(HEADS // 2):
            row = (head % 4) * CHUNKS + chunk
            table_wide[chunk, head] = jnp.broadcast_to(
                table_all[2 * core + head // 4, row : row + 1, :], (8, 128)
            )
    mine = core * (HEADS // 2)

    def bias_copy(rows, step):
        block = bias.at[pl.ds(mine, HEADS // 2), rows]
        return remote(block, block, bias_send.at[step], bias_recv.at[step], flip(rep, 0), shard)

    def on_the_way(step, table_of_steps):
        for when, actions in table_of_steps.items():

            @pl.when(step == when)
            def _():
                for action, matrix, phase in actions:
                    action(matrix, phase)

    def advance(matrix, phase):
        arrived(matrix, phase)
        if phase < CORE_PHASE:
            start(matrix, phase + 1)

    schedule = {
        4: [(advance, 0, Z_PHASE)],
        8: [(advance, 0, FIRST_PHASE)],
        15: [(advance, 0, SECOND_PHASE)],
        17: [(start, 1, Z_PHASE), (start, 2, Z_PHASE), (start, 3, Z_PHASE)],
    }
    later = {
        1: [(advance, 1, Z_PHASE), (advance, 2, Z_PHASE), (advance, 3, Z_PHASE)],
        8: [(advance, 1, FIRST_PHASE), (advance, 2, FIRST_PHASE), (advance, 3, FIRST_PHASE)],
        21: [(advance, 1, SECOND_PHASE), (advance, 2, SECOND_PHASE), (advance, 3, SECOND_PHASE)],
    }

    def bias_step(step, carry):
        on_the_way(step, schedule)
        rows = pl.ds(pl.multiple_of(step * 16, 16), 16)
        for tile in range(LANES // 128):
            lanes = slice(tile * 128, (tile + 1) * 128)
            here = index[rows, lanes]
            halves = [(here[s : s + 8] & 127, here[s : s + 8] >> 7) for s in (0, 8)]
            found = [[None, None] for _ in range(HEADS // 2)]
            for chunk in range(CHUNKS):
                for s, (low, high) in enumerate(halves):
                    hit = high == chunk
                    for head in range(HEADS // 2):
                        value = jnp.take_along_axis(table_wide[chunk, head], low, axis=1)
                        if chunk:
                            value = jnp.where(hit, value, found[head][s])
                        found[head][s] = value
            for head in range(HEADS // 2):
                bias[mine + head, rows, lanes] = jnp.concatenate(found[head], 0).astype(bf16)
        bias_copy(rows, step).start()
        return carry

    lax.fori_loop(0, PAD // 16, bias_step, 0)

    arrived(0, CORE_PHASE)
    own[0].wait()
    fetch = pltpu.make_async_copy(qkv_whole, weights, local.at[4])
    fetch.start()
    fetch.wait()
    q_bias, v_bias = small_row(small_all, Q_BIAS), small_row(small_all, V_BIAS)
    mixed_bias = jnp.concatenate([q_bias, jnp.zeros_like(q_bias), v_bias], 1).astype(f32)
    gain, shift = small_row(small_all, LN1_GAIN), small_row(small_all, LN1_SHIFT)

    def norm_step(step, carry):
        rows = pl.ds(pl.multiple_of(step * 208, 16), 208)
        normal, _ = norm_rows(arriving[rows, :].astype(f32))
        rolled[rows, :] = (normal * gain.astype(f32) + shift.astype(f32)).astype(bf16)
        return carry

    for window in range(2):
        for copy in roll_copies(window):
            copy.wait_recv()
        span = slice(window * PAD, (window + 1) * PAD)
        lax.fori_loop(2 * window, 2 * window + 2, norm_step, 0)
        for part in range(3):
            lanes = slice(part * D, (part + 1) * D)
            got = dot(rolled[span, :], weights[...].reshape(D, 3 * D)[:, lanes])
            mixed[span, lanes] = (got + mixed_bias[:, lanes]).astype(bf16)
    keep = [
        pltpu.make_async_copy(rolled, rolled_out, local.at[4]),
        pltpu.make_async_copy(mixed, mixed_out, local.at[5]),
        pltpu.make_async_copy(index, rel_out, local.at[6]),
        pltpu.make_async_copy(small_all, small_out, local.at[7]),
    ]
    for copy in keep:
        copy.start()

    def bias_wait(step, carry):
        bias_copy(pl.ds(pl.multiple_of(step * 16, 16), 16), step).wait_recv()
        return carry

    lax.fori_loop(0, PAD // 16, bias_wait, 0)

    head_of = lax.broadcasted_iota(jnp.int32, (1, 128), 1) // HD
    none = jnp.zeros((), bf16)

    def attend_copy(step):
        window, head, slot = step // HEADS, lax.rem(step, HEADS), lax.rem(step, 2)
        return pltpu.make_async_copy(
            attend.at[slot], attend_out.at[window, head], attend_sem.at[slot]
        )

    def back_copies(step):
        window, group = step // HEADS, lax.rem(step // GROUP, HEADS // GROUP)
        lanes = pl.ds(pl.multiple_of(group * 128, 128), 128)
        return pieces_to(
            contexts,
            back_out,
            lambda n: back_send.at[window, group, n],
            lambda n: back_recv.at[window, group, n],
            rep,
            shard,
            window,
            lanes,
        )

    def attend_step(step, carry):
        on_the_way(step, later)
        window, head = step // HEADS, lax.rem(step, HEADS)
        group, member, slot = head // GROUP, lax.rem(head, GROUP), lax.rem(step, 2)
        rows = pl.ds(pl.multiple_of(window * PAD, 16), PAD)

        def lanes(part):
            return pl.ds(pl.multiple_of(part * D + group * 128, 128), 128)

        own_lanes = head_of == member
        query = jnp.where(own_lanes, mixed[rows, lanes(0)], none)
        value = jnp.where(own_lanes, mixed[rows, lanes(2)], none)
        scores = dot(query, mixed[rows, lanes(1)], NT) * SCALE + bias[head, :, :PAD].astype(f32)
        scores = scores + mask[window]
        expo = jnp.exp(scores - jnp.max(scores, -1, keepdims=True))
        weight = (expo * (1.0 / jnp.sum(expo, -1, keepdims=True))).astype(bf16)

        @pl.when(step >= 2)
        def _():
            attend_copy(step - 2).wait()

        attend[slot, :, :PAD] = weight
        attend_copy(step).start()
        result = dot(weight, value).astype(bf16)
        contexts[rows, lanes(0)] = jnp.where(own_lanes, result, contexts[rows, lanes(0)])

        @pl.when(member == GROUP - 1)
        def _():
            for copy in back_copies(step):
                copy.start()

        return carry

    lax.fori_loop(0, 2 * HEADS, attend_step, 0)

    stay = [
        pltpu.make_async_copy(
            contexts.at[pl.ds(w * PAD, LENGTHS[0])],
            back_out.at[pl.ds(w * PAD, LENGTHS[0])],
            local.at[8 + w],
        )
        for w in range(2)
    ]
    for copy in stay:
        copy.start()
    for matrix in (1, 2, 3):
        arrived(matrix, CORE_PHASE)
    attend_copy(2 * HEADS - 2).wait()
    attend_copy(2 * HEADS - 1).wait()

    def back_wait(step, carry):
        for copy in back_copies(step * GROUP):
            copy.wait()
        return carry

    lax.fori_loop(0, 2 * HEADS // GROUP, back_wait, 0)

    def bias_sent(step, carry):
        bias_copy(pl.ds(pl.multiple_of(step * 16, 16), 16), step).wait_send()
        return carry

    lax.fori_loop(0, PAD // 16, bias_sent, 0)
    for copy in small_copies():
        copy.wait_send()
    for window in range(2):
        for copy in roll_copies(window):
            copy.wait_send()
    for matrix in range(4):
        for phase in range(4):
            for copy in gather(matrix, phase):
                copy.wait_send()
    for copy in own[1:] + keep + stay:
        copy.wait()


def front(tokens, small, table, row_ids, rel_index, w_qkv, w_proj, w_fc1, w_fc2):
    anywhere, inside = pl.BlockSpec(memory_space=pl.ANY), pl.BlockSpec(memory_space=pltpu.VMEM)
    cut = (2, 2, 2)
    weights = [
        w.reshape(cut + (w.shape[0] // PARTS, w.shape[1])) for w in (w_qkv, w_proj, w_fc1, w_fc2)
    ]
    wholes = [jax.ShapeDtypeStruct((4,) + w.shape, bf16) for w in weights]
    dma = pltpu.SemaphoreType.DMA
    results = pl.pallas_call(
        front_kernel,
        out_shape=(
            *wholes,
            jax.ShapeDtypeStruct((4, SMALL, 128), bf16),
            jax.ShapeDtypeStruct((2 * PAD, D), bf16),
            jax.ShapeDtypeStruct((2 * PAD, 3 * D), bf16),
            jax.ShapeDtypeStruct((2, HEADS, PAD, LANES), bf16),
            jax.ShapeDtypeStruct((2 * PAD, D), bf16),
            jax.ShapeDtypeStruct((PAD, LANES), jnp.int32),
        ),
        in_specs=[inside] * 7 + [anywhere] * 4,
        out_specs=(anywhere,) * 10,
        scratch_shapes=[
            pltpu.VMEM((4, SMALL, 128), bf16),
            pltpu.VMEM((4, GROUP * CHUNKS, 128), f32),
            pltpu.VMEM((CHUNKS, HEADS // 2, 8, 128), f32),
            pltpu.VMEM((2 * PAD, D), bf16),
            pltpu.VMEM((2 * PAD, D), bf16),
            pltpu.VMEM((2 * PAD, D), bf16),
            pltpu.VMEM(wholes[0].shape, bf16),
            pltpu.VMEM((2 * PAD, 3 * D), bf16),
            pltpu.VMEM((PAD, LANES), jnp.int32),
            pltpu.VMEM((HEADS, PAD, LANES), bf16),
            pltpu.VMEM((2, PAD, PAD), f32),
            pltpu.VMEM((2, PAD, LANES), bf16),
            pltpu.VMEM((2 * PAD, D), bf16),
            dma((4, 4, 3)),
            dma((4, 4, 3)),
            dma((2, 3)),
            dma((2, 3)),
            dma((PAD // 16,)),
            dma((PAD // 16,)),
            dma((2, 3)),
            dma((2, 3)),
            dma((2, HEADS // GROUP, 3)),
            dma((2, HEADS // GROUP, 3)),
            dma((10,)),
            dma((2,)),
        ],
        compiler_params=pltpu.CompilerParams(
            vmem_limit_bytes=VMEM_LIMIT, collective_id=0, has_side_effects=True
        ),
        name="front",
    )(
        tokens,
        jnp.asarray(send_matrix(), bf16),
        jnp.asarray(spread_matrix(), bf16),
        small,
        table,
        row_ids,
        rel_index,
        *weights,
    )
    whole = [w.reshape(-1, w.shape[-1]) for w in results[:4]]
    return (*whole, *results[4:])


CORE_SUM, FIRST_SUM, SECOND_SUM, Z_SUM, SECOND_SHARE, FIRST_SHARE, CORE_SHARE = range(7)
SUMMED = ((16, 2048, True), (64, 512, False), (16, 512, True), (16, 768, True), (16, 768, False))
FC1, FC2, PROJ, QKV_A, QKV_B = range(5)
SPAN = 256
SPANS = -(-TABLE // SPAN)
BATCH = 8
HALF = PAD // 2
TILES = LANES // 128
SLAB = 2 * SPANS * GROUP + SMALL


def back_kernel(
    grad_unrolled,
    order,
    order_back,
    rolled,
    mixed,
    weights,
    rel,
    tokens,
    grad_middle,
    small_all,
    small_grads,
    attend_in,
    fc1_grad,
    fc2_grad,
    proj_grad,
    grad_tokens,
    fc1_out,
    fc2_out,
    proj_out,
    qkv_out_a,
    qkv_out_b,
    slab_out,
    outgoing,
    grad_context,
    attend,
    grads,
    grad_rolled,
    returned,
    pairs,
    pairs_out,
    pairs_in,
    qkv_grad_a,
    qkv_grad_b,
    table_sum,
    slab,
    slab_z,
    slab_rep,
    *rest,
):
    held = [rest[6 * m : 6 * m + 6] for m in range(5)]
    (
        sum_send,
        sum_recv,
        extra_send,
        extra_recv,
        piece_send,
        piece_recv,
        back_send,
        back_recv,
        attend_sem,
        pairs_send,
        pairs_recv,
        slab_send,
        slab_recv,
        local,
    ) = rest[30:]
    rep, shard, core, x_bit, y_bit = place()
    reps = lax.axis_size("rep")
    barrier = pltpu.get_barrier_semaphore()

    def hello(k, carry):
        pl.semaphore_signal(
            barrier,
            inc=1,
            device_id={"rep": lax.rem(rep + k, reps), "shard": shard},
            device_id_type=MESH,
        )
        return carry

    lax.fori_loop(1, reps, hello, 0)
    for k in (1, 2, 3):
        pl.semaphore_signal(
            barrier,
            inc=1,
            device_id={"rep": rep, "shard": lax.rem(shard + k, 4)},
            device_id_type=MESH,
        )
    pl.semaphore_wait(barrier, reps + 2)

    sources = (fc1_grad, fc2_grad, proj_grad, qkv_grad_a, qkv_grad_b)

    def axis_of(matrix, first):
        x_first = SUMMED[matrix][2]
        use_x = x_first == first
        return (1, x_bit) if use_x else (2, y_bit)

    def sum_copies(matrix, phase):
        from_core, kept, from_first, summed, from_z, shared = held[matrix]
        x_first = SUMMED[matrix][2]
        first_bit, first = axis_of(matrix, True)
        second_bit, second = axis_of(matrix, False)

        def one(src, dst, bit, n=0):
            return remote(
                src,
                dst,
                sum_send.at[matrix, phase, n],
                sum_recv.at[matrix, phase, n],
                flip(rep, bit),
                shard,
            )

        if phase == CORE_SUM:
            return [one(sources[matrix].at[:, :, :, 1 - core], from_core, 0)]
        if phase == FIRST_SUM:
            cut = kept.at[:, :, 1 - x_bit] if x_first else kept.at[:, 1 - y_bit]
            return [one(cut, from_first, first_bit)]
        if phase == SECOND_SUM:
            return [one(from_first.at[:, 1 - second], summed, second_bit)]
        if phase == Z_SUM:
            copies = []
            for k in (1, 2, 3):
                to = lax.rem(shard + k, 4)
                copies.append(
                    remote(
                        summed.at[to],
                        from_z.at[3 - k],
                        sum_send.at[matrix, phase, k - 1],
                        sum_recv.at[matrix, phase, 3 - k],
                        rep,
                        to,
                    )
                )
            return copies
        if phase == SECOND_SHARE:
            block = shared.at[y_bit, x_bit, core]
            return [one(block, block, second_bit)]
        if phase == FIRST_SHARE:
            block = shared.at[:, x_bit, core] if x_first else shared.at[y_bit, :, core]
            return [one(block, block, first_bit)]
        block = shared.at[:, :, core]
        return [one(block, block, 0)]

    def own_copy(matrix):
        return pltpu.make_async_copy(
            sources[matrix].at[:, :, :, core], held[matrix][1], local.at[matrix]
        )

    def extra_copy(matrix, bit):
        shared, from_z = held[matrix][5], held[matrix][4]
        return remote(
            shared.at[y_bit, x_bit, core],
            from_z.at[bit],
            extra_send.at[matrix, bit - 3],
            extra_recv.at[matrix, bit - 3],
            flip(rep, bit),
            shard,
        )

    def add(into, at, other, other_at):
        into[at] = (into[at].astype(f32) + other[other_at].astype(f32)).astype(bf16)

    def begin(matrix):
        own_copy(matrix).start()
        for copy in sum_copies(matrix, CORE_SUM):
            copy.start()

    def advance(matrix, phase):
        from_core, kept, from_first, summed, from_z, shared = held[matrix]
        x_first = SUMMED[matrix][2]
        _, second = axis_of(matrix, False)
        for copy in sum_copies(matrix, phase):
            copy.wait_recv()
        if phase == CORE_SUM:
            own_copy(matrix).wait()

            def step(n, carry):
                at = (n // 4, lax.rem(n // 2, 2), lax.rem(n, 2))
                add(kept, at, from_core, at)
                return carry

            lax.fori_loop(0, 16, step, 0)
        elif phase == FIRST_SUM:

            def step(n, carry):
                owner, other = n // 2, lax.rem(n, 2)
                at = (owner, other, x_bit) if x_first else (owner, y_bit, other)
                add(from_first, (owner, other), kept, at)
                return carry

            lax.fori_loop(0, 8, step, 0)
        elif phase == SECOND_SUM:

            def step(owner, carry):
                add(summed, (owner,), from_first, (owner, second))
                return carry

            lax.fori_loop(0, 4, step, 0)
        elif phase == Z_SUM:
            total = summed[shard].astype(f32)
            for n in range(3):
                total = total + from_z[n].astype(f32)
            shared[y_bit, x_bit, core] = total.astype(bf16)
            bit = 3
            while (1 << bit) < reps:
                copy = extra_copy(matrix, bit)
                copy.start()
                copy.wait()
                at = (y_bit, x_bit, core)
                add(shared, at, from_z, (bit,))
                bit += 1
        if phase < CORE_SHARE:
            for copy in sum_copies(matrix, phase + 1):
                copy.start()

    def on_the_way(step, table_of_steps):
        for when, actions in table_of_steps.items():

            @pl.when(step == when)
            def _():
                for matrix, phase in actions:
                    advance(matrix, phase)

    outgoing[...] = dot(order[...], grad_unrolled[...]).astype(bf16)

    def roll_copies(window):
        return pieces_to(
            outgoing,
            grad_context,
            lambda n: piece_send.at[window, n],
            lambda n: piece_recv.at[window, n],
            rep,
            shard,
            window,
        )

    for window in range(2):
        for copy in roll_copies(window):
            copy.start()
        rows = slice(window * PAD, window * PAD + LENGTHS[0])
        grad_context[rows, :] = outgoing[rows, :]
    for matrix in (FC1, FC2, PROJ):
        begin(matrix)

    head_of = lax.broadcasted_iota(jnp.int32, (1, 128), 1) // HD
    none = jnp.zeros((), bf16)

    def attend_copy(step):
        window, head, slot = step // HEADS, lax.rem(step, HEADS), lax.rem(step, 3)
        return pltpu.make_async_copy(
            attend_in.at[window, head], attend.at[slot], attend_sem.at[slot]
        )

    attend_copy(0).start()
    attend_copy(1).start()

    def return_copies(window):
        return pieces_to(
            grad_rolled,
            returned,
            lambda n: back_send.at[window, n],
            lambda n: back_recv.at[window, n],
            rep,
            shard,
            window,
        )

    def give_back(window):
        span = slice(window * PAD, (window + 1) * PAD)
        grad_rolled[span, :] = dot(grads[span, :], weights[...], NT).astype(bf16)
        for copy in return_copies(window):
            copy.start()
        rows = slice(window * PAD, window * PAD + LENGTHS[0])
        returned[rows, :] = grad_rolled[rows, :]

    first_schedule = {
        5: [(FC1, CORE_SUM)],
        7: [(FC2, CORE_SUM)],
        9: [(PROJ, CORE_SUM)],
        17: [(FC1, FIRST_SUM)],
        19: [(FC2, FIRST_SUM)],
        21: [(PROJ, FIRST_SUM)],
        25: [(FC1, SECOND_SUM)],
        27: [(FC2, SECOND_SUM)],
        29: [(PROJ, SECOND_SUM)],
    }
    second_schedule = {
        1: [(FC1, Z_SUM), (QKV_A, CORE_SUM), (QKV_B, CORE_SUM)],
        3: [(FC2, Z_SUM), (PROJ, Z_SUM)],
        5: [(FC1, SECOND_SHARE)],
        7: [(FC2, SECOND_SHARE), (PROJ, SECOND_SHARE), (QKV_A, FIRST_SUM), (QKV_B, FIRST_SUM)],
        9: [(FC1, FIRST_SHARE)],
        11: [(FC2, FIRST_SHARE), (PROJ, FIRST_SHARE), (QKV_A, SECOND_SUM), (QKV_B, SECOND_SUM)],
        15: [(QKV_A, Z_SUM), (QKV_B, Z_SUM), (FC1, CORE_SHARE)],
        18: [(QKV_A, SECOND_SHARE), (QKV_B, SECOND_SHARE), (FC2, CORE_SHARE), (PROJ, CORE_SHARE)],
        21: [(QKV_A, FIRST_SHARE), (QKV_B, FIRST_SHARE)],
    }

    for copy in roll_copies(0):
        copy.wait_recv()

    def head_step(step, carry):
        on_the_way(step, first_schedule)

        @pl.when(step == HEADS)
        def _():
            for copy in roll_copies(1):
                copy.wait_recv()
            give_back(0)

        @pl.when(step + 2 < 2 * HEADS)
        def _():
            attend_copy(step + 2).start()

        attend_copy(step).wait()
        window, head, slot = step // HEADS, lax.rem(step, HEADS), lax.rem(step, 3)
        group, member = head // GROUP, lax.rem(head, GROUP)
        rows = pl.ds(pl.multiple_of(window * PAD, 16), PAD)

        def lanes(part):
            return pl.ds(pl.multiple_of(part * D + group * 128, 128), 128)

        mine = head_of == member
        query = jnp.where(mine, mixed[rows, lanes(0)], none)
        key = jnp.where(mine, mixed[rows, lanes(1)], none)
        grad = jnp.where(mine, grad_context[rows, lanes(0)], none)
        weight_low = attend[slot, :, :PAD]
        weight = weight_low.astype(f32)
        grad_attend = dot(grad, mixed[rows, lanes(2)], NT)
        inner = jnp.sum(weight * grad_attend, -1, keepdims=True)
        grad_scores = (weight * (grad_attend - inner)).astype(bf16)
        wide = grad_scores.astype(f32)
        for tile in range(TILES):
            part = wide[:, tile * 128 : (tile + 1) * 128]
            if part.shape[1] < 128:
                part = jnp.concatenate([part, jnp.zeros((PAD, 128 - part.shape[1]), f32)], 1)
            at = (tile, pl.ds(head, PAD, stride=HEADS), slice(None))

            @pl.when(window == 0)
            def _():
                pairs[at] = part

            @pl.when(window == 1)
            def _():
                pairs[at] = pairs[at] + part

        for part, value in (
            (0, dot(grad_scores, key) * SCALE),
            (1, dot(grad_scores, query, TN) * SCALE),
            (2, dot(weight_low, grad, TN)),
        ):
            grads[rows, lanes(part)] = jnp.where(
                mine, value.astype(bf16), grads[rows, lanes(part)]
            )
        return carry

    lax.fori_loop(0, 2 * HEADS, head_step, 0)

    theirs = (1 - core) * (HALF * HEADS)
    piece_rows = HALF * HEADS // 4

    def round_step(step, carry):
        at = pl.ds(pl.multiple_of(step * piece_rows, 16), piece_rows)
        source = pl.ds(pl.multiple_of(theirs + step * piece_rows, 16), piece_rows)
        for tile in range(TILES):
            pairs_out[tile, at, :] = pairs[tile, source, :].astype(bf16)
        return carry

    lax.fori_loop(0, 4, round_step, 0)
    pairs_copy = remote(
        pairs_out, pairs_in, pairs_send.at[0], pairs_recv.at[0], flip(rep, 0), shard
    )
    pairs_copy.start()

    give_back(1)
    for n, ref in enumerate((qkv_grad_a, qkv_grad_b)):
        columns = slice(n * 768, (n + 1) * 768)
        got = dot(rolled[...], grads[:, columns], TN).astype(bf16)
        ref[...] = got.reshape(ref.shape)
        begin(QKV_A + n)

    low_of = lax.broadcasted_iota(jnp.int32, (SPAN, LANES), 0).astype(f32).astype(bf16)
    table_sum[...] = jnp.zeros_like(table_sum)
    pairs_copy.wait_recv()

    def table_step(step, carry):
        on_the_way(step, second_schedule)
        left, right = [], []
        for k in range(BATCH):
            row = step * BATCH + k
            there = core * HALF + row
            at = pl.ds(pl.multiple_of(there * HEADS, HEADS), HEADS)
            near = pl.ds(pl.multiple_of(row * HEADS, HEADS), HEADS)
            index = rel[pl.ds(there, 1), :]
            low = (index & (SPAN - 1)).astype(f32).astype(bf16)
            high = jnp.broadcast_to((index // SPAN).astype(f32).astype(bf16), (HEADS, LANES))
            total = jnp.concatenate(
                [pairs[t, at, :] + pairs_in[t, near, :].astype(f32) for t in range(TILES)], 1
            ).astype(bf16)
            nothing = jnp.zeros_like(total)
            left.append(
                jnp.concatenate(
                    [jnp.where(high == jnp.asarray(s, bf16), total, nothing) for s in range(SPANS)],
                    0,
                )
            )
            hit = low_of == jnp.broadcast_to(low, (SPAN, LANES))
            right.append(jnp.where(hit, jnp.ones((), bf16), jnp.zeros((), bf16)))
        table_sum[...] += dot(jnp.concatenate(left, 1), jnp.concatenate(right, 1), NT)
        return carry

    lax.fori_loop(0, HALF // BATCH, table_step, 0)

    for window in range(2):
        for copy in return_copies(window):
            copy.wait_recv()
    gain = small_row(small_all, LN1_GAIN).astype(f32)

    def norm_step(step, carry):
        gain_sum, shift_sum = carry
        rows = pl.ds(pl.multiple_of(step * 112, 16), 112)
        grad_out = dot(order_back[rows, :], returned[...])
        normal, inverse = norm_rows(tokens[rows, :].astype(f32))
        scaled = grad_out * gain
        inner = (
            scaled
            - jnp.mean(scaled, -1, keepdims=True)
            - normal * jnp.mean(scaled * normal, -1, keepdims=True)
        )
        grad_tokens[rows, :] = grad_middle[rows, :] + inverse * inner
        return (
            gain_sum + jnp.sum(grad_out * normal, 0, keepdims=True),
            shift_sum + jnp.sum(grad_out, 0, keepdims=True),
        )

    nought = jnp.zeros((1, D), f32)
    gain_sum, shift_sum = lax.fori_loop(0, 7, norm_step, (nought, nought))

    query_sum = jnp.sum(grads[:, :D].astype(f32), 0, keepdims=True)
    value_sum = jnp.sum(grads[:, 2 * D :].astype(f32), 0, keepdims=True)
    for owner in range(4):
        lanes = slice(owner * 128, (owner + 1) * 128)
        sums = jnp.concatenate(
            [table_sum[pl.ds(s * HEADS + GROUP * owner, GROUP), :] for s in range(SPANS)], 0
        )
        slab[owner, : SPANS * GROUP, :] = sums[:, :128]
        slab[owner, SPANS * GROUP : 2 * SPANS * GROUP, :] = sums[:, 128:]
        slab[owner, 2 * SPANS * GROUP :, :] = jnp.concatenate(
            [
                gain_sum[:, lanes],
                shift_sum[:, lanes],
                query_sum[:, lanes],
                value_sum[:, lanes],
                small_grads[owner, V_BIAS + 1 :, :],
            ],
            0,
        )

    def slab_copies():
        return [
            remote(
                slab.at[lax.rem(shard + k, 4)],
                slab_z.at[3 - k],
                slab_send.at[k - 1],
                slab_recv.at[3 - k],
                rep,
                lax.rem(shard + k, 4),
            )
            for k in (1, 2, 3)
        ]

    for copy in slab_copies():
        copy.start()

    for matrix in (QKV_A, QKV_B):
        advance(matrix, CORE_SHARE)
    for copy in slab_copies():
        copy.wait_recv()
    slab_rep[rep] = slab[shard] + (slab_z[0] + slab_z[1] + slab_z[2])

    def slab_share(k):
        return remote(
            slab_rep.at[rep],
            slab_rep.at[rep],
            slab_send.at[2 + k],
            slab_recv.at[2 + reps - k],
            lax.rem(rep + k, reps),
            shard,
        )

    def share_start(k, carry):
        slab_share(k).start()
        return carry

    lax.fori_loop(1, reps, share_start, 0)
    outs = (fc1_out, fc2_out, proj_out, qkv_out_a, qkv_out_b)
    results = [
        pltpu.make_async_copy(held[matrix][5], outs[matrix], local.at[5 + matrix])
        for matrix in range(5)
    ]
    for copy in results:
        copy.start()

    def share_wait(k, carry):
        slab_share(k).wait()
        return carry

    lax.fori_loop(1, reps, share_wait, 0)

    def slab_step(k, total):
        return total + slab_rep[k]

    slab_out[...] = lax.fori_loop(1, reps, slab_step, slab_rep[0])

    for copy in slab_copies():
        copy.wait_send()
    pairs_copy.wait_send()
    for window in range(2):
        for copy in roll_copies(window) + return_copies(window):
            copy.wait_send()
    for matrix in range(5):
        for phase in range(7):
            for copy in sum_copies(matrix, phase):
                copy.wait_send()
    for copy in results:
        copy.wait()


def back(
    grad_unrolled,
    rolled,
    mixed,
    weights,
    rel,
    tokens,
    grad_middle,
    small_all,
    small_grads,
    attend,
    fc1_grad,
    fc2_grad,
    proj_grad,
):
    anywhere, inside = pl.BlockSpec(memory_space=pl.ANY), pl.BlockSpec(memory_space=pltpu.VMEM)
    reps = lax.axis_size("rep")
    dma = pltpu.SemaphoreType.DMA
    order = send_matrix()
    extra = max(1, reps.bit_length() - 4)
    held = []
    for rows, columns, _ in SUMMED:
        held += [
            pltpu.VMEM((4, 2, 2, rows, columns), bf16),
            pltpu.VMEM((4, 2, 2, rows, columns), bf16),
            pltpu.VMEM((4, 2, rows, columns), bf16),
            pltpu.VMEM((4, rows, columns), bf16),
            pltpu.VMEM((3 + extra, rows, columns), bf16),
            pltpu.VMEM((2, 2, 2, rows, columns), bf16),
        ]
    return pl.pallas_call(
        back_kernel,
        out_shape=(
            jax.ShapeDtypeStruct(tokens.shape, f32),
            *[jax.ShapeDtypeStruct((2, 2, 2) + shape[:2], bf16) for shape in SUMMED],
            jax.ShapeDtypeStruct((SLAB, 128), f32),
        ),
        in_specs=[inside] * 11 + [anywhere] * 4,
        out_specs=(inside, *[anywhere] * 5, inside),
        scratch_shapes=[
            pltpu.VMEM((2 * PAD, D), bf16),
            pltpu.VMEM((2 * PAD, D), bf16),
            pltpu.VMEM((3, PAD, LANES), bf16),
            pltpu.VMEM((2 * PAD, 3 * D), bf16),
            pltpu.VMEM((2 * PAD, D), bf16),
            pltpu.VMEM((2 * PAD, D), bf16),
            pltpu.VMEM((TILES, PAD * HEADS, 128), f32),
            pltpu.VMEM((TILES, HALF * HEADS, 128), bf16),
            pltpu.VMEM((TILES, HALF * HEADS, 128), bf16),
            pltpu.VMEM((4, 2, 2, 2, 16, 768), bf16),
            pltpu.VMEM((4, 2, 2, 2, 16, 768), bf16),
            pltpu.VMEM((SPANS * HEADS, SPAN), f32),
            pltpu.VMEM((4, SLAB, 128), f32),
            pltpu.VMEM((3, SLAB, 128), f32),
            pltpu.VMEM((reps, SLAB, 128), f32),
            *held,
            dma((5, 7, 3)),
            dma((5, 7, 3)),
            dma((5, extra)),
            dma((5, extra)),
            dma((2, 3)),
            dma((2, 3)),
            dma((2, 3)),
            dma((2, 3)),
            dma((3,)),
            dma((1,)),
            dma((1,)),
            dma((3 + reps,)),
            dma((3 + reps,)),
            dma((10,)),
        ],
        compiler_params=pltpu.CompilerParams(
            vmem_limit_bytes=VMEM_LIMIT, collective_id=1, has_side_effects=True
        ),
        name="back",
    )(
        grad_unrolled,
        jnp.asarray(order, bf16),
        jnp.asarray(order.T, bf16),
        rolled,
        mixed,
        weights,
        rel,
        tokens,
        grad_middle,
        small_all,
        small_grads,
        attend,
        fc1_grad.reshape(4, 2, 2, 2, 16, 2048),
        fc2_grad.reshape(4, 2, 2, 2, 64, 512),
        proj_grad.reshape(4, 2, 2, 2, 16, 512),
    )


def norm_forward(rows, gain, shift):
    centre = rows - jnp.mean(rows, -1, keepdims=True)
    inverse = lax.rsqrt(jnp.mean(centre * centre, -1, keepdims=True) + 1e-05)
    normal = centre * inverse
    return (normal * gain.astype(jnp.float32) + shift.astype(jnp.float32), normal, inverse)


def norm_backward(grad_out, normal, inverse, gain):
    scaled = grad_out * gain.astype(jnp.float32)
    inner = (
        scaled
        - jnp.mean(scaled, -1, keepdims=True)
        - normal * jnp.mean(scaled * normal, -1, keepdims=True)
    )
    return (inverse * inner, jnp.sum(grad_out * normal, 0), jnp.sum(grad_out, 0))


def shards(
    tokens,
    region,
    rel_index,
    ln1_gain,
    ln1_shift,
    w_qkv,
    q_bias,
    v_bias,
    table,
    w_proj,
    proj_bias,
    ln2_gain,
    ln2_shift,
    w_fc1,
    fc1_bias,
    w_fc2,
    fc2_bias,
    cotangent,
):
    inputs = tokens.reshape(-1, D).astype(jnp.float32)
    small = jnp.concatenate(
        (ln1_gain, ln1_shift, q_bias, v_bias, proj_bias, ln2_gain, ln2_shift, fc2_bias, fc1_bias)
    ).reshape(-1, 128)
    small = jnp.pad(small, ((0, SMALL - small.shape[0]), (0, 0)))
    chunks = jnp.pad(table.astype(f32).T, ((0, 0), (0, CHUNKS * 128 - TABLE)))
    labels = region.reshape(WT, WH, 2, WW).transpose(2, 0, 1, 3).reshape(2, WIN)
    labels = pieces_of(labels, 1, -1)
    row_ids = jnp.pad(labels, ((0, 0), (0, LANES - PAD)), constant_values=-1)[:, None]
    (
        whole_qkv,
        whole_proj,
        whole_fc1,
        whole_fc2,
        small,
        rolled,
        qkv,
        attend,
        contexts,
        rel,
    ) = front(
        tokens.reshape(-1, D),
        small,
        chunks.reshape(-1, 128),
        row_ids,
        rel_index,
        w_qkv,
        w_proj,
        w_fc1,
        w_fc2,
    )
    gain_one, bias_proj = small[:, LN1_GAIN].reshape(-1), small[:, PROJ_BIAS].reshape(-1)
    gain_two, shift_two = small[:, LN2_GAIN].reshape(-1), small[:, LN2_SHIFT].reshape(-1)
    bias_fc2 = small[:, FC2_BIAS].reshape(-1)
    bias_fc1 = small[:, FC1_BIAS : FC1_BIAS + 4].reshape(-1)
    order = jnp.asarray(send_matrix(), bf16)
    unrolled = dot(order, contexts, TN).astype(bf16)
    middle = (
        inputs
        + jnp.dot(unrolled, whole_proj, preferred_element_type=jnp.float32)
        + bias_proj.astype(jnp.float32)
    )
    normed_two, normal_two, inverse_two = norm_forward(middle, gain_two, shift_two)
    normed_low = normed_two.astype(jnp.bfloat16)
    hidden = jnp.dot(normed_low, whole_fc1, preferred_element_type=jnp.float32) + bias_fc1.astype(
        jnp.float32
    )
    active = jax.nn.gelu(hidden, approximate=False).astype(jnp.bfloat16)
    result = (
        middle
        + jnp.dot(active, whole_fc2, preferred_element_type=jnp.float32)
        + bias_fc2.astype(jnp.float32)
    )
    output = result.astype(jnp.bfloat16).reshape(tokens.shape)
    grad_out = cotangent.reshape(-1, D)
    grad_w_fc2 = jnp.einsum("rf,rd->fd", active, grad_out, preferred_element_type=jnp.float32)
    grad_fc2_bias = jnp.sum(grad_out.astype(jnp.float32), 0)
    slope = (
        0.5 * (1.0 + lax.erf(hidden * 0.7071067811865476))
        + hidden * jnp.exp(-0.5 * hidden * hidden) * 0.3989422804014327
    )
    grad_active = jnp.einsum("rd,fd->rf", grad_out, whole_fc2, preferred_element_type=jnp.float32)
    grad_hidden = (grad_active * slope).astype(jnp.bfloat16)
    grad_w_fc1 = jnp.einsum(
        "rd,rf->df", normed_low, grad_hidden, preferred_element_type=jnp.float32
    )
    grad_fc1_bias = jnp.sum(grad_hidden.astype(jnp.float32), 0)
    grad_normed_two = jnp.einsum(
        "rf,df->rd", grad_hidden, whole_fc1, preferred_element_type=jnp.float32
    )
    grad_inner_two, grad_ln2_gain, grad_ln2_shift = norm_backward(
        grad_normed_two, normal_two, inverse_two, gain_two
    )
    grad_middle = grad_out.astype(jnp.float32) + grad_inner_two
    grad_branch = grad_middle.astype(jnp.bfloat16)
    grad_w_proj = jnp.einsum("rd,re->de", unrolled, grad_branch, preferred_element_type=jnp.float32)
    grad_proj_bias = jnp.sum(grad_branch.astype(jnp.float32), 0)
    grad_unrolled = jnp.einsum(
        "re,de->rd", grad_branch, whole_proj, preferred_element_type=jnp.float32
    ).astype(jnp.bfloat16)
    rows = [jnp.zeros((4, 128), f32)] * 4
    for gradient in (grad_proj_bias, grad_ln2_gain, grad_ln2_shift, grad_fc2_bias):
        rows.append(gradient.reshape(4, 128))
    small_grads = jnp.concatenate(
        [jnp.stack(rows, 1), grad_fc1_bias.reshape(4, 4, 128), jnp.zeros((4, 4, 128), f32)], 1
    )
    grad_tokens, grad_w_fc1, grad_w_fc2, grad_w_proj, grad_w_qkv_a, grad_w_qkv_b, slab = back(
        grad_unrolled,
        rolled,
        qkv,
        whole_qkv,
        rel,
        tokens.reshape(-1, D),
        grad_middle,
        small,
        small_grads,
        attend,
        grad_w_fc1.astype(bf16),
        grad_w_fc2.astype(bf16),
        grad_w_proj.astype(bf16),
    )
    grad_tokens = grad_tokens.reshape(tokens.shape)
    grad_w_fc1 = grad_w_fc1.astype(f32).reshape(w_fc1.shape)
    grad_w_fc2 = grad_w_fc2.astype(f32).reshape(w_fc2.shape)
    grad_w_proj = grad_w_proj.astype(f32).reshape(w_proj.shape)
    grad_w_qkv = jnp.concatenate((grad_w_qkv_a, grad_w_qkv_b), -1).astype(f32)
    grad_w_qkv = grad_w_qkv.reshape(w_qkv.shape)
    spans = slab[: 2 * SPANS * GROUP].reshape(2, SPANS, GROUP, 128).transpose(1, 0, 3, 2)
    grad_table = spans.reshape(SPANS * SPAN, GROUP)[:TABLE]
    vectors = slab[2 * SPANS * GROUP :]
    grad_ln1_gain, grad_ln1_shift = vectors[LN1_GAIN], vectors[LN1_SHIFT]
    grad_q_bias, grad_v_bias = vectors[Q_BIAS], vectors[V_BIAS]
    grad_proj_bias, grad_fc2_bias = vectors[PROJ_BIAS], vectors[FC2_BIAS]
    grad_ln2_gain, grad_ln2_shift = vectors[LN2_GAIN], vectors[LN2_SHIFT]
    grad_fc1_bias = vectors[FC1_BIAS : FC1_BIAS + 4].reshape(-1)
    return (
        output,
        grad_tokens,
        grad_ln1_gain,
        grad_ln1_shift,
        grad_w_qkv,
        grad_q_bias,
        grad_v_bias,
        grad_table,
        grad_w_proj,
        grad_proj_bias,
        grad_ln2_gain,
        grad_ln2_shift,
        grad_w_fc1,
        grad_fc1_bias,
        grad_w_fc2,
        grad_fc2_bias,
    )


def solution(mesh):
    return jax.shard_map(
        shards,
        mesh=mesh,
        in_specs=(
            P("rep", "shard", None, None),
            P("shard", None),
            P(),
            P("shard"),
            P("shard"),
            P("shard", None),
            P("shard"),
            P("shard"),
            P(None, "shard"),
            P("shard", None),
            P("shard"),
            P("shard"),
            P("shard"),
            P("shard", None),
            P("shard"),
            P("shard", None),
            P("shard"),
            P("rep", "shard", None, None),
        ),
        out_specs=(
            P("rep", "shard", None, None),
            P("rep", "shard", None, None),
            P("shard"),
            P("shard"),
            P("shard", None),
            P("shard"),
            P("shard"),
            P(None, "shard"),
            P("shard", None),
            P("shard"),
            P("shard"),
            P("shard"),
            P("shard", None),
            P("shard"),
            P("shard", None),
            P("shard"),
        ),
        check_vma=False,
    )
```

```python
import functools

import jax
import jax.numpy as jnp
import numpy as np
from jax import lax
from jax.experimental import pallas as pl
from jax.experimental.pallas import tpu as pltpu
from jax.sharding import PartitionSpec as P

D = 512
HEADS = 16
HD = 32
WT = 8
WH = 7
WW = 7
WIN = 392
TABLE = 2535
PAD = 416
LANES = 512
GROUP = 4
CHUNKS = 20
SCALE = HD ** (-0.5)
NN = (((1,), (0,)), ((), ()))
NT = (((1,), (1,)), ((), ()))
TN = (((0,), (0,)), ((), ()))
VMEM_LIMIT = 60 * 2**20
f32 = jnp.float32
bf16 = jnp.bfloat16

PIECES = (
    ((0, 4), (0, 4), 112, 0),
    ((4, 8), (0, 4), 112, 112),
    ((0, 4), (4, 7), 96, 224),
    ((4, 8), (4, 7), 96, 320),
)


def send_matrix():
    matrix = np.zeros((2 * PAD, WT * WH * 2 * WW), np.float32)
    for window in range(2):
        for (t0, t1), (h0, h1), _, first in PIECES:
            row = window * PAD + first
            for t in range(t0, t1):
                for h in range(h0, h1):
                    for w in range(WW):
                        column = (window * WW + w + WW // 2) % (2 * WW)
                        source = ((t + 4) % WT * WH + (h + 3) % WH) * 2 * WW + column
                        matrix[row, source] = 1.0
                        row += 1
    return matrix


def spread_matrix():
    source = np.arange(WIN).reshape(WT, WH, WW)
    matrix = np.zeros((PAD, WIN), np.float32)
    for (t0, t1), (h0, h1), _, first in PIECES:
        tokens = source[t0:t1, h0:h1].reshape(-1)
        matrix[first + np.arange(tokens.size), tokens] = 1.0
    return matrix


def pieces_of(array, axis, fill):
    shape = array.shape
    split = array.reshape(shape[:axis] + (WT, WH, WW) + shape[axis + 1 :])
    parts = []
    for (t0, t1), (h0, h1), padded, _ in PIECES:
        part = lax.slice_in_dim(lax.slice_in_dim(split, t0, t1, axis=axis), h0, h1, axis=axis + 1)
        length = (t1 - t0) * (h1 - h0) * WW
        part = part.reshape(shape[:axis] + (length,) + shape[axis + 1 :])
        widths = [(0, 0, 0)] * len(shape)
        widths[axis] = (0, padded - length, 0)
        parts.append(lax.pad(part, jnp.asarray(fill, array.dtype), widths))
    return jnp.concatenate(parts, axis)


def dot(a, b, dims=NN):
    return lax.dot_general(a, b, dims, preferred_element_type=f32)


MESH = pl.DeviceIdType.MESH
PARTS = 8
FIRST_ROWS = tuple(first for _, _, _, first in PIECES)
LENGTHS = tuple(padded for _, _, padded, _ in PIECES)
ACROSS = (0, 2, 1, 3)
LN1_GAIN, LN1_SHIFT, Q_BIAS, V_BIAS, PROJ_BIAS, LN2_GAIN, LN2_SHIFT, FC2_BIAS, FC1_BIAS = range(9)
SMALL = 16


def place():
    rep, shard = lax.axis_index("rep"), lax.axis_index("shard")
    return rep, shard, lax.rem(rep, 2), lax.rem(rep // 2, 2), lax.rem(rep // 4, 2)


def flip(rep, bit):
    low = lax.rem(rep // (1 << bit), 2)
    return rep + (1 - 2 * low) * (1 << bit)


def remote(src, dst, send, recv, rep, shard):
    return pltpu.make_async_remote_copy(
        src_ref=src,
        dst_ref=dst,
        send_sem=send,
        recv_sem=recv,
        device_id={"rep": rep, "shard": shard},
        device_id_type=MESH,
    )


def greet(peers):
    barrier = pltpu.get_barrier_semaphore()
    for rep, shard in peers:
        pl.semaphore_signal(
            barrier, inc=1, device_id={"rep": rep, "shard": shard}, device_id_type=MESH
        )
    pl.semaphore_wait(barrier, len(peers))


def peers_of(rep, shard):
    return [(rep, lax.rem(shard + k, 4)) for k in (1, 2, 3)] + [
        (flip(rep, bit), shard) for bit in (0, 1, 2)
    ]


def quarter_across(shard, bits):
    low, high = lax.rem(shard, 2), shard // 2
    if bits & 1:
        low = 1 - low
    if bits & 2:
        high = 1 - high
    return high * 2 + low


def pieces_to(source, target, send, recv, rep, shard, window, columns=None):
    copies = []
    for piece in (1, 2, 3):
        rows = pl.ds(
            pl.multiple_of(window * PAD + FIRST_ROWS[piece], 16), LENGTHS[piece]
        )
        at = (rows,) if columns is None else (rows, columns)
        copies.append(
            remote(
                source.at[at],
                target.at[at],
                send(piece - 1),
                recv(piece - 1),
                rep,
                quarter_across(shard, ACROSS[piece]),
            )
        )
    return copies


def norm_rows(rows):
    centre = rows - jnp.mean(rows, -1, keepdims=True)
    inverse = lax.rsqrt(jnp.mean(centre * centre, -1, keepdims=True) + 1e-05)
    return centre * inverse, inverse


def small_row(ref, row):
    return jnp.concatenate([ref[s, row : row + 1, :] for s in range(4)], 1)


FIXED = 4096.0
TAIL = 112
Z_PHASE, FIRST_PHASE, SECOND_PHASE, CORE_PHASE = range(4)
X_FIRST = (True, False, True, False, True)
HALF_QKV = 3 * D // 2


def front_kernel(
    tokens,
    order,
    spread,
    small,
    table,
    row_ids,
    rel,
    qkv_part,
    proj_part,
    fc1_part,
    fc2_part,
    qkv_whole_a,
    qkv_whole_b,
    proj_whole,
    fc1_whole,
    fc2_whole,
    small_out,
    rolled_out,
    mixed_out,
    attend_out,
    inverse_out,
    context_out,
    back_out,
    rel_out,
    small_all,
    table_all,
    table_wide,
    outgoing,
    arriving,
    rolled,
    weights_a,
    weights_b,
    mixed,
    index,
    index_tail,
    bias_tail,
    bias,
    mask,
    attend,
    inverse,
    contexts,
    gather_send,
    gather_recv,
    small_send,
    small_recv,
    bias_send,
    bias_recv,
    piece_send,
    piece_recv,
    back_send,
    back_recv,
    local,
    attend_sem,
):
    rep, shard, core, x_bit, y_bit = place()
    greet(peers_of(rep, shard))
    first_half, second_half = pl.ds(0, HALF_QKV), pl.ds(HALF_QKV, HALF_QKV)
    parts = (
        qkv_part.at[:, :, :, :, first_half],
        qkv_part.at[:, :, :, :, second_half],
        proj_part,
        fc1_part,
        fc2_part,
    )
    wholes = (qkv_whole_a, qkv_whole_b, proj_whole, fc1_whole, fc2_whole)
    feed_forward = (2, 3, 4)

    def gather(matrix, phase):
        copies = []
        for k in (1, 2, 3):
            at = lax.rem(shard + k, 4)
            whole = wholes[matrix]
            if phase == Z_PHASE:
                copies.append(
                    remote(
                        parts[matrix].at[y_bit, x_bit, core],
                        whole.at[shard, y_bit, x_bit, core],
                        gather_send.at[matrix, phase, k - 1],
                        gather_recv.at[matrix, phase, 3 - k],
                        rep,
                        at,
                    )
                )
                continue
            x_first = X_FIRST[matrix]
            if phase == FIRST_PHASE:
                block, partner = whole.at[at, y_bit, x_bit, core], flip(rep, 1 if x_first else 2)
            elif phase == SECOND_PHASE and x_first:
                block, partner = whole.at[at, y_bit, :, core], flip(rep, 2)
            elif phase == SECOND_PHASE:
                block, partner = whole.at[at, :, x_bit, core], flip(rep, 1)
            else:
                block, partner = whole.at[at, :, :, core], flip(rep, 0)
            copies.append(
                remote(
                    block,
                    block,
                    gather_send.at[matrix, phase, k - 1],
                    gather_recv.at[matrix, phase, k - 1],
                    partner,
                    shard,
                )
            )
        return copies

    def start(matrix, phase):
        for copy in gather(matrix, phase):
            copy.start()

    def arrived(matrix, phase):
        for copy in gather(matrix, phase):
            copy.wait_recv()

    def small_copies():
        copies = []
        for k in (1, 2, 3):
            for n, ref in enumerate((table_all, small_all)):
                copies.append(
                    remote(
                        ref.at[shard],
                        ref.at[shard],
                        small_send.at[n, k - 1],
                        small_recv.at[n, 3 - k],
                        rep,
                        lax.rem(shard + k, 4),
                    )
                )
        return copies

    small_all[shard] = small[...]
    table_all[shard] = table[...]
    for copy in small_copies():
        copy.start()
    start(0, Z_PHASE)
    start(1, Z_PHASE)
    own = [
        pltpu.make_async_copy(parts[m], wholes[m].at[shard], local.at[m]) for m in range(5)
    ]
    for copy in own:
        copy.start()

    outgoing[...] = dot(order[...], tokens[...]).astype(bf16)

    def roll_copies(window):
        return pieces_to(
            outgoing,
            arriving,
            lambda n: piece_send.at[window, n],
            lambda n: piece_recv.at[window, n],
            rep,
            shard,
            window,
        )

    for copy in roll_copies(0):
        copy.start()
    for matrix in feed_forward:
        start(matrix, Z_PHASE)
    for window in range(2):
        rows = slice(window * PAD, window * PAD + LENGTHS[0])
        arriving[rows, :] = outgoing[rows, :]

    rel_index = rel[...]
    digits = (rel_index // 256).astype(f32).astype(bf16), (rel_index & 255).astype(f32).astype(bf16)
    moved = []
    for digit in digits:
        half = dot(spread[...], digit).astype(bf16)
        moved.append(dot(half, spread[...], NT).astype(jnp.int32))
    index[:, :PAD] = moved[0] * 256 + moved[1]
    index[:, PAD:] = jnp.zeros((PAD, LANES - PAD), jnp.int32)

    ids = lax.broadcasted_iota(jnp.int32, (8, LANES), 0)
    for window in range(2):
        kinds = jnp.where(row_ids[window] + 1 == ids, 1.0, 0.0).astype(bf16)[:, :PAD]
        mask[window] = (dot(kinds, kinds, TN) - 1.0) * 1e30

    for copy in small_copies():
        copy.wait_recv()

    for block in range(4):
        count = min(TAIL, PAD - block * TAIL)
        lanes = slice(block * 32, block * 32 + 32)
        index_tail[:count, lanes] = index[block * TAIL : block * TAIL + count, PAD - 32 : PAD]
        if count < TAIL:
            index_tail[count:, lanes] = jnp.zeros((TAIL - count, 32), jnp.int32)

    upper, lower = (
        jnp.floor(table_all[2 * core + n] * FIXED + 0.5).astype(jnp.int32) for n in range(2)
    )
    words = upper * 65536 + (lower + 32768)
    for chunk in range(CHUNKS):
        for head in range(GROUP):
            row = head * CHUNKS + chunk
            table_wide[chunk, head] = jnp.broadcast_to(words[row : row + 1, :], (8, 128))
    mine = core * (HEADS // 2)

    def bias_copy(rows, step):
        block = bias.at[pl.ds(mine, HEADS // 2), rows]
        return remote(block, block, bias_send.at[step], bias_recv.at[step], flip(rep, 0), shard)

    def on_the_way(step, table_of_steps):
        for when, actions in table_of_steps.items():

            @pl.when(step == when)
            def _():
                for action, matrix, phase in actions:
                    action(matrix, phase)

    def advance(matrix, phase):
        arrived(matrix, phase)
        if phase < CORE_PHASE:
            start(matrix, phase + 1)

    schedule = {
        5: [(advance, 0, Z_PHASE), (advance, 1, Z_PHASE)],
        13: [(advance, 0, FIRST_PHASE), (advance, 1, FIRST_PHASE)],
        23: [(advance, 0, SECOND_PHASE), (advance, 1, SECOND_PHASE)],
    }
    later = {
        3: [(advance, m, Z_PHASE) for m in feed_forward],
        10: [(advance, m, FIRST_PHASE) for m in feed_forward],
    }

    def look_up(here):
        halves = [(here[s : s + 8] & 127, here[s : s + 8] >> 7) for s in (0, 8)]
        found = [[None, None] for _ in range(GROUP)]
        for chunk in range(CHUNKS):
            for s, (low, high) in enumerate(halves):
                hit = high == chunk
                for head in range(GROUP):
                    value = jnp.take_along_axis(table_wide[chunk, head], low, axis=1)
                    if chunk:
                        value = jnp.where(hit, value, found[head][s])
                    found[head][s] = value
        joined = [jnp.concatenate(pair, 0) for pair in found]
        uppers = [(word >> 16).astype(f32) for word in joined]
        lowers = [((word & 65535) - 32768).astype(f32) for word in joined]
        return [(value * (1 / FIXED)).astype(bf16) for value in uppers + lowers]

    def tail_step(step, carry):
        rows = pl.ds(pl.multiple_of(step * 16, 16), 16)
        for head, value in enumerate(look_up(index_tail[rows, :])):
            bias_tail[head, rows, :] = value
        return carry

    lax.fori_loop(0, TAIL // 16, tail_step, 0)

    def untail_step(head, carry):
        for block in range(4):
            count = min(TAIL, PAD - block * TAIL)
            value = bias_tail[head, :count, block * 32 : block * 32 + 32]
            bias[mine + head, block * TAIL : block * TAIL + count, PAD - 32 : PAD] = value
        return carry

    lax.fori_loop(0, HEADS // 2, untail_step, 0)

    def bias_step(step, carry):
        on_the_way(step, schedule)
        rows = pl.ds(pl.multiple_of(step * 16, 16), 16)
        for tile in range(3):
            lanes = slice(tile * 128, (tile + 1) * 128)
            for head, value in enumerate(look_up(index[rows, lanes])):
                bias[mine + head, rows, lanes] = value
        bias_copy(rows, step).start()
        return carry

    lax.fori_loop(0, PAD // 16, bias_step, 0)
    for copy in roll_copies(1):
        copy.start()

    fetches = []
    for n, (whole, weight) in enumerate(((qkv_whole_a, weights_a), (qkv_whole_b, weights_b))):
        arrived(n, CORE_PHASE)
        own[n].wait()
        fetches.append(pltpu.make_async_copy(whole, weight, local.at[5 + n]))
        fetches[-1].start()
    for copy in fetches:
        copy.wait()
    q_bias, v_bias = small_row(small_all, Q_BIAS), small_row(small_all, V_BIAS)
    mixed_bias = jnp.concatenate([q_bias, jnp.zeros_like(q_bias), v_bias], 1).astype(f32)
    gain, shift = small_row(small_all, LN1_GAIN), small_row(small_all, LN1_SHIFT)

    def norm_step(step, carry):
        rows = pl.ds(pl.multiple_of(step * 208, 16), 208)
        normal, _ = norm_rows(arriving[rows, :].astype(f32))
        rolled[rows, :] = (normal * gain.astype(f32) + shift.astype(f32)).astype(bf16)
        return carry

    def mix(window):
        for copy in roll_copies(window):
            copy.wait_recv()
        lax.fori_loop(2 * window, 2 * window + 2, norm_step, 0)
        span = slice(window * PAD, (window + 1) * PAD)
        for n, weight in enumerate((weights_a, weights_b)):
            lanes = slice(n * HALF_QKV, (n + 1) * HALF_QKV)
            got = dot(rolled[span, :], weight[...].reshape(D, HALF_QKV))
            mixed[span, lanes] = (got + mixed_bias[:, lanes]).astype(bf16)

    mix(0)
    keep = [
        pltpu.make_async_copy(rolled, rolled_out, local.at[5]),
        pltpu.make_async_copy(mixed, mixed_out, local.at[6]),
        pltpu.make_async_copy(index, rel_out, local.at[7]),
        pltpu.make_async_copy(small_all, small_out, local.at[8]),
        pltpu.make_async_copy(inverse, inverse_out, local.at[9]),
        pltpu.make_async_copy(contexts, context_out, local.at[12]),
    ]

    def bias_wait(step, carry):
        bias_copy(pl.ds(pl.multiple_of(step * 16, 16), 16), step).wait_recv()
        return carry

    lax.fori_loop(0, PAD // 16, bias_wait, 0)

    head_of = lax.broadcasted_iota(jnp.int32, (1, 128), 1) // HD
    none = jnp.zeros((), bf16)
    ones = jnp.ones((PAD, 128), bf16)

    def attend_copy(step):
        window, pair, slot = step // (HEADS // 2), lax.rem(step, HEADS // 2), lax.rem(step, 2)
        return pltpu.make_async_copy(
            attend.at[slot], attend_out.at[window, pl.ds(2 * pair, 2)], attend_sem.at[slot]
        )

    def back_copies(step):
        window, group = step // (HEADS // 2), lax.rem(step // 2, HEADS // GROUP)
        lanes = pl.ds(pl.multiple_of(group * 128, 128), 128)
        return pieces_to(
            contexts,
            back_out,
            lambda n: back_send.at[window, group, n],
            lambda n: back_recv.at[window, group, n],
            rep,
            shard,
            window,
            lanes,
        )

    def attend_step(step, carry):
        on_the_way(step, later)

        @pl.when(step == HEADS // 2)
        def _():
            mix(1)

        @pl.when(step >= 2)
        def _():
            attend_copy(step - 2).wait()

        window, slot = step // (HEADS // 2), lax.rem(step, 2)
        rows = pl.ds(pl.multiple_of(window * PAD, 16), PAD)
        for n in range(2):
            head = 2 * lax.rem(step, HEADS // 2) + n
            group, member = head // GROUP, lax.rem(head, GROUP)

            def lanes(part):
                return pl.ds(pl.multiple_of(part * D + group * 128, 128), 128)

            own_lanes = head_of == member
            query = jnp.where(own_lanes, mixed[rows, lanes(0)], none)
            value = jnp.where(own_lanes, mixed[rows, lanes(2)], none)
            scores = dot(query, mixed[rows, lanes(1)], NT) * SCALE
            scores = scores + bias[head, :, :PAD].astype(f32) + mask[window]
            expo = jnp.exp(scores - jnp.max(scores, -1, keepdims=True)).astype(bf16)
            attend[slot, n, :, :PAD] = expo
            result = dot(expo, jnp.concatenate([value, ones], 1))
            over = 1.0 / result[:, 128:]
            context = (result[:, :128] * over).astype(bf16)
            contexts[rows, lanes(0)] = jnp.where(own_lanes, context, contexts[rows, lanes(0)])
            inverse[rows, lanes(0)] = jnp.where(own_lanes, over, inverse[rows, lanes(0)])
        attend_copy(step).start()

        @pl.when(lax.rem(step, 2) == 1)
        def _():
            for copy in back_copies(step):
                copy.start()

        return carry

    lax.fori_loop(0, HEADS, attend_step, 0)
    for copy in keep:
        copy.start()
    for matrix in feed_forward:
        advance(matrix, SECOND_PHASE)
    stay = [
        pltpu.make_async_copy(
            contexts.at[pl.ds(w * PAD, LENGTHS[0])],
            back_out.at[pl.ds(w * PAD, LENGTHS[0])],
            local.at[10 + w],
        )
        for w in range(2)
    ]
    for copy in stay:
        copy.start()
    for matrix in feed_forward:
        arrived(matrix, CORE_PHASE)
    attend_copy(HEADS - 2).wait()
    attend_copy(HEADS - 1).wait()

    def back_wait(step, carry):
        for copy in back_copies(step * 2):
            copy.wait()
        return carry

    lax.fori_loop(0, 2 * HEADS // GROUP, back_wait, 0)

    def bias_sent(step, carry):
        bias_copy(pl.ds(pl.multiple_of(step * 16, 16), 16), step).wait_send()
        return carry

    lax.fori_loop(0, PAD // 16, bias_sent, 0)
    for copy in small_copies():
        copy.wait_send()
    for window in range(2):
        for copy in roll_copies(window):
            copy.wait_send()
    for matrix in range(5):
        for phase in range(4):
            for copy in gather(matrix, phase):
                copy.wait_send()
    for copy in own[2:] + keep + stay:
        copy.wait()


def front(tokens, small, table, row_ids, rel_index, w_qkv, w_proj, w_fc1, w_fc2):
    anywhere, inside = pl.BlockSpec(memory_space=pl.ANY), pl.BlockSpec(memory_space=pltpu.VMEM)
    cut = (2, 2, 2)
    weights = [
        w.reshape(cut + (w.shape[0] // PARTS, w.shape[1])) for w in (w_qkv, w_proj, w_fc1, w_fc2)
    ]
    half = (4,) + weights[0].shape[:-1] + (HALF_QKV,)
    wholes = [jax.ShapeDtypeStruct(half, bf16)] * 2
    wholes += [jax.ShapeDtypeStruct((4,) + w.shape, bf16) for w in weights[1:]]
    dma = pltpu.SemaphoreType.DMA
    results = pl.pallas_call(
        front_kernel,
        out_shape=(
            *wholes,
            jax.ShapeDtypeStruct((4, SMALL, 128), bf16),
            jax.ShapeDtypeStruct((2 * PAD, D), bf16),
            jax.ShapeDtypeStruct((2 * PAD, 3 * D), bf16),
            jax.ShapeDtypeStruct((2, HEADS, PAD, LANES), bf16),
            jax.ShapeDtypeStruct((2 * PAD, D), f32),
            jax.ShapeDtypeStruct((2 * PAD, D), bf16),
            jax.ShapeDtypeStruct((2 * PAD, D), bf16),
            jax.ShapeDtypeStruct((PAD, LANES), jnp.int32),
        ),
        in_specs=[inside] * 7 + [anywhere] * 4,
        out_specs=(anywhere,) * 13,
        scratch_shapes=[
            pltpu.VMEM((4, SMALL, 128), bf16),
            pltpu.VMEM((4, GROUP * CHUNKS, 128), f32),
            pltpu.VMEM((CHUNKS, GROUP, 8, 128), jnp.int32),
            pltpu.VMEM((2 * PAD, D), bf16),
            pltpu.VMEM((2 * PAD, D), bf16),
            pltpu.VMEM((2 * PAD, D), bf16),
            pltpu.VMEM(half, bf16),
            pltpu.VMEM(half, bf16),
            pltpu.VMEM((2 * PAD, 3 * D), bf16),
            pltpu.VMEM((PAD, LANES), jnp.int32),
            pltpu.VMEM((TAIL, 128), jnp.int32),
            pltpu.VMEM((HEADS // 2, TAIL, 128), bf16),
            pltpu.VMEM((HEADS, PAD, LANES), bf16),
            pltpu.VMEM((2, PAD, PAD), f32),
            pltpu.VMEM((2, 2, PAD, LANES), bf16),
            pltpu.VMEM((2 * PAD, D), f32),
            pltpu.VMEM((2 * PAD, D), bf16),
            dma((5, 4, 3)),
            dma((5, 4, 3)),
            dma((2, 3)),
            dma((2, 3)),
            dma((PAD // 16,)),
            dma((PAD // 16,)),
            dma((2, 3)),
            dma((2, 3)),
            dma((2, HEADS // GROUP, 3)),
            dma((2, HEADS // GROUP, 3)),
            dma((13,)),
            dma((2,)),
        ],
        compiler_params=pltpu.CompilerParams(
            vmem_limit_bytes=VMEM_LIMIT, collective_id=0, has_side_effects=True
        ),
        name="front",
    )(
        tokens,
        jnp.asarray(send_matrix(), bf16),
        jnp.asarray(spread_matrix(), bf16),
        small,
        table,
        row_ids,
        rel_index,
        *weights,
    )
    whole = [w.reshape(-1, w.shape[-1]) for w in results[:5]]
    return (*whole, *results[5:])


CORE_SUM, FIRST_SUM, SECOND_SUM, Z_SUM, SHARE = range(5)
SUMMED = ((16, 2048, True), (64, 512, False), (16, 512, True))
SUMMED += tuple((16, 3 * 128, group % 2 == 0) for group in range(HEADS // GROUP))
FC1, FC2, PROJ, QKV = range(4)
STRIDE = HEADS + 1
SPAN = 256
SPANS = -(-TABLE // SPAN)
BATCH = 8
HALF = PAD // 2
TILES = LANES // 128
SLAB = 2 * SPANS * GROUP + SMALL


def back_kernel(
    grad_unrolled,
    order,
    order_back,
    rolled,
    mixed,
    weights_a,
    weights_b,
    inverse,
    contexts,
    rel,
    tokens,
    grad_middle,
    small_all,
    small_grads,
    attend_in,
    fc1_grad,
    fc2_grad,
    proj_grad,
    grad_tokens,
    fc1_out,
    fc2_out,
    proj_out,
    qkv_out_0,
    qkv_out_1,
    qkv_out_2,
    qkv_out_3,
    slab_out,
    outgoing,
    grad_context,
    attend,
    grads,
    rolled_back,
    returned,
    pairs,
    pairs_out,
    pairs_in,
    qkv_grads,
    table_sum,
    slab,
    slab_z,
    slab_rep,
    *rest,
):
    count = len(SUMMED)
    held = [rest[6 * m : 6 * m + 6] for m in range(count)]
    (
        sum_send,
        sum_recv,
        extra_send,
        extra_recv,
        piece_send,
        piece_recv,
        back_send,
        back_recv,
        attend_sem,
        pairs_send,
        pairs_recv,
        slab_send,
        slab_recv,
        local,
    ) = rest[6 * count :]
    rep, shard, core, x_bit, y_bit = place()
    reps = lax.axis_size("rep")
    barrier = pltpu.get_barrier_semaphore()

    def hello(k, carry):
        pl.semaphore_signal(
            barrier,
            inc=1,
            device_id={"rep": lax.rem(rep + k, reps), "shard": shard},
            device_id_type=MESH,
        )
        return carry

    lax.fori_loop(1, reps, hello, 0)
    for k in (1, 2, 3):
        pl.semaphore_signal(
            barrier,
            inc=1,
            device_id={"rep": rep, "shard": lax.rem(shard + k, 4)},
            device_id_type=MESH,
        )
    pl.semaphore_wait(barrier, reps + 2)

    sources = (fc1_grad, fc2_grad, proj_grad) + tuple(qkv_grads.at[g] for g in range(4))

    def axis_of(matrix, first):
        x_first = SUMMED[matrix][2]
        use_x = x_first == first
        return (1, x_bit) if use_x else (2, y_bit)

    def sum_copies(matrix, phase):
        from_core, kept, from_first, summed, from_z, shared = held[matrix]
        x_first = SUMMED[matrix][2]
        first_bit, first = axis_of(matrix, True)
        second_bit, second = axis_of(matrix, False)

        def one(src, dst, bit, n=0):
            return remote(
                src,
                dst,
                sum_send.at[matrix, phase, n],
                sum_recv.at[matrix, phase, n],
                flip(rep, bit),
                shard,
            )

        if phase == CORE_SUM:
            return [one(sources[matrix].at[:, :, :, 1 - core], from_core, 0)]
        if phase == FIRST_SUM:
            cut = kept.at[:, :, 1 - x_bit] if x_first else kept.at[:, 1 - y_bit]
            return [one(cut, from_first, first_bit)]
        if phase == SECOND_SUM:
            return [one(from_first.at[:, 1 - second], summed, second_bit)]
        if phase == Z_SUM:
            copies = []
            for k in (1, 2, 3):
                to = lax.rem(shard + k, 4)
                copies.append(
                    remote(
                        summed.at[to],
                        from_z.at[3 - k],
                        sum_send.at[matrix, phase, k - 1],
                        sum_recv.at[matrix, phase, 3 - k],
                        rep,
                        to,
                    )
                )
            return copies
        block = shared.at[y_bit, x_bit, core]
        copies = []
        for n in range(1, PARTS):
            partner = rep
            for bit in range(3):
                if n >> bit & 1:
                    partner = flip(partner, bit)
            copies.append(
                remote(
                    block,
                    block,
                    sum_send.at[matrix, phase, n - 1],
                    sum_recv.at[matrix, phase, n - 1],
                    partner,
                    shard,
                )
            )
        return copies

    def own_copy(matrix):
        return pltpu.make_async_copy(
            sources[matrix].at[:, :, :, core], held[matrix][1], local.at[matrix]
        )

    def extra_copy(matrix, bit):
        shared, from_z = held[matrix][5], held[matrix][4]
        return remote(
            shared.at[y_bit, x_bit, core],
            from_z.at[bit],
            extra_send.at[matrix, bit - 3],
            extra_recv.at[matrix, bit - 3],
            flip(rep, bit),
            shard,
        )

    def add(into, at, other, other_at):
        into[at] = (into[at].astype(f32) + other[other_at].astype(f32)).astype(bf16)

    def begin(matrix):
        own_copy(matrix).start()
        for copy in sum_copies(matrix, CORE_SUM):
            copy.start()

    def advance(matrix, phase):
        from_core, kept, from_first, summed, from_z, shared = held[matrix]
        x_first = SUMMED[matrix][2]
        _, second = axis_of(matrix, False)
        for copy in sum_copies(matrix, phase):
            copy.wait_recv()
        if phase == CORE_SUM:
            own_copy(matrix).wait()

            def step(n, carry):
                at = (n // 4, lax.rem(n // 2, 2), lax.rem(n, 2))
                add(kept, at, from_core, at)
                return carry

            lax.fori_loop(0, 16, step, 0)
        elif phase == FIRST_SUM:

            def step(n, carry):
                owner, other = n // 2, lax.rem(n, 2)
                at = (owner, other, x_bit) if x_first else (owner, y_bit, other)
                add(from_first, (owner, other), kept, at)
                return carry

            lax.fori_loop(0, 8, step, 0)
        elif phase == SECOND_SUM:

            def step(owner, carry):
                add(summed, (owner,), from_first, (owner, second))
                return carry

            lax.fori_loop(0, 4, step, 0)
        elif phase == Z_SUM:
            total = summed[shard].astype(f32)
            for n in range(3):
                total = total + from_z[n].astype(f32)
            shared[y_bit, x_bit, core] = total.astype(bf16)
            bit = 3
            while (1 << bit) < reps:
                copy = extra_copy(matrix, bit)
                copy.start()
                copy.wait()
                at = (y_bit, x_bit, core)
                add(shared, at, from_z, (bit,))
                bit += 1
        if phase < SHARE:
            for copy in sum_copies(matrix, phase + 1):
                copy.start()

    def on_the_way(step, table_of_steps):
        for when, actions in table_of_steps.items():

            @pl.when(step == when)
            def _():
                for matrix, phase in actions:
                    advance(matrix, phase)

    outgoing[...] = dot(order[...], grad_unrolled[...]).astype(bf16)

    def roll_copies(window):
        return pieces_to(
            outgoing,
            grad_context,
            lambda n: piece_send.at[window, n],
            lambda n: piece_recv.at[window, n],
            rep,
            shard,
            window,
        )

    for window in range(2):
        for copy in roll_copies(window):
            copy.start()
        rows = slice(window * PAD, window * PAD + LENGTHS[0])
        grad_context[rows, :] = outgoing[rows, :]
    for matrix in (FC1, FC2, PROJ):
        begin(matrix)

    head_of = lax.broadcasted_iota(jnp.int32, (1, 128), 1) // HD
    none = jnp.zeros((), bf16)

    def attend_copy(head):
        slot = lax.rem(head, 2)
        return pltpu.make_async_copy(
            attend_in.at[:, head], attend.at[slot], attend_sem.at[slot]
        )

    attend_copy(0).start()
    same = lax.broadcasted_iota(jnp.int32, (D, D), 0) == lax.broadcasted_iota(
        jnp.int32, (D, D), 1
    )
    unit = jnp.where(same, jnp.ones((), bf16), none)
    rolled_back[...] = dot(unit, rolled[...], NT).astype(bf16)

    def qkv_group(group):
        columns = [
            grads[:, part * D + group * 128 : part * D + (group + 1) * 128] for part in range(3)
        ]
        got = dot(rolled_back[...], jnp.concatenate(columns, 1)).astype(bf16)
        qkv_grads[group] = got.reshape(qkv_grads.shape[1:])
        begin(QKV + group)

    first_schedule = {
        10: [(FC1, FIRST_SUM), (FC2, FIRST_SUM), (PROJ, FIRST_SUM)],
        6: [(QKV, CORE_SUM)],
        9: [(QKV, FIRST_SUM)],
        11: [(QKV + 1, CORE_SUM), (QKV, SECOND_SUM)],
        13: [(QKV + 1, FIRST_SUM)],
        14: [(QKV + 2, CORE_SUM), (QKV, Z_SUM)],
        15: [
            (FC1, SECOND_SUM),
            (FC2, SECOND_SUM),
            (PROJ, SECOND_SUM),
            (QKV + 1, SECOND_SUM),
            (QKV + 2, FIRST_SUM),
        ],
    }
    second_schedule = {
        1: [(QKV + 3, CORE_SUM), (QKV + 1, Z_SUM), (QKV + 2, SECOND_SUM)],
        4: [(QKV + 3, FIRST_SUM), (QKV + 2, Z_SUM)],
        8: [(QKV + 3, SECOND_SUM)],
        13: [(QKV + 3, Z_SUM), (FC1, Z_SUM), (FC2, Z_SUM), (PROJ, Z_SUM)],
    }

    for matrix in (FC1, FC2, PROJ):
        advance(matrix, CORE_SUM)
    for window in range(2):
        for copy in roll_copies(window):
            copy.wait_recv()

    def head_step(head, carry):
        on_the_way(head, first_schedule)
        for done in range(1, HEADS // GROUP):

            @pl.when(head == done * GROUP)
            def _():
                qkv_group(done - 1)

        @pl.when(head + 1 < HEADS)
        def _():
            attend_copy(head + 1).start()

        attend_copy(head).wait()
        slot = lax.rem(head, 2)
        group, member = head // GROUP, lax.rem(head, GROUP)

        def lanes(part):
            return pl.ds(pl.multiple_of(part * D + group * 128, 128), 128)

        mine = head_of == member
        both = []
        for window in range(2):
            rows = pl.ds(window * PAD, PAD)
            query = jnp.where(mine, mixed[rows, lanes(0)], none)
            key = jnp.where(mine, mixed[rows, lanes(1)], none)
            grad = grad_context[rows, lanes(0)].astype(f32) * inverse[rows, lanes(0)]
            grad = jnp.where(mine, grad, 0.0).astype(bf16)
            expo = attend[slot, window, :, :PAD]
            grad_attend = dot(grad, mixed[rows, lanes(2)], NT)
            inner = jnp.sum(
                grad.astype(f32) * contexts[rows, lanes(0)].astype(f32), -1, keepdims=True
            )
            grad_scores = (expo.astype(f32) * (grad_attend - inner)).astype(bf16)
            both.append(grad_scores)
            for part, value in (
                (0, dot(grad_scores, key) * SCALE),
                (1, dot(grad_scores, query, TN) * SCALE),
                (2, dot(expo, grad, TN)),
            ):
                grads[rows, lanes(part)] = jnp.where(
                    mine, value.astype(bf16), grads[rows, lanes(part)]
                )
        total = both[0].astype(f32) + both[1].astype(f32)
        for tile in range(TILES):
            part = total[:, tile * 128 : (tile + 1) * 128]
            if part.shape[1] < 128:
                part = jnp.concatenate([part, jnp.zeros((PAD, 128 - part.shape[1]), f32)], 1)
            pairs[tile, pl.ds(head, PAD, stride=STRIDE), :] = part
        return carry

    lax.fori_loop(0, HEADS, head_step, 0)

    for window in range(2):
        for copy in roll_copies(window):
            copy.wait_send()

    def return_copies(window):
        return pieces_to(
            outgoing,
            returned,
            lambda n: back_send.at[window, n],
            lambda n: back_recv.at[window, n],
            rep,
            shard,
            window,
        )

    for window in range(2):
        span = slice(window * PAD, (window + 1) * PAD)
        got = dot(grads[span, :HALF_QKV], weights_a[...], NT)
        got = got + dot(grads[span, HALF_QKV:], weights_b[...], NT)
        outgoing[span, :] = got.astype(bf16)
        for copy in return_copies(window):
            copy.start()
        rows = slice(window * PAD, window * PAD + LENGTHS[0])
        returned[rows, :] = outgoing[rows, :]
    qkv_group(HEADS // GROUP - 1)

    def round_step(step, carry):
        source = pl.ds(((1 - core) * HALF + step) * STRIDE, HEADS)
        at = pl.ds(pl.multiple_of(step * HEADS, HEADS), HEADS)
        for tile in range(TILES):
            pairs_out[tile, at, :] = pairs[tile, source, :].astype(bf16)
        return carry

    def pairs_copy(half):
        block = pl.ds(half * (HALF * HEADS // 2), HALF * HEADS // 2)
        return remote(
            pairs_out.at[:, block],
            pairs_in.at[:, block],
            pairs_send.at[half],
            pairs_recv.at[half],
            flip(rep, 0),
            shard,
        )

    for half in range(2):
        lax.fori_loop(half * (HALF // 2), (half + 1) * (HALF // 2), round_step, 0)
        pairs_copy(half).start()

    low_of = lax.broadcasted_iota(jnp.int32, (SPAN, LANES), 0).astype(f32).astype(bf16)
    table_sum[...] = jnp.zeros_like(table_sum)
    for half in range(2):
        pairs_copy(half).wait_recv()

    def table_step(step, carry):
        on_the_way(step, second_schedule)
        left, right = [], []
        for k in range(BATCH):
            row = step * BATCH + k
            there = core * HALF + row
            at = pl.ds(there * STRIDE, HEADS)
            near = pl.ds(pl.multiple_of(row * HEADS, HEADS), HEADS)
            index = rel[pl.ds(there, 1), :]
            low = (index & (SPAN - 1)).astype(f32).astype(bf16)
            high = jnp.broadcast_to((index // SPAN).astype(f32).astype(bf16), (HEADS, LANES))
            total = jnp.concatenate(
                [pairs[t, at, :] + pairs_in[t, near, :].astype(f32) for t in range(TILES)], 1
            ).astype(bf16)
            nothing = jnp.zeros_like(total)
            left.append(
                jnp.concatenate(
                    [jnp.where(high == jnp.asarray(s, bf16), total, nothing) for s in range(SPANS)],
                    0,
                )
            )
            hit = low_of == jnp.broadcast_to(low, (SPAN, LANES))
            right.append(jnp.where(hit, jnp.ones((), bf16), jnp.zeros((), bf16)))
        table_sum[...] += dot(jnp.concatenate(left, 1), jnp.concatenate(right, 1), NT)
        return carry

    lax.fori_loop(0, HALF // BATCH, table_step, 0)

    for window in range(2):
        for copy in return_copies(window):
            copy.wait_recv()
    gain = small_row(small_all, LN1_GAIN).astype(f32)

    def norm_step(step, carry):
        gain_sum, shift_sum = carry
        rows = pl.ds(pl.multiple_of(step * 112, 16), 112)
        grad_out = dot(order_back[rows, :], returned[...])
        normal, inverse = norm_rows(tokens[rows, :].astype(f32))
        scaled = grad_out * gain
        inner = (
            scaled
            - jnp.mean(scaled, -1, keepdims=True)
            - normal * jnp.mean(scaled * normal, -1, keepdims=True)
        )
        grad_tokens[rows, :] = grad_middle[rows, :] + inverse * inner
        return (
            gain_sum + jnp.sum(grad_out * normal, 0, keepdims=True),
            shift_sum + jnp.sum(grad_out, 0, keepdims=True),
        )

    nought = jnp.zeros((1, D), f32)
    gain_sum, shift_sum = lax.fori_loop(0, 7, norm_step, (nought, nought))

    query_sum = jnp.sum(grads[:, :D].astype(f32), 0, keepdims=True)
    value_sum = jnp.sum(grads[:, 2 * D :].astype(f32), 0, keepdims=True)
    for owner in range(4):
        lanes = slice(owner * 128, (owner + 1) * 128)
        sums = jnp.concatenate(
            [table_sum[pl.ds(s * HEADS + GROUP * owner, GROUP), :] for s in range(SPANS)], 0
        )
        slab[owner, : SPANS * GROUP, :] = sums[:, :128]
        slab[owner, SPANS * GROUP : 2 * SPANS * GROUP, :] = sums[:, 128:]
        slab[owner, 2 * SPANS * GROUP :, :] = jnp.concatenate(
            [
                gain_sum[:, lanes],
                shift_sum[:, lanes],
                query_sum[:, lanes],
                value_sum[:, lanes],
                small_grads[owner, V_BIAS + 1 :, :],
            ],
            0,
        )

    def slab_copies():
        return [
            remote(
                slab.at[lax.rem(shard + k, 4)],
                slab_z.at[3 - k],
                slab_send.at[k - 1],
                slab_recv.at[3 - k],
                rep,
                lax.rem(shard + k, 4),
            )
            for k in (1, 2, 3)
        ]

    for copy in slab_copies():
        copy.start()

    for matrix in range(count):
        advance(matrix, SHARE)
    for copy in slab_copies():
        copy.wait_recv()
    slab_rep[rep] = slab[shard] + (slab_z[0] + slab_z[1] + slab_z[2])

    def slab_share(k):
        return remote(
            slab_rep.at[rep],
            slab_rep.at[rep],
            slab_send.at[2 + k],
            slab_recv.at[2 + reps - k],
            lax.rem(rep + k, reps),
            shard,
        )

    def share_start(k, carry):
        slab_share(k).start()
        return carry

    lax.fori_loop(1, reps, share_start, 0)
    outs = (fc1_out, fc2_out, proj_out, qkv_out_0, qkv_out_1, qkv_out_2, qkv_out_3)
    results = [
        pltpu.make_async_copy(held[matrix][5], outs[matrix], local.at[count + matrix])
        for matrix in range(count)
    ]
    for copy in results:
        copy.start()

    def share_wait(k, carry):
        slab_share(k).wait()
        return carry

    lax.fori_loop(1, reps, share_wait, 0)

    def slab_step(k, total):
        return total + slab_rep[k]

    slab_out[...] = lax.fori_loop(1, reps, slab_step, slab_rep[0])

    for copy in slab_copies():
        copy.wait_send()
    for window in range(2):
        pairs_copy(window).wait_send()
        for copy in return_copies(window):
            copy.wait_send()
    for matrix in range(count):
        for phase in range(SHARE + 1):
            for copy in sum_copies(matrix, phase):
                copy.wait_send()
    for copy in results:
        copy.wait()


def back(
    grad_unrolled,
    rolled,
    mixed,
    weights_a,
    weights_b,
    inverse,
    contexts,
    rel,
    tokens,
    grad_middle,
    small_all,
    small_grads,
    attend,
    fc1_grad,
    fc2_grad,
    proj_grad,
):
    anywhere, inside = pl.BlockSpec(memory_space=pl.ANY), pl.BlockSpec(memory_space=pltpu.VMEM)
    reps = lax.axis_size("rep")
    dma = pltpu.SemaphoreType.DMA
    order = send_matrix()
    extra = max(1, reps.bit_length() - 4)
    held = []
    for rows, columns, _ in SUMMED:
        held += [
            pltpu.VMEM((4, 2, 2, rows, columns), bf16),
            pltpu.VMEM((4, 2, 2, rows, columns), bf16),
            pltpu.VMEM((4, 2, rows, columns), bf16),
            pltpu.VMEM((4, rows, columns), bf16),
            pltpu.VMEM((3 + extra, rows, columns), bf16),
            pltpu.VMEM((2, 2, 2, rows, columns), bf16),
        ]
    return pl.pallas_call(
        back_kernel,
        out_shape=(
            jax.ShapeDtypeStruct(tokens.shape, f32),
            *[jax.ShapeDtypeStruct((2, 2, 2) + shape[:2], bf16) for shape in SUMMED],
            jax.ShapeDtypeStruct((SLAB, 128), f32),
        ),
        in_specs=[inside] * 14 + [anywhere] * 4,
        out_specs=(inside, *[anywhere] * len(SUMMED), inside),
        scratch_shapes=[
            pltpu.VMEM((2 * PAD, D), bf16),
            pltpu.VMEM((2 * PAD, D), bf16),
            pltpu.VMEM((2, 2, PAD, LANES), bf16),
            pltpu.VMEM((2 * PAD, 3 * D), bf16),
            pltpu.VMEM((D, 2 * PAD), bf16),
            pltpu.VMEM((2 * PAD, D), bf16),
            pltpu.VMEM((TILES, PAD * STRIDE, 128), f32),
            pltpu.VMEM((TILES, HALF * HEADS, 128), bf16),
            pltpu.VMEM((TILES, HALF * HEADS, 128), bf16),
            pltpu.VMEM((HEADS // GROUP, 4, 2, 2, 2, 16, 3 * 128), bf16),
            pltpu.VMEM((SPANS * HEADS, SPAN), f32),
            pltpu.VMEM((4, SLAB, 128), f32),
            pltpu.VMEM((3, SLAB, 128), f32),
            pltpu.VMEM((reps, SLAB, 128), f32),
            *held,
            dma((len(SUMMED), SHARE + 1, PARTS - 1)),
            dma((len(SUMMED), SHARE + 1, PARTS - 1)),
            dma((len(SUMMED), extra)),
            dma((len(SUMMED), extra)),
            dma((2, 3)),
            dma((2, 3)),
            dma((2, 3)),
            dma((2, 3)),
            dma((2,)),
            dma((2,)),
            dma((2,)),
            dma((3 + reps,)),
            dma((3 + reps,)),
            dma((2 * len(SUMMED),)),
        ],
        compiler_params=pltpu.CompilerParams(
            vmem_limit_bytes=VMEM_LIMIT, collective_id=1, has_side_effects=True
        ),
        name="back",
    )(
        grad_unrolled,
        jnp.asarray(order, bf16),
        jnp.asarray(order.T, bf16),
        rolled,
        mixed,
        weights_a,
        weights_b,
        inverse,
        contexts,
        rel,
        tokens,
        grad_middle,
        small_all,
        small_grads,
        attend,
        fc1_grad.reshape(4, 2, 2, 2, 16, 2048),
        fc2_grad.reshape(4, 2, 2, 2, 64, 512),
        proj_grad.reshape(4, 2, 2, 2, 16, 512),
    )


def norm_forward(rows, gain, shift):
    centre = rows - jnp.mean(rows, -1, keepdims=True)
    inverse = lax.rsqrt(jnp.mean(centre * centre, -1, keepdims=True) + 1e-05)
    normal = centre * inverse
    return (normal * gain.astype(jnp.float32) + shift.astype(jnp.float32), normal, inverse)


def norm_backward(grad_out, normal, inverse, gain):
    scaled = grad_out * gain.astype(jnp.float32)
    inner = (
        scaled
        - jnp.mean(scaled, -1, keepdims=True)
        - normal * jnp.mean(scaled * normal, -1, keepdims=True)
    )
    return (inverse * inner, jnp.sum(grad_out * normal, 0), jnp.sum(grad_out, 0))


def shards(
    tokens,
    region,
    rel_index,
    ln1_gain,
    ln1_shift,
    w_qkv,
    q_bias,
    v_bias,
    table,
    w_proj,
    proj_bias,
    ln2_gain,
    ln2_shift,
    w_fc1,
    fc1_bias,
    w_fc2,
    fc2_bias,
    cotangent,
):
    inputs = tokens.reshape(-1, D).astype(jnp.float32)
    small = jnp.concatenate(
        (ln1_gain, ln1_shift, q_bias, v_bias, proj_bias, ln2_gain, ln2_shift, fc2_bias, fc1_bias)
    ).reshape(-1, 128)
    small = jnp.pad(small, ((0, SMALL - small.shape[0]), (0, 0)))
    chunks = jnp.pad(table.astype(f32).T, ((0, 0), (0, CHUNKS * 128 - TABLE)))
    labels = region.reshape(WT, WH, 2, WW).transpose(2, 0, 1, 3).reshape(2, WIN)
    labels = pieces_of(labels, 1, -1)
    row_ids = jnp.pad(labels, ((0, 0), (0, LANES - PAD)), constant_values=-1)[:, None]
    (
        whole_qkv_a,
        whole_qkv_b,
        whole_proj,
        whole_fc1,
        whole_fc2,
        small,
        rolled,
        qkv,
        attend,
        inverse,
        contexts,
        returned,
        rel,
    ) = front(
        tokens.reshape(-1, D),
        small,
        chunks.reshape(-1, 128),
        row_ids,
        rel_index,
        w_qkv,
        w_proj,
        w_fc1,
        w_fc2,
    )
    gain_one, bias_proj = small[:, LN1_GAIN].reshape(-1), small[:, PROJ_BIAS].reshape(-1)
    gain_two, shift_two = small[:, LN2_GAIN].reshape(-1), small[:, LN2_SHIFT].reshape(-1)
    bias_fc2 = small[:, FC2_BIAS].reshape(-1)
    bias_fc1 = small[:, FC1_BIAS : FC1_BIAS + 4].reshape(-1)
    order = jnp.asarray(send_matrix(), bf16)
    unrolled = dot(order, returned, TN).astype(bf16)
    middle = (
        inputs
        + jnp.dot(unrolled, whole_proj, preferred_element_type=jnp.float32)
        + bias_proj.astype(jnp.float32)
    )
    normed_two, normal_two, inverse_two = norm_forward(middle, gain_two, shift_two)
    normed_low = normed_two.astype(jnp.bfloat16)
    hidden = jnp.dot(normed_low, whole_fc1, preferred_element_type=jnp.float32) + bias_fc1.astype(
        jnp.float32
    )
    active = jax.nn.gelu(hidden, approximate=False).astype(jnp.bfloat16)
    result = (
        middle
        + jnp.dot(active, whole_fc2, preferred_element_type=jnp.float32)
        + bias_fc2.astype(jnp.float32)
    )
    output = result.astype(jnp.bfloat16).reshape(tokens.shape)
    grad_out = cotangent.reshape(-1, D)
    grad_w_fc2 = jnp.einsum("rf,rd->fd", active, grad_out, preferred_element_type=jnp.float32)
    grad_fc2_bias = jnp.sum(grad_out.astype(jnp.float32), 0)
    slope = (
        0.5 * (1.0 + lax.erf(hidden * 0.7071067811865476))
        + hidden * jnp.exp(-0.5 * hidden * hidden) * 0.3989422804014327
    )
    grad_active = jnp.einsum("rd,fd->rf", grad_out, whole_fc2, preferred_element_type=jnp.float32)
    grad_hidden = (grad_active * slope).astype(jnp.bfloat16)
    grad_w_fc1 = jnp.einsum(
        "rd,rf->df", normed_low, grad_hidden, preferred_element_type=jnp.float32
    )
    grad_fc1_bias = jnp.sum(grad_hidden.astype(jnp.float32), 0)
    grad_normed_two = jnp.einsum(
        "rf,df->rd", grad_hidden, whole_fc1, preferred_element_type=jnp.float32
    )
    grad_inner_two, grad_ln2_gain, grad_ln2_shift = norm_backward(
        grad_normed_two, normal_two, inverse_two, gain_two
    )
    grad_middle = grad_out.astype(jnp.float32) + grad_inner_two
    grad_branch = grad_middle.astype(jnp.bfloat16)
    grad_w_proj = jnp.einsum("rd,re->de", unrolled, grad_branch, preferred_element_type=jnp.float32)
    grad_proj_bias = jnp.sum(grad_branch.astype(jnp.float32), 0)
    grad_unrolled = jnp.einsum(
        "re,de->rd", grad_branch, whole_proj, preferred_element_type=jnp.float32
    ).astype(jnp.bfloat16)
    rows = [jnp.zeros((4, 128), f32)] * 4
    for gradient in (grad_proj_bias, grad_ln2_gain, grad_ln2_shift, grad_fc2_bias):
        rows.append(gradient.reshape(4, 128))
    small_grads = jnp.concatenate(
        [jnp.stack(rows, 1), grad_fc1_bias.reshape(4, 4, 128), jnp.zeros((4, 4, 128), f32)], 1
    )
    grad_tokens, grad_w_fc1, grad_w_fc2, grad_w_proj, *grads_qkv, slab = back(
        grad_unrolled,
        rolled,
        qkv,
        whole_qkv_a,
        whole_qkv_b,
        inverse,
        contexts,
        rel,
        tokens.reshape(-1, D),
        grad_middle,
        small,
        small_grads,
        attend,
        grad_w_fc1.astype(bf16),
        grad_w_fc2.astype(bf16),
        grad_w_proj.astype(bf16),
    )
    grad_tokens = grad_tokens.reshape(tokens.shape)
    grad_w_fc1 = grad_w_fc1.astype(f32).reshape(w_fc1.shape)
    grad_w_fc2 = grad_w_fc2.astype(f32).reshape(w_fc2.shape)
    grad_w_proj = grad_w_proj.astype(f32).reshape(w_proj.shape)
    parts = [g.reshape(-1, 3, 128) for g in grads_qkv]
    grad_w_qkv = jnp.stack(parts, 2).astype(f32)
    grad_w_qkv = grad_w_qkv.reshape(w_qkv.shape)
    spans = slab[: 2 * SPANS * GROUP].reshape(2, SPANS, GROUP, 128).transpose(1, 0, 3, 2)
    grad_table = spans.reshape(SPANS * SPAN, GROUP)[:TABLE]
    vectors = slab[2 * SPANS * GROUP :]
    grad_ln1_gain, grad_ln1_shift = vectors[LN1_GAIN], vectors[LN1_SHIFT]
    grad_q_bias, grad_v_bias = vectors[Q_BIAS], vectors[V_BIAS]
    grad_proj_bias, grad_fc2_bias = vectors[PROJ_BIAS], vectors[FC2_BIAS]
    grad_ln2_gain, grad_ln2_shift = vectors[LN2_GAIN], vectors[LN2_SHIFT]
    grad_fc1_bias = vectors[FC1_BIAS : FC1_BIAS + 4].reshape(-1)
    return (
        output,
        grad_tokens,
        grad_ln1_gain,
        grad_ln1_shift,
        grad_w_qkv,
        grad_q_bias,
        grad_v_bias,
        grad_table,
        grad_w_proj,
        grad_proj_bias,
        grad_ln2_gain,
        grad_ln2_shift,
        grad_w_fc1,
        grad_fc1_bias,
        grad_w_fc2,
        grad_fc2_bias,
    )


def solution(mesh):
    return jax.shard_map(
        shards,
        mesh=mesh,
        in_specs=(
            P("rep", "shard", None, None),
            P("shard", None),
            P(),
            P("shard"),
            P("shard"),
            P("shard", None),
            P("shard"),
            P("shard"),
            P(None, "shard"),
            P("shard", None),
            P("shard"),
            P("shard"),
            P("shard"),
            P("shard", None),
            P("shard"),
            P("shard", None),
            P("shard"),
            P("rep", "shard", None, None),
        ),
        out_specs=(
            P("rep", "shard", None, None),
            P("rep", "shard", None, None),
            P("shard"),
            P("shard"),
            P("shard", None),
            P("shard"),
            P("shard"),
            P(None, "shard"),
            P("shard", None),
            P("shard"),
            P("shard"),
            P("shard"),
            P("shard", None),
            P("shard"),
            P("shard", None),
            P("shard"),
        ),
        check_vma=False,
    )
```

```python
import functools

import jax
import jax.numpy as jnp
import numpy as np
from jax import lax
from jax.experimental import pallas as pl
from jax.experimental.pallas import tpu as pltpu
from jax.sharding import PartitionSpec as P

D = 512
HEADS = 16
HD = 32
WT = 8
WH = 7
WW = 7
WIN = 392
TABLE = 2535
FF = 2048
FF_TILE = 256
PAD = 416
LANES = 512
GROUP = 4
CHUNKS = 20
SCALE = HD ** (-0.5)
NN = (((1,), (0,)), ((), ()))
NT = (((1,), (1,)), ((), ()))
TN = (((0,), (0,)), ((), ()))
VMEM_LIMIT = 60 * 2**20
f32 = jnp.float32
bf16 = jnp.bfloat16

PIECES = (
    ((0, 4), (0, 4), 112, 0),
    ((4, 8), (0, 4), 112, 112),
    ((0, 4), (4, 7), 96, 224),
    ((4, 8), (4, 7), 96, 320),
)


def send_matrix():
    matrix = np.zeros((2 * PAD, WT * WH * 2 * WW), np.float32)
    for window in range(2):
        for (t0, t1), (h0, h1), _, first in PIECES:
            row = window * PAD + first
            for t in range(t0, t1):
                for h in range(h0, h1):
                    for w in range(WW):
                        column = (window * WW + w + WW // 2) % (2 * WW)
                        source = ((t + 4) % WT * WH + (h + 3) % WH) * 2 * WW + column
                        matrix[row, source] = 1.0
                        row += 1
    return matrix


def spread_matrix():
    source = np.arange(WIN).reshape(WT, WH, WW)
    matrix = np.zeros((PAD, WIN), np.float32)
    for (t0, t1), (h0, h1), _, first in PIECES:
        tokens = source[t0:t1, h0:h1].reshape(-1)
        matrix[first + np.arange(tokens.size), tokens] = 1.0
    return matrix


def pieces_of(array, axis, fill):
    shape = array.shape
    split = array.reshape(shape[:axis] + (WT, WH, WW) + shape[axis + 1 :])
    parts = []
    for (t0, t1), (h0, h1), padded, _ in PIECES:
        part = lax.slice_in_dim(lax.slice_in_dim(split, t0, t1, axis=axis), h0, h1, axis=axis + 1)
        length = (t1 - t0) * (h1 - h0) * WW
        part = part.reshape(shape[:axis] + (length,) + shape[axis + 1 :])
        widths = [(0, 0, 0)] * len(shape)
        widths[axis] = (0, padded - length, 0)
        parts.append(lax.pad(part, jnp.asarray(fill, array.dtype), widths))
    return jnp.concatenate(parts, axis)


def dot(a, b, dims=NN):
    return lax.dot_general(a, b, dims, preferred_element_type=f32)


MESH = pl.DeviceIdType.MESH
PARTS = 8
FIRST_ROWS = tuple(first for _, _, _, first in PIECES)
LENGTHS = tuple(padded for _, _, padded, _ in PIECES)
ACROSS = (0, 2, 1, 3)
LN1_GAIN, LN1_SHIFT, Q_BIAS, V_BIAS, PROJ_BIAS, LN2_GAIN, LN2_SHIFT, FC2_BIAS, FC1_BIAS = range(9)
SMALL = 16


def place():
    rep, shard = lax.axis_index("rep"), lax.axis_index("shard")
    return rep, shard, lax.rem(rep, 2), lax.rem(rep // 2, 2), lax.rem(rep // 4, 2)


def flip(rep, bit):
    low = lax.rem(rep // (1 << bit), 2)
    return rep + (1 - 2 * low) * (1 << bit)


def remote(src, dst, send, recv, rep, shard):
    return pltpu.make_async_remote_copy(
        src_ref=src,
        dst_ref=dst,
        send_sem=send,
        recv_sem=recv,
        device_id={"rep": rep, "shard": shard},
        device_id_type=MESH,
    )


def greet(peers):
    barrier = pltpu.get_barrier_semaphore()
    for rep, shard in peers:
        pl.semaphore_signal(
            barrier, inc=1, device_id={"rep": rep, "shard": shard}, device_id_type=MESH
        )
    pl.semaphore_wait(barrier, len(peers))


def peers_of(rep, shard):
    return [(rep, lax.rem(shard + k, 4)) for k in (1, 2, 3)] + [
        (flip(rep, bit), shard) for bit in (0, 1, 2)
    ]


def quarter_across(shard, bits):
    low, high = lax.rem(shard, 2), shard // 2
    if bits & 1:
        low = 1 - low
    if bits & 2:
        high = 1 - high
    return high * 2 + low


def pieces_to(source, target, send, recv, rep, shard, window, columns=None, which=(1, 2, 3)):
    copies = []
    for piece in which:
        rows = pl.ds(
            pl.multiple_of(window * PAD + FIRST_ROWS[piece], 16), LENGTHS[piece]
        )
        at = (rows,) if columns is None else (rows, columns)
        copies.append(
            remote(
                source.at[at],
                target.at[at],
                send(piece - 1),
                recv(piece - 1),
                rep,
                quarter_across(shard, ACROSS[piece]),
            )
        )
    return copies


def norm_rows(rows):
    centre = rows - jnp.mean(rows, -1, keepdims=True)
    inverse = lax.rsqrt(jnp.mean(centre * centre, -1, keepdims=True) + 1e-05)
    return centre * inverse, inverse


def small_row(ref, row):
    return jnp.concatenate([ref[s, row : row + 1, :] for s in range(4)], 1)


FIXED = 4096.0
TAIL = 112
Z_PHASE, FIRST_PHASE, SECOND_PHASE, CORE_PHASE = range(4)
X_FIRST = (True, False, True, False, True)
HALF_QKV = 3 * D // 2


def front_kernel(
    tokens,
    order,
    spread,
    small,
    table,
    row_ids,
    rel,
    qkv_part,
    proj_part,
    fc1_part,
    fc2_part,
    qkv_whole_a,
    qkv_whole_b,
    proj_whole,
    fc1_whole,
    fc2_whole,
    small_out,
    rolled_out,
    mixed_out,
    attend_out,
    inverse_out,
    context_out,
    back_out,
    rel_out,
    small_all,
    table_all,
    table_wide,
    outgoing,
    arriving,
    rolled,
    weights_a,
    weights_b,
    mixed,
    index,
    index_tail,
    bias_tail,
    bias,
    mask,
    attend,
    inverse,
    contexts,
    gather_send,
    gather_recv,
    small_send,
    small_recv,
    bias_send,
    bias_recv,
    piece_send,
    piece_recv,
    back_send,
    back_recv,
    local,
    attend_sem,
):
    rep, shard, core, x_bit, y_bit = place()
    greet(peers_of(rep, shard))
    first_half, second_half = pl.ds(0, HALF_QKV), pl.ds(HALF_QKV, HALF_QKV)
    parts = (
        qkv_part.at[:, :, :, :, first_half],
        qkv_part.at[:, :, :, :, second_half],
        proj_part,
        fc1_part,
        fc2_part,
    )
    wholes = (qkv_whole_a, qkv_whole_b, proj_whole, fc1_whole, fc2_whole)
    feed_forward = (2, 3, 4)

    def gather(matrix, phase):
        copies = []
        for k in (1, 2, 3):
            at = lax.rem(shard + k, 4)
            whole = wholes[matrix]
            if phase == Z_PHASE:
                copies.append(
                    remote(
                        parts[matrix].at[y_bit, x_bit, core],
                        whole.at[shard, y_bit, x_bit, core],
                        gather_send.at[matrix, phase, k - 1],
                        gather_recv.at[matrix, phase, 3 - k],
                        rep,
                        at,
                    )
                )
                continue
            x_first = X_FIRST[matrix]
            if phase == FIRST_PHASE:
                block, partner = whole.at[at, y_bit, x_bit, core], flip(rep, 1 if x_first else 2)
            elif phase == SECOND_PHASE and x_first:
                block, partner = whole.at[at, y_bit, :, core], flip(rep, 2)
            elif phase == SECOND_PHASE:
                block, partner = whole.at[at, :, x_bit, core], flip(rep, 1)
            else:
                block, partner = whole.at[at, :, :, core], flip(rep, 0)
            copies.append(
                remote(
                    block,
                    block,
                    gather_send.at[matrix, phase, k - 1],
                    gather_recv.at[matrix, phase, k - 1],
                    partner,
                    shard,
                )
            )
        return copies

    def start(matrix, phase):
        for copy in gather(matrix, phase):
            copy.start()

    def arrived(matrix, phase):
        for copy in gather(matrix, phase):
            copy.wait_recv()

    def small_copies():
        copies = []
        for k in (1, 2, 3):
            for n, ref in enumerate((table_all, small_all)):
                copies.append(
                    remote(
                        ref.at[shard],
                        ref.at[shard],
                        small_send.at[n, k - 1],
                        small_recv.at[n, 3 - k],
                        rep,
                        lax.rem(shard + k, 4),
                    )
                )
        return copies

    small_all[shard] = small[...]
    table_all[shard] = table[...]
    for copy in small_copies():
        copy.start()
    start(0, Z_PHASE)
    start(1, Z_PHASE)
    own = [
        pltpu.make_async_copy(parts[m], wholes[m].at[shard], local.at[m]) for m in range(5)
    ]
    for copy in own:
        copy.start()

    outgoing[...] = dot(order[...], tokens[...]).astype(bf16)

    def roll_copies(window):
        return pieces_to(
            outgoing,
            arriving,
            lambda n: piece_send.at[window, n],
            lambda n: piece_recv.at[window, n],
            rep,
            shard,
            window,
        )

    for copy in roll_copies(0):
        copy.start()
    for matrix in feed_forward:
        start(matrix, Z_PHASE)
    for window in range(2):
        rows = slice(window * PAD, window * PAD + LENGTHS[0])
        arriving[rows, :] = outgoing[rows, :]

    rel_index = rel[...]
    digits = (rel_index // 256).astype(f32).astype(bf16), (rel_index & 255).astype(f32).astype(bf16)
    moved = []
    for digit in digits:
        half = dot(spread[...], digit).astype(bf16)
        moved.append(dot(half, spread[...], NT).astype(jnp.int32))
    index[:, :PAD] = moved[0] * 256 + moved[1]
    index[:, PAD:] = jnp.zeros((PAD, LANES - PAD), jnp.int32)

    ids = lax.broadcasted_iota(jnp.int32, (8, LANES), 0)
    for window in range(2):
        kinds = jnp.where(row_ids[window] + 1 == ids, 1.0, 0.0).astype(bf16)[:, :PAD]
        mask[window] = (dot(kinds, kinds, TN) - 1.0) * 1e30

    for copy in small_copies():
        copy.wait_recv()

    for block in range(4):
        count = min(TAIL, PAD - block * TAIL)
        lanes = slice(block * 32, block * 32 + 32)
        index_tail[:count, lanes] = index[block * TAIL : block * TAIL + count, PAD - 32 : PAD]
        if count < TAIL:
            index_tail[count:, lanes] = jnp.zeros((TAIL - count, 32), jnp.int32)

    upper, lower = (
        jnp.floor(table_all[2 * core + n] * FIXED + 0.5).astype(jnp.int32) for n in range(2)
    )
    words = upper * 65536 + (lower + 32768)
    for chunk in range(CHUNKS):
        for head in range(GROUP):
            row = head * CHUNKS + chunk
            table_wide[chunk, head] = jnp.broadcast_to(words[row : row + 1, :], (8, 128))
    mine = core * (HEADS // 2)

    def bias_copy(rows, step):
        block = bias.at[pl.ds(mine, HEADS // 2), rows]
        return remote(block, block, bias_send.at[step], bias_recv.at[step], flip(rep, 0), shard)

    def on_the_way(step, table_of_steps):
        for when, actions in table_of_steps.items():

            @pl.when(step == when)
            def _():
                for action, matrix, phase in actions:
                    action(matrix, phase)

    def advance(matrix, phase):
        arrived(matrix, phase)
        if phase < CORE_PHASE:
            start(matrix, phase + 1)

    schedule = {
        5: [(advance, 0, Z_PHASE), (advance, 1, Z_PHASE)],
        13: [(advance, 0, FIRST_PHASE), (advance, 1, FIRST_PHASE)],
        23: [(advance, 0, SECOND_PHASE), (advance, 1, SECOND_PHASE)],
    }
    later = {
        3: [(advance, m, Z_PHASE) for m in feed_forward],
        10: [(advance, m, FIRST_PHASE) for m in feed_forward],
    }

    def look_up(here):
        halves = [(here[s : s + 8] & 127, here[s : s + 8] >> 7) for s in (0, 8)]
        found = [[None, None] for _ in range(GROUP)]
        for chunk in range(CHUNKS):
            for s, (low, high) in enumerate(halves):
                hit = high == chunk
                for head in range(GROUP):
                    value = jnp.take_along_axis(table_wide[chunk, head], low, axis=1)
                    if chunk:
                        value = jnp.where(hit, value, found[head][s])
                    found[head][s] = value
        joined = [jnp.concatenate(pair, 0) for pair in found]
        uppers = [(word >> 16).astype(f32) for word in joined]
        lowers = [((word & 65535) - 32768).astype(f32) for word in joined]
        return [(value * (1 / FIXED)).astype(bf16) for value in uppers + lowers]

    def tail_step(step, carry):
        rows = pl.ds(pl.multiple_of(step * 16, 16), 16)
        for head, value in enumerate(look_up(index_tail[rows, :])):
            bias_tail[head, rows, :] = value
        return carry

    lax.fori_loop(0, TAIL // 16, tail_step, 0)

    def untail_step(head, carry):
        for block in range(4):
            count = min(TAIL, PAD - block * TAIL)
            value = bias_tail[head, :count, block * 32 : block * 32 + 32]
            bias[mine + head, block * TAIL : block * TAIL + count, PAD - 32 : PAD] = value
        return carry

    lax.fori_loop(0, HEADS // 2, untail_step, 0)

    def bias_step(step, carry):
        on_the_way(step, schedule)
        rows = pl.ds(pl.multiple_of(step * 16, 16), 16)
        for tile in range(3):
            lanes = slice(tile * 128, (tile + 1) * 128)
            for head, value in enumerate(look_up(index[rows, lanes])):
                bias[mine + head, rows, lanes] = value
        bias_copy(rows, step).start()
        return carry

    lax.fori_loop(0, PAD // 16, bias_step, 0)
    for copy in roll_copies(1):
        copy.start()

    fetches = []
    for n, (whole, weight) in enumerate(((qkv_whole_a, weights_a), (qkv_whole_b, weights_b))):
        arrived(n, CORE_PHASE)
        own[n].wait()
        fetches.append(pltpu.make_async_copy(whole, weight, local.at[5 + n]))
        fetches[-1].start()
    for copy in fetches:
        copy.wait()
    q_bias, v_bias = small_row(small_all, Q_BIAS), small_row(small_all, V_BIAS)
    mixed_bias = jnp.concatenate([q_bias, jnp.zeros_like(q_bias), v_bias], 1).astype(f32)
    gain, shift = small_row(small_all, LN1_GAIN), small_row(small_all, LN1_SHIFT)

    def norm_step(step, carry):
        rows = pl.ds(pl.multiple_of(step * 208, 16), 208)
        normal, _ = norm_rows(arriving[rows, :].astype(f32))
        rolled[rows, :] = (normal * gain.astype(f32) + shift.astype(f32)).astype(bf16)
        return carry

    def mix(window):
        for copy in roll_copies(window):
            copy.wait_recv()
        lax.fori_loop(2 * window, 2 * window + 2, norm_step, 0)
        span = slice(window * PAD, (window + 1) * PAD)
        for n, weight in enumerate((weights_a, weights_b)):
            lanes = slice(n * HALF_QKV, (n + 1) * HALF_QKV)
            got = dot(rolled[span, :], weight[...].reshape(D, HALF_QKV))
            mixed[span, lanes] = (got + mixed_bias[:, lanes]).astype(bf16)

    mix(0)
    keep = [
        pltpu.make_async_copy(rolled, rolled_out, local.at[5]),
        pltpu.make_async_copy(mixed, mixed_out, local.at[6]),
        pltpu.make_async_copy(index, rel_out, local.at[7]),
        pltpu.make_async_copy(small_all, small_out, local.at[8]),
        pltpu.make_async_copy(inverse, inverse_out, local.at[9]),
        pltpu.make_async_copy(contexts, context_out, local.at[12]),
    ]

    def bias_wait(step, carry):
        bias_copy(pl.ds(pl.multiple_of(step * 16, 16), 16), step).wait_recv()
        return carry

    lax.fori_loop(0, PAD // 16, bias_wait, 0)

    head_of = lax.broadcasted_iota(jnp.int32, (1, 128), 1) // HD
    none = jnp.zeros((), bf16)
    ones = jnp.ones((PAD, 128), bf16)

    def attend_copy(step):
        window, pair, slot = step // (HEADS // 2), lax.rem(step, HEADS // 2), lax.rem(step, 2)
        return pltpu.make_async_copy(
            attend.at[slot], attend_out.at[window, pl.ds(2 * pair, 2)], attend_sem.at[slot]
        )

    def back_copies(step):
        window, group = step // (HEADS // 2), lax.rem(step // 2, HEADS // GROUP)
        lanes = pl.ds(pl.multiple_of(group * 128, 128), 128)
        return pieces_to(
            contexts,
            back_out,
            lambda n: back_send.at[window, group, n],
            lambda n: back_recv.at[window, group, n],
            rep,
            shard,
            window,
            lanes,
        )

    def attend_step(step, carry):
        on_the_way(step, later)

        @pl.when(step == HEADS // 2)
        def _():
            mix(1)

        @pl.when(step >= 2)
        def _():
            attend_copy(step - 2).wait()

        window, slot = step // (HEADS // 2), lax.rem(step, 2)
        rows = pl.ds(pl.multiple_of(window * PAD, 16), PAD)
        for n in range(2):
            head = 2 * lax.rem(step, HEADS // 2) + n
            group, member = head // GROUP, lax.rem(head, GROUP)

            def lanes(part):
                return pl.ds(pl.multiple_of(part * D + group * 128, 128), 128)

            own_lanes = head_of == member
            query = jnp.where(own_lanes, mixed[rows, lanes(0)], none)
            value = jnp.where(own_lanes, mixed[rows, lanes(2)], none)
            scores = dot(query, mixed[rows, lanes(1)], NT) * SCALE
            scores = scores + bias[head, :, :PAD].astype(f32) + mask[window]
            expo = jnp.exp(scores - jnp.max(scores, -1, keepdims=True)).astype(bf16)
            attend[slot, n, :, :PAD] = expo
            result = dot(expo, jnp.concatenate([value, ones], 1))
            over = 1.0 / result[:, 128:]
            context = (result[:, :128] * over).astype(bf16)
            contexts[rows, lanes(0)] = jnp.where(own_lanes, context, contexts[rows, lanes(0)])
            inverse[rows, lanes(0)] = jnp.where(own_lanes, over, inverse[rows, lanes(0)])
        attend_copy(step).start()

        @pl.when(lax.rem(step, 2) == 1)
        def _():
            for copy in back_copies(step):
                copy.start()

        return carry

    lax.fori_loop(0, HEADS, attend_step, 0)
    for copy in keep:
        copy.start()
    for matrix in feed_forward:
        advance(matrix, SECOND_PHASE)
    stay = [
        pltpu.make_async_copy(
            contexts.at[pl.ds(w * PAD, LENGTHS[0])],
            back_out.at[pl.ds(w * PAD, LENGTHS[0])],
            local.at[10 + w],
        )
        for w in range(2)
    ]
    for copy in stay:
        copy.start()
    for matrix in feed_forward:
        arrived(matrix, CORE_PHASE)
    attend_copy(HEADS - 2).wait()
    attend_copy(HEADS - 1).wait()

    def back_wait(step, carry):
        for copy in back_copies(step * 2):
            copy.wait()
        return carry

    lax.fori_loop(0, 2 * HEADS // GROUP, back_wait, 0)

    def bias_sent(step, carry):
        bias_copy(pl.ds(pl.multiple_of(step * 16, 16), 16), step).wait_send()
        return carry

    lax.fori_loop(0, PAD // 16, bias_sent, 0)
    for copy in small_copies():
        copy.wait_send()
    for window in range(2):
        for copy in roll_copies(window):
            copy.wait_send()
    for matrix in range(5):
        for phase in range(4):
            for copy in gather(matrix, phase):
                copy.wait_send()
    for copy in own[2:] + keep + stay:
        copy.wait()


def front(tokens, small, table, row_ids, rel_index, w_qkv, w_proj, w_fc1, w_fc2):
    anywhere, inside = pl.BlockSpec(memory_space=pl.ANY), pl.BlockSpec(memory_space=pltpu.VMEM)
    cut = (2, 2, 2)
    weights = [
        w.reshape(cut + (w.shape[0] // PARTS, w.shape[1])) for w in (w_qkv, w_proj, w_fc1, w_fc2)
    ]
    half = (4,) + weights[0].shape[:-1] + (HALF_QKV,)
    wholes = [jax.ShapeDtypeStruct(half, bf16)] * 2
    wholes += [jax.ShapeDtypeStruct((4,) + w.shape, bf16) for w in weights[1:]]
    dma = pltpu.SemaphoreType.DMA
    results = pl.pallas_call(
        front_kernel,
        out_shape=(
            *wholes,
            jax.ShapeDtypeStruct((4, SMALL, 128), bf16),
            jax.ShapeDtypeStruct((2 * PAD, D), bf16),
            jax.ShapeDtypeStruct((2 * PAD, 3 * D), bf16),
            jax.ShapeDtypeStruct((2, HEADS, PAD, LANES), bf16),
            jax.ShapeDtypeStruct((2 * PAD, D), f32),
            jax.ShapeDtypeStruct((2 * PAD, D), bf16),
            jax.ShapeDtypeStruct((2 * PAD, D), bf16),
            jax.ShapeDtypeStruct((PAD, LANES), jnp.int32),
        ),
        in_specs=[inside] * 7 + [anywhere] * 4,
        out_specs=(anywhere,) * 13,
        scratch_shapes=[
            pltpu.VMEM((4, SMALL, 128), bf16),
            pltpu.VMEM((4, GROUP * CHUNKS, 128), f32),
            pltpu.VMEM((CHUNKS, GROUP, 8, 128), jnp.int32),
            pltpu.VMEM((2 * PAD, D), bf16),
            pltpu.VMEM((2 * PAD, D), bf16),
            pltpu.VMEM((2 * PAD, D), bf16),
            pltpu.VMEM(half, bf16),
            pltpu.VMEM(half, bf16),
            pltpu.VMEM((2 * PAD, 3 * D), bf16),
            pltpu.VMEM((PAD, LANES), jnp.int32),
            pltpu.VMEM((TAIL, 128), jnp.int32),
            pltpu.VMEM((HEADS // 2, TAIL, 128), bf16),
            pltpu.VMEM((HEADS, PAD, LANES), bf16),
            pltpu.VMEM((2, PAD, PAD), f32),
            pltpu.VMEM((2, 2, PAD, LANES), bf16),
            pltpu.VMEM((2 * PAD, D), f32),
            pltpu.VMEM((2 * PAD, D), bf16),
            dma((5, 4, 3)),
            dma((5, 4, 3)),
            dma((2, 3)),
            dma((2, 3)),
            dma((PAD // 16,)),
            dma((PAD // 16,)),
            dma((2, 3)),
            dma((2, 3)),
            dma((2, HEADS // GROUP, 3)),
            dma((2, HEADS // GROUP, 3)),
            dma((13,)),
            dma((2,)),
        ],
        compiler_params=pltpu.CompilerParams(
            vmem_limit_bytes=VMEM_LIMIT, collective_id=0, has_side_effects=True
        ),
        name="front",
    )(
        tokens,
        jnp.asarray(send_matrix(), bf16),
        jnp.asarray(spread_matrix(), bf16),
        small,
        table,
        row_ids,
        rel_index,
        *weights,
    )
    whole = [w.reshape(-1, w.shape[-1]) for w in results[:5]]
    return (*whole, *results[5:])


CORE_SUM, FIRST_SUM, SECOND_SUM, Z_SUM, SHARE = range(5)
SUMMED = ((16, 2048, True), (64, 512, False), (16, 512, True))
SUMMED += tuple((16, 3 * 128, group % 2 == 0) for group in range(HEADS // GROUP))
FC1, FC2, PROJ, QKV = range(4)
STRIDE = HEADS + 1
CHUNK_ROWS = ((0, 400, (1, 3)), (400, 384, (0, 2)))
SPAN = 256
SPANS = -(-TABLE // SPAN)
BATCH = 8
HALF = PAD // 2
TILES = LANES // 128
SLAB = 2 * SPANS * GROUP + SMALL


def rear_kernel(
    order_back,
    tokens,
    small_all,
    returned_in,
    order_in,
    cotangent_in,
    proj_in,
    fc1_in,
    fc2_in,
    weights_a_in,
    weights_b_in,
    rolled_in,
    mixed_in,
    inverse_in,
    contexts_in,
    rel_in,
    attend_in,
    output,
    grad_tokens,
    fc1_out,
    fc2_out,
    proj_out,
    qkv_out_0,
    qkv_out_1,
    qkv_out_2,
    qkv_out_3,
    slab_out,
    weights_a,
    weights_b,
    rolled,
    mixed,
    inverse,
    contexts,
    rel,
    outgoing,
    grad_context,
    grad_middle,
    returned,
    pairs_in,
    fc1_grad,
    fc2_grad,
    proj_grad,
    qkv_grads,
    sums,
    fc1_sum,
    table_sum,
    slab,
    slab_z,
    slab_rep,
    *rest,
):
    count = len(SUMMED)
    held = [rest[5 * m : 5 * m + 5] for m in range(count)]
    (
        sum_send,
        sum_recv,
        extra_send,
        extra_recv,
        piece_send,
        piece_recv,
        back_send,
        back_recv,
        attend_sem,
        pairs_send,
        pairs_recv,
        slab_send,
        slab_recv,
        local,
        load,
    ) = rest[5 * count :]
    rep, shard, core, x_bit, y_bit = place()
    reps = lax.axis_size("rep")
    barrier = pltpu.get_barrier_semaphore()

    def hello(k, carry):
        pl.semaphore_signal(
            barrier,
            inc=1,
            device_id={"rep": lax.rem(rep + k, reps), "shard": shard},
            device_id_type=MESH,
        )
        return carry

    lax.fori_loop(1, reps, hello, 0)
    for k in (1, 2, 3):
        pl.semaphore_signal(
            barrier,
            inc=1,
            device_id={"rep": rep, "shard": lax.rem(shard + k, 4)},
            device_id_type=MESH,
        )
    pl.semaphore_wait(barrier, reps + 2)

    sources = (fc1_grad, fc2_grad, proj_grad) + tuple(qkv_grads.at[g] for g in range(4))

    def axis_of(matrix, first):
        x_first = SUMMED[matrix][2]
        use_x = x_first == first
        return (1, x_bit) if use_x else (2, y_bit)

    def sum_copies(matrix, phase):
        from_core, from_first, summed, from_z, shared = held[matrix]
        source = sources[matrix]
        x_first = SUMMED[matrix][2]
        first_bit, first = axis_of(matrix, True)
        second_bit, second = axis_of(matrix, False)

        def one(src, dst, bit, n=0):
            return remote(
                src,
                dst,
                sum_send.at[matrix, phase, n],
                sum_recv.at[matrix, phase, n],
                flip(rep, bit),
                shard,
            )

        if phase == CORE_SUM:
            return [one(source.at[:, :, :, 1 - core], from_core, 0)]
        if phase == FIRST_SUM:
            cut = source.at[:, :, 1 - x_bit, core] if x_first else source.at[:, 1 - y_bit, :, core]
            return [one(cut, from_first, first_bit)]
        if phase == SECOND_SUM:
            return [one(from_first.at[:, 1 - second], summed, second_bit)]
        if phase == Z_SUM:
            copies = []
            for k in (1, 2, 3):
                to = lax.rem(shard + k, 4)
                copies.append(
                    remote(
                        summed.at[to],
                        from_z.at[3 - k],
                        sum_send.at[matrix, phase, k - 1],
                        sum_recv.at[matrix, phase, 3 - k],
                        rep,
                        to,
                    )
                )
            return copies
        block = shared.at[y_bit, x_bit, core]
        copies = []
        for n in range(1, PARTS):
            partner = rep
            for bit in range(3):
                if n >> bit & 1:
                    partner = flip(partner, bit)
            copies.append(
                remote(
                    block,
                    block,
                    sum_send.at[matrix, phase, n - 1],
                    sum_recv.at[matrix, phase, n - 1],
                    partner,
                    shard,
                )
            )
        return copies

    def extra_copy(matrix, bit):
        shared, from_z = held[matrix][4], held[matrix][3]
        return remote(
            shared.at[y_bit, x_bit, core],
            from_z.at[bit],
            extra_send.at[matrix, bit - 3],
            extra_recv.at[matrix, bit - 3],
            flip(rep, bit),
            shard,
        )

    def add(into, at, other, other_at):
        into[at] = (into[at].astype(f32) + other[other_at].astype(f32)).astype(bf16)

    def begin(matrix):
        for copy in sum_copies(matrix, CORE_SUM):
            copy.start()

    def advance(matrix, phase):
        from_core, from_first, summed, from_z, shared = held[matrix]
        source = sources[matrix]
        x_first = SUMMED[matrix][2]
        _, second = axis_of(matrix, False)
        for copy in sum_copies(matrix, phase):
            copy.wait_recv()
        if phase == CORE_SUM:

            def step(n, carry):
                at = (n // 4, lax.rem(n // 2, 2), lax.rem(n, 2))
                add(source, at + (core,), from_core, at)
                return carry

            lax.fori_loop(0, 16, step, 0)
        elif phase == FIRST_SUM:

            def step(n, carry):
                owner, other = n // 2, lax.rem(n, 2)
                at = (owner, other, x_bit) if x_first else (owner, y_bit, other)
                add(from_first, (owner, other), source, at + (core,))
                return carry

            lax.fori_loop(0, 8, step, 0)
        elif phase == SECOND_SUM:

            def step(owner, carry):
                add(summed, (owner,), from_first, (owner, second))
                return carry

            lax.fori_loop(0, 4, step, 0)
        elif phase == Z_SUM:
            total = summed[shard].astype(f32)
            for n in range(3):
                total = total + from_z[n].astype(f32)
            shared[y_bit, x_bit, core] = total.astype(bf16)
            bit = 3
            while (1 << bit) < reps:
                copy = extra_copy(matrix, bit)
                copy.start()
                copy.wait()
                at = (y_bit, x_bit, core)
                add(shared, at, from_z, (bit,))
                bit += 1
        if phase < SHARE:
            for copy in sum_copies(matrix, phase + 1):
                copy.start()

    def on_the_way(step, table_of_steps):
        for when, actions in table_of_steps.items():

            @pl.when(step == when)
            def _():
                for matrix, phase in actions:
                    advance(matrix, phase)

    fetched = (
        (weights_a_in, weights_a),
        (weights_b_in, weights_b),
        (rolled_in, rolled),
        (mixed_in, mixed),
        (inverse_in, inverse),
        (contexts_in, contexts),
        (rel_in, rel),
    )
    fetches = [
        pltpu.make_async_copy(src, dst, load.at[n]) for n, (src, dst) in enumerate(fetched)
    ]

    def roll_copies(window, which=(1, 2, 3)):
        return pieces_to(
            outgoing,
            grad_context,
            lambda n: piece_send.at[window, n],
            lambda n: piece_recv.at[window, n],
            rep,
            shard,
            window,
            which=which,
        )

    def feed_forward(
        proj, fc1, fc2, middle, normed, normed_back, active, grad_hidden, total, grad_normed, branch,
        unrolled, grad_unrolled, final, fc1_bias, returned_context, order, cotangent,
    ):
        loads = [
            pltpu.make_async_copy(src, dst, load.at[len(fetched) + n])
            for n, (src, dst) in enumerate(
                (
                    (returned_in, returned_context),
                    (proj_in, proj),
                    (cotangent_in, cotangent),
                    (fc1_in, fc1),
                    (fc2_in, fc2),
                    (order_in, order),
                )
            )
        ]
        for copy in loads + fetches:
            copy.start()
        proj_bias = small_row(small_all, PROJ_BIAS).astype(f32)
        gain, shift = (small_row(small_all, row).astype(f32) for row in (LN2_GAIN, LN2_SHIFT))
        fc2_bias = small_row(small_all, FC2_BIAS).astype(f32)
        for owner in range(4):
            for k in range(4):
                lanes = slice(owner * D + k * 128, owner * D + (k + 1) * 128)
                fc1_bias[:, lanes] = small_all[owner, FC1_BIAS + k : FC1_BIAS + k + 1, :].astype(f32)
        sums[...] = jnp.zeros_like(sums)
        fc1_sum[...] = jnp.zeros_like(fc1_sum)
        for copy in loads[:2]:
            copy.wait()
        for first, length, pieces in CHUNK_ROWS:
            rows = pl.ds(first, length)
            unrolled[rows, :] = dot(order_back[rows, :], returned_context[...]).astype(bf16)
            got = dot(unrolled[rows, :], proj[...]) + proj_bias
            middle[rows, :] = tokens[rows, :].astype(f32) + got
            normal, _ = norm_rows(middle[rows, :])
            normed[rows, :] = (normal * gain + shift).astype(bf16)
            if first == 0:
                for copy in loads[2:]:
                    copy.wait()

            def tile_step(tile, carry):
                for n in range(2):
                    at = (2 * tile + n) * FF_TILE
                    lanes = pl.ds(pl.multiple_of(at, FF_TILE), FF_TILE)
                    hidden = dot(normed[rows, :], fc1[:, lanes]) + fc1_bias[:, lanes]
                    grad_active = dot(cotangent[rows, :], fc2[lanes, :], NT)
                    share = 0.5 + 0.5 * lax.erf(hidden * 0.7071067811865476)
                    active[rows, lanes] = (hidden * share).astype(bf16)
                    slope = share + hidden * jnp.exp(-0.5 * hidden * hidden) * 0.3989422804014327
                    grad = (grad_active * slope).astype(bf16)
                    grad_hidden[rows, lanes] = grad
                    fc1_sum[:, lanes] += jnp.sum(grad.astype(f32), 0, keepdims=True)
                return carry

            lax.fori_loop(0, FF // FF_TILE // 2, tile_step, 0)
            total[rows, :] = dot(active[rows, :], fc2[...])
            grad_normed[rows, :] = dot(grad_hidden[rows, :], fc1[...], NT)
            result = middle[rows, :] + total[rows, :] + fc2_bias
            final[rows, :] = result.astype(bf16)
            normal, over = norm_rows(middle[rows, :])
            grad_out = grad_normed[rows, :]
            scaled = grad_out * gain
            inner = (
                scaled
                - jnp.mean(scaled, -1, keepdims=True)
                - normal * jnp.mean(scaled * normal, -1, keepdims=True)
            )
            upper = cotangent[rows, :].astype(f32)
            grad_middle[rows, :] = upper + over * inner
            branch[rows, :] = grad_middle[rows, :].astype(bf16)
            for row, value in (
                (PROJ_BIAS, branch[rows, :].astype(f32)),
                (LN2_GAIN, grad_out * normal),
                (LN2_SHIFT, grad_out),
                (FC2_BIAS, upper),
            ):
                sums[row : row + 1, :] += jnp.sum(value, 0, keepdims=True)
            grad_unrolled[rows, :] = dot(branch[rows, :], proj[...], NT).astype(bf16)
            source = pl.ds(0, 400) if first == 0 else pl.ds(384, 400)
            for window in range(2):
                for piece in pieces:
                    at = pl.ds(window * PAD + FIRST_ROWS[piece], LENGTHS[piece])
                    got = dot(order[at, source], grad_unrolled[source, :]).astype(bf16)
                    if piece:
                        outgoing[at, :] = got
                    else:
                        grad_context[at, :] = got
            for window in range(2):
                for copy in roll_copies(window, [piece for piece in pieces if piece]):
                    copy.start()
        written = pltpu.make_async_copy(final, output, load.at[len(fetched) + 6])
        written.start()

        same = lax.broadcasted_iota(jnp.int32, (D, D), 0) == lax.broadcasted_iota(
            jnp.int32, (D, D), 1
        )
        unit = jnp.where(same, jnp.ones((), bf16), jnp.zeros((), bf16))
        normed_back[...] = dot(unit, normed[...], NT).astype(bf16)

        def fc1_step(tile, carry):
            lanes = pl.ds(pl.multiple_of(tile * 512, 512), 512)
            got = dot(normed_back[...], grad_hidden[:, lanes]).astype(bf16)
            fc1_grad[:, :, :, :, :, lanes] = got.reshape(4, 2, 2, 2, 16, 512)
            return carry

        lax.fori_loop(0, FF // 512, fc1_step, 0)
        begin(FC1)

        def fc2_step(tile, carry):
            lanes = pl.ds(pl.multiple_of(tile * 256, 256), 256)
            got = dot(active[:, lanes], cotangent[...], TN).astype(bf16)
            fc2_grad[tile // 2, lax.rem(tile, 2)] = got.reshape(2, 2, 64, D)
            return carry

        lax.fori_loop(0, FF // 256, fc2_step, 0)
        begin(FC2)
        got = dot(unrolled[...], branch[...], TN).astype(bf16)
        proj_grad[...] = got.reshape(proj_grad.shape)
        begin(PROJ)
        written.wait()

    count_rows = tokens.shape[0]
    pl.run_scoped(
        feed_forward,
        pltpu.VMEM((D, D), bf16),
        pltpu.VMEM((D, FF), bf16),
        pltpu.VMEM((FF, D), bf16),
        pltpu.VMEM((count_rows, D), f32),
        pltpu.VMEM((count_rows, D), bf16),
        pltpu.VMEM((D, count_rows), bf16),
        pltpu.VMEM((count_rows, FF), bf16),
        pltpu.VMEM((count_rows, FF), bf16),
        pltpu.VMEM((count_rows, D), f32),
        pltpu.VMEM((count_rows, D), f32),
        pltpu.VMEM((count_rows, D), bf16),
        pltpu.VMEM((count_rows, D), bf16),
        pltpu.VMEM((count_rows, D), bf16),
        pltpu.VMEM((count_rows, D), bf16),
        pltpu.VMEM((1, FF), f32),
        pltpu.VMEM((2 * PAD, D), bf16),
        pltpu.VMEM((2 * PAD, count_rows), bf16),
        pltpu.VMEM((count_rows, D), bf16),
    )
    for copy in fetches:
        copy.wait()
    def return_copies(window):
        return pieces_to(
            outgoing,
            returned,
            lambda n: back_send.at[window, n],
            lambda n: back_recv.at[window, n],
            rep,
            shard,
            window,
        )

    def attend_back(attend, grads, rolled_back, pairs, pairs_out):
        head_of = lax.broadcasted_iota(jnp.int32, (1, 128), 1) // HD
        none = jnp.zeros((), bf16)

        def attend_copy(head):
            slot = lax.rem(head, 2)
            return pltpu.make_async_copy(
                attend_in.at[:, head], attend.at[slot], attend_sem.at[slot]
            )

        attend_copy(0).start()
        same = lax.broadcasted_iota(jnp.int32, (D, D), 0) == lax.broadcasted_iota(
            jnp.int32, (D, D), 1
        )
        unit = jnp.where(same, jnp.ones((), bf16), none)
        rolled_back[...] = dot(unit, rolled[...], NT).astype(bf16)

        def qkv_group(group):
            columns = [
                grads[:, part * D + group * 128 : part * D + (group + 1) * 128] for part in range(3)
            ]
            got = dot(rolled_back[...], jnp.concatenate(columns, 1)).astype(bf16)
            qkv_grads[group] = got.reshape(qkv_grads.shape[1:])
            begin(QKV + group)

        first_schedule = {
            9: [(FC1, FIRST_SUM), (FC2, FIRST_SUM), (PROJ, FIRST_SUM)],
            6: [(QKV, CORE_SUM)],
            8: [(QKV, FIRST_SUM)],
            11: [(QKV + 1, CORE_SUM), (QKV, SECOND_SUM)],
            13: [(QKV + 1, FIRST_SUM)],
            14: [(QKV + 2, CORE_SUM), (QKV, Z_SUM)],
            15: [
                (QKV + 1, SECOND_SUM),
                (QKV + 2, FIRST_SUM),
                (FC1, SECOND_SUM),
                (FC2, SECOND_SUM),
                (PROJ, SECOND_SUM),
            ],
        }
        second_schedule = {
            1: [(QKV + 3, CORE_SUM), (QKV + 1, Z_SUM), (QKV + 2, SECOND_SUM)],
            4: [(QKV + 3, FIRST_SUM), (QKV + 2, Z_SUM)],
            8: [(QKV + 3, SECOND_SUM)],
            13: [(QKV + 3, Z_SUM), (FC1, Z_SUM), (FC2, Z_SUM), (PROJ, Z_SUM)],
        }

        for matrix in (FC1, FC2, PROJ):
            advance(matrix, CORE_SUM)
        for window in range(2):
            for copy in roll_copies(window):
                copy.wait_recv()

        def head_step(head, carry):
            on_the_way(head, first_schedule)
            for done in range(1, HEADS // GROUP):

                @pl.when(head == done * GROUP)
                def _():
                    qkv_group(done - 1)

            @pl.when(head + 1 < HEADS)
            def _():
                attend_copy(head + 1).start()

            attend_copy(head).wait()
            slot = lax.rem(head, 2)
            group, member = head // GROUP, lax.rem(head, GROUP)

            def lanes(part):
                return pl.ds(pl.multiple_of(part * D + group * 128, 128), 128)

            mine = head_of == member
            both = []
            for window in range(2):
                rows = pl.ds(window * PAD, PAD)
                query = jnp.where(mine, mixed[rows, lanes(0)], none)
                key = jnp.where(mine, mixed[rows, lanes(1)], none)
                grad = grad_context[rows, lanes(0)].astype(f32) * inverse[rows, lanes(0)]
                grad = jnp.where(mine, grad, 0.0).astype(bf16)
                expo = attend[slot, window, :, :PAD]
                grad_attend = dot(grad, mixed[rows, lanes(2)], NT)
                inner = jnp.sum(
                    grad.astype(f32) * contexts[rows, lanes(0)].astype(f32), -1, keepdims=True
                )
                grad_scores = (expo.astype(f32) * (grad_attend - inner)).astype(bf16)
                both.append(grad_scores)
                for part, value in (
                    (0, dot(grad_scores, key) * SCALE),
                    (1, dot(grad_scores, query, TN) * SCALE),
                    (2, dot(expo, grad, TN)),
                ):
                    grads[rows, lanes(part)] = jnp.where(
                        mine, value.astype(bf16), grads[rows, lanes(part)]
                    )
            total = both[0].astype(f32) + both[1].astype(f32)
            for tile in range(TILES):
                part = total[:, tile * 128 : (tile + 1) * 128]
                if part.shape[1] < 128:
                    part = jnp.concatenate([part, jnp.zeros((PAD, 128 - part.shape[1]), f32)], 1)
                pairs[tile, pl.ds(head, PAD, stride=STRIDE), :] = part
            return carry

        lax.fori_loop(0, HEADS, head_step, 0)

        for window in range(2):
            for copy in roll_copies(window):
                copy.wait_send()

        for window in range(2):
            span = slice(window * PAD, (window + 1) * PAD)
            got = dot(grads[span, :HALF_QKV], weights_a[...], NT)
            got = got + dot(grads[span, HALF_QKV:], weights_b[...], NT)
            outgoing[span, :] = got.astype(bf16)
            for copy in return_copies(window):
                copy.start()
            rows = slice(window * PAD, window * PAD + LENGTHS[0])
            returned[rows, :] = outgoing[rows, :]
        qkv_group(HEADS // GROUP - 1)

        def round_step(step, carry):
            source = pl.ds(((1 - core) * HALF + step) * STRIDE, HEADS)
            at = pl.ds(pl.multiple_of(step * HEADS, HEADS), HEADS)
            for tile in range(TILES):
                pairs_out[tile, at, :] = pairs[tile, source, :].astype(bf16)
            return carry

        def pairs_copy(half):
            block = pl.ds(half * (HALF * HEADS // 2), HALF * HEADS // 2)
            return remote(
                pairs_out.at[:, block],
                pairs_in.at[:, block],
                pairs_send.at[half],
                pairs_recv.at[half],
                flip(rep, 0),
                shard,
            )

        for half in range(2):
            lax.fori_loop(half * (HALF // 2), (half + 1) * (HALF // 2), round_step, 0)
            pairs_copy(half).start()

        low_of = lax.broadcasted_iota(jnp.int32, (SPAN, LANES), 0).astype(f32).astype(bf16)
        table_sum[...] = jnp.zeros_like(table_sum)
        for half in range(2):
            pairs_copy(half).wait_recv()

        def table_step(step, carry):
            on_the_way(step, second_schedule)
            left, right = [], []
            for k in range(BATCH):
                row = step * BATCH + k
                there = core * HALF + row
                at = pl.ds(there * STRIDE, HEADS)
                near = pl.ds(pl.multiple_of(row * HEADS, HEADS), HEADS)
                index = rel[pl.ds(there, 1), :]
                low = (index & (SPAN - 1)).astype(f32).astype(bf16)
                high = jnp.broadcast_to((index // SPAN).astype(f32).astype(bf16), (HEADS, LANES))
                total = jnp.concatenate(
                    [pairs[t, at, :] + pairs_in[t, near, :].astype(f32) for t in range(TILES)], 1
                ).astype(bf16)
                nothing = jnp.zeros_like(total)
                left.append(
                    jnp.concatenate(
                        [jnp.where(high == jnp.asarray(s, bf16), total, nothing) for s in range(SPANS)],
                        0,
                    )
                )
                hit = low_of == jnp.broadcast_to(low, (SPAN, LANES))
                right.append(jnp.where(hit, jnp.ones((), bf16), jnp.zeros((), bf16)))
            table_sum[...] += dot(jnp.concatenate(left, 1), jnp.concatenate(right, 1), NT)
            return carry

        lax.fori_loop(0, HALF // BATCH, table_step, 0)
        for half in range(2):
            pairs_copy(half).wait_send()
        sums[Q_BIAS : Q_BIAS + 1, :] = jnp.sum(grads[:, :D].astype(f32), 0, keepdims=True)
        sums[V_BIAS : V_BIAS + 1, :] = jnp.sum(grads[:, 2 * D :].astype(f32), 0, keepdims=True)

    pl.run_scoped(
        attend_back,
        pltpu.VMEM((2, 2, PAD, LANES), bf16),
        pltpu.VMEM((2 * PAD, 3 * D), bf16),
        pltpu.VMEM((D, 2 * PAD), bf16),
        pltpu.VMEM((TILES, PAD * STRIDE, 128), f32),
        pltpu.VMEM((TILES, HALF * HEADS, 128), bf16),
    )

    for window in range(2):
        for copy in return_copies(window):
            copy.wait_recv()
    gain = small_row(small_all, LN1_GAIN).astype(f32)

    def norm_step(step, carry):
        gain_sum, shift_sum = carry
        rows = pl.ds(pl.multiple_of(step * 112, 16), 112)
        grad_out = dot(order_back[rows, :], returned[...])
        normal, over = norm_rows(tokens[rows, :].astype(f32))
        scaled = grad_out * gain
        inner = (
            scaled
            - jnp.mean(scaled, -1, keepdims=True)
            - normal * jnp.mean(scaled * normal, -1, keepdims=True)
        )
        grad_middle[rows, :] += over * inner
        return (
            gain_sum + jnp.sum(grad_out * normal, 0, keepdims=True),
            shift_sum + jnp.sum(grad_out, 0, keepdims=True),
        )

    nought = jnp.zeros((1, D), f32)
    gain_sum, shift_sum = lax.fori_loop(0, 7, norm_step, (nought, nought))

    sums[LN1_GAIN : LN1_GAIN + 1, :] = gain_sum
    sums[LN1_SHIFT : LN1_SHIFT + 1, :] = shift_sum
    tokens_copy = pltpu.make_async_copy(grad_middle, grad_tokens, load.at[0])
    tokens_copy.start()

    for owner in range(4):
        lanes = slice(owner * 128, (owner + 1) * 128)
        entries = jnp.concatenate(
            [table_sum[pl.ds(s * HEADS + GROUP * owner, GROUP), :] for s in range(SPANS)], 0
        )
        slab[owner, : SPANS * GROUP, :] = entries[:, :128]
        slab[owner, SPANS * GROUP : 2 * SPANS * GROUP, :] = entries[:, 128:]
        slab[owner, 2 * SPANS * GROUP :, :] = jnp.concatenate(
            [sums[:, lanes]]
            + [fc1_sum[:, owner * D + k * 128 : owner * D + (k + 1) * 128] for k in range(4)]
            + [jnp.zeros((4, 128), f32)],
            0,
        )

    def slab_copies():
        return [
            remote(
                slab.at[lax.rem(shard + k, 4)],
                slab_z.at[3 - k],
                slab_send.at[k - 1],
                slab_recv.at[3 - k],
                rep,
                lax.rem(shard + k, 4),
            )
            for k in (1, 2, 3)
        ]

    for copy in slab_copies():
        copy.start()

    for matrix in range(count):
        advance(matrix, SHARE)
    for copy in slab_copies():
        copy.wait_recv()
    slab_rep[rep] = slab[shard] + (slab_z[0] + slab_z[1] + slab_z[2])

    def slab_share(k):
        return remote(
            slab_rep.at[rep],
            slab_rep.at[rep],
            slab_send.at[2 + k],
            slab_recv.at[2 + reps - k],
            lax.rem(rep + k, reps),
            shard,
        )

    def share_start(k, carry):
        slab_share(k).start()
        return carry

    lax.fori_loop(1, reps, share_start, 0)
    outs = (fc1_out, fc2_out, proj_out, qkv_out_0, qkv_out_1, qkv_out_2, qkv_out_3)
    results = [
        pltpu.make_async_copy(held[matrix][4], outs[matrix], local.at[count + matrix])
        for matrix in range(count)
    ]
    for copy in results:
        copy.start()

    def share_wait(k, carry):
        slab_share(k).wait()
        return carry

    lax.fori_loop(1, reps, share_wait, 0)

    def slab_step(k, total):
        return total + slab_rep[k]

    slab_out[...] = lax.fori_loop(1, reps, slab_step, slab_rep[0])

    for copy in slab_copies():
        copy.wait_send()
    for window in range(2):
        for copy in return_copies(window):
            copy.wait_send()
    for matrix in range(count):
        for phase in range(SHARE + 1):
            for copy in sum_copies(matrix, phase):
                copy.wait_send()
    for copy in results + [tokens_copy]:
        copy.wait()


def rear(
    returned_context,
    tokens,
    cotangent,
    small_all,
    whole_proj,
    whole_fc1,
    whole_fc2,
    weights_a,
    weights_b,
    rolled,
    mixed,
    inverse,
    contexts,
    rel,
    attend,
):
    anywhere, inside = pl.BlockSpec(memory_space=pl.ANY), pl.BlockSpec(memory_space=pltpu.VMEM)
    reps = lax.axis_size("rep")
    dma = pltpu.SemaphoreType.DMA
    order = send_matrix()
    extra = max(1, reps.bit_length() - 4)
    held = []
    for rows, columns, _ in SUMMED:
        held += [
            pltpu.VMEM((4, 2, 2, rows, columns), bf16),
            pltpu.VMEM((4, 2, rows, columns), bf16),
            pltpu.VMEM((4, rows, columns), bf16),
            pltpu.VMEM((3 + extra, rows, columns), bf16),
            pltpu.VMEM((2, 2, 2, rows, columns), bf16),
        ]
    return pl.pallas_call(
        rear_kernel,
        out_shape=(
            jax.ShapeDtypeStruct(tokens.shape, bf16),
            jax.ShapeDtypeStruct(tokens.shape, f32),
            *[jax.ShapeDtypeStruct((2, 2, 2) + shape[:2], bf16) for shape in SUMMED],
            jax.ShapeDtypeStruct((SLAB, 128), f32),
        ),
        in_specs=[inside] * 3 + [anywhere] * 14,
        out_specs=(*[anywhere] * (2 + len(SUMMED)), inside),
        scratch_shapes=[
            pltpu.VMEM(weights_a.shape, bf16),
            pltpu.VMEM(weights_b.shape, bf16),
            pltpu.VMEM(rolled.shape, bf16),
            pltpu.VMEM(mixed.shape, bf16),
            pltpu.VMEM(inverse.shape, f32),
            pltpu.VMEM(contexts.shape, bf16),
            pltpu.VMEM(rel.shape, jnp.int32),
            pltpu.VMEM((2 * PAD, D), bf16),
            pltpu.VMEM((2 * PAD, D), bf16),
            pltpu.VMEM(tokens.shape, f32),
            pltpu.VMEM((2 * PAD, D), bf16),
            pltpu.VMEM((TILES, HALF * HEADS, 128), bf16),
            pltpu.VMEM((4, 2, 2, 2, 16, 2048), bf16),
            pltpu.VMEM((4, 2, 2, 2, 64, 512), bf16),
            pltpu.VMEM((4, 2, 2, 2, 16, 512), bf16),
            pltpu.VMEM((HEADS // GROUP, 4, 2, 2, 2, 16, 3 * 128), bf16),
            pltpu.VMEM((8, D), f32),
            pltpu.VMEM((1, FF), f32),
            pltpu.VMEM((SPANS * HEADS, SPAN), f32),
            pltpu.VMEM((4, SLAB, 128), f32),
            pltpu.VMEM((3, SLAB, 128), f32),
            pltpu.VMEM((reps, SLAB, 128), f32),
            *held,
            dma((len(SUMMED), SHARE + 1, PARTS - 1)),
            dma((len(SUMMED), SHARE + 1, PARTS - 1)),
            dma((len(SUMMED), extra)),
            dma((len(SUMMED), extra)),
            dma((2, 3)),
            dma((2, 3)),
            dma((2, 3)),
            dma((2, 3)),
            dma((2,)),
            dma((2,)),
            dma((2,)),
            dma((3 + reps,)),
            dma((3 + reps,)),
            dma((2 * len(SUMMED),)),
            dma((14,)),
        ],
        compiler_params=pltpu.CompilerParams(
            vmem_limit_bytes=VMEM_LIMIT, collective_id=1, has_side_effects=True
        ),
        name="rear",
    )(
        jnp.asarray(order.T, bf16),
        tokens,
        small_all,
        returned_context,
        jnp.asarray(order, bf16),
        cotangent,
        whole_proj,
        whole_fc1,
        whole_fc2,
        weights_a,
        weights_b,
        rolled,
        mixed,
        inverse,
        contexts,
        rel,
        attend,
    )


def shards(
    tokens,
    region,
    rel_index,
    ln1_gain,
    ln1_shift,
    w_qkv,
    q_bias,
    v_bias,
    table,
    w_proj,
    proj_bias,
    ln2_gain,
    ln2_shift,
    w_fc1,
    fc1_bias,
    w_fc2,
    fc2_bias,
    cotangent,
):
    small = jnp.concatenate(
        (ln1_gain, ln1_shift, q_bias, v_bias, proj_bias, ln2_gain, ln2_shift, fc2_bias, fc1_bias)
    ).reshape(-1, 128)
    small = jnp.pad(small, ((0, SMALL - small.shape[0]), (0, 0)))
    chunks = jnp.pad(table.astype(f32).T, ((0, 0), (0, CHUNKS * 128 - TABLE)))
    labels = region.reshape(WT, WH, 2, WW).transpose(2, 0, 1, 3).reshape(2, WIN)
    labels = pieces_of(labels, 1, -1)
    row_ids = jnp.pad(labels, ((0, 0), (0, LANES - PAD)), constant_values=-1)[:, None]
    (
        whole_qkv_a,
        whole_qkv_b,
        whole_proj,
        whole_fc1,
        whole_fc2,
        small,
        rolled,
        qkv,
        attend,
        inverse,
        contexts,
        returned,
        rel,
    ) = front(
        tokens.reshape(-1, D),
        small,
        chunks.reshape(-1, 128),
        row_ids,
        rel_index,
        w_qkv,
        w_proj,
        w_fc1,
        w_fc2,
    )
    output, grad_tokens, grad_w_fc1, grad_w_fc2, grad_w_proj, *grads_qkv, slab = rear(
        returned,
        tokens.reshape(-1, D),
        cotangent.reshape(-1, D),
        small,
        whole_proj,
        whole_fc1,
        whole_fc2,
        whole_qkv_a,
        whole_qkv_b,
        rolled,
        qkv,
        inverse,
        contexts,
        rel,
        attend,
    )
    output = output.reshape(tokens.shape)
    grad_tokens = grad_tokens.reshape(tokens.shape)
    grad_w_fc1 = grad_w_fc1.astype(f32).reshape(w_fc1.shape)
    grad_w_fc2 = grad_w_fc2.astype(f32).reshape(w_fc2.shape)
    grad_w_proj = grad_w_proj.astype(f32).reshape(w_proj.shape)
    parts = [g.reshape(-1, 3, 128) for g in grads_qkv]
    grad_w_qkv = jnp.stack(parts, 2).astype(f32)
    grad_w_qkv = grad_w_qkv.reshape(w_qkv.shape)
    spans = slab[: 2 * SPANS * GROUP].reshape(2, SPANS, GROUP, 128).transpose(1, 0, 3, 2)
    grad_table = spans.reshape(SPANS * SPAN, GROUP)[:TABLE]
    vectors = slab[2 * SPANS * GROUP :]
    grad_ln1_gain, grad_ln1_shift = vectors[LN1_GAIN], vectors[LN1_SHIFT]
    grad_q_bias, grad_v_bias = vectors[Q_BIAS], vectors[V_BIAS]
    grad_proj_bias, grad_fc2_bias = vectors[PROJ_BIAS], vectors[FC2_BIAS]
    grad_ln2_gain, grad_ln2_shift = vectors[LN2_GAIN], vectors[LN2_SHIFT]
    grad_fc1_bias = vectors[FC1_BIAS : FC1_BIAS + 4].reshape(-1)
    return (
        output,
        grad_tokens,
        grad_ln1_gain,
        grad_ln1_shift,
        grad_w_qkv,
        grad_q_bias,
        grad_v_bias,
        grad_table,
        grad_w_proj,
        grad_proj_bias,
        grad_ln2_gain,
        grad_ln2_shift,
        grad_w_fc1,
        grad_fc1_bias,
        grad_w_fc2,
        grad_fc2_bias,
    )


def solution(mesh):
    return jax.shard_map(
        shards,
        mesh=mesh,
        in_specs=(
            P("rep", "shard", None, None),
            P("shard", None),
            P(),
            P("shard"),
            P("shard"),
            P("shard", None),
            P("shard"),
            P("shard"),
            P(None, "shard"),
            P("shard", None),
            P("shard"),
            P("shard"),
            P("shard"),
            P("shard", None),
            P("shard"),
            P("shard", None),
            P("shard"),
            P("rep", "shard", None, None),
        ),
        out_specs=(
            P("rep", "shard", None, None),
            P("rep", "shard", None, None),
            P("shard"),
            P("shard"),
            P("shard", None),
            P("shard"),
            P("shard"),
            P(None, "shard"),
            P("shard", None),
            P("shard"),
            P("shard"),
            P("shard"),
            P("shard", None),
            P("shard"),
            P("shard", None),
            P("shard"),
        ),
        check_vma=False,
    )
```

```python
import functools

import jax
import jax.numpy as jnp
import numpy as np
from jax import lax
from jax.experimental import pallas as pl
from jax.experimental.pallas import tpu as pltpu
from jax.sharding import PartitionSpec as P

D = 512
HEADS = 16
HD = 32
WT = 8
WH = 7
WW = 7
WIN = 392
TABLE = 2535
FF = 2048
FF_TILE = 256
PAD = 416
LANES = 512
GROUP = 4
CHUNKS = 20
SCALE = HD ** (-0.5)
NN = (((1,), (0,)), ((), ()))
NT = (((1,), (1,)), ((), ()))
TN = (((0,), (0,)), ((), ()))
VMEM_LIMIT = 60 * 2**20
f32 = jnp.float32
bf16 = jnp.bfloat16

PIECES = (
    ((0, 4), (0, 4), 112, 0),
    ((4, 8), (0, 4), 112, 112),
    ((0, 4), (4, 7), 96, 224),
    ((4, 8), (4, 7), 96, 320),
)


def send_matrix():
    matrix = np.zeros((2 * PAD, WT * WH * 2 * WW), np.float32)
    for window in range(2):
        for (t0, t1), (h0, h1), _, first in PIECES:
            row = window * PAD + first
            for t in range(t0, t1):
                for h in range(h0, h1):
                    for w in range(WW):
                        column = (window * WW + w + WW // 2) % (2 * WW)
                        source = ((t + 4) % WT * WH + (h + 3) % WH) * 2 * WW + column
                        matrix[row, source] = 1.0
                        row += 1
    return matrix


def spread_matrix():
    source = np.arange(WIN).reshape(WT, WH, WW)
    matrix = np.zeros((PAD, WIN), np.float32)
    for (t0, t1), (h0, h1), _, first in PIECES:
        tokens = source[t0:t1, h0:h1].reshape(-1)
        matrix[first + np.arange(tokens.size), tokens] = 1.0
    return matrix


def pieces_of(array, axis, fill):
    shape = array.shape
    split = array.reshape(shape[:axis] + (WT, WH, WW) + shape[axis + 1 :])
    parts = []
    for (t0, t1), (h0, h1), padded, _ in PIECES:
        part = lax.slice_in_dim(lax.slice_in_dim(split, t0, t1, axis=axis), h0, h1, axis=axis + 1)
        length = (t1 - t0) * (h1 - h0) * WW
        part = part.reshape(shape[:axis] + (length,) + shape[axis + 1 :])
        widths = [(0, 0, 0)] * len(shape)
        widths[axis] = (0, padded - length, 0)
        parts.append(lax.pad(part, jnp.asarray(fill, array.dtype), widths))
    return jnp.concatenate(parts, axis)


def dot(a, b, dims=NN):
    return lax.dot_general(a, b, dims, preferred_element_type=f32)


MESH = pl.DeviceIdType.MESH
PARTS = 8
FIRST_ROWS = tuple(first for _, _, _, first in PIECES)
LENGTHS = tuple(padded for _, _, padded, _ in PIECES)
ACROSS = (0, 2, 1, 3)
LN1_GAIN, LN1_SHIFT, Q_BIAS, V_BIAS, PROJ_BIAS, LN2_GAIN, LN2_SHIFT, FC2_BIAS, FC1_BIAS = range(9)
SMALL = 16


def place():
    rep, shard = lax.axis_index("rep"), lax.axis_index("shard")
    return rep, shard, lax.rem(rep, 2), lax.rem(rep // 2, 2), lax.rem(rep // 4, 2)


def flip(rep, bit):
    low = lax.rem(rep // (1 << bit), 2)
    return rep + (1 - 2 * low) * (1 << bit)


def remote(src, dst, send, recv, rep, shard):
    return pltpu.make_async_remote_copy(
        src_ref=src,
        dst_ref=dst,
        send_sem=send,
        recv_sem=recv,
        device_id={"rep": rep, "shard": shard},
        device_id_type=MESH,
    )


def greet(peers):
    barrier = pltpu.get_barrier_semaphore()
    for rep, shard in peers:
        pl.semaphore_signal(
            barrier, inc=1, device_id={"rep": rep, "shard": shard}, device_id_type=MESH
        )
    pl.semaphore_wait(barrier, len(peers))


def peers_of(rep, shard):
    return [(rep, lax.rem(shard + k, 4)) for k in (1, 2, 3)] + [
        (flip(rep, bit), shard) for bit in (0, 1, 2)
    ]


def quarter_across(shard, bits):
    low, high = lax.rem(shard, 2), shard // 2
    if bits & 1:
        low = 1 - low
    if bits & 2:
        high = 1 - high
    return high * 2 + low


def pieces_to(source, target, send, recv, rep, shard, window, columns=None, which=(1, 2, 3)):
    copies = []
    for piece in which:
        rows = pl.ds(
            pl.multiple_of(window * PAD + FIRST_ROWS[piece], 16), LENGTHS[piece]
        )
        at = (rows,) if columns is None else (rows, columns)
        copies.append(
            remote(
                source.at[at],
                target.at[at],
                send(piece - 1),
                recv(piece - 1),
                rep,
                quarter_across(shard, ACROSS[piece]),
            )
        )
    return copies


def norm_rows(rows):
    centre = rows - jnp.mean(rows, -1, keepdims=True)
    inverse = lax.rsqrt(jnp.mean(centre * centre, -1, keepdims=True) + 1e-05)
    return centre * inverse, inverse


def small_row(ref, row):
    return jnp.concatenate([ref[s, row : row + 1, :] for s in range(4)], 1)


FIXED = 4096.0
TAIL = 112
Z_PHASE, NEXT_PHASE, FIRST_PHASE, SECOND_PHASE, CORE_PHASE = range(5)
X_FIRST = (True, False, True, False, True)
HALF_QKV = 3 * D // 2


def front_kernel(
    tokens,
    order,
    spread,
    small,
    table,
    row_ids,
    rel,
    qkv_part,
    proj_part,
    fc1_part,
    fc2_part,
    qkv_whole_a,
    qkv_whole_b,
    proj_whole,
    fc1_whole,
    fc2_whole,
    small_out,
    rolled_out,
    mixed_out,
    attend_out,
    inverse_out,
    context_out,
    back_out,
    rel_out,
    small_all,
    table_all,
    table_wide,
    outgoing,
    arriving,
    rolled,
    weights_a,
    weights_b,
    mixed,
    index,
    index_tail,
    bias_tail,
    bias,
    mask,
    attend,
    inverse,
    contexts,
    gather_send,
    gather_recv,
    small_send,
    small_recv,
    bias_send,
    bias_recv,
    piece_send,
    piece_recv,
    back_send,
    back_recv,
    local,
    attend_sem,
):
    rep, shard, core, x_bit, y_bit = place()
    greet(peers_of(rep, shard))
    first_half, second_half = pl.ds(0, HALF_QKV), pl.ds(HALF_QKV, HALF_QKV)
    parts = (
        qkv_part.at[:, :, :, :, first_half],
        qkv_part.at[:, :, :, :, second_half],
        proj_part,
        fc1_part,
        fc2_part,
    )
    wholes = (weights_a, weights_b, proj_whole, fc1_whole, fc2_whole)
    feed_forward = (2, 3, 4)

    def gather(matrix, phase):
        copies = []
        whole = wholes[matrix]
        here = (y_bit, x_bit, core)

        def along_z(n, source, at, bits):
            return remote(
                source,
                whole.at[(at,) + here],
                gather_send.at[matrix, phase, n],
                gather_recv.at[matrix, phase, n],
                rep,
                quarter_across(shard, bits),
            )

        if phase == Z_PHASE:
            own_part = parts[matrix].at[here]
            return [along_z(0, own_part, shard, 2), along_z(1, own_part, shard, 1)]
        if phase == NEXT_PHASE:
            across = quarter_across(shard, 2)
            return [along_z(0, whole.at[(across,) + here], across, 1)]
        for k in (1, 2, 3):
            at = lax.rem(shard + k, 4)
            x_first = X_FIRST[matrix]
            if phase == FIRST_PHASE:
                block, partner = whole.at[at, y_bit, x_bit, core], flip(rep, 1 if x_first else 2)
            elif phase == SECOND_PHASE and x_first:
                block, partner = whole.at[at, y_bit, :, core], flip(rep, 2)
            elif phase == SECOND_PHASE:
                block, partner = whole.at[at, :, x_bit, core], flip(rep, 1)
            else:
                block, partner = whole.at[at, :, :, core], flip(rep, 0)
            copies.append(
                remote(
                    block,
                    block,
                    gather_send.at[matrix, phase, k - 1],
                    gather_recv.at[matrix, phase, k - 1],
                    partner,
                    shard,
                )
            )
        return copies

    def start(matrix, phase):
        for copy in gather(matrix, phase):
            copy.start()

    def arrived(matrix, phase):
        for copy in gather(matrix, phase):
            copy.wait_recv()

    def small_copies():
        copies = []
        for k in (1, 2, 3):
            for n, ref in enumerate((table_all, small_all)):
                copies.append(
                    remote(
                        ref.at[shard],
                        ref.at[shard],
                        small_send.at[n, k - 1],
                        small_recv.at[n, 3 - k],
                        rep,
                        lax.rem(shard + k, 4),
                    )
                )
        return copies

    small_all[shard] = small[...]
    table_all[shard] = table[...]
    for copy in small_copies():
        copy.start()
    start(0, Z_PHASE)
    start(1, Z_PHASE)
    own = [
        pltpu.make_async_copy(parts[m], wholes[m].at[shard], local.at[m]) for m in feed_forward
    ]
    for copy in own:
        copy.start()
    weights_a[shard] = qkv_part[..., :HALF_QKV]
    weights_b[shard] = qkv_part[..., HALF_QKV:]

    outgoing[...] = dot(order[...], tokens[...]).astype(bf16)

    def roll_copies(window):
        return pieces_to(
            outgoing,
            arriving,
            lambda n: piece_send.at[window, n],
            lambda n: piece_recv.at[window, n],
            rep,
            shard,
            window,
        )

    for copy in roll_copies(0):
        copy.start()
    for window in range(2):
        rows = slice(window * PAD, window * PAD + LENGTHS[0])
        arriving[rows, :] = outgoing[rows, :]

    rel_index = rel[...]
    digits = (rel_index // 256).astype(f32).astype(bf16), (rel_index & 255).astype(f32).astype(bf16)
    moved = []
    for digit in digits:
        half = dot(spread[...], digit).astype(bf16)
        moved.append(dot(half, spread[...], NT).astype(jnp.int32))
    index[:, :PAD] = moved[0] * 256 + moved[1]
    index[:, PAD:] = jnp.zeros((PAD, LANES - PAD), jnp.int32)

    ids = lax.broadcasted_iota(jnp.int32, (8, LANES), 0)
    for window in range(2):
        kinds = jnp.where(row_ids[window] + 1 == ids, 1.0, 0.0).astype(bf16)[:, :PAD]
        mask[window] = (dot(kinds, kinds, TN) - 1.0) * 1e30

    for copy in small_copies():
        copy.wait_recv()

    for block in range(4):
        count = min(TAIL, PAD - block * TAIL)
        lanes = slice(block * 32, block * 32 + 32)
        index_tail[:count, lanes] = index[block * TAIL : block * TAIL + count, PAD - 32 : PAD]
        if count < TAIL:
            index_tail[count:, lanes] = jnp.zeros((TAIL - count, 32), jnp.int32)

    upper, lower = (
        jnp.floor(table_all[2 * core + n] * FIXED + 0.5).astype(jnp.int32) for n in range(2)
    )
    words = upper * 65536 + (lower + 32768)
    for chunk in range(CHUNKS):
        for head in range(GROUP):
            row = head * CHUNKS + chunk
            table_wide[chunk, head] = jnp.broadcast_to(words[row : row + 1, :], (8, 128))
    mine = core * (HEADS // 2)

    def bias_copy(rows, step):
        block = bias.at[pl.ds(mine, HEADS // 2), rows]
        return remote(block, block, bias_send.at[step], bias_recv.at[step], flip(rep, 0), shard)

    def on_the_way(step, table_of_steps):
        for when, actions in table_of_steps.items():

            @pl.when(step == when)
            def _():
                for action, matrix, phase in actions:
                    action(matrix, phase)

    def advance(matrix, phase):
        arrived(matrix, phase)
        if phase < CORE_PHASE:
            start(matrix, phase + 1)

    schedule = {
        4: [(advance, 0, Z_PHASE), (advance, 1, Z_PHASE)],
        11: [(advance, 0, NEXT_PHASE), (advance, 1, NEXT_PHASE)]
        + [(start, m, Z_PHASE) for m in feed_forward],
        18: [(advance, 0, FIRST_PHASE), (advance, 1, FIRST_PHASE)],
    }
    later = {
        1: [(advance, m, Z_PHASE) for m in feed_forward],
        5: [(advance, m, NEXT_PHASE) for m in feed_forward],
        10: [(advance, m, FIRST_PHASE) for m in feed_forward],
    }

    def look_up(here):
        found = [[] for _ in range(GROUP)]
        for s in (0, 8):
            low, high = here[s : s + 8] & 127, here[s : s + 8] >> 7
            values = [None] * GROUP
            for chunk in range(CHUNKS):
                hit = high == chunk
                for head in range(GROUP):
                    value = jnp.take_along_axis(table_wide[chunk, head], low, axis=1)
                    values[head] = jnp.where(hit, value, values[head]) if chunk else value
            for head in range(GROUP):
                found[head].append(values[head])
        joined = [jnp.concatenate(pair, 0) for pair in found]
        uppers = [(word >> 16).astype(f32) for word in joined]
        lowers = [((word & 65535) - 32768).astype(f32) for word in joined]
        return [(value * (1 / FIXED)).astype(bf16) for value in uppers + lowers]

    def tail_step(step, carry):
        rows = pl.ds(pl.multiple_of(step * 16, 16), 16)
        for head, value in enumerate(look_up(index_tail[rows, :])):
            bias_tail[head, rows, :] = value
        return carry

    lax.fori_loop(0, TAIL // 16, tail_step, 0)

    def untail_step(head, carry):
        for block in range(4):
            count = min(TAIL, PAD - block * TAIL)
            value = bias_tail[head, :count, block * 32 : block * 32 + 32]
            bias[mine + head, block * TAIL : block * TAIL + count, PAD - 32 : PAD] = value
        return carry

    lax.fori_loop(0, HEADS // 2, untail_step, 0)

    def bias_step(step, carry):
        on_the_way(step, schedule)
        rows = pl.ds(pl.multiple_of(step * 16, 16), 16)
        for tile in range(3):
            lanes = slice(tile * 128, (tile + 1) * 128)
            for head, value in enumerate(look_up(index[rows, lanes])):
                bias[mine + head, rows, lanes] = value
        bias_copy(rows, step).start()
        return carry

    lax.fori_loop(0, PAD // 16, bias_step, 0)
    for copy in roll_copies(1):
        copy.start()
    for n in range(2):
        advance(n, SECOND_PHASE)

    for n in range(2):
        arrived(n, CORE_PHASE)
    q_bias, v_bias = small_row(small_all, Q_BIAS), small_row(small_all, V_BIAS)
    mixed_bias = jnp.concatenate([q_bias, jnp.zeros_like(q_bias), v_bias], 1).astype(f32)
    gain, shift = small_row(small_all, LN1_GAIN), small_row(small_all, LN1_SHIFT)

    def norm_step(step, carry):
        rows = pl.ds(pl.multiple_of(step * 208, 16), 208)
        normal, _ = norm_rows(arriving[rows, :].astype(f32))
        rolled[rows, :] = (normal * gain.astype(f32) + shift.astype(f32)).astype(bf16)
        return carry

    def mix(window):
        for copy in roll_copies(window):
            copy.wait_recv()
        lax.fori_loop(2 * window, 2 * window + 2, norm_step, 0)
        span = slice(window * PAD, (window + 1) * PAD)
        for n, weight in enumerate((weights_a, weights_b)):
            lanes = slice(n * HALF_QKV, (n + 1) * HALF_QKV)
            got = dot(rolled[span, :], weight[...].reshape(D, HALF_QKV))
            mixed[span, lanes] = (got + mixed_bias[:, lanes]).astype(bf16)

    mix(0)
    keep = [
        pltpu.make_async_copy(rolled, rolled_out, local.at[5]),
        pltpu.make_async_copy(mixed, mixed_out, local.at[6]),
        pltpu.make_async_copy(index, rel_out, local.at[7]),
        pltpu.make_async_copy(small_all, small_out, local.at[8]),
        pltpu.make_async_copy(inverse, inverse_out, local.at[9]),
        pltpu.make_async_copy(contexts, context_out, local.at[12]),
        pltpu.make_async_copy(weights_a, qkv_whole_a, local.at[0]),
        pltpu.make_async_copy(weights_b, qkv_whole_b, local.at[1]),
    ]

    def bias_wait(step, carry):
        bias_copy(pl.ds(pl.multiple_of(step * 16, 16), 16), step).wait_recv()
        return carry

    lax.fori_loop(0, PAD // 16, bias_wait, 0)

    head_of = lax.broadcasted_iota(jnp.int32, (1, 128), 1) // HD
    none = jnp.zeros((), bf16)
    ones = jnp.ones((PAD, 128), bf16)

    def attend_copy(step):
        window, pair, slot = step // (HEADS // 2), lax.rem(step, HEADS // 2), lax.rem(step, 2)
        return pltpu.make_async_copy(
            attend.at[slot], attend_out.at[window, pl.ds(2 * pair, 2)], attend_sem.at[slot]
        )

    def back_copies(step):
        window, group = step // (HEADS // 2), lax.rem(step // 2, HEADS // GROUP)
        lanes = pl.ds(pl.multiple_of(group * 128, 128), 128)
        return pieces_to(
            contexts,
            back_out,
            lambda n: back_send.at[window, group, n],
            lambda n: back_recv.at[window, group, n],
            rep,
            shard,
            window,
            lanes,
        )

    def attend_step(step, carry):
        on_the_way(step, later)

        @pl.when(step == HEADS // 2)
        def _():
            mix(1)

        @pl.when(step >= 2)
        def _():
            attend_copy(step - 2).wait()

        window, slot = step // (HEADS // 2), lax.rem(step, 2)
        rows = pl.ds(pl.multiple_of(window * PAD, 16), PAD)
        for n in range(2):
            head = 2 * lax.rem(step, HEADS // 2) + n
            group, member = head // GROUP, lax.rem(head, GROUP)

            def lanes(part):
                return pl.ds(pl.multiple_of(part * D + group * 128, 128), 128)

            own_lanes = head_of == member
            query = jnp.where(own_lanes, mixed[rows, lanes(0)], none)
            value = jnp.where(own_lanes, mixed[rows, lanes(2)], none)
            scores = dot(query, mixed[rows, lanes(1)], NT) * SCALE
            scores = scores + bias[head, :, :PAD].astype(f32) + mask[window]
            expo = jnp.exp(scores - jnp.max(scores, -1, keepdims=True)).astype(bf16)
            attend[slot, n, :, :PAD] = expo
            result = dot(expo, jnp.concatenate([value, ones], 1))
            over = 1.0 / result[:, 128:]
            context = (result[:, :128] * over).astype(bf16)
            contexts[rows, lanes(0)] = jnp.where(own_lanes, context, contexts[rows, lanes(0)])
            inverse[rows, lanes(0)] = jnp.where(own_lanes, over, inverse[rows, lanes(0)])
        attend_copy(step).start()

        @pl.when(lax.rem(step, 2) == 1)
        def _():
            for copy in back_copies(step):
                copy.start()

        return carry

    lax.fori_loop(0, HEADS, attend_step, 0)
    for copy in keep:
        copy.start()
    for matrix in feed_forward:
        advance(matrix, SECOND_PHASE)
    stay = [
        pltpu.make_async_copy(
            contexts.at[pl.ds(w * PAD, LENGTHS[0])],
            back_out.at[pl.ds(w * PAD, LENGTHS[0])],
            local.at[10 + w],
        )
        for w in range(2)
    ]
    for copy in stay:
        copy.start()
    for matrix in feed_forward:
        arrived(matrix, CORE_PHASE)
    attend_copy(HEADS - 2).wait()
    attend_copy(HEADS - 1).wait()

    def back_wait(step, carry):
        for copy in back_copies(step * 2):
            copy.wait()
        return carry

    lax.fori_loop(0, 2 * HEADS // GROUP, back_wait, 0)

    def bias_sent(step, carry):
        bias_copy(pl.ds(pl.multiple_of(step * 16, 16), 16), step).wait_send()
        return carry

    lax.fori_loop(0, PAD // 16, bias_sent, 0)
    for copy in small_copies():
        copy.wait_send()
    for window in range(2):
        for copy in roll_copies(window):
            copy.wait_send()
    for matrix in range(5):
        for phase in range(CORE_PHASE + 1):
            for copy in gather(matrix, phase):
                copy.wait_send()
    for copy in own + keep + stay:
        copy.wait()


def front(tokens, small, table, row_ids, rel_index, w_qkv, w_proj, w_fc1, w_fc2):
    anywhere, inside = pl.BlockSpec(memory_space=pl.ANY), pl.BlockSpec(memory_space=pltpu.VMEM)
    cut = (2, 2, 2)
    weights = [
        w.reshape(cut + (w.shape[0] // PARTS, w.shape[1])) for w in (w_qkv, w_proj, w_fc1, w_fc2)
    ]
    half = (4,) + weights[0].shape[:-1] + (HALF_QKV,)
    wholes = [jax.ShapeDtypeStruct(half, bf16)] * 2
    wholes += [jax.ShapeDtypeStruct((4,) + w.shape, bf16) for w in weights[1:]]
    dma = pltpu.SemaphoreType.DMA
    results = pl.pallas_call(
        front_kernel,
        out_shape=(
            *wholes,
            jax.ShapeDtypeStruct((4, SMALL, 128), bf16),
            jax.ShapeDtypeStruct((2 * PAD, D), bf16),
            jax.ShapeDtypeStruct((2 * PAD, 3 * D), bf16),
            jax.ShapeDtypeStruct((2, HEADS, PAD, LANES), bf16),
            jax.ShapeDtypeStruct((2 * PAD, D), f32),
            jax.ShapeDtypeStruct((2 * PAD, D), bf16),
            jax.ShapeDtypeStruct((2 * PAD, D), bf16),
            jax.ShapeDtypeStruct((PAD, LANES), jnp.int32),
        ),
        in_specs=[inside] * 11,
        out_specs=(anywhere,) * 13,
        scratch_shapes=[
            pltpu.VMEM((4, SMALL, 128), bf16),
            pltpu.VMEM((4, GROUP * CHUNKS, 128), f32),
            pltpu.VMEM((CHUNKS, GROUP, 8, 128), jnp.int32),
            pltpu.VMEM((2 * PAD, D), bf16),
            pltpu.VMEM((2 * PAD, D), bf16),
            pltpu.VMEM((2 * PAD, D), bf16),
            pltpu.VMEM(half, bf16),
            pltpu.VMEM(half, bf16),
            pltpu.VMEM((2 * PAD, 3 * D), bf16),
            pltpu.VMEM((PAD, LANES), jnp.int32),
            pltpu.VMEM((TAIL, 128), jnp.int32),
            pltpu.VMEM((HEADS // 2, TAIL, 128), bf16),
            pltpu.VMEM((HEADS, PAD, LANES), bf16),
            pltpu.VMEM((2, PAD, PAD), f32),
            pltpu.VMEM((2, 2, PAD, LANES), bf16),
            pltpu.VMEM((2 * PAD, D), f32),
            pltpu.VMEM((2 * PAD, D), bf16),
            dma((5, CORE_PHASE + 1, 3)),
            dma((5, CORE_PHASE + 1, 3)),
            dma((2, 3)),
            dma((2, 3)),
            dma((PAD // 16,)),
            dma((PAD // 16,)),
            dma((2, 3)),
            dma((2, 3)),
            dma((2, HEADS // GROUP, 3)),
            dma((2, HEADS // GROUP, 3)),
            dma((13,)),
            dma((2,)),
        ],
        compiler_params=pltpu.CompilerParams(
            vmem_limit_bytes=VMEM_LIMIT, collective_id=0, has_side_effects=True
        ),
        name="front",
    )(
        tokens,
        jnp.asarray(send_matrix(), bf16),
        jnp.asarray(spread_matrix(), bf16),
        small,
        table,
        row_ids,
        rel_index,
        *weights,
    )
    whole = [w.reshape(-1, w.shape[-1]) for w in results[:5]]
    return (*whole, *results[5:])


CORE_SUM, FIRST_SUM, SECOND_SUM, NEXT_SUM, Z_SUM, SHARE, CORE_SHARE = range(7)
SUMMED = ((16, 2048, True), (64, 512, False), (16, 512, True))
SUMMED += tuple((16, 3 * 128, group % 2 == 0) for group in range(HEADS // GROUP))
FC1, FC2, PROJ, QKV = range(4)
STRIDE = HEADS + 1
CHUNK_ROWS = ((0, 400, (1, 3)), (400, 384, (0, 2)))
SPAN = 256
SPANS = -(-TABLE // SPAN)
BATCH = 8
HALF = PAD // 2
TILES = LANES // 128
SLAB = 2 * SPANS * GROUP + SMALL


def rear_kernel(
    order_back,
    tokens,
    small_all,
    returned_in,
    order_in,
    cotangent_in,
    proj_in,
    fc1_in,
    fc2_in,
    weights_a_in,
    weights_b_in,
    rolled_in,
    mixed_in,
    inverse_in,
    contexts_in,
    rel_in,
    attend_in,
    output,
    grad_tokens,
    fc1_out,
    fc2_out,
    proj_out,
    qkv_out_0,
    qkv_out_1,
    qkv_out_2,
    qkv_out_3,
    slab_out,
    weights_a,
    weights_b,
    rolled,
    mixed,
    inverse,
    contexts,
    rel,
    outgoing,
    grad_context,
    grad_middle,
    returned,
    pairs_in,
    fc1_grad,
    fc2_grad,
    proj_grad,
    qkv_grads,
    sums,
    fc1_sum,
    table_sum,
    slab,
    slab_z,
    slab_rep,
    *rest,
):
    count = len(SUMMED)
    held = [rest[6 * m : 6 * m + 6] for m in range(count)]
    (
        sum_send,
        sum_recv,
        extra_send,
        extra_recv,
        piece_send,
        piece_recv,
        back_send,
        back_recv,
        attend_sem,
        pairs_send,
        pairs_recv,
        slab_send,
        slab_recv,
        local,
        load,
    ) = rest[6 * count :]
    rep, shard, core, x_bit, y_bit = place()
    reps = lax.axis_size("rep")
    barrier = pltpu.get_barrier_semaphore()

    def hello(k, carry):
        pl.semaphore_signal(
            barrier,
            inc=1,
            device_id={"rep": lax.rem(rep + k, reps), "shard": shard},
            device_id_type=MESH,
        )
        return carry

    lax.fori_loop(1, reps, hello, 0)
    for k in (1, 2, 3):
        pl.semaphore_signal(
            barrier,
            inc=1,
            device_id={"rep": rep, "shard": lax.rem(shard + k, 4)},
            device_id_type=MESH,
        )
    pl.semaphore_wait(barrier, reps + 2)

    sources = (fc1_grad, fc2_grad, proj_grad) + tuple(qkv_grads.at[g] for g in range(4))

    def axis_of(matrix, first):
        x_first = SUMMED[matrix][2]
        use_x = x_first == first
        return (1, x_bit) if use_x else (2, y_bit)

    def sum_copies(matrix, phase):
        from_core, from_first, summed, from_next, from_z, shared = held[matrix]
        source = sources[matrix]
        x_first = SUMMED[matrix][2]
        first_bit, first = axis_of(matrix, True)
        second_bit, second = axis_of(matrix, False)

        def one(src, dst, bit, n=0):
            return remote(
                src,
                dst,
                sum_send.at[matrix, phase, n],
                sum_recv.at[matrix, phase, n],
                flip(rep, bit),
                shard,
            )

        if phase == CORE_SUM:
            return [one(source.at[:, :, :, 1 - core], from_core, 0)]
        if phase == FIRST_SUM:
            cut = source.at[:, :, 1 - x_bit, core] if x_first else source.at[:, 1 - y_bit, :, core]
            return [one(cut, from_first, first_bit)]
        if phase == SECOND_SUM:
            return [one(from_first.at[:, 1 - second], summed, second_bit)]
        if phase in (NEXT_SUM, Z_SUM):
            low, high = lax.rem(shard, 2), shard // 2
            if phase == NEXT_SUM:
                moves = [(2 * n + 1 - low, from_next.at[n]) for n in range(2)]
            else:
                moves = [(2 * (1 - high) + low, from_z.at[0])]
            return [
                remote(
                    summed.at[owner],
                    target,
                    sum_send.at[matrix, phase, n],
                    sum_recv.at[matrix, phase, n],
                    rep,
                    quarter_across(shard, 1 if phase == NEXT_SUM else 2),
                )
                for n, (owner, target) in enumerate(moves)
            ]
        if phase == CORE_SHARE:
            block = shared.at[:, :, core]
            return [one(block, block, 0)]
        block = shared.at[y_bit, x_bit, core]
        across = flip(flip(rep, 1), 2)
        return [
            remote(
                block,
                block,
                sum_send.at[matrix, phase, n],
                sum_recv.at[matrix, phase, n],
                partner,
                shard,
            )
            for n, partner in enumerate((flip(rep, 1), flip(rep, 2), across))
        ]

    def extra_copy(matrix, bit):
        shared, from_z = held[matrix][5], held[matrix][4]
        return remote(
            shared.at[y_bit, x_bit, core],
            from_z.at[bit - 2],
            extra_send.at[matrix, bit - 3],
            extra_recv.at[matrix, bit - 3],
            flip(rep, bit),
            shard,
        )

    def add(into, at, other, other_at):
        into[at] = (into[at].astype(f32) + other[other_at].astype(f32)).astype(bf16)

    def begin(matrix):
        for copy in sum_copies(matrix, CORE_SUM):
            copy.start()

    def advance(matrix, phase):
        from_core, from_first, summed, from_next, from_z, shared = held[matrix]
        source = sources[matrix]
        x_first = SUMMED[matrix][2]
        _, second = axis_of(matrix, False)
        for copy in sum_copies(matrix, phase):
            copy.wait_recv()
        if phase == CORE_SUM:

            def step(n, carry):
                at = (n // 4, lax.rem(n // 2, 2), lax.rem(n, 2))
                add(source, at + (core,), from_core, at)
                return carry

            lax.fori_loop(0, 16, step, 0)
        elif phase == FIRST_SUM:

            def step(n, carry):
                owner, other = n // 2, lax.rem(n, 2)
                at = (owner, other, x_bit) if x_first else (owner, y_bit, other)
                add(from_first, (owner, other), source, at + (core,))
                return carry

            lax.fori_loop(0, 8, step, 0)
        elif phase == SECOND_SUM:

            def step(owner, carry):
                add(summed, (owner,), from_first, (owner, second))
                return carry

            lax.fori_loop(0, 4, step, 0)
        elif phase == NEXT_SUM:
            low = lax.rem(shard, 2)
            for high in range(2):
                add(summed, (2 * high + low,), from_next, (high,))
        elif phase == Z_SUM:
            total = summed[shard].astype(f32) + from_z[0].astype(f32)
            shared[y_bit, x_bit, core] = total.astype(bf16)
            bit = 3
            while (1 << bit) < reps:
                copy = extra_copy(matrix, bit)
                copy.start()
                copy.wait()
                at = (y_bit, x_bit, core)
                add(shared, at, from_z, (bit - 2,))
                bit += 1
        if phase < CORE_SHARE:
            for copy in sum_copies(matrix, phase + 1):
                copy.start()

    def on_the_way(step, table_of_steps):
        for when, actions in table_of_steps.items():

            @pl.when(step == when)
            def _():
                for matrix, phase in actions:
                    advance(matrix, phase)

    fetched = (
        (weights_a_in, weights_a),
        (weights_b_in, weights_b),
        (rolled_in, rolled),
        (mixed_in, mixed),
        (inverse_in, inverse),
        (contexts_in, contexts),
        (rel_in, rel),
    )
    fetches = [
        pltpu.make_async_copy(src, dst, load.at[n]) for n, (src, dst) in enumerate(fetched)
    ]

    def roll_copies(window, which=(1, 2, 3)):
        return pieces_to(
            outgoing,
            grad_context,
            lambda n: piece_send.at[window, n],
            lambda n: piece_recv.at[window, n],
            rep,
            shard,
            window,
            which=which,
        )

    def feed_forward(
        proj,
        fc1,
        fc2,
        middle,
        normed,
        normed_back,
        active,
        grad_hidden,
        grad_normed,
        branch,
        unrolled,
        grad_unrolled,
        final,
        fc1_bias,
        returned_context,
        order,
        cotangent,
    ):
        loads = [
            pltpu.make_async_copy(src, dst, load.at[len(fetched) + n])
            for n, (src, dst) in enumerate(
                (
                    (returned_in, returned_context),
                    (proj_in, proj),
                    (cotangent_in, cotangent),
                    (fc1_in, fc1),
                    (fc2_in, fc2),
                    (order_in, order),
                )
            )
        ]
        for copy in loads + fetches:
            copy.start()
        proj_bias = small_row(small_all, PROJ_BIAS).astype(f32)
        gain, shift = (small_row(small_all, row).astype(f32) for row in (LN2_GAIN, LN2_SHIFT))
        fc2_bias = small_row(small_all, FC2_BIAS).astype(f32)
        for owner in range(4):
            for k in range(4):
                lanes = slice(owner * D + k * 128, owner * D + (k + 1) * 128)
                fc1_bias[:, lanes] = small_all[owner, FC1_BIAS + k : FC1_BIAS + k + 1, :].astype(f32)
        sums[...] = jnp.zeros_like(sums)
        fc1_sum[...] = jnp.zeros_like(fc1_sum)
        for copy in loads[:2]:
            copy.wait()
        for first, length, _ in CHUNK_ROWS:
            rows = pl.ds(first, length)
            unrolled[rows, :] = dot(order_back[rows, :], returned_context[...]).astype(bf16)
            got = dot(unrolled[rows, :], proj[...]) + proj_bias
            middle[rows, :] = tokens[rows, :].astype(f32) + got
            normal, _ = norm_rows(middle[rows, :])
            normed[rows, :] = (normal * gain + shift).astype(bf16)
        for copy in loads[2:]:
            copy.wait()

        def forward_step(tile, carry):
            for n in range(2):
                lanes = pl.ds(pl.multiple_of((2 * tile + n) * FF_TILE, FF_TILE), FF_TILE)
                hidden = dot(normed[...], fc1[:, lanes]) + fc1_bias[:, lanes]
                share = 0.5 + 0.5 * lax.erf(hidden * 0.7071067811865476)
                active[:, lanes] = (hidden * share).astype(bf16)
                slope = share + hidden * jnp.exp(-0.5 * hidden * hidden) * 0.3989422804014327
                grad_hidden[:, lanes] = slope.astype(bf16)
            return carry

        lax.fori_loop(0, FF // FF_TILE // 2, forward_step, 0)

        def fc2_step(tile, carry):
            lanes = pl.ds(pl.multiple_of(tile * 256, 256), 256)
            got = dot(active[:, lanes], cotangent[...], TN).astype(bf16)
            fc2_grad[tile // 2, lax.rem(tile, 2)] = got.reshape(2, 2, 64, D)
            return carry

        lax.fori_loop(0, FF // 256, fc2_step, 0)
        begin(FC2)
        for first, length, pieces in CHUNK_ROWS:
            rows = pl.ds(first, length)

            def backward_step(tile, carry):
                lanes = pl.ds(pl.multiple_of(tile * D, D), D)
                grad_active = dot(cotangent[rows, :], fc2[lanes, :], NT)
                grad = (grad_active * grad_hidden[rows, lanes].astype(f32)).astype(bf16)
                grad_hidden[rows, lanes] = grad
                fc1_sum[:, lanes] += jnp.sum(grad.astype(f32), 0, keepdims=True)
                return carry

            lax.fori_loop(0, FF // D, backward_step, 0)
            grad_normed[rows, :] = dot(grad_hidden[rows, :], fc1[...], NT)
            normal, over = norm_rows(middle[rows, :])
            grad_out = grad_normed[rows, :]
            scaled = grad_out * gain
            inner = (
                scaled
                - jnp.mean(scaled, -1, keepdims=True)
                - normal * jnp.mean(scaled * normal, -1, keepdims=True)
            )
            upper = cotangent[rows, :].astype(f32)
            grad_middle[rows, :] = upper + over * inner
            branch[rows, :] = grad_middle[rows, :].astype(bf16)
            for row, value in (
                (PROJ_BIAS, branch[rows, :].astype(f32)),
                (LN2_GAIN, grad_out * normal),
                (LN2_SHIFT, grad_out),
                (FC2_BIAS, upper),
            ):
                sums[row : row + 1, :] += jnp.sum(value, 0, keepdims=True)
            grad_unrolled[rows, :] = dot(branch[rows, :], proj[...], NT).astype(bf16)
            source = pl.ds(0, 400) if first == 0 else pl.ds(384, 400)
            for window in range(2):
                for piece in pieces:
                    at = pl.ds(window * PAD + FIRST_ROWS[piece], LENGTHS[piece])
                    got = dot(order[at, source], grad_unrolled[source, :]).astype(bf16)
                    if piece:
                        outgoing[at, :] = got
                    else:
                        grad_context[at, :] = got
            for window in range(2):
                for copy in roll_copies(window, [piece for piece in pieces if piece]):
                    copy.start()
        same = lax.broadcasted_iota(jnp.int32, (D, D), 0) == lax.broadcasted_iota(
            jnp.int32, (D, D), 1
        )
        unit = jnp.where(same, jnp.ones((), bf16), jnp.zeros((), bf16))
        normed_back[...] = dot(unit, normed[...], NT).astype(bf16)

        def fc1_step(tile, carry):
            lanes = pl.ds(pl.multiple_of(tile * 512, 512), 512)
            got = dot(normed_back[...], grad_hidden[:, lanes]).astype(bf16)
            fc1_grad[:, :, :, :, :, lanes] = got.reshape(4, 2, 2, 2, 16, 512)
            return carry

        lax.fori_loop(0, FF // 512, fc1_step, 0)
        begin(FC1)

        got = dot(unrolled[...], branch[...], TN).astype(bf16)
        proj_grad[...] = got.reshape(proj_grad.shape)
        begin(PROJ)
        advance(FC2, CORE_SUM)
        final[...] = (middle[...] + dot(active[...], fc2[...]) + fc2_bias).astype(bf16)
        written = pltpu.make_async_copy(final, output, load.at[len(fetched) + 6])
        written.start()
        for matrix in (FC1, PROJ):
            advance(matrix, CORE_SUM)
        written.wait()

    count_rows = tokens.shape[0]
    pl.run_scoped(
        feed_forward,
        pltpu.VMEM((D, D), bf16),
        pltpu.VMEM((D, FF), bf16),
        pltpu.VMEM((FF, D), bf16),
        pltpu.VMEM((count_rows, D), f32),
        pltpu.VMEM((count_rows, D), bf16),
        pltpu.VMEM((D, count_rows), bf16),
        pltpu.VMEM((count_rows, FF), bf16),
        pltpu.VMEM((count_rows, FF), bf16),
        pltpu.VMEM((count_rows, D), f32),
        pltpu.VMEM((count_rows, D), bf16),
        pltpu.VMEM((count_rows, D), bf16),
        pltpu.VMEM((count_rows, D), bf16),
        pltpu.VMEM((count_rows, D), bf16),
        pltpu.VMEM((1, FF), f32),
        pltpu.VMEM((2 * PAD, D), bf16),
        pltpu.VMEM((2 * PAD, count_rows), bf16),
        pltpu.VMEM((count_rows, D), bf16),
    )
    for copy in fetches:
        copy.wait()
    def return_copies(window):
        return pieces_to(
            outgoing,
            returned,
            lambda n: back_send.at[window, n],
            lambda n: back_recv.at[window, n],
            rep,
            shard,
            window,
        )

    def attend_back(attend, grads, rolled_back, pairs, pairs_out):
        head_of = lax.broadcasted_iota(jnp.int32, (1, 128), 1) // HD
        none = jnp.zeros((), bf16)

        def attend_copy(head):
            slot = lax.rem(head, 2)
            return pltpu.make_async_copy(
                attend_in.at[:, head], attend.at[slot], attend_sem.at[slot]
            )

        attend_copy(0).start()
        same = lax.broadcasted_iota(jnp.int32, (D, D), 0) == lax.broadcasted_iota(
            jnp.int32, (D, D), 1
        )
        unit = jnp.where(same, jnp.ones((), bf16), none)
        rolled_back[...] = dot(unit, rolled[...], NT).astype(bf16)

        def qkv_group(group):
            columns = [
                grads[:, part * D + group * 128 : part * D + (group + 1) * 128] for part in range(3)
            ]
            got = dot(rolled_back[...], jnp.concatenate(columns, 1)).astype(bf16)
            qkv_grads[group] = got.reshape(qkv_grads.shape[1:])
            begin(QKV + group)

        slow = (FC1, PROJ)
        first_schedule = {
            0: [(FC2, FIRST_SUM)],
            6: [(QKV, CORE_SUM)],
            8: [(FC2, SECOND_SUM)],
            9: [(QKV, FIRST_SUM)],
            10: [(QKV + 1, CORE_SUM)] + [(m, FIRST_SUM) for m in slow],
            12: [(QKV, SECOND_SUM), (FC2, NEXT_SUM)],
            13: [(QKV + 1, FIRST_SUM)],
            14: [(QKV + 2, CORE_SUM)],
            15: [(QKV, NEXT_SUM), (FC2, Z_SUM)],
        }
        second_schedule = {
            0: [(QKV + 1, SECOND_SUM)],
            1: [(QKV + 2, FIRST_SUM)] + [(m, SECOND_SUM) for m in slow],
            2: [(QKV, Z_SUM), (QKV + 3, CORE_SUM)],
            3: [(QKV + 1, NEXT_SUM)],
            4: [(QKV + 2, SECOND_SUM)],
            5: [(QKV + 3, FIRST_SUM)],
            6: [(QKV + 1, Z_SUM), (FC2, SHARE)],
            7: [(QKV + 2, NEXT_SUM)] + [(m, NEXT_SUM) for m in slow],
            8: [(QKV + 3, SECOND_SUM), (QKV, SHARE)],
            10: [(QKV + 2, Z_SUM)],
            12: [(QKV + 3, NEXT_SUM), (QKV + 1, SHARE)],
            14: [(m, Z_SUM) for m in slow],
            16: [(QKV + 3, Z_SUM)],
            18: [(QKV + 2, SHARE)],
            24: [(QKV + 3, SHARE)] + [(m, SHARE) for m in slow],
        }

        for window in range(2):
            for copy in roll_copies(window):
                copy.wait_recv()

        def head_step(head, carry):
            on_the_way(head, first_schedule)
            for done in range(1, HEADS // GROUP):

                @pl.when(head == done * GROUP)
                def _():
                    qkv_group(done - 1)

            @pl.when(head + 1 < HEADS)
            def _():
                attend_copy(head + 1).start()

            attend_copy(head).wait()
            slot = lax.rem(head, 2)
            group, member = head // GROUP, lax.rem(head, GROUP)

            def lanes(part):
                return pl.ds(pl.multiple_of(part * D + group * 128, 128), 128)

            mine = head_of == member
            both = []
            for window in range(2):
                rows = pl.ds(window * PAD, PAD)
                query = jnp.where(mine, mixed[rows, lanes(0)], none)
                key = jnp.where(mine, mixed[rows, lanes(1)], none)
                grad = grad_context[rows, lanes(0)].astype(f32) * inverse[rows, lanes(0)]
                grad = jnp.where(mine, grad, 0.0).astype(bf16)
                expo = attend[slot, window, :, :PAD]
                grad_attend = dot(grad, mixed[rows, lanes(2)], NT)
                inner = jnp.sum(
                    grad.astype(f32) * contexts[rows, lanes(0)].astype(f32), -1, keepdims=True
                )
                grad_scores = (expo.astype(f32) * (grad_attend - inner)).astype(bf16)
                both.append(grad_scores)
                for part, value in (
                    (0, dot(grad_scores, key) * SCALE),
                    (1, dot(grad_scores, query, TN) * SCALE),
                    (2, dot(expo, grad, TN)),
                ):
                    grads[rows, lanes(part)] = jnp.where(
                        mine, value.astype(bf16), grads[rows, lanes(part)]
                    )
            total = both[0].astype(f32) + both[1].astype(f32)
            for tile in range(TILES):
                part = total[:, tile * 128 : (tile + 1) * 128]
                if part.shape[1] < 128:
                    part = jnp.concatenate([part, jnp.zeros((PAD, 128 - part.shape[1]), f32)], 1)
                pairs[tile, pl.ds(head, PAD, stride=STRIDE), :] = part
            return carry

        lax.fori_loop(0, HEADS, head_step, 0)

        for window in range(2):
            for copy in roll_copies(window):
                copy.wait_send()

        for window in range(2):
            span = slice(window * PAD, (window + 1) * PAD)
            got = dot(grads[span, :HALF_QKV], weights_a[...], NT)
            got = got + dot(grads[span, HALF_QKV:], weights_b[...], NT)
            outgoing[span, :] = got.astype(bf16)
            for copy in return_copies(window):
                copy.start()
            rows = slice(window * PAD, window * PAD + LENGTHS[0])
            returned[rows, :] = outgoing[rows, :]
        qkv_group(HEADS // GROUP - 1)

        def round_step(step, carry):
            source = pl.ds(((1 - core) * HALF + step) * STRIDE, HEADS)
            at = pl.ds(pl.multiple_of(step * HEADS, HEADS), HEADS)
            for tile in range(TILES):
                pairs_out[tile, at, :] = pairs[tile, source, :].astype(bf16)
            return carry

        def pairs_copy(half):
            block = pl.ds(half * (HALF * HEADS // 2), HALF * HEADS // 2)
            return remote(
                pairs_out.at[:, block],
                pairs_in.at[:, block],
                pairs_send.at[half],
                pairs_recv.at[half],
                flip(rep, 0),
                shard,
            )

        for half in range(2):
            lax.fori_loop(half * (HALF // 2), (half + 1) * (HALF // 2), round_step, 0)
            pairs_copy(half).start()

        low_of = lax.broadcasted_iota(jnp.int32, (SPAN, LANES), 0).astype(f32).astype(bf16)
        table_sum[...] = jnp.zeros_like(table_sum)
        for half in range(2):
            pairs_copy(half).wait_recv()

        def table_step(step, carry):
            on_the_way(step, second_schedule)
            left, right = [], []
            for k in range(BATCH):
                row = step * BATCH + k
                there = core * HALF + row
                at = pl.ds(there * STRIDE, HEADS)
                near = pl.ds(pl.multiple_of(row * HEADS, HEADS), HEADS)
                index = rel[pl.ds(there, 1), :]
                low = (index & (SPAN - 1)).astype(f32).astype(bf16)
                high = jnp.broadcast_to((index // SPAN).astype(f32).astype(bf16), (HEADS, LANES))
                total = jnp.concatenate(
                    [pairs[t, at, :] + pairs_in[t, near, :].astype(f32) for t in range(TILES)], 1
                ).astype(bf16)
                nothing = jnp.zeros_like(total)
                left.append(
                    jnp.concatenate(
                        [jnp.where(high == jnp.asarray(s, bf16), total, nothing) for s in range(SPANS)],
                        0,
                    )
                )
                hit = low_of == jnp.broadcast_to(low, (SPAN, LANES))
                right.append(jnp.where(hit, jnp.ones((), bf16), jnp.zeros((), bf16)))
            table_sum[...] += dot(jnp.concatenate(left, 1), jnp.concatenate(right, 1), NT)
            return carry

        lax.fori_loop(0, HALF // BATCH, table_step, 0)
        for half in range(2):
            pairs_copy(half).wait_send()
        sums[Q_BIAS : Q_BIAS + 1, :] = jnp.sum(grads[:, :D].astype(f32), 0, keepdims=True)
        sums[V_BIAS : V_BIAS + 1, :] = jnp.sum(grads[:, 2 * D :].astype(f32), 0, keepdims=True)

    pl.run_scoped(
        attend_back,
        pltpu.VMEM((2, 2, PAD, LANES), bf16),
        pltpu.VMEM((2 * PAD, 3 * D), bf16),
        pltpu.VMEM((D, 2 * PAD), bf16),
        pltpu.VMEM((TILES, PAD * STRIDE, 128), f32),
        pltpu.VMEM((TILES, HALF * HEADS, 128), bf16),
    )

    for window in range(2):
        for copy in return_copies(window):
            copy.wait_recv()
    gain = small_row(small_all, LN1_GAIN).astype(f32)

    def norm_step(step, carry):
        gain_sum, shift_sum = carry
        rows = pl.ds(pl.multiple_of(step * 112, 16), 112)
        grad_out = dot(order_back[rows, :], returned[...])
        normal, over = norm_rows(tokens[rows, :].astype(f32))
        scaled = grad_out * gain
        inner = (
            scaled
            - jnp.mean(scaled, -1, keepdims=True)
            - normal * jnp.mean(scaled * normal, -1, keepdims=True)
        )
        grad_middle[rows, :] += over * inner
        return (
            gain_sum + jnp.sum(grad_out * normal, 0, keepdims=True),
            shift_sum + jnp.sum(grad_out, 0, keepdims=True),
        )

    nought = jnp.zeros((1, D), f32)
    gain_sum, shift_sum = lax.fori_loop(0, 7, norm_step, (nought, nought))

    sums[LN1_GAIN : LN1_GAIN + 1, :] = gain_sum
    sums[LN1_SHIFT : LN1_SHIFT + 1, :] = shift_sum
    tokens_copy = pltpu.make_async_copy(grad_middle, grad_tokens, load.at[0])
    tokens_copy.start()

    for owner in range(4):
        lanes = slice(owner * 128, (owner + 1) * 128)
        entries = jnp.concatenate(
            [table_sum[pl.ds(s * HEADS + GROUP * owner, GROUP), :] for s in range(SPANS)], 0
        )
        slab[owner, : SPANS * GROUP, :] = entries[:, :128]
        slab[owner, SPANS * GROUP : 2 * SPANS * GROUP, :] = entries[:, 128:]
        slab[owner, 2 * SPANS * GROUP :, :] = jnp.concatenate(
            [sums[:, lanes]]
            + [fc1_sum[:, owner * D + k * 128 : owner * D + (k + 1) * 128] for k in range(4)]
            + [jnp.zeros((4, 128), f32)],
            0,
        )

    def slab_copies():
        return [
            remote(
                slab.at[lax.rem(shard + k, 4)],
                slab_z.at[3 - k],
                slab_send.at[k - 1],
                slab_recv.at[3 - k],
                rep,
                lax.rem(shard + k, 4),
            )
            for k in (1, 2, 3)
        ]

    for copy in slab_copies():
        copy.start()

    for matrix in range(count):
        advance(matrix, CORE_SHARE)
    for copy in slab_copies():
        copy.wait_recv()
    slab_rep[rep] = slab[shard] + (slab_z[0] + slab_z[1] + slab_z[2])

    def slab_share(k):
        return remote(
            slab_rep.at[rep],
            slab_rep.at[rep],
            slab_send.at[2 + k],
            slab_recv.at[2 + reps - k],
            lax.rem(rep + k, reps),
            shard,
        )

    def share_start(k, carry):
        slab_share(k).start()
        return carry

    lax.fori_loop(1, reps, share_start, 0)
    outs = (fc1_out, fc2_out, proj_out, qkv_out_0, qkv_out_1, qkv_out_2, qkv_out_3)
    results = [
        pltpu.make_async_copy(held[matrix][5], outs[matrix], local.at[count + matrix])
        for matrix in range(count)
    ]
    for copy in results:
        copy.start()

    def share_wait(k, carry):
        slab_share(k).wait()
        return carry

    lax.fori_loop(1, reps, share_wait, 0)

    def slab_step(k, total):
        return total + slab_rep[k]

    slab_out[...] = lax.fori_loop(1, reps, slab_step, slab_rep[0])

    for copy in slab_copies():
        copy.wait_send()
    for window in range(2):
        for copy in return_copies(window):
            copy.wait_send()
    for matrix in range(count):
        for phase in range(CORE_SHARE + 1):
            for copy in sum_copies(matrix, phase):
                copy.wait_send()
    for copy in results + [tokens_copy]:
        copy.wait()


def rear(
    returned_context,
    tokens,
    cotangent,
    small_all,
    whole_proj,
    whole_fc1,
    whole_fc2,
    weights_a,
    weights_b,
    rolled,
    mixed,
    inverse,
    contexts,
    rel,
    attend,
):
    anywhere, inside = pl.BlockSpec(memory_space=pl.ANY), pl.BlockSpec(memory_space=pltpu.VMEM)
    reps = lax.axis_size("rep")
    dma = pltpu.SemaphoreType.DMA
    order = send_matrix()
    extra = max(1, reps.bit_length() - 4)
    held = []
    for rows, columns, _ in SUMMED:
        held += [
            pltpu.VMEM((4, 2, 2, rows, columns), bf16),
            pltpu.VMEM((4, 2, rows, columns), bf16),
            pltpu.VMEM((4, rows, columns), bf16),
            pltpu.VMEM((2, rows, columns), bf16),
            pltpu.VMEM((1 + extra, rows, columns), bf16),
            pltpu.VMEM((2, 2, 2, rows, columns), bf16),
        ]
    return pl.pallas_call(
        rear_kernel,
        out_shape=(
            jax.ShapeDtypeStruct(tokens.shape, bf16),
            jax.ShapeDtypeStruct(tokens.shape, f32),
            *[jax.ShapeDtypeStruct((2, 2, 2) + shape[:2], bf16) for shape in SUMMED],
            jax.ShapeDtypeStruct((SLAB, 128), f32),
        ),
        in_specs=[inside] * 3 + [anywhere] * 14,
        out_specs=(*[anywhere] * (2 + len(SUMMED)), inside),
        scratch_shapes=[
            pltpu.VMEM(weights_a.shape, bf16),
            pltpu.VMEM(weights_b.shape, bf16),
            pltpu.VMEM(rolled.shape, bf16),
            pltpu.VMEM(mixed.shape, bf16),
            pltpu.VMEM(inverse.shape, f32),
            pltpu.VMEM(contexts.shape, bf16),
            pltpu.VMEM(rel.shape, jnp.int32),
            pltpu.VMEM((2 * PAD, D), bf16),
            pltpu.VMEM((2 * PAD, D), bf16),
            pltpu.VMEM(tokens.shape, f32),
            pltpu.VMEM((2 * PAD, D), bf16),
            pltpu.VMEM((TILES, HALF * HEADS, 128), bf16),
            pltpu.VMEM((4, 2, 2, 2, 16, 2048), bf16),
            pltpu.VMEM((4, 2, 2, 2, 64, 512), bf16),
            pltpu.VMEM((4, 2, 2, 2, 16, 512), bf16),
            pltpu.VMEM((HEADS // GROUP, 4, 2, 2, 2, 16, 3 * 128), bf16),
            pltpu.VMEM((8, D), f32),
            pltpu.VMEM((1, FF), f32),
            pltpu.VMEM((SPANS * HEADS, SPAN), f32),
            pltpu.VMEM((4, SLAB, 128), f32),
            pltpu.VMEM((3, SLAB, 128), f32),
            pltpu.VMEM((reps, SLAB, 128), f32),
            *held,
            dma((len(SUMMED), CORE_SHARE + 1, 3)),
            dma((len(SUMMED), CORE_SHARE + 1, 3)),
            dma((len(SUMMED), extra)),
            dma((len(SUMMED), extra)),
            dma((2, 3)),
            dma((2, 3)),
            dma((2, 3)),
            dma((2, 3)),
            dma((2,)),
            dma((2,)),
            dma((2,)),
            dma((3 + reps,)),
            dma((3 + reps,)),
            dma((2 * len(SUMMED),)),
            dma((14,)),
        ],
        compiler_params=pltpu.CompilerParams(
            vmem_limit_bytes=VMEM_LIMIT, collective_id=1, has_side_effects=True
        ),
        name="rear",
    )(
        jnp.asarray(order.T, bf16),
        tokens,
        small_all,
        returned_context,
        jnp.asarray(order, bf16),
        cotangent,
        whole_proj,
        whole_fc1,
        whole_fc2,
        weights_a,
        weights_b,
        rolled,
        mixed,
        inverse,
        contexts,
        rel,
        attend,
    )


def shards(
    tokens,
    region,
    rel_index,
    ln1_gain,
    ln1_shift,
    w_qkv,
    q_bias,
    v_bias,
    table,
    w_proj,
    proj_bias,
    ln2_gain,
    ln2_shift,
    w_fc1,
    fc1_bias,
    w_fc2,
    fc2_bias,
    cotangent,
):
    small = jnp.zeros((SMALL, 128), f32)
    vectors = (ln1_gain, ln1_shift, q_bias, v_bias, proj_bias, ln2_gain, ln2_shift, fc2_bias, fc1_bias)
    for row, vector in enumerate(vectors):
        block = vector.reshape(-1, 128).astype(f32)
        small += jnp.pad(block, ((row, SMALL - row - block.shape[0]), (0, 0)))
    small = small.astype(bf16)
    chunks = jnp.pad(table.astype(f32).T, ((0, 0), (0, CHUNKS * 128 - TABLE)))
    labels = region.reshape(WT, WH, 2, WW).transpose(2, 0, 1, 3).reshape(2, WIN)
    labels = pieces_of(labels, 1, -1)
    row_ids = jnp.pad(labels, ((0, 0), (0, LANES - PAD)), constant_values=-1)[:, None]
    (
        whole_qkv_a,
        whole_qkv_b,
        whole_proj,
        whole_fc1,
        whole_fc2,
        small,
        rolled,
        qkv,
        attend,
        inverse,
        contexts,
        returned,
        rel,
    ) = front(
        tokens.reshape(-1, D),
        small,
        chunks.reshape(-1, 128),
        row_ids,
        rel_index,
        w_qkv,
        w_proj,
        w_fc1,
        w_fc2,
    )
    output, grad_tokens, grad_w_fc1, grad_w_fc2, grad_w_proj, *grads_qkv, slab = rear(
        returned,
        tokens.reshape(-1, D),
        cotangent.reshape(-1, D),
        small,
        whole_proj,
        whole_fc1,
        whole_fc2,
        whole_qkv_a,
        whole_qkv_b,
        rolled,
        qkv,
        inverse,
        contexts,
        rel,
        attend,
    )
    output = output.reshape(tokens.shape)
    grad_tokens = grad_tokens.reshape(tokens.shape)
    grad_w_fc1 = grad_w_fc1.astype(f32).reshape(w_fc1.shape)
    grad_w_fc2 = grad_w_fc2.astype(f32).reshape(w_fc2.shape)
    grad_w_proj = grad_w_proj.astype(f32).reshape(w_proj.shape)
    parts = [g.reshape(-1, 3, 128) for g in grads_qkv]
    grad_w_qkv = jnp.stack(parts, 2).astype(f32)
    grad_w_qkv = grad_w_qkv.reshape(w_qkv.shape)
    spans = slab[: 2 * SPANS * GROUP].reshape(2, SPANS, GROUP, 128).transpose(1, 0, 3, 2)
    grad_table = spans.reshape(SPANS * SPAN, GROUP)[:TABLE]
    vectors = slab[2 * SPANS * GROUP :]
    grad_ln1_gain, grad_ln1_shift = vectors[LN1_GAIN], vectors[LN1_SHIFT]
    grad_q_bias, grad_v_bias = vectors[Q_BIAS], vectors[V_BIAS]
    grad_proj_bias, grad_fc2_bias = vectors[PROJ_BIAS], vectors[FC2_BIAS]
    grad_ln2_gain, grad_ln2_shift = vectors[LN2_GAIN], vectors[LN2_SHIFT]
    grad_fc1_bias = vectors[FC1_BIAS : FC1_BIAS + 4].reshape(-1)
    return (
        output,
        grad_tokens,
        grad_ln1_gain,
        grad_ln1_shift,
        grad_w_qkv,
        grad_q_bias,
        grad_v_bias,
        grad_table,
        grad_w_proj,
        grad_proj_bias,
        grad_ln2_gain,
        grad_ln2_shift,
        grad_w_fc1,
        grad_fc1_bias,
        grad_w_fc2,
        grad_fc2_bias,
    )


def solution(mesh):
    return jax.shard_map(
        shards,
        mesh=mesh,
        in_specs=(
            P("rep", "shard", None, None),
            P("shard", None),
            P(),
            P("shard"),
            P("shard"),
            P("shard", None),
            P("shard"),
            P("shard"),
            P(None, "shard"),
            P("shard", None),
            P("shard"),
            P("shard"),
            P("shard"),
            P("shard", None),
            P("shard"),
            P("shard", None),
            P("shard"),
            P("rep", "shard", None, None),
        ),
        out_specs=(
            P("rep", "shard", None, None),
            P("rep", "shard", None, None),
            P("shard"),
            P("shard"),
            P("shard", None),
            P("shard"),
            P("shard"),
            P(None, "shard"),
            P("shard", None),
            P("shard"),
            P("shard"),
            P("shard"),
            P("shard", None),
            P("shard"),
            P("shard", None),
            P("shard"),
        ),
        check_vma=False,
    )
```

```python
import functools

import jax
import jax.numpy as jnp
import numpy as np
from jax import lax
from jax.experimental import pallas as pl
from jax.experimental.pallas import tpu as pltpu
from jax.sharding import PartitionSpec as P

D = 512
HEADS = 16
HD = 32
WT = 8
WH = 7
WW = 7
WIN = 392
TABLE = 2535
FF = 2048
FF_TILE = 256
PAD = 416
LANES = 512
GROUP = 4
CHUNKS = 20
SCALE = HD ** (-0.5)
NN = (((1,), (0,)), ((), ()))
NT = (((1,), (1,)), ((), ()))
TN = (((0,), (0,)), ((), ()))
VMEM_LIMIT = 60 * 2**20
f32 = jnp.float32
bf16 = jnp.bfloat16

PIECES = (
    ((0, 4), (0, 4), 112, 0),
    ((4, 8), (0, 4), 112, 112),
    ((0, 4), (4, 7), 96, 224),
    ((4, 8), (4, 7), 96, 320),
)


def send_matrix():
    matrix = np.zeros((2 * PAD, WT * WH * 2 * WW), np.float32)
    for window in range(2):
        for (t0, t1), (h0, h1), _, first in PIECES:
            row = window * PAD + first
            for t in range(t0, t1):
                for h in range(h0, h1):
                    for w in range(WW):
                        column = (window * WW + w + WW // 2) % (2 * WW)
                        source = ((t + 4) % WT * WH + (h + 3) % WH) * 2 * WW + column
                        matrix[row, source] = 1.0
                        row += 1
    return matrix


def spread_matrix():
    source = np.arange(WIN).reshape(WT, WH, WW)
    matrix = np.zeros((PAD, WIN), np.float32)
    for (t0, t1), (h0, h1), _, first in PIECES:
        tokens = source[t0:t1, h0:h1].reshape(-1)
        matrix[first + np.arange(tokens.size), tokens] = 1.0
    return matrix


def pieces_of(array, axis, fill):
    shape = array.shape
    split = array.reshape(shape[:axis] + (WT, WH, WW) + shape[axis + 1 :])
    parts = []
    for (t0, t1), (h0, h1), padded, _ in PIECES:
        part = lax.slice_in_dim(lax.slice_in_dim(split, t0, t1, axis=axis), h0, h1, axis=axis + 1)
        length = (t1 - t0) * (h1 - h0) * WW
        part = part.reshape(shape[:axis] + (length,) + shape[axis + 1 :])
        widths = [(0, 0, 0)] * len(shape)
        widths[axis] = (0, padded - length, 0)
        parts.append(lax.pad(part, jnp.asarray(fill, array.dtype), widths))
    return jnp.concatenate(parts, axis)


def dot(a, b, dims=NN):
    return lax.dot_general(a, b, dims, preferred_element_type=f32)


MESH = pl.DeviceIdType.MESH
PARTS = 8
FIRST_ROWS = tuple(first for _, _, _, first in PIECES)
LENGTHS = tuple(padded for _, _, padded, _ in PIECES)
ACROSS = (0, 2, 1, 3)
LN1_GAIN, LN1_SHIFT, Q_BIAS, V_BIAS, PROJ_BIAS, LN2_GAIN, LN2_SHIFT, FC2_BIAS, FC1_BIAS = range(9)
SMALL = 16


def place():
    rep, shard = lax.axis_index("rep"), lax.axis_index("shard")
    return rep, shard, lax.rem(rep, 2), lax.rem(rep // 2, 2), lax.rem(rep // 4, 2)


def flip(rep, bit):
    low = lax.rem(rep // (1 << bit), 2)
    return rep + (1 - 2 * low) * (1 << bit)


def remote(src, dst, send, recv, rep, shard):
    return pltpu.make_async_remote_copy(
        src_ref=src,
        dst_ref=dst,
        send_sem=send,
        recv_sem=recv,
        device_id={"rep": rep, "shard": shard},
        device_id_type=MESH,
    )


def greet(peers):
    barrier = pltpu.get_barrier_semaphore()
    for rep, shard in peers:
        pl.semaphore_signal(
            barrier, inc=1, device_id={"rep": rep, "shard": shard}, device_id_type=MESH
        )
    pl.semaphore_wait(barrier, len(peers))


def peers_of(rep, shard):
    return [(rep, lax.rem(shard + k, 4)) for k in (1, 2, 3)] + [
        (flip(rep, bit), shard) for bit in (0, 1, 2)
    ]


def quarter_across(shard, bits):
    low, high = lax.rem(shard, 2), shard // 2
    if bits & 1:
        low = 1 - low
    if bits & 2:
        high = 1 - high
    return high * 2 + low


def pieces_to(source, target, send, recv, rep, shard, window, columns=None, which=(1, 2, 3)):
    copies = []
    for piece in which:
        rows = pl.ds(
            pl.multiple_of(window * PAD + FIRST_ROWS[piece], 16), LENGTHS[piece]
        )
        at = (rows,) if columns is None else (rows, columns)
        copies.append(
            remote(
                source.at[at],
                target.at[at],
                send(piece - 1),
                recv(piece - 1),
                rep,
                quarter_across(shard, ACROSS[piece]),
            )
        )
    return copies


def norm_rows(rows):
    centre = rows - jnp.mean(rows, -1, keepdims=True)
    inverse = lax.rsqrt(jnp.mean(centre * centre, -1, keepdims=True) + 1e-05)
    return centre * inverse, inverse


def small_row(ref, row):
    return jnp.concatenate([ref[s, row : row + 1, :] for s in range(4)], 1)


FIXED = 4096.0
TAIL = 112
Z_PHASE, NEXT_PHASE, FIRST_PHASE, SECOND_PHASE, CORE_PHASE = range(5)
X_FIRST = (True, False, True, False, True)
HALF_QKV = 3 * D // 2


def front_kernel(
    tokens,
    order,
    spread,
    small,
    table,
    row_ids,
    rel,
    qkv_part,
    proj_part,
    fc1_part,
    fc2_part,
    qkv_whole_a,
    qkv_whole_b,
    proj_whole,
    fc1_whole,
    fc2_whole,
    small_out,
    rolled_out,
    mixed_out,
    attend_out,
    inverse_out,
    context_out,
    back_out,
    rel_out,
    small_all,
    table_all,
    table_wide,
    outgoing,
    arriving,
    rolled,
    weights_a,
    weights_b,
    mixed,
    index,
    index_tail,
    bias_tail,
    bias,
    mask,
    attend,
    inverse,
    contexts,
    gather_send,
    gather_recv,
    small_send,
    small_recv,
    bias_send,
    bias_recv,
    piece_send,
    piece_recv,
    back_send,
    back_recv,
    local,
    attend_sem,
):
    rep, shard, core, x_bit, y_bit = place()
    greet(peers_of(rep, shard))
    first_half, second_half = pl.ds(0, HALF_QKV), pl.ds(HALF_QKV, HALF_QKV)
    parts = (
        qkv_part.at[:, :, :, :, first_half],
        qkv_part.at[:, :, :, :, second_half],
        proj_part,
        fc1_part,
        fc2_part,
    )
    wholes = (weights_a, weights_b, proj_whole, fc1_whole, fc2_whole)
    feed_forward = (2, 3, 4)

    def gather(matrix, phase):
        copies = []
        whole = wholes[matrix]
        here = (y_bit, x_bit, core)

        def along_z(n, source, at, bits):
            return remote(
                source,
                whole.at[(at,) + here],
                gather_send.at[matrix, phase, n],
                gather_recv.at[matrix, phase, n],
                rep,
                quarter_across(shard, bits),
            )

        if phase == Z_PHASE:
            own_part = parts[matrix].at[here]
            return [along_z(0, own_part, shard, 2), along_z(1, own_part, shard, 1)]
        if phase == NEXT_PHASE:
            across = quarter_across(shard, 2)
            return [along_z(0, whole.at[(across,) + here], across, 1)]
        for k in (1, 2, 3):
            at = lax.rem(shard + k, 4)
            x_first = X_FIRST[matrix]
            if phase == FIRST_PHASE:
                block, partner = whole.at[at, y_bit, x_bit, core], flip(rep, 1 if x_first else 2)
            elif phase == SECOND_PHASE and x_first:
                block, partner = whole.at[at, y_bit, :, core], flip(rep, 2)
            elif phase == SECOND_PHASE:
                block, partner = whole.at[at, :, x_bit, core], flip(rep, 1)
            else:
                block, partner = whole.at[at, :, :, core], flip(rep, 0)
            copies.append(
                remote(
                    block,
                    block,
                    gather_send.at[matrix, phase, k - 1],
                    gather_recv.at[matrix, phase, k - 1],
                    partner,
                    shard,
                )
            )
        return copies

    def start(matrix, phase):
        for copy in gather(matrix, phase):
            copy.start()

    def arrived(matrix, phase):
        for copy in gather(matrix, phase):
            copy.wait_recv()

    def small_copies():
        copies = []
        for k in (1, 2, 3):
            for n, ref in enumerate((table_all, small_all)):
                copies.append(
                    remote(
                        ref.at[shard],
                        ref.at[shard],
                        small_send.at[n, k - 1],
                        small_recv.at[n, 3 - k],
                        rep,
                        lax.rem(shard + k, 4),
                    )
                )
        return copies

    small_all[shard] = small[...]
    table_all[shard] = table[...]
    for copy in small_copies():
        copy.start()
    start(0, Z_PHASE)
    start(1, Z_PHASE)
    own = [
        pltpu.make_async_copy(parts[m], wholes[m].at[shard], local.at[m]) for m in feed_forward
    ]
    for copy in own:
        copy.start()
    weights_a[shard] = qkv_part[..., :HALF_QKV]
    weights_b[shard] = qkv_part[..., HALF_QKV:]

    outgoing[...] = dot(order[...], tokens[...]).astype(bf16)

    def roll_copies(window):
        return pieces_to(
            outgoing,
            arriving,
            lambda n: piece_send.at[window, n],
            lambda n: piece_recv.at[window, n],
            rep,
            shard,
            window,
        )

    for copy in roll_copies(0):
        copy.start()
    for window in range(2):
        rows = slice(window * PAD, window * PAD + LENGTHS[0])
        arriving[rows, :] = outgoing[rows, :]

    rel_index = rel[...]
    digits = (rel_index // 256).astype(f32).astype(bf16), (rel_index & 255).astype(f32).astype(bf16)
    moved = []
    for digit in digits:
        half = dot(spread[...], digit).astype(bf16)
        moved.append(dot(half, spread[...], NT).astype(jnp.int32))
    index[:, :PAD] = moved[0] * 256 + moved[1]
    index[:, PAD:] = jnp.zeros((PAD, LANES - PAD), jnp.int32)

    ids = lax.broadcasted_iota(jnp.int32, (8, LANES), 0)
    for window in range(2):
        kinds = jnp.where(row_ids[window] + 1 == ids, 1.0, 0.0).astype(bf16)[:, :PAD]
        mask[window] = (dot(kinds, kinds, TN) - 1.0) * 1e30

    for copy in small_copies():
        copy.wait_recv()

    for block in range(4):
        count = min(TAIL, PAD - block * TAIL)
        lanes = slice(block * 32, block * 32 + 32)
        index_tail[:count, lanes] = index[block * TAIL : block * TAIL + count, PAD - 32 : PAD]
        if count < TAIL:
            index_tail[count:, lanes] = jnp.zeros((TAIL - count, 32), jnp.int32)

    upper, lower = (
        jnp.floor(table_all[2 * core + n] * FIXED + 0.5).astype(jnp.int32) for n in range(2)
    )
    words = upper * 65536 + (lower + 32768)
    for chunk in range(CHUNKS):
        for head in range(GROUP):
            row = head * CHUNKS + chunk
            table_wide[chunk, head] = jnp.broadcast_to(words[row : row + 1, :], (8, 128))
    mine = core * (HEADS // 2)

    def bias_copy(rows, step):
        block = bias.at[pl.ds(mine, HEADS // 2), rows]
        return remote(block, block, bias_send.at[step], bias_recv.at[step], flip(rep, 0), shard)

    def on_the_way(step, table_of_steps):
        for when, actions in table_of_steps.items():

            @pl.when(step == when)
            def _():
                for action, matrix, phase in actions:
                    action(matrix, phase)

    def advance(matrix, phase):
        arrived(matrix, phase)
        if phase < CORE_PHASE:
            start(matrix, phase + 1)

    schedule = {
        4: [(advance, 0, Z_PHASE), (advance, 1, Z_PHASE)],
        11: [(advance, 0, NEXT_PHASE), (advance, 1, NEXT_PHASE)]
        + [(start, m, Z_PHASE) for m in feed_forward],
        18: [(advance, 0, FIRST_PHASE), (advance, 1, FIRST_PHASE)],
    }
    later = {
        1: [(advance, m, Z_PHASE) for m in feed_forward],
        5: [(advance, m, NEXT_PHASE) for m in feed_forward],
        10: [(advance, m, FIRST_PHASE) for m in feed_forward],
    }

    def look_up(here):
        found = [[] for _ in range(GROUP)]
        for s in (0, 8):
            low, high = here[s : s + 8] & 127, here[s : s + 8] >> 7
            values = [None] * GROUP
            for chunk in range(CHUNKS):
                hit = high == chunk
                for head in range(GROUP):
                    value = jnp.take_along_axis(table_wide[chunk, head], low, axis=1)
                    values[head] = jnp.where(hit, value, values[head]) if chunk else value
            for head in range(GROUP):
                found[head].append(values[head])
        joined = [jnp.concatenate(pair, 0) for pair in found]
        uppers = [(word >> 16).astype(f32) for word in joined]
        lowers = [((word & 65535) - 32768).astype(f32) for word in joined]
        return [(value * (1 / FIXED)).astype(bf16) for value in uppers + lowers]

    def tail_step(step, carry):
        rows = pl.ds(pl.multiple_of(step * 16, 16), 16)
        for head, value in enumerate(look_up(index_tail[rows, :])):
            bias_tail[head, rows, :] = value
        return carry

    lax.fori_loop(0, TAIL // 16, tail_step, 0)

    def untail_step(head, carry):
        for block in range(4):
            count = min(TAIL, PAD - block * TAIL)
            value = bias_tail[head, :count, block * 32 : block * 32 + 32]
            bias[mine + head, block * TAIL : block * TAIL + count, PAD - 32 : PAD] = value
        return carry

    lax.fori_loop(0, HEADS // 2, untail_step, 0)

    def bias_step(step, carry):
        on_the_way(step, schedule)
        rows = pl.ds(pl.multiple_of(step * 16, 16), 16)
        for tile in range(3):
            lanes = slice(tile * 128, (tile + 1) * 128)
            for head, value in enumerate(look_up(index[rows, lanes])):
                bias[mine + head, rows, lanes] = value
        bias_copy(rows, step).start()
        return carry

    lax.fori_loop(0, PAD // 16, bias_step, 0)
    for copy in roll_copies(1):
        copy.start()
    for n in range(2):
        advance(n, SECOND_PHASE)

    for n in range(2):
        arrived(n, CORE_PHASE)
    q_bias, v_bias = small_row(small_all, Q_BIAS), small_row(small_all, V_BIAS)
    mixed_bias = jnp.concatenate([q_bias, jnp.zeros_like(q_bias), v_bias], 1).astype(f32)
    gain, shift = small_row(small_all, LN1_GAIN), small_row(small_all, LN1_SHIFT)

    def norm_step(step, carry):
        rows = pl.ds(pl.multiple_of(step * 208, 16), 208)
        normal, _ = norm_rows(arriving[rows, :].astype(f32))
        rolled[rows, :] = (normal * gain.astype(f32) + shift.astype(f32)).astype(bf16)
        return carry

    def mix(window):
        for copy in roll_copies(window):
            copy.wait_recv()
        lax.fori_loop(2 * window, 2 * window + 2, norm_step, 0)
        span = slice(window * PAD, (window + 1) * PAD)
        for n, weight in enumerate((weights_a, weights_b)):
            lanes = slice(n * HALF_QKV, (n + 1) * HALF_QKV)
            got = dot(rolled[span, :], weight[...].reshape(D, HALF_QKV))
            mixed[span, lanes] = (got + mixed_bias[:, lanes]).astype(bf16)

    mix(0)
    keep = [
        pltpu.make_async_copy(rolled, rolled_out, local.at[5]),
        pltpu.make_async_copy(mixed, mixed_out, local.at[6]),
        pltpu.make_async_copy(index, rel_out, local.at[7]),
        pltpu.make_async_copy(small_all, small_out, local.at[8]),
        pltpu.make_async_copy(inverse, inverse_out, local.at[9]),
        pltpu.make_async_copy(contexts, context_out, local.at[12]),
        pltpu.make_async_copy(weights_a, qkv_whole_a, local.at[0]),
        pltpu.make_async_copy(weights_b, qkv_whole_b, local.at[1]),
    ]

    def bias_wait(step, carry):
        bias_copy(pl.ds(pl.multiple_of(step * 16, 16), 16), step).wait_recv()
        return carry

    lax.fori_loop(0, PAD // 16, bias_wait, 0)

    head_of = lax.broadcasted_iota(jnp.int32, (1, 128), 1) // HD
    none = jnp.zeros((), bf16)
    ones = jnp.ones((PAD, 128), bf16)

    def attend_copy(step):
        window, pair, slot = step // (HEADS // 2), lax.rem(step, HEADS // 2), lax.rem(step, 2)
        return pltpu.make_async_copy(
            attend.at[slot], attend_out.at[window, pl.ds(2 * pair, 2)], attend_sem.at[slot]
        )

    def back_copies(step):
        window, group = step // (HEADS // 2), lax.rem(step // 2, HEADS // GROUP)
        lanes = pl.ds(pl.multiple_of(group * 128, 128), 128)
        return pieces_to(
            contexts,
            back_out,
            lambda n: back_send.at[window, group, n],
            lambda n: back_recv.at[window, group, n],
            rep,
            shard,
            window,
            lanes,
        )

    def attend_step(step, carry):
        on_the_way(step, later)

        @pl.when(step == HEADS // 2)
        def _():
            mix(1)

        @pl.when(step >= 2)
        def _():
            attend_copy(step - 2).wait()

        window, slot = step // (HEADS // 2), lax.rem(step, 2)
        rows = pl.ds(pl.multiple_of(window * PAD, 16), PAD)
        for n in range(2):
            head = 2 * lax.rem(step, HEADS // 2) + n
            group, member = head // GROUP, lax.rem(head, GROUP)

            def lanes(part):
                return pl.ds(pl.multiple_of(part * D + group * 128, 128), 128)

            own_lanes = head_of == member
            query = jnp.where(own_lanes, mixed[rows, lanes(0)], none)
            value = jnp.where(own_lanes, mixed[rows, lanes(2)], none)
            scores = dot(query, mixed[rows, lanes(1)], NT) * SCALE
            scores = scores + bias[head, :, :PAD].astype(f32) + mask[window]
            expo = jnp.exp(scores - jnp.max(scores, -1, keepdims=True)).astype(bf16)
            attend[slot, n, :, :PAD] = expo
            result = dot(expo, jnp.concatenate([value, ones], 1))
            over = 1.0 / result[:, 128:]
            context = (result[:, :128] * over).astype(bf16)
            contexts[rows, lanes(0)] = jnp.where(own_lanes, context, contexts[rows, lanes(0)])
            inverse[rows, lanes(0)] = jnp.where(own_lanes, over, inverse[rows, lanes(0)])
        attend_copy(step).start()

        @pl.when(lax.rem(step, 2) == 1)
        def _():
            for copy in back_copies(step):
                copy.start()

        return carry

    lax.fori_loop(0, HEADS, attend_step, 0)
    for copy in keep:
        copy.start()
    for matrix in feed_forward:
        advance(matrix, SECOND_PHASE)
    stay = [
        pltpu.make_async_copy(
            contexts.at[pl.ds(w * PAD, LENGTHS[0])],
            back_out.at[pl.ds(w * PAD, LENGTHS[0])],
            local.at[10 + w],
        )
        for w in range(2)
    ]
    for copy in stay:
        copy.start()
    for matrix in feed_forward:
        arrived(matrix, CORE_PHASE)
    attend_copy(HEADS - 2).wait()
    attend_copy(HEADS - 1).wait()

    def back_wait(step, carry):
        for copy in back_copies(step * 2):
            copy.wait()
        return carry

    lax.fori_loop(0, 2 * HEADS // GROUP, back_wait, 0)

    def bias_sent(step, carry):
        bias_copy(pl.ds(pl.multiple_of(step * 16, 16), 16), step).wait_send()
        return carry

    lax.fori_loop(0, PAD // 16, bias_sent, 0)
    for copy in small_copies():
        copy.wait_send()
    for window in range(2):
        for copy in roll_copies(window):
            copy.wait_send()
    for matrix in range(5):
        for phase in range(CORE_PHASE + 1):
            for copy in gather(matrix, phase):
                copy.wait_send()
    for copy in own + keep + stay:
        copy.wait()


def front(tokens, small, table, row_ids, rel_index, w_qkv, w_proj, w_fc1, w_fc2):
    anywhere, inside = pl.BlockSpec(memory_space=pl.ANY), pl.BlockSpec(memory_space=pltpu.VMEM)
    cut = (2, 2, 2)
    weights = [
        w.reshape(cut + (w.shape[0] // PARTS, w.shape[1])) for w in (w_qkv, w_proj, w_fc1, w_fc2)
    ]
    half = (4,) + weights[0].shape[:-1] + (HALF_QKV,)
    wholes = [jax.ShapeDtypeStruct(half, bf16)] * 2
    wholes += [jax.ShapeDtypeStruct((4,) + w.shape, bf16) for w in weights[1:]]
    dma = pltpu.SemaphoreType.DMA
    results = pl.pallas_call(
        front_kernel,
        out_shape=(
            *wholes,
            jax.ShapeDtypeStruct((4, SMALL, 128), bf16),
            jax.ShapeDtypeStruct((2 * PAD, D), bf16),
            jax.ShapeDtypeStruct((2 * PAD, 3 * D), bf16),
            jax.ShapeDtypeStruct((2, HEADS, PAD, LANES), bf16),
            jax.ShapeDtypeStruct((2 * PAD, D), f32),
            jax.ShapeDtypeStruct((2 * PAD, D), bf16),
            jax.ShapeDtypeStruct((2 * PAD, D), bf16),
            jax.ShapeDtypeStruct((PAD, LANES), jnp.int32),
        ),
        in_specs=[inside] * 11,
        out_specs=(anywhere,) * 13,
        scratch_shapes=[
            pltpu.VMEM((4, SMALL, 128), bf16),
            pltpu.VMEM((4, GROUP * CHUNKS, 128), f32),
            pltpu.VMEM((CHUNKS, GROUP, 8, 128), jnp.int32),
            pltpu.VMEM((2 * PAD, D), bf16),
            pltpu.VMEM((2 * PAD, D), bf16),
            pltpu.VMEM((2 * PAD, D), bf16),
            pltpu.VMEM(half, bf16),
            pltpu.VMEM(half, bf16),
            pltpu.VMEM((2 * PAD, 3 * D), bf16),
            pltpu.VMEM((PAD, LANES), jnp.int32),
            pltpu.VMEM((TAIL, 128), jnp.int32),
            pltpu.VMEM((HEADS // 2, TAIL, 128), bf16),
            pltpu.VMEM((HEADS, PAD, LANES), bf16),
            pltpu.VMEM((2, PAD, PAD), f32),
            pltpu.VMEM((2, 2, PAD, LANES), bf16),
            pltpu.VMEM((2 * PAD, D), f32),
            pltpu.VMEM((2 * PAD, D), bf16),
            dma((5, CORE_PHASE + 1, 3)),
            dma((5, CORE_PHASE + 1, 3)),
            dma((2, 3)),
            dma((2, 3)),
            dma((PAD // 16,)),
            dma((PAD // 16,)),
            dma((2, 3)),
            dma((2, 3)),
            dma((2, HEADS // GROUP, 3)),
            dma((2, HEADS // GROUP, 3)),
            dma((13,)),
            dma((2,)),
        ],
        compiler_params=pltpu.CompilerParams(
            vmem_limit_bytes=VMEM_LIMIT, collective_id=0, has_side_effects=True
        ),
        name="front",
    )(
        tokens,
        jnp.asarray(send_matrix(), bf16),
        jnp.asarray(spread_matrix(), bf16),
        small,
        table,
        row_ids,
        rel_index,
        *weights,
    )
    whole = [w.reshape(-1, w.shape[-1]) for w in results[:5]]
    return (*whole, *results[5:])


CORE_SUM, FIRST_SUM, SECOND_SUM, NEXT_SUM, Z_SUM, SHARE, CORE_SHARE = range(7)
SUMMED = ((16, 2048, True), (64, 512, False), (16, 512, True))
SUMMED += tuple((16, 3 * 128, group % 2 == 0) for group in range(HEADS // GROUP))
FC1, FC2, PROJ, QKV = range(4)
STRIDE = HEADS + 1
CHUNK_ROWS = ((0, 400, (1, 3)), (400, 384, (0, 2)))
SPAN = 256
SPANS = -(-TABLE // SPAN)
BATCH = 16
HALF = PAD // 2
TILES = LANES // 128
TABLE_ROWS = 2 * SPANS * GROUP
SLAB = TABLE_ROWS + SMALL


def rear_kernel(
    order_back,
    tokens,
    small_all,
    returned_in,
    order_in,
    cotangent_in,
    proj_in,
    fc1_in,
    fc2_in,
    weights_a_in,
    weights_b_in,
    rolled_in,
    mixed_in,
    inverse_in,
    contexts_in,
    rel_in,
    attend_in,
    output,
    grad_tokens,
    fc1_out,
    fc2_out,
    proj_out,
    qkv_out_0,
    qkv_out_1,
    qkv_out_2,
    qkv_out_3,
    slab_out,
    weights_a,
    weights_b,
    rolled,
    mixed,
    inverse,
    contexts,
    rel,
    outgoing,
    grad_context,
    grad_middle,
    returned,
    pairs_in,
    fc1_grad,
    fc2_grad,
    proj_grad,
    qkv_grads,
    sums,
    fc1_sum,
    table_sum,
    slab,
    slab_z,
    slab_rep,
    *rest,
):
    count = len(SUMMED)
    held = [rest[6 * m : 6 * m + 6] for m in range(count)]
    (
        sum_send,
        sum_recv,
        extra_send,
        extra_recv,
        piece_send,
        piece_recv,
        back_send,
        back_recv,
        attend_sem,
        pairs_send,
        pairs_recv,
        slab_send,
        slab_recv,
        local,
        load,
    ) = rest[6 * count :]
    rep, shard, core, x_bit, y_bit = place()
    reps = lax.axis_size("rep")
    barrier = pltpu.get_barrier_semaphore()

    def hello(k, carry):
        pl.semaphore_signal(
            barrier,
            inc=1,
            device_id={"rep": lax.rem(rep + k, reps), "shard": shard},
            device_id_type=MESH,
        )
        return carry

    lax.fori_loop(1, reps, hello, 0)
    for k in (1, 2, 3):
        pl.semaphore_signal(
            barrier,
            inc=1,
            device_id={"rep": rep, "shard": lax.rem(shard + k, 4)},
            device_id_type=MESH,
        )
    pl.semaphore_wait(barrier, reps + 2)

    sources = (fc1_grad, fc2_grad, proj_grad) + tuple(qkv_grads.at[g] for g in range(4))

    def axis_of(matrix, first):
        x_first = SUMMED[matrix][2]
        use_x = x_first == first
        return (1, x_bit) if use_x else (2, y_bit)

    def sum_copies(matrix, phase):
        from_core, from_first, summed, from_next, from_z, shared = held[matrix]
        source = sources[matrix]
        x_first = SUMMED[matrix][2]
        first_bit, first = axis_of(matrix, True)
        second_bit, second = axis_of(matrix, False)

        def one(src, dst, bit, n=0):
            return remote(
                src,
                dst,
                sum_send.at[matrix, phase, n],
                sum_recv.at[matrix, phase, n],
                flip(rep, bit),
                shard,
            )

        if phase == CORE_SUM:
            return [one(source.at[:, :, :, 1 - core], from_core, 0)]
        if phase == FIRST_SUM:
            cut = source.at[:, :, 1 - x_bit, core] if x_first else source.at[:, 1 - y_bit, :, core]
            return [one(cut, from_first, first_bit)]
        if phase == SECOND_SUM:
            return [one(from_first.at[:, 1 - second], summed, second_bit)]
        if phase in (NEXT_SUM, Z_SUM):
            low, high = lax.rem(shard, 2), shard // 2
            if phase == NEXT_SUM:
                moves = [(2 * n + 1 - low, from_next.at[n]) for n in range(2)]
            else:
                moves = [(2 * (1 - high) + low, from_z.at[0])]
            return [
                remote(
                    summed.at[owner],
                    target,
                    sum_send.at[matrix, phase, n],
                    sum_recv.at[matrix, phase, n],
                    rep,
                    quarter_across(shard, 1 if phase == NEXT_SUM else 2),
                )
                for n, (owner, target) in enumerate(moves)
            ]
        if phase == CORE_SHARE:
            block = shared.at[:, :, core]
            return [one(block, block, 0)]
        block = shared.at[y_bit, x_bit, core]
        across = flip(flip(rep, 1), 2)
        return [
            remote(
                block,
                block,
                sum_send.at[matrix, phase, n],
                sum_recv.at[matrix, phase, n],
                partner,
                shard,
            )
            for n, partner in enumerate((flip(rep, 1), flip(rep, 2), across))
        ]

    def extra_copy(matrix, bit):
        shared, from_z = held[matrix][5], held[matrix][4]
        return remote(
            shared.at[y_bit, x_bit, core],
            from_z.at[bit - 2],
            extra_send.at[matrix, bit - 3],
            extra_recv.at[matrix, bit - 3],
            flip(rep, bit),
            shard,
        )

    def add(into, at, other, other_at):
        into[at] = into[at] + other[other_at]

    def begin(matrix):
        for copy in sum_copies(matrix, CORE_SUM):
            copy.start()

    def advance(matrix, phase):
        from_core, from_first, summed, from_next, from_z, shared = held[matrix]
        source = sources[matrix]
        x_first = SUMMED[matrix][2]
        _, second = axis_of(matrix, False)
        for copy in sum_copies(matrix, phase):
            copy.wait_recv()
        if phase == CORE_SUM:

            def step(n, carry):
                at = (n // 4, lax.rem(n // 2, 2), lax.rem(n, 2))
                add(source, at + (core,), from_core, at)
                return carry

            lax.fori_loop(0, 16, step, 0)
        elif phase == FIRST_SUM:

            def step(n, carry):
                owner, other = n // 2, lax.rem(n, 2)
                at = (owner, other, x_bit) if x_first else (owner, y_bit, other)
                add(from_first, (owner, other), source, at + (core,))
                return carry

            lax.fori_loop(0, 8, step, 0)
        elif phase == SECOND_SUM:

            def step(owner, carry):
                add(summed, (owner,), from_first, (owner, second))
                return carry

            lax.fori_loop(0, 4, step, 0)
        elif phase == NEXT_SUM:
            low = lax.rem(shard, 2)
            for high in range(2):
                add(summed, (2 * high + low,), from_next, (high,))
        elif phase == Z_SUM:
            total = summed[shard].astype(f32) + from_z[0].astype(f32)
            shared[y_bit, x_bit, core] = total.astype(bf16)
            bit = 3
            while (1 << bit) < reps:
                copy = extra_copy(matrix, bit)
                copy.start()
                copy.wait()
                at = (y_bit, x_bit, core)
                add(shared, at, from_z, (bit - 2,))
                bit += 1
        if phase < CORE_SHARE:
            for copy in sum_copies(matrix, phase + 1):
                copy.start()

    def on_the_way(step, table_of_steps):
        for when, actions in table_of_steps.items():

            @pl.when(step == when)
            def _():
                for matrix, phase in actions:
                    advance(matrix, phase)

    fetched = (
        (weights_a_in, weights_a),
        (weights_b_in, weights_b),
        (rolled_in, rolled),
        (mixed_in, mixed),
        (inverse_in, inverse),
        (contexts_in, contexts),
        (rel_in, rel),
    )
    fetches = [
        pltpu.make_async_copy(src, dst, load.at[n]) for n, (src, dst) in enumerate(fetched)
    ]

    def roll_copies(window, which=(1, 2, 3)):
        return pieces_to(
            outgoing,
            grad_context,
            lambda n: piece_send.at[window, n],
            lambda n: piece_recv.at[window, n],
            rep,
            shard,
            window,
            which=which,
        )

    def feed_forward(
        proj,
        fc1,
        fc2,
        middle,
        normed,
        normed_back,
        active,
        grad_hidden,
        grad_normed,
        branch,
        unrolled,
        grad_unrolled,
        final,
        fc1_bias,
        returned_context,
        order,
        cotangent,
    ):
        loads = [
            pltpu.make_async_copy(src, dst, load.at[len(fetched) + n])
            for n, (src, dst) in enumerate(
                (
                    (returned_in, returned_context),
                    (proj_in, proj),
                    (cotangent_in, cotangent),
                    (fc1_in, fc1),
                    (fc2_in, fc2),
                    (order_in, order),
                )
            )
        ]
        for copy in loads:
            copy.start()
        proj_bias = small_row(small_all, PROJ_BIAS).astype(f32)
        gain, shift = (small_row(small_all, row).astype(f32) for row in (LN2_GAIN, LN2_SHIFT))
        fc2_bias = small_row(small_all, FC2_BIAS).astype(f32)
        for owner in range(4):
            for k in range(4):
                lanes = slice(owner * D + k * 128, owner * D + (k + 1) * 128)
                fc1_bias[:, lanes] = small_all[owner, FC1_BIAS + k : FC1_BIAS + k + 1, :].astype(f32)
        sums[...] = jnp.zeros_like(sums)
        fc1_sum[...] = jnp.zeros_like(fc1_sum)
        for copy in loads[:2]:
            copy.wait()
        for first, length, _ in CHUNK_ROWS:
            rows = pl.ds(first, length)
            unrolled[rows, :] = dot(order_back[rows, :], returned_context[...]).astype(bf16)
            got = dot(unrolled[rows, :], proj[...]) + proj_bias
            middle[rows, :] = tokens[rows, :].astype(f32) + got
            normal, _ = norm_rows(middle[rows, :])
            normed[rows, :] = (normal * gain + shift).astype(bf16)
        for copy in loads[2:]:
            copy.wait()

        def forward_step(tile, carry):
            for n in range(2):
                lanes = pl.ds(pl.multiple_of((2 * tile + n) * FF_TILE, FF_TILE), FF_TILE)
                hidden = dot(normed[...], fc1[:, lanes]) + fc1_bias[:, lanes]
                share = 0.5 + 0.5 * lax.erf(hidden * 0.7071067811865476)
                active[:, lanes] = (hidden * share).astype(bf16)
                slope = share + hidden * jnp.exp(-0.5 * hidden * hidden) * 0.3989422804014327
                grad_hidden[:, lanes] = slope.astype(bf16)
            return carry

        for copy in fetches:
            copy.start()
        lax.fori_loop(0, FF // FF_TILE // 2, forward_step, 0)

        def fc2_step(tile, carry):
            lanes = pl.ds(pl.multiple_of(tile * 256, 256), 256)
            got = dot(active[:, lanes], cotangent[...], TN).astype(bf16)
            fc2_grad[tile // 2, lax.rem(tile, 2)] = got.reshape(2, 2, 64, D)
            return carry

        lax.fori_loop(0, FF // 256, fc2_step, 0)
        begin(FC2)
        for first, length, pieces in CHUNK_ROWS:
            rows = pl.ds(first, length)

            def backward_step(tile, carry):
                lanes = pl.ds(pl.multiple_of(tile * D, D), D)
                grad_active = dot(cotangent[rows, :], fc2[lanes, :], NT)
                grad = (grad_active * grad_hidden[rows, lanes].astype(f32)).astype(bf16)
                grad_hidden[rows, lanes] = grad
                fc1_sum[:, lanes] += jnp.sum(grad.astype(f32), 0, keepdims=True)
                return carry

            lax.fori_loop(0, FF // D, backward_step, 0)
            grad_normed[rows, :] = dot(grad_hidden[rows, :], fc1[...], NT)
            normal, over = norm_rows(middle[rows, :])
            grad_out = grad_normed[rows, :]
            scaled = grad_out * gain
            inner = (
                scaled
                - jnp.mean(scaled, -1, keepdims=True)
                - normal * jnp.mean(scaled * normal, -1, keepdims=True)
            )
            upper = cotangent[rows, :].astype(f32)
            grad_middle[rows, :] = upper + over * inner
            branch[rows, :] = grad_middle[rows, :].astype(bf16)
            for row, value in (
                (PROJ_BIAS, branch[rows, :].astype(f32)),
                (LN2_GAIN, grad_out * normal),
                (LN2_SHIFT, grad_out),
                (FC2_BIAS, upper),
            ):
                sums[row : row + 1, :] += jnp.sum(value, 0, keepdims=True)
            grad_unrolled[rows, :] = dot(branch[rows, :], proj[...], NT).astype(bf16)
            source = pl.ds(0, 400) if first == 0 else pl.ds(384, 400)
            for window in range(2):
                for piece in pieces:
                    at = pl.ds(window * PAD + FIRST_ROWS[piece], LENGTHS[piece])
                    got = dot(order[at, source], grad_unrolled[source, :]).astype(bf16)
                    if piece:
                        outgoing[at, :] = got
                    else:
                        grad_context[at, :] = got
            for window in range(2):
                for copy in roll_copies(window, [piece for piece in pieces if piece]):
                    copy.start()
        same = lax.broadcasted_iota(jnp.int32, (D, D), 0) == lax.broadcasted_iota(
            jnp.int32, (D, D), 1
        )
        unit = jnp.where(same, jnp.ones((), bf16), jnp.zeros((), bf16))
        normed_back[...] = dot(unit, normed[...], NT).astype(bf16)

        def fc1_step(tile, carry):
            lanes = pl.ds(pl.multiple_of(tile * 512, 512), 512)
            got = dot(normed_back[...], grad_hidden[:, lanes]).astype(bf16)
            fc1_grad[:, :, :, :, :, lanes] = got.reshape(4, 2, 2, 2, 16, 512)
            return carry

        lax.fori_loop(0, FF // 512, fc1_step, 0)
        begin(FC1)

        got = dot(unrolled[...], branch[...], TN).astype(bf16)
        proj_grad[...] = got.reshape(proj_grad.shape)
        begin(PROJ)
        advance(FC2, CORE_SUM)
        final[...] = (middle[...] + dot(active[...], fc2[...]) + fc2_bias).astype(bf16)
        written = pltpu.make_async_copy(final, output, load.at[len(fetched) + 6])
        written.start()
        for matrix in (FC1, PROJ):
            advance(matrix, CORE_SUM)
        written.wait()

    count_rows = tokens.shape[0]
    pl.run_scoped(
        feed_forward,
        pltpu.VMEM((D, D), bf16),
        pltpu.VMEM((D, FF), bf16),
        pltpu.VMEM((FF, D), bf16),
        pltpu.VMEM((count_rows, D), f32),
        pltpu.VMEM((count_rows, D), bf16),
        pltpu.VMEM((D, count_rows), bf16),
        pltpu.VMEM((count_rows, FF), bf16),
        pltpu.VMEM((count_rows, FF), bf16),
        pltpu.VMEM((count_rows, D), f32),
        pltpu.VMEM((count_rows, D), bf16),
        pltpu.VMEM((count_rows, D), bf16),
        pltpu.VMEM((count_rows, D), bf16),
        pltpu.VMEM((count_rows, D), bf16),
        pltpu.VMEM((1, FF), f32),
        pltpu.VMEM((2 * PAD, D), bf16),
        pltpu.VMEM((2 * PAD, count_rows), bf16),
        pltpu.VMEM((count_rows, D), bf16),
    )
    for copy in fetches:
        copy.wait()
    def return_copies(window):
        return pieces_to(
            outgoing,
            returned,
            lambda n: back_send.at[window, n],
            lambda n: back_recv.at[window, n],
            rep,
            shard,
            window,
        )

    def attend_back(attend, grads, rolled_back, pairs, pairs_out):
        head_of = lax.broadcasted_iota(jnp.int32, (1, 128), 1) // HD
        none = jnp.zeros((), bf16)

        def attend_copy(head):
            slot = lax.rem(head, 2)
            return pltpu.make_async_copy(
                attend_in.at[:, head], attend.at[slot], attend_sem.at[slot]
            )

        attend_copy(0).start()
        same = lax.broadcasted_iota(jnp.int32, (D, D), 0) == lax.broadcasted_iota(
            jnp.int32, (D, D), 1
        )
        unit = jnp.where(same, jnp.ones((), bf16), none)
        rolled_back[...] = dot(unit, rolled[...], NT).astype(bf16)

        def qkv_group(group):
            columns = [
                grads[:, part * D + group * 128 : part * D + (group + 1) * 128] for part in range(3)
            ]
            got = dot(rolled_back[...], jnp.concatenate(columns, 1)).astype(bf16)
            qkv_grads[group] = got.reshape(qkv_grads.shape[1:])
            begin(QKV + group)

        slow = (FC1, PROJ)
        first_schedule = {
            0: [(FC2, FIRST_SUM)],
            6: [(QKV, CORE_SUM)],
            8: [(FC2, SECOND_SUM)],
            9: [(QKV, FIRST_SUM)],
            10: [(QKV + 1, CORE_SUM)] + [(m, FIRST_SUM) for m in slow],
            12: [(QKV, SECOND_SUM), (FC2, NEXT_SUM)],
            13: [(QKV + 1, FIRST_SUM)],
            14: [(QKV + 2, CORE_SUM)],
            15: [(QKV, NEXT_SUM), (FC2, Z_SUM)],
        }
        second_schedule = {
            0: [(QKV + 1, SECOND_SUM), (QKV + 2, FIRST_SUM)] + [(m, SECOND_SUM) for m in slow],
            1: [(QKV, Z_SUM), (QKV + 3, CORE_SUM), (QKV + 1, NEXT_SUM)],
            2: [(QKV + 2, SECOND_SUM)],
            3: [(QKV + 3, FIRST_SUM), (QKV + 1, Z_SUM), (FC2, SHARE)],
            4: [(QKV + 2, NEXT_SUM), (QKV, SHARE)] + [(m, NEXT_SUM) for m in slow],
            5: [(QKV + 3, SECOND_SUM)],
            6: [(QKV + 2, Z_SUM)],
            7: [(QKV + 3, NEXT_SUM), (QKV + 1, SHARE)] + [(m, Z_SUM) for m in slow],
            9: [(QKV + 3, Z_SUM), (QKV + 2, SHARE)],
            12: [(QKV + 3, SHARE)] + [(m, SHARE) for m in slow],
        }

        for window in range(2):
            for copy in roll_copies(window):
                copy.wait_recv()

        def head_step(head, carry):
            on_the_way(head, first_schedule)
            for done in range(1, HEADS // GROUP):

                @pl.when(head == done * GROUP)
                def _():
                    qkv_group(done - 1)

            @pl.when(head + 1 < HEADS)
            def _():
                attend_copy(head + 1).start()

            attend_copy(head).wait()
            slot = lax.rem(head, 2)
            group, member = head // GROUP, lax.rem(head, GROUP)

            def lanes(part):
                return pl.ds(pl.multiple_of(part * D + group * 128, 128), 128)

            mine = head_of == member
            both = []
            for window in range(2):
                rows = pl.ds(window * PAD, PAD)
                query = jnp.where(mine, mixed[rows, lanes(0)], none)
                key = jnp.where(mine, mixed[rows, lanes(1)], none)
                grad = grad_context[rows, lanes(0)].astype(f32) * inverse[rows, lanes(0)]
                grad = jnp.where(mine, grad, 0.0).astype(bf16)
                expo = attend[slot, window, :, :PAD]
                grad_attend = dot(grad, mixed[rows, lanes(2)], NT)
                inner = jnp.sum(
                    grad.astype(f32) * contexts[rows, lanes(0)].astype(f32), -1, keepdims=True
                )
                grad_scores = (expo.astype(f32) * (grad_attend - inner)).astype(bf16)
                both.append(grad_scores)
                for part, value in (
                    (0, dot(grad_scores, key) * SCALE),
                    (1, dot(grad_scores, query, TN) * SCALE),
                    (2, dot(expo, grad, TN)),
                ):
                    grads[rows, lanes(part)] = jnp.where(
                        mine, value.astype(bf16), grads[rows, lanes(part)]
                    )
            total = both[0].astype(f32) + both[1].astype(f32)
            for tile in range(TILES):
                part = total[:, tile * 128 : (tile + 1) * 128]
                if part.shape[1] < 128:
                    part = jnp.concatenate([part, jnp.zeros((PAD, 128 - part.shape[1]), f32)], 1)
                pairs[tile, pl.ds(head, PAD, stride=STRIDE), :] = part
            return carry

        lax.fori_loop(0, HEADS, head_step, 0)

        for window in range(2):
            for copy in roll_copies(window):
                copy.wait_send()

        for window in range(2):
            span = slice(window * PAD, (window + 1) * PAD)
            got = dot(grads[span, :HALF_QKV], weights_a[...], NT)
            got = got + dot(grads[span, HALF_QKV:], weights_b[...], NT)
            outgoing[span, :] = got.astype(bf16)
            for copy in return_copies(window):
                copy.start()
            rows = slice(window * PAD, window * PAD + LENGTHS[0])
            returned[rows, :] = outgoing[rows, :]
        qkv_group(HEADS // GROUP - 1)

        def round_step(step, carry):
            source = pl.ds(((1 - core) * HALF + step) * STRIDE, HEADS)
            at = pl.ds(pl.multiple_of(step * HEADS, HEADS), HEADS)
            for tile in range(TILES):
                pairs_out[tile, at, :] = pairs[tile, source, :].astype(bf16)
            return carry

        def pairs_copy(half):
            block = pl.ds(half * (HALF * HEADS // 2), HALF * HEADS // 2)
            return remote(
                pairs_out.at[:, block],
                pairs_in.at[:, block],
                pairs_send.at[half],
                pairs_recv.at[half],
                flip(rep, 0),
                shard,
            )

        for half in range(2):
            lax.fori_loop(half * (HALF // 2), (half + 1) * (HALF // 2), round_step, 0)
            pairs_copy(half).start()

        low_of = lax.broadcasted_iota(jnp.int32, (SPAN, LANES - 128), 0).astype(f32).astype(bf16)
        table_sum[...] = jnp.zeros_like(table_sum)
        for half in range(2):
            pairs_copy(half).wait_recv()

        def operands(total, index):
            width = index.shape[1]
            low = (index & (SPAN - 1)).astype(f32).astype(bf16)
            high = jnp.broadcast_to((index // SPAN).astype(f32).astype(bf16), (HEADS, width))
            nothing = jnp.zeros_like(total)
            left = jnp.concatenate(
                [jnp.where(high == jnp.asarray(s, bf16), total, nothing) for s in range(SPANS)], 0
            )
            hit = low_of[:, :width] == jnp.broadcast_to(low, (SPAN, width))
            return left, jnp.where(hit, jnp.ones((), bf16), jnp.zeros((), bf16))

        lane_of = lax.broadcasted_iota(jnp.int32, (1, 128), 1)

        def table_step(step, carry):
            on_the_way(step, second_schedule)
            factors = []
            for k in range(BATCH):
                row = step * BATCH + k
                there = core * HALF + row
                at = pl.ds(there * STRIDE, HEADS)
                near = pl.ds(pl.multiple_of(row * HEADS, HEADS), HEADS)
                index = rel[pl.ds(there, 1), :]
                sums_of = [pairs[t, at, :] + pairs_in[t, near, :].astype(f32) for t in range(TILES)]
                total = jnp.concatenate(sums_of[:-1], 1).astype(bf16)
                factors.append(operands(total, index[:, : LANES - 128]))
                last, places, turn = sums_of[-1], index[:, LANES - 128 :], 32 * (k % 4)
                if turn:
                    last = tail + pltpu.roll(last, turn, 1)
                    places = jnp.where(lane_of >= turn, pltpu.roll(places, turn, 1), tail_places)
                tail, tail_places = last, places
                if k % 4 == 3:
                    factors.append(operands(tail.astype(bf16), tail_places))
            left, right = zip(*factors)
            table_sum[...] += dot(jnp.concatenate(left, 1), jnp.concatenate(right, 1), NT)
            return carry

        lax.fori_loop(0, HALF // BATCH, table_step, 0)
        for half in range(2):
            pairs_copy(half).wait_send()
        sums[Q_BIAS : Q_BIAS + 1, :] = jnp.sum(grads[:, :D].astype(f32), 0, keepdims=True)
        sums[V_BIAS : V_BIAS + 1, :] = jnp.sum(grads[:, 2 * D :].astype(f32), 0, keepdims=True)

    pl.run_scoped(
        attend_back,
        pltpu.VMEM((2, 2, PAD, LANES), bf16),
        pltpu.VMEM((2 * PAD, 3 * D), bf16),
        pltpu.VMEM((D, 2 * PAD), bf16),
        pltpu.VMEM((TILES, PAD * STRIDE, 128), f32),
        pltpu.VMEM((TILES, HALF * HEADS, 128), bf16),
    )

    slab_rows = (pl.ds(0, TABLE_ROWS), pl.ds(TABLE_ROWS, SMALL))

    def slab_copies(part):
        return [
            remote(
                slab.at[lax.rem(shard + k, 4), slab_rows[part]],
                slab_z.at[3 - k, slab_rows[part]],
                slab_send.at[part, k - 1],
                slab_recv.at[part, 3 - k],
                rep,
                lax.rem(shard + k, 4),
            )
            for k in (1, 2, 3)
        ]

    def slab_share(part, k):
        block = slab_rep.at[rep, slab_rows[part]]
        return remote(
            block,
            block,
            slab_send.at[part, 2 + k],
            slab_recv.at[part, 2 + reps - k],
            lax.rem(rep + k, reps),
            shard,
        )

    def slab_onward(part):
        for copy in slab_copies(part):
            copy.wait_recv()
        rows = slab_rows[part]
        slab_rep[rep, rows] = slab[shard, rows] + (
            slab_z[0, rows] + slab_z[1, rows] + slab_z[2, rows]
        )

        def share_start(k, carry):
            slab_share(part, k).start()
            return carry

        lax.fori_loop(1, reps, share_start, 0)

    for owner in range(4):
        entries = jnp.concatenate(
            [table_sum[pl.ds(s * HEADS + GROUP * owner, GROUP), :] for s in range(SPANS)], 0
        )
        slab[owner, : SPANS * GROUP, :] = entries[:, :128]
        slab[owner, SPANS * GROUP : TABLE_ROWS, :] = entries[:, 128:]
    for copy in slab_copies(0):
        copy.start()

    for window in range(2):
        for copy in return_copies(window):
            copy.wait_recv()
    gain = small_row(small_all, LN1_GAIN).astype(f32)

    def norm_step(step, carry):
        gain_sum, shift_sum = carry
        rows = pl.ds(pl.multiple_of(step * 112, 16), 112)
        grad_out = dot(order_back[rows, :], returned[...])
        normal, over = norm_rows(tokens[rows, :].astype(f32))
        scaled = grad_out * gain
        inner = (
            scaled
            - jnp.mean(scaled, -1, keepdims=True)
            - normal * jnp.mean(scaled * normal, -1, keepdims=True)
        )
        grad_middle[rows, :] += over * inner
        return (
            gain_sum + jnp.sum(grad_out * normal, 0, keepdims=True),
            shift_sum + jnp.sum(grad_out, 0, keepdims=True),
        )

    nought = jnp.zeros((1, D), f32)
    some = lax.fori_loop(0, 4, norm_step, (nought, nought))
    slab_onward(0)
    gain_sum, shift_sum = lax.fori_loop(4, 7, norm_step, some)
    sums[LN1_GAIN : LN1_GAIN + 1, :] = gain_sum
    sums[LN1_SHIFT : LN1_SHIFT + 1, :] = shift_sum
    for owner in range(4):
        lanes = slice(owner * 128, (owner + 1) * 128)
        slab[owner, TABLE_ROWS:, :] = jnp.concatenate(
            [sums[:, lanes]]
            + [fc1_sum[:, owner * D + k * 128 : owner * D + (k + 1) * 128] for k in range(4)]
            + [jnp.zeros((4, 128), f32)],
            0,
        )
    for copy in slab_copies(1):
        copy.start()
    tokens_copy = pltpu.make_async_copy(grad_middle, grad_tokens, load.at[0])
    tokens_copy.start()

    for matrix in range(count):
        advance(matrix, CORE_SHARE)
    outs = (fc1_out, fc2_out, proj_out, qkv_out_0, qkv_out_1, qkv_out_2, qkv_out_3)
    results = [
        pltpu.make_async_copy(held[matrix][5], outs[matrix], local.at[count + matrix])
        for matrix in range(count)
    ]
    for copy in results:
        copy.start()
    slab_onward(1)

    def share_wait(k, carry):
        for part in range(2):
            slab_share(part, k).wait()
        return carry

    lax.fori_loop(1, reps, share_wait, 0)

    def slab_step(k, total):
        return total + slab_rep[k]

    slab_out[...] = lax.fori_loop(1, reps, slab_step, slab_rep[0])

    for part in range(2):
        for copy in slab_copies(part):
            copy.wait_send()
    for window in range(2):
        for copy in return_copies(window):
            copy.wait_send()
    for matrix in range(count):
        for phase in range(CORE_SHARE + 1):
            for copy in sum_copies(matrix, phase):
                copy.wait_send()
    for copy in results + [tokens_copy]:
        copy.wait()


def rear(
    returned_context,
    tokens,
    cotangent,
    small_all,
    whole_proj,
    whole_fc1,
    whole_fc2,
    weights_a,
    weights_b,
    rolled,
    mixed,
    inverse,
    contexts,
    rel,
    attend,
):
    anywhere, inside = pl.BlockSpec(memory_space=pl.ANY), pl.BlockSpec(memory_space=pltpu.VMEM)
    reps = lax.axis_size("rep")
    dma = pltpu.SemaphoreType.DMA
    order = send_matrix()
    extra = max(1, reps.bit_length() - 4)
    held = []
    for rows, columns, _ in SUMMED:
        held += [
            pltpu.VMEM((4, 2, 2, rows, columns), bf16),
            pltpu.VMEM((4, 2, rows, columns), bf16),
            pltpu.VMEM((4, rows, columns), bf16),
            pltpu.VMEM((2, rows, columns), bf16),
            pltpu.VMEM((1 + extra, rows, columns), bf16),
            pltpu.VMEM((2, 2, 2, rows, columns), bf16),
        ]
    return pl.pallas_call(
        rear_kernel,
        out_shape=(
            jax.ShapeDtypeStruct(tokens.shape, bf16),
            jax.ShapeDtypeStruct(tokens.shape, f32),
            *[jax.ShapeDtypeStruct((2, 2, 2) + shape[:2], bf16) for shape in SUMMED],
            jax.ShapeDtypeStruct((SLAB, 128), f32),
        ),
        in_specs=[inside] * 3 + [anywhere] * 14,
        out_specs=(*[anywhere] * (2 + len(SUMMED)), inside),
        scratch_shapes=[
            pltpu.VMEM(weights_a.shape, bf16),
            pltpu.VMEM(weights_b.shape, bf16),
            pltpu.VMEM(rolled.shape, bf16),
            pltpu.VMEM(mixed.shape, bf16),
            pltpu.VMEM(inverse.shape, f32),
            pltpu.VMEM(contexts.shape, bf16),
            pltpu.VMEM(rel.shape, jnp.int32),
            pltpu.VMEM((2 * PAD, D), bf16),
            pltpu.VMEM((2 * PAD, D), bf16),
            pltpu.VMEM(tokens.shape, f32),
            pltpu.VMEM((2 * PAD, D), bf16),
            pltpu.VMEM((TILES, HALF * HEADS, 128), bf16),
            pltpu.VMEM((4, 2, 2, 2, 16, 2048), bf16),
            pltpu.VMEM((4, 2, 2, 2, 64, 512), bf16),
            pltpu.VMEM((4, 2, 2, 2, 16, 512), bf16),
            pltpu.VMEM((HEADS // GROUP, 4, 2, 2, 2, 16, 3 * 128), bf16),
            pltpu.VMEM((8, D), f32),
            pltpu.VMEM((1, FF), f32),
            pltpu.VMEM((SPANS * HEADS, SPAN), f32),
            pltpu.VMEM((4, SLAB, 128), f32),
            pltpu.VMEM((3, SLAB, 128), f32),
            pltpu.VMEM((reps, SLAB, 128), f32),
            *held,
            dma((len(SUMMED), CORE_SHARE + 1, 3)),
            dma((len(SUMMED), CORE_SHARE + 1, 3)),
            dma((len(SUMMED), extra)),
            dma((len(SUMMED), extra)),
            dma((2, 3)),
            dma((2, 3)),
            dma((2, 3)),
            dma((2, 3)),
            dma((2,)),
            dma((2,)),
            dma((2,)),
            dma((2, 3 + reps)),
            dma((2, 3 + reps)),
            dma((2 * len(SUMMED),)),
            dma((14,)),
        ],
        compiler_params=pltpu.CompilerParams(
            vmem_limit_bytes=VMEM_LIMIT, collective_id=1, has_side_effects=True
        ),
        name="rear",
    )(
        jnp.asarray(order.T, bf16),
        tokens,
        small_all,
        returned_context,
        jnp.asarray(order, bf16),
        cotangent,
        whole_proj,
        whole_fc1,
        whole_fc2,
        weights_a,
        weights_b,
        rolled,
        mixed,
        inverse,
        contexts,
        rel,
        attend,
    )


def finish_kernel(
    output_in,
    tokens_in,
    fc1_in,
    fc2_in,
    proj_in,
    qkv_0,
    qkv_1,
    qkv_2,
    qkv_3,
    slab,
    output,
    tokens,
    fc1,
    fc2,
    proj,
    qkv,
    table,
    fc1_bias,
    *vectors,
):
    output[...] = output_in[...]
    tokens[...] = tokens_in[...]
    for part, whole in ((fc1_in, fc1), (fc2_in, fc2), (proj_in, proj)):
        whole[...] = part[...].astype(f32).reshape(whole.shape)
    for group, part in enumerate((qkv_0, qkv_1, qkv_2, qkv_3)):
        got = part[...].astype(f32).reshape(qkv.shape[0], 3 * 128)
        for n in range(3):
            first = n * D + group * 128
            qkv[:, first : first + 128] = got[:, n * 128 : (n + 1) * 128]
    entries = [
        slab[pl.ds((half * SPANS + span) * GROUP, GROUP), :]
        for span in range(SPANS)
        for half in range(2)
    ]
    table[...] = jnp.concatenate(entries, 1)[:, :TABLE]
    for row, vector in enumerate(vectors):
        vector[...] = slab[TABLE_ROWS + row : TABLE_ROWS + row + 1, :]
    first = TABLE_ROWS + FC1_BIAS
    fc1_bias[...] = jnp.concatenate([slab[first + k : first + k + 1, :] for k in range(4)], 1)


def finish(output, grad_tokens, fc1, fc2, proj, qkv, slab):
    inside = pl.BlockSpec(memory_space=pltpu.VMEM)
    shapes = [(128, FF), (FF // 4, D), (128, D), (128, 3 * D), (GROUP, TABLE), (1, D)]
    shapes += [(1, 128)] * FC1_BIAS
    return pl.pallas_call(
        finish_kernel,
        out_shape=(
            jax.ShapeDtypeStruct(output.shape, bf16),
            jax.ShapeDtypeStruct(grad_tokens.shape, f32),
            *[jax.ShapeDtypeStruct(shape, f32) for shape in shapes],
        ),
        in_specs=[inside] * 10,
        out_specs=(inside,) * (2 + len(shapes)),
        compiler_params=pltpu.CompilerParams(vmem_limit_bytes=VMEM_LIMIT),
        name="finish",
    )(output, grad_tokens, fc1, fc2, proj, *qkv, slab)


def shards(
    tokens,
    region,
    rel_index,
    ln1_gain,
    ln1_shift,
    w_qkv,
    q_bias,
    v_bias,
    table,
    w_proj,
    proj_bias,
    ln2_gain,
    ln2_shift,
    w_fc1,
    fc1_bias,
    w_fc2,
    fc2_bias,
    cotangent,
):
    small = jnp.zeros((SMALL, 128), f32)
    vectors = (ln1_gain, ln1_shift, q_bias, v_bias, proj_bias, ln2_gain, ln2_shift, fc2_bias, fc1_bias)
    for row, vector in enumerate(vectors):
        block = vector.reshape(-1, 128).astype(f32)
        small += jnp.pad(block, ((row, SMALL - row - block.shape[0]), (0, 0)))
    small = small.astype(bf16)
    chunks = jnp.pad(table.astype(f32).T, ((0, 0), (0, CHUNKS * 128 - TABLE)))
    labels = region.reshape(WT, WH, 2, WW).transpose(2, 0, 1, 3).reshape(2, WIN)
    labels = pieces_of(labels, 1, -1)
    row_ids = jnp.pad(labels, ((0, 0), (0, LANES - PAD)), constant_values=-1)[:, None]
    (
        whole_qkv_a,
        whole_qkv_b,
        whole_proj,
        whole_fc1,
        whole_fc2,
        small,
        rolled,
        qkv,
        attend,
        inverse,
        contexts,
        returned,
        rel,
    ) = front(
        tokens.reshape(-1, D),
        small,
        chunks.reshape(-1, 128),
        row_ids,
        rel_index,
        w_qkv,
        w_proj,
        w_fc1,
        w_fc2,
    )
    output, grad_tokens, grad_w_fc1, grad_w_fc2, grad_w_proj, *grads_qkv, slab = rear(
        returned,
        tokens.reshape(-1, D),
        cotangent.reshape(-1, D),
        small,
        whole_proj,
        whole_fc1,
        whole_fc2,
        whole_qkv_a,
        whole_qkv_b,
        rolled,
        qkv,
        inverse,
        contexts,
        rel,
        attend,
    )
    (
        output,
        grad_tokens,
        grad_w_fc1,
        grad_w_fc2,
        grad_w_proj,
        grad_w_qkv,
        grad_table,
        grad_fc1_bias,
        *vectors,
    ) = finish(output, grad_tokens, grad_w_fc1, grad_w_fc2, grad_w_proj, grads_qkv, slab)
    output = output.reshape(tokens.shape)
    grad_tokens = grad_tokens.reshape(tokens.shape)
    grad_table = grad_table.T
    grad_fc1_bias = grad_fc1_bias.reshape(-1)
    vectors = [vector.reshape(-1) for vector in vectors]
    grad_ln1_gain, grad_ln1_shift = vectors[LN1_GAIN], vectors[LN1_SHIFT]
    grad_q_bias, grad_v_bias = vectors[Q_BIAS], vectors[V_BIAS]
    grad_proj_bias, grad_fc2_bias = vectors[PROJ_BIAS], vectors[FC2_BIAS]
    grad_ln2_gain, grad_ln2_shift = vectors[LN2_GAIN], vectors[LN2_SHIFT]
    return (
        output,
        grad_tokens,
        grad_ln1_gain,
        grad_ln1_shift,
        grad_w_qkv,
        grad_q_bias,
        grad_v_bias,
        grad_table,
        grad_w_proj,
        grad_proj_bias,
        grad_ln2_gain,
        grad_ln2_shift,
        grad_w_fc1,
        grad_fc1_bias,
        grad_w_fc2,
        grad_fc2_bias,
    )


def solution(mesh):
    return jax.shard_map(
        shards,
        mesh=mesh,
        in_specs=(
            P("rep", "shard", None, None),
            P("shard", None),
            P(),
            P("shard"),
            P("shard"),
            P("shard", None),
            P("shard"),
            P("shard"),
            P(None, "shard"),
            P("shard", None),
            P("shard"),
            P("shard"),
            P("shard"),
            P("shard", None),
            P("shard"),
            P("shard", None),
            P("shard"),
            P("rep", "shard", None, None),
        ),
        out_specs=(
            P("rep", "shard", None, None),
            P("rep", "shard", None, None),
            P("shard"),
            P("shard"),
            P("shard", None),
            P("shard"),
            P("shard"),
            P(None, "shard"),
            P("shard", None),
            P("shard"),
            P("shard"),
            P("shard"),
            P("shard", None),
            P("shard"),
            P("shard", None),
            P("shard"),
        ),
        check_vma=False,
    )
```

```python
import functools

import jax
import jax.numpy as jnp
import numpy as np
from jax import lax
from jax.experimental import pallas as pl
from jax.experimental.pallas import tpu as pltpu
from jax.sharding import PartitionSpec as P

D = 512
HEADS = 16
HD = 32
WT = 8
WH = 7
WW = 7
WIN = 392
TABLE = 2535
FF = 2048
FF_TILE = 256
PAD = 416
LANES = 512
GROUP = 4
CHUNKS = 20
SCALE = HD ** (-0.5)
NN = (((1,), (0,)), ((), ()))
NT = (((1,), (1,)), ((), ()))
TN = (((0,), (0,)), ((), ()))
VMEM_LIMIT = 60 * 2**20
f32 = jnp.float32
bf16 = jnp.bfloat16

PIECES = (
    ((0, 4), (0, 4), 112, 0),
    ((4, 8), (0, 4), 112, 112),
    ((0, 4), (4, 7), 96, 224),
    ((4, 8), (4, 7), 96, 320),
)


def send_matrix():
    matrix = np.zeros((2 * PAD, WT * WH * 2 * WW), np.float32)
    for window in range(2):
        for (t0, t1), (h0, h1), _, first in PIECES:
            row = window * PAD + first
            for t in range(t0, t1):
                for h in range(h0, h1):
                    for w in range(WW):
                        column = (window * WW + w + WW // 2) % (2 * WW)
                        source = ((t + 4) % WT * WH + (h + 3) % WH) * 2 * WW + column
                        matrix[row, source] = 1.0
                        row += 1
    return matrix


def spread_matrix():
    source = np.arange(WIN).reshape(WT, WH, WW)
    matrix = np.zeros((PAD, WIN), np.float32)
    for (t0, t1), (h0, h1), _, first in PIECES:
        tokens = source[t0:t1, h0:h1].reshape(-1)
        matrix[first + np.arange(tokens.size), tokens] = 1.0
    return matrix


def pieces_of(array, axis, fill):
    shape = array.shape
    split = array.reshape(shape[:axis] + (WT, WH, WW) + shape[axis + 1 :])
    parts = []
    for (t0, t1), (h0, h1), padded, _ in PIECES:
        part = lax.slice_in_dim(lax.slice_in_dim(split, t0, t1, axis=axis), h0, h1, axis=axis + 1)
        length = (t1 - t0) * (h1 - h0) * WW
        part = part.reshape(shape[:axis] + (length,) + shape[axis + 1 :])
        widths = [(0, 0, 0)] * len(shape)
        widths[axis] = (0, padded - length, 0)
        parts.append(lax.pad(part, jnp.asarray(fill, array.dtype), widths))
    return jnp.concatenate(parts, axis)


def dot(a, b, dims=NN):
    return lax.dot_general(a, b, dims, preferred_element_type=f32)


MESH = pl.DeviceIdType.MESH
PARTS = 8
FIRST_ROWS = tuple(first for _, _, _, first in PIECES)
LENGTHS = tuple(padded for _, _, padded, _ in PIECES)
ACROSS = (0, 2, 1, 3)
LN1_GAIN, LN1_SHIFT, Q_BIAS, V_BIAS, PROJ_BIAS, LN2_GAIN, LN2_SHIFT, FC2_BIAS, FC1_BIAS = range(9)
SMALL = 16


def place():
    rep, shard = lax.axis_index("rep"), lax.axis_index("shard")
    return rep, shard, lax.rem(rep, 2), lax.rem(rep // 2, 2), lax.rem(rep // 4, 2)


def flip(rep, bit):
    low = lax.rem(rep // (1 << bit), 2)
    return rep + (1 - 2 * low) * (1 << bit)


def remote(src, dst, send, recv, rep, shard):
    return pltpu.make_async_remote_copy(
        src_ref=src,
        dst_ref=dst,
        send_sem=send,
        recv_sem=recv,
        device_id={"rep": rep, "shard": shard},
        device_id_type=MESH,
    )


def greet(peers):
    barrier = pltpu.get_barrier_semaphore()
    for rep, shard in peers:
        pl.semaphore_signal(
            barrier, inc=1, device_id={"rep": rep, "shard": shard}, device_id_type=MESH
        )
    pl.semaphore_wait(barrier, len(peers))


def peers_of(rep, shard):
    return [(rep, lax.rem(shard + k, 4)) for k in (1, 2, 3)] + [
        (flip(rep, bit), shard) for bit in (0, 1, 2)
    ]


def quarter_across(shard, bits):
    low, high = lax.rem(shard, 2), shard // 2
    if bits & 1:
        low = 1 - low
    if bits & 2:
        high = 1 - high
    return high * 2 + low


def pieces_to(source, target, send, recv, rep, shard, window, columns=None, which=(1, 2, 3)):
    copies = []
    for piece in which:
        rows = pl.ds(
            pl.multiple_of(window * PAD + FIRST_ROWS[piece], 16), LENGTHS[piece]
        )
        at = (rows,) if columns is None else (rows, columns)
        copies.append(
            remote(
                source.at[at],
                target.at[at],
                send(piece - 1),
                recv(piece - 1),
                rep,
                quarter_across(shard, ACROSS[piece]),
            )
        )
    return copies


def norm_rows(rows):
    centre = rows - jnp.mean(rows, -1, keepdims=True)
    inverse = lax.rsqrt(jnp.mean(centre * centre, -1, keepdims=True) + 1e-05)
    return centre * inverse, inverse


def small_row(ref, row):
    return jnp.concatenate([ref[s, row : row + 1, :] for s in range(4)], 1)


FIXED = 4096.0
TAIL = 112
Z_PHASE, NEXT_PHASE, FIRST_PHASE, SECOND_PHASE, CORE_PHASE = range(5)
X_FIRST = (True, False, True, False, True)
HALF_QKV = 3 * D // 2


def front_kernel(
    tokens,
    order,
    spread,
    small,
    table,
    row_ids,
    rel,
    qkv_part,
    proj_part,
    fc1_part,
    fc2_part,
    qkv_whole_a,
    qkv_whole_b,
    proj_whole,
    fc1_whole,
    fc2_whole,
    small_out,
    rolled_out,
    mixed_out,
    attend_out,
    inverse_out,
    context_out,
    back_out,
    rel_out,
    small_all,
    table_all,
    table_wide,
    outgoing,
    arriving,
    rolled,
    weights_a,
    weights_b,
    mixed,
    index,
    index_tail,
    bias_tail,
    bias,
    mask,
    attend,
    inverse,
    contexts,
    gather_send,
    gather_recv,
    small_send,
    small_recv,
    bias_send,
    bias_recv,
    piece_send,
    piece_recv,
    back_send,
    back_recv,
    local,
    attend_sem,
):
    rep, shard, core, x_bit, y_bit = place()
    greet(peers_of(rep, shard))
    first_half, second_half = pl.ds(0, HALF_QKV), pl.ds(HALF_QKV, HALF_QKV)
    parts = (
        qkv_part.at[:, :, :, :, first_half],
        qkv_part.at[:, :, :, :, second_half],
        proj_part,
        fc1_part,
        fc2_part,
    )
    wholes = (weights_a, weights_b, proj_whole, fc1_whole, fc2_whole)
    feed_forward = (2, 3, 4)

    def gather(matrix, phase):
        copies = []
        whole = wholes[matrix]
        here = (y_bit, x_bit, core)

        def along_z(n, source, at, bits):
            return remote(
                source,
                whole.at[(at,) + here],
                gather_send.at[matrix, phase, n],
                gather_recv.at[matrix, phase, n],
                rep,
                quarter_across(shard, bits),
            )

        if phase == Z_PHASE:
            own_part = parts[matrix].at[here]
            return [along_z(0, own_part, shard, 2), along_z(1, own_part, shard, 1)]
        if phase == NEXT_PHASE:
            across = quarter_across(shard, 2)
            return [along_z(0, whole.at[(across,) + here], across, 1)]
        for k in (1, 2, 3):
            at = lax.rem(shard + k, 4)
            x_first = X_FIRST[matrix]
            if phase == FIRST_PHASE:
                block, partner = whole.at[at, y_bit, x_bit, core], flip(rep, 1 if x_first else 2)
            elif phase == SECOND_PHASE and x_first:
                block, partner = whole.at[at, y_bit, :, core], flip(rep, 2)
            elif phase == SECOND_PHASE:
                block, partner = whole.at[at, :, x_bit, core], flip(rep, 1)
            else:
                block, partner = whole.at[at, :, :, core], flip(rep, 0)
            copies.append(
                remote(
                    block,
                    block,
                    gather_send.at[matrix, phase, k - 1],
                    gather_recv.at[matrix, phase, k - 1],
                    partner,
                    shard,
                )
            )
        return copies

    def start(matrix, phase):
        for copy in gather(matrix, phase):
            copy.start()

    def arrived(matrix, phase):
        for copy in gather(matrix, phase):
            copy.wait_recv()

    def small_copies():
        return [
            remote(
                small_all.at[shard],
                small_all.at[shard],
                small_send.at[0, k - 1],
                small_recv.at[0, 3 - k],
                rep,
                lax.rem(shard + k, 4),
            )
            for k in (1, 2, 3)
        ]

    def table_copy(k):
        return remote(
            table_all.at[shard],
            table_all.at[shard],
            small_send.at[1, k - 1],
            small_recv.at[1, 3 - k],
            rep,
            lax.rem(shard + k, 4),
        )

    def table_copies(action):
        for k in (1, 2, 3):
            if action == "recv":
                wanted = lax.rem(shard + 4 - k, 4) // 2 == core
            else:
                wanted = shard // 2 == core

            @pl.when(wanted)
            def _():
                if action == "start":
                    table_copy(k).start()
                elif action == "recv":
                    table_copy(k).wait_recv()
                else:
                    table_copy(k).wait_send()

    small_all[shard] = small[...]
    columns = table[...].astype(f32)
    spare = jnp.zeros((GROUP, CHUNKS * 128 - TABLE), f32)
    for chunk in range(CHUNKS):
        piece = columns[:, chunk * 128 : (chunk + 1) * 128]
        if chunk == CHUNKS - 1:
            piece = jnp.concatenate([piece, spare], 1)
        table_all[shard, chunk * GROUP : (chunk + 1) * GROUP, :] = piece
    table_copies("start")
    for copy in small_copies():
        copy.start()
    start(0, Z_PHASE)
    start(1, Z_PHASE)
    own = [
        pltpu.make_async_copy(parts[m], wholes[m].at[shard], local.at[m]) for m in feed_forward
    ]
    for copy in own:
        copy.start()
    weights_a[shard] = qkv_part[..., :HALF_QKV]
    weights_b[shard] = qkv_part[..., HALF_QKV:]

    outgoing[...] = dot(order[...], tokens[...]).astype(bf16)

    def roll_copies(window):
        return pieces_to(
            outgoing,
            arriving,
            lambda n: piece_send.at[window, n],
            lambda n: piece_recv.at[window, n],
            rep,
            shard,
            window,
        )

    for copy in roll_copies(0):
        copy.start()
    for window in range(2):
        rows = slice(window * PAD, window * PAD + LENGTHS[0])
        arriving[rows, :] = outgoing[rows, :]

    rel_index = rel[...]
    digits = (rel_index // 256).astype(f32).astype(bf16), (rel_index & 255).astype(f32).astype(bf16)
    moved = []
    for digit in digits:
        half = dot(spread[...], digit).astype(bf16)
        moved.append(dot(half, spread[...], NT).astype(jnp.int32))
    index[:, :PAD] = moved[0] * 256 + moved[1]
    index[:, PAD:] = jnp.zeros((PAD, LANES - PAD), jnp.int32)

    ids = lax.broadcasted_iota(jnp.int32, (8, LANES), 0)
    for window in range(2):
        kinds = jnp.where(row_ids[window] + 1 == ids, 1.0, 0.0).astype(bf16)[:, :PAD]
        mask[window] = (dot(kinds, kinds, TN) - 1.0) * 1e30

    for copy in small_copies():
        copy.wait_recv()
    table_copies("recv")

    for block in range(4):
        count = min(TAIL, PAD - block * TAIL)
        lanes = slice(block * 32, block * 32 + 32)
        index_tail[:count, lanes] = index[block * TAIL : block * TAIL + count, PAD - 32 : PAD]
        if count < TAIL:
            index_tail[count:, lanes] = jnp.zeros((TAIL - count, 32), jnp.int32)

    upper, lower = (
        jnp.floor(table_all[2 * core + n] * FIXED + 0.5).astype(jnp.int32) for n in range(2)
    )
    words = upper * 65536 + (lower + 32768)
    for chunk in range(CHUNKS):
        for head in range(GROUP):
            row = chunk * GROUP + head
            table_wide[chunk, head] = jnp.broadcast_to(words[row : row + 1, :], (8, 128))
    mine = core * (HEADS // 2)

    def bias_copy(rows, step):
        block = bias.at[pl.ds(mine, HEADS // 2), rows]
        return remote(block, block, bias_send.at[step], bias_recv.at[step], flip(rep, 0), shard)

    def on_the_way(step, table_of_steps):
        for when, actions in table_of_steps.items():

            @pl.when(step == when)
            def _():
                for action, matrix, phase in actions:
                    action(matrix, phase)

    def advance(matrix, phase):
        arrived(matrix, phase)
        if phase < CORE_PHASE:
            start(matrix, phase + 1)

    schedule = {
        4: [(advance, 0, Z_PHASE), (advance, 1, Z_PHASE), *[(start, m, Z_PHASE) for m in feed_forward]],
        11: [(advance, 0, NEXT_PHASE), (advance, 1, NEXT_PHASE)],
        18: [(advance, 0, FIRST_PHASE), (advance, 1, FIRST_PHASE)],
        20: [*[(advance, m, Z_PHASE) for m in feed_forward]],
    }
    later = {
        1: [*[(advance, m, NEXT_PHASE) for m in feed_forward]],
        6: [*[(advance, m, FIRST_PHASE) for m in feed_forward]],
    }

    def look_up(here):
        found = [[] for _ in range(GROUP)]
        for s in (0, 8):
            low, high = here[s : s + 8] & 127, here[s : s + 8] >> 7
            values = [None] * GROUP
            for chunk in range(CHUNKS):
                hit = high == chunk
                for head in range(GROUP):
                    value = jnp.take_along_axis(table_wide[chunk, head], low, axis=1)
                    values[head] = jnp.where(hit, value, values[head]) if chunk else value
            for head in range(GROUP):
                found[head].append(values[head])
        joined = [jnp.concatenate(pair, 0) for pair in found]
        uppers = [(word >> 16).astype(f32) for word in joined]
        lowers = [((word & 65535) - 32768).astype(f32) for word in joined]
        return [(value * (1 / FIXED)).astype(bf16) for value in uppers + lowers]

    def tail_step(step, carry):
        rows = pl.ds(pl.multiple_of(step * 16, 16), 16)
        for head, value in enumerate(look_up(index_tail[rows, :])):
            bias_tail[head, rows, :] = value
        return carry

    lax.fori_loop(0, TAIL // 16, tail_step, 0)

    def untail_step(head, carry):
        for block in range(4):
            count = min(TAIL, PAD - block * TAIL)
            value = bias_tail[head, :count, block * 32 : block * 32 + 32]
            bias[mine + head, block * TAIL : block * TAIL + count, PAD - 32 : PAD] = value
        return carry

    lax.fori_loop(0, HEADS // 2, untail_step, 0)

    def bias_step(step, carry):
        on_the_way(step, schedule)
        rows = pl.ds(pl.multiple_of(step * 16, 16), 16)
        for tile in range(3):
            lanes = slice(tile * 128, (tile + 1) * 128)
            for head, value in enumerate(look_up(index[rows, lanes])):
                bias[mine + head, rows, lanes] = value
        bias_copy(rows, step).start()
        return carry

    lax.fori_loop(0, PAD // 16, bias_step, 0)
    for copy in roll_copies(1):
        copy.start()
    for n in range(2):
        advance(n, SECOND_PHASE)

    for n in range(2):
        arrived(n, CORE_PHASE)
    q_bias, v_bias = small_row(small_all, Q_BIAS), small_row(small_all, V_BIAS)
    mixed_bias = jnp.concatenate([q_bias, jnp.zeros_like(q_bias), v_bias], 1).astype(f32)
    gain, shift = small_row(small_all, LN1_GAIN), small_row(small_all, LN1_SHIFT)

    def norm_step(step, carry):
        rows = pl.ds(pl.multiple_of(step * 208, 16), 208)
        normal, _ = norm_rows(arriving[rows, :].astype(f32))
        rolled[rows, :] = (normal * gain.astype(f32) + shift.astype(f32)).astype(bf16)
        return carry

    def mix(window):
        for copy in roll_copies(window):
            copy.wait_recv()
        lax.fori_loop(2 * window, 2 * window + 2, norm_step, 0)
        span = slice(window * PAD, (window + 1) * PAD)
        for n, weight in enumerate((weights_a, weights_b)):
            lanes = slice(n * HALF_QKV, (n + 1) * HALF_QKV)
            got = dot(rolled[span, :], weight[...].reshape(D, HALF_QKV))
            mixed[span, lanes] = (got + mixed_bias[:, lanes]).astype(bf16)

    mix(0)
    keep = [
        pltpu.make_async_copy(rolled, rolled_out, local.at[5]),
        pltpu.make_async_copy(mixed, mixed_out, local.at[6]),
        pltpu.make_async_copy(index, rel_out, local.at[7]),
        pltpu.make_async_copy(small_all, small_out, local.at[8]),
        pltpu.make_async_copy(inverse, inverse_out, local.at[9]),
        pltpu.make_async_copy(contexts, context_out, local.at[12]),
        pltpu.make_async_copy(weights_a, qkv_whole_a, local.at[0]),
        pltpu.make_async_copy(weights_b, qkv_whole_b, local.at[1]),
    ]

    def bias_wait(step, carry):
        bias_copy(pl.ds(pl.multiple_of(step * 16, 16), 16), step).wait_recv()
        return carry

    lax.fori_loop(0, PAD // 16, bias_wait, 0)

    head_of = lax.broadcasted_iota(jnp.int32, (1, 128), 1) // HD
    none = jnp.zeros((), bf16)
    ones = jnp.ones((PAD, 128), bf16)

    def attend_copy(step):
        window, pair, slot = step // (HEADS // 2), lax.rem(step, HEADS // 2), lax.rem(step, 2)
        return pltpu.make_async_copy(
            attend.at[slot], attend_out.at[window, pl.ds(2 * pair, 2)], attend_sem.at[slot]
        )

    def back_copies(step):
        window, group = step // (HEADS // 2), lax.rem(step // 2, HEADS // GROUP)
        lanes = pl.ds(pl.multiple_of(group * 128, 128), 128)
        return pieces_to(
            contexts,
            back_out,
            lambda n: back_send.at[window, group, n],
            lambda n: back_recv.at[window, group, n],
            rep,
            shard,
            window,
            lanes,
        )

    def attend_step(step, carry):
        on_the_way(step, later)

        @pl.when(step == HEADS // 2)
        def _():
            mix(1)

        @pl.when(step >= 2)
        def _():
            attend_copy(step - 2).wait()

        window, slot = step // (HEADS // 2), lax.rem(step, 2)
        rows = pl.ds(pl.multiple_of(window * PAD, 16), PAD)
        for n in range(2):
            head = 2 * lax.rem(step, HEADS // 2) + n
            group, member = head // GROUP, lax.rem(head, GROUP)

            def lanes(part):
                return pl.ds(pl.multiple_of(part * D + group * 128, 128), 128)

            own_lanes = head_of == member
            query = jnp.where(own_lanes, mixed[rows, lanes(0)], none)
            value = jnp.where(own_lanes, mixed[rows, lanes(2)], none)
            scores = dot(query, mixed[rows, lanes(1)], NT) * SCALE
            scores = scores + bias[head, :, :PAD].astype(f32) + mask[window]
            expo = jnp.exp(scores - jnp.max(scores, -1, keepdims=True)).astype(bf16)
            attend[slot, n, :, :PAD] = expo
            result = dot(expo, jnp.concatenate([value, ones], 1))
            over = 1.0 / result[:, 128:]
            context = (result[:, :128] * over).astype(bf16)
            contexts[rows, lanes(0)] = jnp.where(own_lanes, context, contexts[rows, lanes(0)])
            inverse[rows, lanes(0)] = jnp.where(own_lanes, over, inverse[rows, lanes(0)])
        attend_copy(step).start()

        @pl.when(lax.rem(step, 2) == 1)
        def _():
            for copy in back_copies(step):
                copy.start()

        return carry

    lax.fori_loop(0, HEADS, attend_step, 0)
    for copy in keep:
        copy.start()
    for matrix in feed_forward:
        advance(matrix, SECOND_PHASE)
    stay = [
        pltpu.make_async_copy(
            contexts.at[pl.ds(w * PAD, LENGTHS[0])],
            back_out.at[pl.ds(w * PAD, LENGTHS[0])],
            local.at[10 + w],
        )
        for w in range(2)
    ]
    for copy in stay:
        copy.start()
    for matrix in feed_forward:
        arrived(matrix, CORE_PHASE)
    attend_copy(HEADS - 2).wait()
    attend_copy(HEADS - 1).wait()

    def back_wait(step, carry):
        for copy in back_copies(step * 2):
            copy.wait()
        return carry

    lax.fori_loop(0, 2 * HEADS // GROUP, back_wait, 0)

    def bias_sent(step, carry):
        bias_copy(pl.ds(pl.multiple_of(step * 16, 16), 16), step).wait_send()
        return carry

    lax.fori_loop(0, PAD // 16, bias_sent, 0)
    for copy in small_copies():
        copy.wait_send()
    table_copies("send")
    for window in range(2):
        for copy in roll_copies(window):
            copy.wait_send()
    for matrix in range(5):
        for phase in range(CORE_PHASE + 1):
            for copy in gather(matrix, phase):
                copy.wait_send()
    for copy in own + keep + stay:
        copy.wait()


def front(tokens, small, table, row_ids, rel_index, w_qkv, w_proj, w_fc1, w_fc2):
    anywhere, inside = pl.BlockSpec(memory_space=pl.ANY), pl.BlockSpec(memory_space=pltpu.VMEM)
    cut = (2, 2, 2)
    weights = [
        w.reshape(cut + (w.shape[0] // PARTS, w.shape[1])) for w in (w_qkv, w_proj, w_fc1, w_fc2)
    ]
    half = (4,) + weights[0].shape[:-1] + (HALF_QKV,)
    wholes = [jax.ShapeDtypeStruct(half, bf16)] * 2
    wholes += [jax.ShapeDtypeStruct((4,) + w.shape, bf16) for w in weights[1:]]
    dma = pltpu.SemaphoreType.DMA
    results = pl.pallas_call(
        front_kernel,
        out_shape=(
            *wholes,
            jax.ShapeDtypeStruct((4, SMALL, 128), bf16),
            jax.ShapeDtypeStruct((2 * PAD, D), bf16),
            jax.ShapeDtypeStruct((2 * PAD, 3 * D), bf16),
            jax.ShapeDtypeStruct((2, HEADS, PAD, LANES), bf16),
            jax.ShapeDtypeStruct((2 * PAD, D), f32),
            jax.ShapeDtypeStruct((2 * PAD, D), bf16),
            jax.ShapeDtypeStruct((2 * PAD, D), bf16),
            jax.ShapeDtypeStruct((PAD, LANES), jnp.int32),
        ),
        in_specs=[inside] * 11,
        out_specs=(anywhere,) * 13,
        scratch_shapes=[
            pltpu.VMEM((4, SMALL, 128), bf16),
            pltpu.VMEM((4, GROUP * CHUNKS, 128), f32),
            pltpu.VMEM((CHUNKS, GROUP, 8, 128), jnp.int32),
            pltpu.VMEM((2 * PAD, D), bf16),
            pltpu.VMEM((2 * PAD, D), bf16),
            pltpu.VMEM((2 * PAD, D), bf16),
            pltpu.VMEM(half, bf16),
            pltpu.VMEM(half, bf16),
            pltpu.VMEM((2 * PAD, 3 * D), bf16),
            pltpu.VMEM((PAD, LANES), jnp.int32),
            pltpu.VMEM((TAIL, 128), jnp.int32),
            pltpu.VMEM((HEADS // 2, TAIL, 128), bf16),
            pltpu.VMEM((HEADS, PAD, LANES), bf16),
            pltpu.VMEM((2, PAD, PAD), f32),
            pltpu.VMEM((2, 2, PAD, LANES), bf16),
            pltpu.VMEM((2 * PAD, D), f32),
            pltpu.VMEM((2 * PAD, D), bf16),
            dma((5, CORE_PHASE + 1, 3)),
            dma((5, CORE_PHASE + 1, 3)),
            dma((2, 3)),
            dma((2, 3)),
            dma((PAD // 16,)),
            dma((PAD // 16,)),
            dma((2, 3)),
            dma((2, 3)),
            dma((2, HEADS // GROUP, 3)),
            dma((2, HEADS // GROUP, 3)),
            dma((13,)),
            dma((2,)),
        ],
        compiler_params=pltpu.CompilerParams(
            vmem_limit_bytes=VMEM_LIMIT, collective_id=0, has_side_effects=True
        ),
        name="front",
    )(
        tokens,
        jnp.asarray(send_matrix(), bf16),
        jnp.asarray(spread_matrix(), bf16),
        small,
        table,
        row_ids,
        rel_index,
        *weights,
    )
    whole = [w.reshape(-1, w.shape[-1]) for w in results[:5]]
    return (*whole, *results[5:])


CORE_SUM, FIRST_SUM, SECOND_SUM, NEXT_SUM, Z_SUM, SHARE, CORE_SHARE = range(7)
SUMMED = ((16, 2048, True), (64, 512, False), (16, 512, True))
SUMMED += tuple((16, 3 * 128, group % 2 == 0) for group in range(HEADS // GROUP))
FC1, FC2, PROJ, QKV = range(4)
STRIDE = HEADS + 1
CHUNK_ROWS = ((0, 400, (1, 3)), (400, 384, (0, 2)))
SPAN = 256
SPANS = -(-TABLE // SPAN)
BATCH = 16
HALF = PAD // 2
TILES = LANES // 128
TABLE_ROWS = 2 * SPANS * GROUP
SLAB = TABLE_ROWS + SMALL


def rear_kernel(
    order_back,
    tokens,
    small_all,
    returned_in,
    order_in,
    cotangent_in,
    proj_in,
    fc1_in,
    fc2_in,
    weights_a_in,
    weights_b_in,
    rolled_in,
    mixed_in,
    inverse_in,
    contexts_in,
    rel_in,
    attend_in,
    output,
    grad_tokens,
    fc1_out,
    fc2_out,
    proj_out,
    qkv_out_0,
    qkv_out_1,
    qkv_out_2,
    qkv_out_3,
    slab_out,
    weights_a,
    weights_b,
    rolled,
    mixed,
    inverse,
    contexts,
    rel,
    outgoing,
    grad_context,
    grad_middle,
    returned,
    pairs_in,
    fc1_grad,
    fc2_grad,
    proj_grad,
    qkv_grads,
    sums,
    fc1_sum,
    table_sum,
    slab,
    slab_z,
    slab_rep,
    *rest,
):
    count = len(SUMMED)
    held = [rest[6 * m : 6 * m + 6] for m in range(count)]
    (
        sum_send,
        sum_recv,
        extra_send,
        extra_recv,
        piece_send,
        piece_recv,
        back_send,
        back_recv,
        attend_sem,
        pairs_send,
        pairs_recv,
        slab_send,
        slab_recv,
        local,
        load,
    ) = rest[6 * count :]
    rep, shard, core, x_bit, y_bit = place()
    reps = lax.axis_size("rep")
    barrier = pltpu.get_barrier_semaphore()

    def hello(k, carry):
        pl.semaphore_signal(
            barrier,
            inc=1,
            device_id={"rep": lax.rem(rep + k, reps), "shard": shard},
            device_id_type=MESH,
        )
        return carry

    lax.fori_loop(1, reps, hello, 0)
    for k in (1, 2, 3):
        pl.semaphore_signal(
            barrier,
            inc=1,
            device_id={"rep": rep, "shard": lax.rem(shard + k, 4)},
            device_id_type=MESH,
        )
    pl.semaphore_wait(barrier, reps + 2)

    sources = (fc1_grad, fc2_grad, proj_grad) + tuple(qkv_grads.at[g] for g in range(4))

    def axis_of(matrix, first):
        x_first = SUMMED[matrix][2]
        use_x = x_first == first
        return (1, x_bit) if use_x else (2, y_bit)

    def sum_copies(matrix, phase):
        from_core, from_first, summed, from_next, from_z, shared = held[matrix]
        source = sources[matrix]
        x_first = SUMMED[matrix][2]
        first_bit, first = axis_of(matrix, True)
        second_bit, second = axis_of(matrix, False)

        def one(src, dst, bit, n=0):
            return remote(
                src,
                dst,
                sum_send.at[matrix, phase, n],
                sum_recv.at[matrix, phase, n],
                flip(rep, bit),
                shard,
            )

        if phase == CORE_SUM:
            return [one(source.at[:, :, :, 1 - core], from_core, 0)]
        if phase == FIRST_SUM:
            cut = source.at[:, :, 1 - x_bit, core] if x_first else source.at[:, 1 - y_bit, :, core]
            return [one(cut, from_first, first_bit)]
        if phase == SECOND_SUM:
            return [one(from_first.at[:, 1 - second], summed, second_bit)]
        if phase in (NEXT_SUM, Z_SUM):
            low, high = lax.rem(shard, 2), shard // 2
            if phase == NEXT_SUM:
                moves = [(2 * n + 1 - low, from_next.at[n]) for n in range(2)]
            else:
                moves = [(2 * (1 - high) + low, from_z.at[0])]
            return [
                remote(
                    summed.at[owner],
                    target,
                    sum_send.at[matrix, phase, n],
                    sum_recv.at[matrix, phase, n],
                    rep,
                    quarter_across(shard, 1 if phase == NEXT_SUM else 2),
                )
                for n, (owner, target) in enumerate(moves)
            ]
        if phase == CORE_SHARE:
            block = shared.at[:, :, core]
            return [one(block, block, 0)]
        block = shared.at[y_bit, x_bit, core]
        across = flip(flip(rep, 1), 2)
        return [
            remote(
                block,
                block,
                sum_send.at[matrix, phase, n],
                sum_recv.at[matrix, phase, n],
                partner,
                shard,
            )
            for n, partner in enumerate((flip(rep, 1), flip(rep, 2), across))
        ]

    def extra_copy(matrix, bit):
        shared, from_z = held[matrix][5], held[matrix][4]
        return remote(
            shared.at[y_bit, x_bit, core],
            from_z.at[bit - 2],
            extra_send.at[matrix, bit - 3],
            extra_recv.at[matrix, bit - 3],
            flip(rep, bit),
            shard,
        )

    def add(into, at, other, other_at):
        into[at] = into[at] + other[other_at]

    def begin(matrix):
        for copy in sum_copies(matrix, CORE_SUM):
            copy.start()

    def advance(matrix, phase):
        from_core, from_first, summed, from_next, from_z, shared = held[matrix]
        source = sources[matrix]
        x_first = SUMMED[matrix][2]
        _, second = axis_of(matrix, False)
        for copy in sum_copies(matrix, phase):
            copy.wait_recv()
        if phase == CORE_SUM:

            def step(n, carry):
                at = (n // 4, lax.rem(n // 2, 2), lax.rem(n, 2))
                add(source, at + (core,), from_core, at)
                return carry

            lax.fori_loop(0, 16, step, 0)
        elif phase == FIRST_SUM:

            def step(n, carry):
                owner, other = n // 2, lax.rem(n, 2)
                at = (owner, other, x_bit) if x_first else (owner, y_bit, other)
                add(from_first, (owner, other), source, at + (core,))
                return carry

            lax.fori_loop(0, 8, step, 0)
        elif phase == SECOND_SUM:

            def step(owner, carry):
                add(summed, (owner,), from_first, (owner, second))
                return carry

            lax.fori_loop(0, 4, step, 0)
        elif phase == NEXT_SUM:
            low = lax.rem(shard, 2)
            for high in range(2):
                add(summed, (2 * high + low,), from_next, (high,))
        elif phase == Z_SUM:
            total = summed[shard].astype(f32) + from_z[0].astype(f32)
            shared[y_bit, x_bit, core] = total.astype(bf16)
            bit = 3
            while (1 << bit) < reps:
                copy = extra_copy(matrix, bit)
                copy.start()
                copy.wait()
                at = (y_bit, x_bit, core)
                add(shared, at, from_z, (bit - 2,))
                bit += 1
        if phase < CORE_SHARE:
            for copy in sum_copies(matrix, phase + 1):
                copy.start()

    def on_the_way(step, table_of_steps):
        for when, actions in table_of_steps.items():

            @pl.when(step == when)
            def _():
                for matrix, phase in actions:
                    advance(matrix, phase)

    fetched = (
        (weights_a_in, weights_a),
        (weights_b_in, weights_b),
        (rolled_in, rolled),
        (mixed_in, mixed),
        (inverse_in, inverse),
        (contexts_in, contexts),
        (rel_in, rel),
    )
    fetches = [
        pltpu.make_async_copy(src, dst, load.at[n]) for n, (src, dst) in enumerate(fetched)
    ]

    def roll_copies(window, which=(1, 2, 3)):
        return pieces_to(
            outgoing,
            grad_context,
            lambda n: piece_send.at[window, n],
            lambda n: piece_recv.at[window, n],
            rep,
            shard,
            window,
            which=which,
        )

    def feed_forward(
        proj,
        fc1,
        fc2,
        middle,
        normed,
        normed_back,
        active,
        grad_hidden,
        grad_normed,
        branch,
        unrolled,
        grad_unrolled,
        final,
        fc1_bias,
        returned_context,
        order,
        cotangent,
    ):
        loads = [
            pltpu.make_async_copy(src, dst, load.at[len(fetched) + n])
            for n, (src, dst) in enumerate(
                (
                    (returned_in, returned_context),
                    (proj_in, proj),
                    (cotangent_in, cotangent),
                    (fc1_in, fc1),
                    (fc2_in, fc2),
                    (order_in, order),
                )
            )
        ]
        for copy in loads:
            copy.start()
        proj_bias = small_row(small_all, PROJ_BIAS).astype(f32)
        gain, shift = (small_row(small_all, row).astype(f32) for row in (LN2_GAIN, LN2_SHIFT))
        fc2_bias = small_row(small_all, FC2_BIAS).astype(f32)
        for owner in range(4):
            for k in range(4):
                lanes = slice(owner * D + k * 128, owner * D + (k + 1) * 128)
                fc1_bias[:, lanes] = small_all[owner, FC1_BIAS + k : FC1_BIAS + k + 1, :].astype(f32)
        sums[...] = jnp.zeros_like(sums)
        fc1_sum[...] = jnp.zeros_like(fc1_sum)
        for copy in loads[:2]:
            copy.wait()
        for first, length, _ in CHUNK_ROWS:
            rows = pl.ds(first, length)
            unrolled[rows, :] = dot(order_back[rows, :], returned_context[...]).astype(bf16)
            got = dot(unrolled[rows, :], proj[...]) + proj_bias
            middle[rows, :] = tokens[rows, :].astype(f32) + got
            normal, _ = norm_rows(middle[rows, :])
            normed[rows, :] = (normal * gain + shift).astype(bf16)
        for copy in loads[2:]:
            copy.wait()

        def forward_step(tile, carry):
            for n in range(2):
                lanes = pl.ds(pl.multiple_of((2 * tile + n) * FF_TILE, FF_TILE), FF_TILE)
                hidden = dot(normed[...], fc1[:, lanes]) + fc1_bias[:, lanes]
                share = 0.5 + 0.5 * lax.erf(hidden * 0.7071067811865476)
                active[:, lanes] = (hidden * share).astype(bf16)
                slope = share + hidden * jnp.exp(-0.5 * hidden * hidden) * 0.3989422804014327
                grad_hidden[:, lanes] = slope.astype(bf16)
            return carry

        for copy in fetches:
            copy.start()
        lax.fori_loop(0, FF // FF_TILE // 2, forward_step, 0)

        def fc2_step(tile, carry):
            lanes = pl.ds(pl.multiple_of(tile * 256, 256), 256)
            got = dot(active[:, lanes], cotangent[...], TN).astype(bf16)
            fc2_grad[tile // 2, lax.rem(tile, 2)] = got.reshape(2, 2, 64, D)
            return carry

        lax.fori_loop(0, FF // 256, fc2_step, 0)
        begin(FC2)
        for first, length, pieces in CHUNK_ROWS:
            rows = pl.ds(first, length)

            def backward_step(tile, carry):
                lanes = pl.ds(pl.multiple_of(tile * D, D), D)
                grad_active = dot(cotangent[rows, :], fc2[lanes, :], NT)
                grad = (grad_active * grad_hidden[rows, lanes].astype(f32)).astype(bf16)
                grad_hidden[rows, lanes] = grad
                fc1_sum[:, lanes] += jnp.sum(grad.astype(f32), 0, keepdims=True)
                return carry

            lax.fori_loop(0, FF // D, backward_step, 0)
            grad_normed[rows, :] = dot(grad_hidden[rows, :], fc1[...], NT)
            normal, over = norm_rows(middle[rows, :])
            grad_out = grad_normed[rows, :]
            scaled = grad_out * gain
            inner = (
                scaled
                - jnp.mean(scaled, -1, keepdims=True)
                - normal * jnp.mean(scaled * normal, -1, keepdims=True)
            )
            upper = cotangent[rows, :].astype(f32)
            grad_middle[rows, :] = upper + over * inner
            branch[rows, :] = grad_middle[rows, :].astype(bf16)
            for row, value in (
                (PROJ_BIAS, branch[rows, :].astype(f32)),
                (LN2_GAIN, grad_out * normal),
                (LN2_SHIFT, grad_out),
                (FC2_BIAS, upper),
            ):
                sums[row : row + 1, :] += jnp.sum(value, 0, keepdims=True)
            grad_unrolled[rows, :] = dot(branch[rows, :], proj[...], NT).astype(bf16)
            source = pl.ds(0, 400) if first == 0 else pl.ds(384, 400)
            for window in range(2):
                for piece in pieces:
                    at = pl.ds(window * PAD + FIRST_ROWS[piece], LENGTHS[piece])
                    got = dot(order[at, source], grad_unrolled[source, :]).astype(bf16)
                    if piece:
                        outgoing[at, :] = got
                    else:
                        grad_context[at, :] = got
            for window in range(2):
                for copy in roll_copies(window, [piece for piece in pieces if piece]):
                    copy.start()
        same = lax.broadcasted_iota(jnp.int32, (D, D), 0) == lax.broadcasted_iota(
            jnp.int32, (D, D), 1
        )
        unit = jnp.where(same, jnp.ones((), bf16), jnp.zeros((), bf16))
        normed_back[...] = dot(unit, normed[...], NT).astype(bf16)

        def fc1_step(tile, carry):
            lanes = pl.ds(pl.multiple_of(tile * 512, 512), 512)
            got = dot(normed_back[...], grad_hidden[:, lanes]).astype(bf16)
            fc1_grad[:, :, :, :, :, lanes] = got.reshape(4, 2, 2, 2, 16, 512)
            return carry

        lax.fori_loop(0, FF // 512, fc1_step, 0)
        begin(FC1)

        got = dot(unrolled[...], branch[...], TN).astype(bf16)
        proj_grad[...] = got.reshape(proj_grad.shape)
        begin(PROJ)
        advance(FC2, CORE_SUM)
        final[...] = (middle[...] + dot(active[...], fc2[...]) + fc2_bias).astype(bf16)
        written = pltpu.make_async_copy(final, output, load.at[len(fetched) + 6])
        written.start()
        for matrix in (FC1, PROJ):
            advance(matrix, CORE_SUM)
        written.wait()

    count_rows = tokens.shape[0]
    pl.run_scoped(
        feed_forward,
        pltpu.VMEM((D, D), bf16),
        pltpu.VMEM((D, FF), bf16),
        pltpu.VMEM((FF, D), bf16),
        pltpu.VMEM((count_rows, D), f32),
        pltpu.VMEM((count_rows, D), bf16),
        pltpu.VMEM((D, count_rows), bf16),
        pltpu.VMEM((count_rows, FF), bf16),
        pltpu.VMEM((count_rows, FF), bf16),
        pltpu.VMEM((count_rows, D), f32),
        pltpu.VMEM((count_rows, D), bf16),
        pltpu.VMEM((count_rows, D), bf16),
        pltpu.VMEM((count_rows, D), bf16),
        pltpu.VMEM((count_rows, D), bf16),
        pltpu.VMEM((1, FF), f32),
        pltpu.VMEM((2 * PAD, D), bf16),
        pltpu.VMEM((2 * PAD, count_rows), bf16),
        pltpu.VMEM((count_rows, D), bf16),
    )
    for copy in fetches:
        copy.wait()
    def return_copies(window):
        return pieces_to(
            outgoing,
            returned,
            lambda n: back_send.at[window, n],
            lambda n: back_recv.at[window, n],
            rep,
            shard,
            window,
        )

    def attend_back(attend, grads, rolled_back, pairs, pairs_out):
        head_of = lax.broadcasted_iota(jnp.int32, (1, 128), 1) // HD
        none = jnp.zeros((), bf16)

        def attend_copy(head):
            slot = lax.rem(head, 2)
            return pltpu.make_async_copy(
                attend_in.at[:, head], attend.at[slot], attend_sem.at[slot]
            )

        attend_copy(0).start()
        same = lax.broadcasted_iota(jnp.int32, (D, D), 0) == lax.broadcasted_iota(
            jnp.int32, (D, D), 1
        )
        unit = jnp.where(same, jnp.ones((), bf16), none)
        rolled_back[...] = dot(unit, rolled[...], NT).astype(bf16)

        def qkv_group(group):
            columns = [
                grads[:, part * D + group * 128 : part * D + (group + 1) * 128] for part in range(3)
            ]
            got = dot(rolled_back[...], jnp.concatenate(columns, 1)).astype(bf16)
            qkv_grads[group] = got.reshape(qkv_grads.shape[1:])
            begin(QKV + group)

        slow = (FC1, PROJ)
        first_schedule = {
            1: [(FC2, FIRST_SUM)],
            6: [(QKV + 0, CORE_SUM), *[(m, FIRST_SUM) for m in slow]],
            7: [(FC2, SECOND_SUM)],
            9: [(QKV + 0, FIRST_SUM)],
            10: [(QKV + 1, CORE_SUM), (FC2, NEXT_SUM)],
            12: [(QKV + 0, SECOND_SUM), *[(m, SECOND_SUM) for m in slow]],
            13: [(QKV + 1, FIRST_SUM), (FC2, Z_SUM)],
            14: [(QKV + 2, CORE_SUM)],
            15: [(QKV + 0, NEXT_SUM), *[(m, NEXT_SUM) for m in slow]],
        }
        second_schedule = {
            0: [(QKV + 1, SECOND_SUM)],
            1: [(QKV + 2, FIRST_SUM)],
            2: [(QKV + 3, CORE_SUM), (QKV + 1, NEXT_SUM), (QKV + 0, Z_SUM), (FC2, SHARE), *[(m, Z_SUM) for m in slow]],
            3: [(QKV + 2, SECOND_SUM)],
            4: [(QKV + 3, FIRST_SUM)],
            5: [(QKV + 2, NEXT_SUM), (QKV + 1, Z_SUM)],
            6: [(QKV + 3, SECOND_SUM), (QKV + 0, SHARE)],
            8: [(QKV + 2, Z_SUM), *[(m, SHARE) for m in slow]],
            9: [(QKV + 3, NEXT_SUM), (QKV + 1, SHARE)],
            11: [(QKV + 3, Z_SUM)],
            12: [(QKV + 2, SHARE)],
        }

        for window in range(2):
            for copy in roll_copies(window):
                copy.wait_recv()

        def head_step(head, carry):
            on_the_way(head, first_schedule)
            for done in range(1, HEADS // GROUP):

                @pl.when(head == done * GROUP)
                def _():
                    qkv_group(done - 1)

            @pl.when(head + 1 < HEADS)
            def _():
                attend_copy(head + 1).start()

            attend_copy(head).wait()
            slot = lax.rem(head, 2)
            group, member = head // GROUP, lax.rem(head, GROUP)

            def lanes(part):
                return pl.ds(pl.multiple_of(part * D + group * 128, 128), 128)

            mine = head_of == member
            both = []
            for window in range(2):
                rows = pl.ds(window * PAD, PAD)
                query = jnp.where(mine, mixed[rows, lanes(0)], none)
                key = jnp.where(mine, mixed[rows, lanes(1)], none)
                grad = grad_context[rows, lanes(0)].astype(f32) * inverse[rows, lanes(0)]
                grad = jnp.where(mine, grad, 0.0).astype(bf16)
                expo = attend[slot, window, :, :PAD]
                grad_attend = dot(grad, mixed[rows, lanes(2)], NT)
                inner = jnp.sum(
                    grad.astype(f32) * contexts[rows, lanes(0)].astype(f32), -1, keepdims=True
                )
                grad_scores = (expo.astype(f32) * (grad_attend - inner)).astype(bf16)
                both.append(grad_scores)
                for part, value in (
                    (0, dot(grad_scores, key) * SCALE),
                    (1, dot(grad_scores, query, TN) * SCALE),
                    (2, dot(expo, grad, TN)),
                ):
                    grads[rows, lanes(part)] = jnp.where(
                        mine, value.astype(bf16), grads[rows, lanes(part)]
                    )
            total = both[0].astype(f32) + both[1].astype(f32)
            for tile in range(TILES):
                part = total[:, tile * 128 : (tile + 1) * 128]
                if part.shape[1] < 128:
                    part = jnp.concatenate([part, jnp.zeros((PAD, 128 - part.shape[1]), f32)], 1)
                pairs[tile, pl.ds(head, PAD, stride=STRIDE), :] = part
            return carry

        lax.fori_loop(0, HEADS, head_step, 0)

        for window in range(2):
            for copy in roll_copies(window):
                copy.wait_send()

        for window in range(2):
            span = slice(window * PAD, (window + 1) * PAD)
            got = dot(grads[span, :HALF_QKV], weights_a[...], NT)
            got = got + dot(grads[span, HALF_QKV:], weights_b[...], NT)
            outgoing[span, :] = got.astype(bf16)
            for copy in return_copies(window):
                copy.start()
            rows = slice(window * PAD, window * PAD + LENGTHS[0])
            returned[rows, :] = outgoing[rows, :]
        qkv_group(HEADS // GROUP - 1)

        def round_step(step, carry):
            source = pl.ds(((1 - core) * HALF + step) * STRIDE, HEADS)
            at = pl.ds(pl.multiple_of(step * HEADS, HEADS), HEADS)
            for tile in range(TILES):
                pairs_out[tile, at, :] = pairs[tile, source, :].astype(bf16)
            return carry

        def pairs_copy(half):
            block = pl.ds(half * (HALF * HEADS // 2), HALF * HEADS // 2)
            return remote(
                pairs_out.at[:, block],
                pairs_in.at[:, block],
                pairs_send.at[half],
                pairs_recv.at[half],
                flip(rep, 0),
                shard,
            )

        for half in range(2):
            lax.fori_loop(half * (HALF // 2), (half + 1) * (HALF // 2), round_step, 0)
            pairs_copy(half).start()

        low_of = lax.broadcasted_iota(jnp.int32, (SPAN, LANES - 128), 0).astype(f32).astype(bf16)
        table_sum[...] = jnp.zeros_like(table_sum)
        for half in range(2):
            pairs_copy(half).wait_recv()

        def operands(total, index):
            width = index.shape[1]
            low = (index & (SPAN - 1)).astype(f32).astype(bf16)
            high = jnp.broadcast_to((index // SPAN).astype(f32).astype(bf16), (HEADS, width))
            nothing = jnp.zeros_like(total)
            left = jnp.concatenate(
                [jnp.where(high == jnp.asarray(s, bf16), total, nothing) for s in range(SPANS)], 0
            )
            hit = low_of[:, :width] == jnp.broadcast_to(low, (SPAN, width))
            return left, jnp.where(hit, jnp.ones((), bf16), jnp.zeros((), bf16))

        lane_of = lax.broadcasted_iota(jnp.int32, (1, 128), 1)

        def table_step(step, carry):
            on_the_way(step, second_schedule)
            factors = []
            for k in range(BATCH):
                row = step * BATCH + k
                there = core * HALF + row
                at = pl.ds(there * STRIDE, HEADS)
                near = pl.ds(pl.multiple_of(row * HEADS, HEADS), HEADS)
                index = rel[pl.ds(there, 1), :]
                sums_of = [pairs[t, at, :] + pairs_in[t, near, :].astype(f32) for t in range(TILES)]
                total = jnp.concatenate(sums_of[:-1], 1).astype(bf16)
                factors.append(operands(total, index[:, : LANES - 128]))
                last, places, turn = sums_of[-1], index[:, LANES - 128 :], 32 * (k % 4)
                if turn:
                    last = tail + pltpu.roll(last, turn, 1)
                    places = jnp.where(lane_of >= turn, pltpu.roll(places, turn, 1), tail_places)
                tail, tail_places = last, places
                if k % 4 == 3:
                    factors.append(operands(tail.astype(bf16), tail_places))
            left, right = zip(*factors)
            table_sum[...] += dot(jnp.concatenate(left, 1), jnp.concatenate(right, 1), NT)
            return carry

        lax.fori_loop(0, HALF // BATCH, table_step, 0)
        for half in range(2):
            pairs_copy(half).wait_send()
        sums[Q_BIAS : Q_BIAS + 1, :] = jnp.sum(grads[:, :D].astype(f32), 0, keepdims=True)
        sums[V_BIAS : V_BIAS + 1, :] = jnp.sum(grads[:, 2 * D :].astype(f32), 0, keepdims=True)

    pl.run_scoped(
        attend_back,
        pltpu.VMEM((2, 2, PAD, LANES), bf16),
        pltpu.VMEM((2 * PAD, 3 * D), bf16),
        pltpu.VMEM((D, 2 * PAD), bf16),
        pltpu.VMEM((TILES, PAD * STRIDE, 128), f32),
        pltpu.VMEM((TILES, HALF * HEADS, 128), bf16),
    )

    slab_rows = (pl.ds(0, TABLE_ROWS), pl.ds(TABLE_ROWS, SMALL))

    def slab_copies(part):
        return [
            remote(
                slab.at[lax.rem(shard + k, 4), slab_rows[part]],
                slab_z.at[3 - k, slab_rows[part]],
                slab_send.at[part, k - 1],
                slab_recv.at[part, 3 - k],
                rep,
                lax.rem(shard + k, 4),
            )
            for k in (1, 2, 3)
        ]

    def slab_share(part, k):
        block = slab_rep.at[rep, slab_rows[part]]
        return remote(
            block,
            block,
            slab_send.at[part, 2 + k],
            slab_recv.at[part, 2 + reps - k],
            lax.rem(rep + k, reps),
            shard,
        )

    def slab_onward(part):
        for copy in slab_copies(part):
            copy.wait_recv()
        rows = slab_rows[part]
        slab_rep[rep, rows] = slab[shard, rows] + (
            slab_z[0, rows] + slab_z[1, rows] + slab_z[2, rows]
        )

        def share_start(k, carry):
            slab_share(part, k).start()
            return carry

        lax.fori_loop(1, reps, share_start, 0)

    for owner in range(4):
        entries = jnp.concatenate(
            [table_sum[pl.ds(s * HEADS + GROUP * owner, GROUP), :] for s in range(SPANS)], 0
        )
        slab[owner, : SPANS * GROUP, :] = entries[:, :128]
        slab[owner, SPANS * GROUP : TABLE_ROWS, :] = entries[:, 128:]
    for copy in slab_copies(0):
        copy.start()

    for window in range(2):
        for copy in return_copies(window):
            copy.wait_recv()
    gain = small_row(small_all, LN1_GAIN).astype(f32)

    def norm_step(step, carry):
        gain_sum, shift_sum = carry
        rows = pl.ds(pl.multiple_of(step * 112, 16), 112)
        grad_out = dot(order_back[rows, :], returned[...])
        normal, over = norm_rows(tokens[rows, :].astype(f32))
        scaled = grad_out * gain
        inner = (
            scaled
            - jnp.mean(scaled, -1, keepdims=True)
            - normal * jnp.mean(scaled * normal, -1, keepdims=True)
        )
        grad_middle[rows, :] += over * inner
        return (
            gain_sum + jnp.sum(grad_out * normal, 0, keepdims=True),
            shift_sum + jnp.sum(grad_out, 0, keepdims=True),
        )

    nought = jnp.zeros((1, D), f32)
    some = lax.fori_loop(0, 4, norm_step, (nought, nought))
    slab_onward(0)
    gain_sum, shift_sum = lax.fori_loop(4, 7, norm_step, some)
    sums[LN1_GAIN : LN1_GAIN + 1, :] = gain_sum
    sums[LN1_SHIFT : LN1_SHIFT + 1, :] = shift_sum
    for owner in range(4):
        lanes = slice(owner * 128, (owner + 1) * 128)
        slab[owner, TABLE_ROWS:, :] = jnp.concatenate(
            [sums[:, lanes]]
            + [fc1_sum[:, owner * D + k * 128 : owner * D + (k + 1) * 128] for k in range(4)]
            + [jnp.zeros((4, 128), f32)],
            0,
        )
    for copy in slab_copies(1):
        copy.start()
    tokens_copy = pltpu.make_async_copy(grad_middle, grad_tokens, load.at[0])
    tokens_copy.start()

    slow = (FC1, PROJ)
    for matrix, phase in [(QKV + 3, SHARE)]:
        advance(matrix, phase)

    for matrix in range(count):
        advance(matrix, CORE_SHARE)
    outs = (fc1_out, fc2_out, proj_out, qkv_out_0, qkv_out_1, qkv_out_2, qkv_out_3)
    results = [
        pltpu.make_async_copy(held[matrix][5], outs[matrix], local.at[count + matrix])
        for matrix in range(count)
    ]
    for copy in results:
        copy.start()
    slab_onward(1)

    def share_wait(k, carry):
        for part in range(2):
            slab_share(part, k).wait()
        return carry

    lax.fori_loop(1, reps, share_wait, 0)

    def slab_step(k, total):
        return total + slab_rep[k]

    slab_out[...] = lax.fori_loop(1, reps, slab_step, slab_rep[0])

    for part in range(2):
        for copy in slab_copies(part):
            copy.wait_send()
    for window in range(2):
        for copy in return_copies(window):
            copy.wait_send()
    for matrix in range(count):
        for phase in range(CORE_SHARE + 1):
            for copy in sum_copies(matrix, phase):
                copy.wait_send()
    for copy in results + [tokens_copy]:
        copy.wait()


def rear(
    returned_context,
    tokens,
    cotangent,
    small_all,
    whole_proj,
    whole_fc1,
    whole_fc2,
    weights_a,
    weights_b,
    rolled,
    mixed,
    inverse,
    contexts,
    rel,
    attend,
):
    anywhere, inside = pl.BlockSpec(memory_space=pl.ANY), pl.BlockSpec(memory_space=pltpu.VMEM)
    reps = lax.axis_size("rep")
    dma = pltpu.SemaphoreType.DMA
    order = send_matrix()
    extra = max(1, reps.bit_length() - 4)
    held = []
    for rows, columns, _ in SUMMED:
        held += [
            pltpu.VMEM((4, 2, 2, rows, columns), bf16),
            pltpu.VMEM((4, 2, rows, columns), bf16),
            pltpu.VMEM((4, rows, columns), bf16),
            pltpu.VMEM((2, rows, columns), bf16),
            pltpu.VMEM((1 + extra, rows, columns), bf16),
            pltpu.VMEM((2, 2, 2, rows, columns), bf16),
        ]
    return pl.pallas_call(
        rear_kernel,
        out_shape=(
            jax.ShapeDtypeStruct(tokens.shape, bf16),
            jax.ShapeDtypeStruct(tokens.shape, f32),
            *[jax.ShapeDtypeStruct((2, 2, 2) + shape[:2], bf16) for shape in SUMMED],
            jax.ShapeDtypeStruct((SLAB, 128), f32),
        ),
        in_specs=[inside] * 3 + [anywhere] * 14,
        out_specs=(*[anywhere] * (2 + len(SUMMED)), inside),
        scratch_shapes=[
            pltpu.VMEM(weights_a.shape, bf16),
            pltpu.VMEM(weights_b.shape, bf16),
            pltpu.VMEM(rolled.shape, bf16),
            pltpu.VMEM(mixed.shape, bf16),
            pltpu.VMEM(inverse.shape, f32),
            pltpu.VMEM(contexts.shape, bf16),
            pltpu.VMEM(rel.shape, jnp.int32),
            pltpu.VMEM((2 * PAD, D), bf16),
            pltpu.VMEM((2 * PAD, D), bf16),
            pltpu.VMEM(tokens.shape, f32),
            pltpu.VMEM((2 * PAD, D), bf16),
            pltpu.VMEM((TILES, HALF * HEADS, 128), bf16),
            pltpu.VMEM((4, 2, 2, 2, 16, 2048), bf16),
            pltpu.VMEM((4, 2, 2, 2, 64, 512), bf16),
            pltpu.VMEM((4, 2, 2, 2, 16, 512), bf16),
            pltpu.VMEM((HEADS // GROUP, 4, 2, 2, 2, 16, 3 * 128), bf16),
            pltpu.VMEM((8, D), f32),
            pltpu.VMEM((1, FF), f32),
            pltpu.VMEM((SPANS * HEADS, SPAN), f32),
            pltpu.VMEM((4, SLAB, 128), f32),
            pltpu.VMEM((3, SLAB, 128), f32),
            pltpu.VMEM((reps, SLAB, 128), f32),
            *held,
            dma((len(SUMMED), CORE_SHARE + 1, 3)),
            dma((len(SUMMED), CORE_SHARE + 1, 3)),
            dma((len(SUMMED), extra)),
            dma((len(SUMMED), extra)),
            dma((2, 3)),
            dma((2, 3)),
            dma((2, 3)),
            dma((2, 3)),
            dma((2,)),
            dma((2,)),
            dma((2,)),
            dma((2, 3 + reps)),
            dma((2, 3 + reps)),
            dma((2 * len(SUMMED),)),
            dma((14,)),
        ],
        compiler_params=pltpu.CompilerParams(
            vmem_limit_bytes=VMEM_LIMIT, collective_id=1, has_side_effects=True
        ),
        name="rear",
    )(
        jnp.asarray(order.T, bf16),
        tokens,
        small_all,
        returned_context,
        jnp.asarray(order, bf16),
        cotangent,
        whole_proj,
        whole_fc1,
        whole_fc2,
        weights_a,
        weights_b,
        rolled,
        mixed,
        inverse,
        contexts,
        rel,
        attend,
    )


def finish_kernel(
    output_in,
    tokens_in,
    fc1_in,
    fc2_in,
    proj_in,
    qkv_0,
    qkv_1,
    qkv_2,
    qkv_3,
    slab,
    output,
    tokens,
    fc1,
    fc2,
    proj,
    qkv,
    table,
    fc1_bias,
    *vectors,
):
    output[...] = output_in[...]
    tokens[...] = tokens_in[...]
    for part, whole in ((fc1_in, fc1), (fc2_in, fc2), (proj_in, proj)):
        whole[...] = part[...].astype(f32).reshape(whole.shape)
    for group, part in enumerate((qkv_0, qkv_1, qkv_2, qkv_3)):
        got = part[...].astype(f32).reshape(qkv.shape[0], 3 * 128)
        for n in range(3):
            first = n * D + group * 128
            qkv[:, first : first + 128] = got[:, n * 128 : (n + 1) * 128]
    entries = [
        slab[pl.ds((half * SPANS + span) * GROUP, GROUP), :]
        for span in range(SPANS)
        for half in range(2)
    ]
    table[...] = jnp.concatenate(entries, 1)[:, :TABLE]
    for row, vector in enumerate(vectors):
        vector[...] = slab[TABLE_ROWS + row : TABLE_ROWS + row + 1, :]
    first = TABLE_ROWS + FC1_BIAS
    fc1_bias[...] = jnp.concatenate([slab[first + k : first + k + 1, :] for k in range(4)], 1)


def finish(output, grad_tokens, fc1, fc2, proj, qkv, slab):
    inside = pl.BlockSpec(memory_space=pltpu.VMEM)
    shapes = [(128, FF), (FF // 4, D), (128, D), (128, 3 * D), (GROUP, TABLE), (1, D)]
    shapes += [(1, 128)] * FC1_BIAS
    return pl.pallas_call(
        finish_kernel,
        out_shape=(
            jax.ShapeDtypeStruct(output.shape, bf16),
            jax.ShapeDtypeStruct(grad_tokens.shape, f32),
            *[jax.ShapeDtypeStruct(shape, f32) for shape in shapes],
        ),
        in_specs=[inside] * 10,
        out_specs=(inside,) * (2 + len(shapes)),
        compiler_params=pltpu.CompilerParams(vmem_limit_bytes=VMEM_LIMIT),
        name="finish",
    )(output, grad_tokens, fc1, fc2, proj, *qkv, slab)


def shards(
    tokens,
    region,
    rel_index,
    ln1_gain,
    ln1_shift,
    w_qkv,
    q_bias,
    v_bias,
    table,
    w_proj,
    proj_bias,
    ln2_gain,
    ln2_shift,
    w_fc1,
    fc1_bias,
    w_fc2,
    fc2_bias,
    cotangent,
):
    small = jnp.zeros((SMALL, 128), f32)
    vectors = (ln1_gain, ln1_shift, q_bias, v_bias, proj_bias, ln2_gain, ln2_shift, fc2_bias, fc1_bias)
    for row, vector in enumerate(vectors):
        block = vector.reshape(-1, 128).astype(f32)
        small += jnp.pad(block, ((row, SMALL - row - block.shape[0]), (0, 0)))
    small = small.astype(bf16)
    labels = region.reshape(WT, WH, 2, WW).transpose(2, 0, 1, 3).reshape(2, WIN)
    labels = pieces_of(labels, 1, -1)
    row_ids = jnp.pad(labels, ((0, 0), (0, LANES - PAD)), constant_values=-1)[:, None]
    (
        whole_qkv_a,
        whole_qkv_b,
        whole_proj,
        whole_fc1,
        whole_fc2,
        small,
        rolled,
        qkv,
        attend,
        inverse,
        contexts,
        returned,
        rel,
    ) = front(
        tokens.reshape(-1, D),
        small,
        table.T,
        row_ids,
        rel_index,
        w_qkv,
        w_proj,
        w_fc1,
        w_fc2,
    )
    output, grad_tokens, grad_w_fc1, grad_w_fc2, grad_w_proj, *grads_qkv, slab = rear(
        returned,
        tokens.reshape(-1, D),
        cotangent.reshape(-1, D),
        small,
        whole_proj,
        whole_fc1,
        whole_fc2,
        whole_qkv_a,
        whole_qkv_b,
        rolled,
        qkv,
        inverse,
        contexts,
        rel,
        attend,
    )
    (
        output,
        grad_tokens,
        grad_w_fc1,
        grad_w_fc2,
        grad_w_proj,
        grad_w_qkv,
        grad_table,
        grad_fc1_bias,
        *vectors,
    ) = finish(output, grad_tokens, grad_w_fc1, grad_w_fc2, grad_w_proj, grads_qkv, slab)
    output = output.reshape(tokens.shape)
    grad_tokens = grad_tokens.reshape(tokens.shape)
    grad_table = grad_table.T
    grad_fc1_bias = grad_fc1_bias.reshape(-1)
    vectors = [vector.reshape(-1) for vector in vectors]
    grad_ln1_gain, grad_ln1_shift = vectors[LN1_GAIN], vectors[LN1_SHIFT]
    grad_q_bias, grad_v_bias = vectors[Q_BIAS], vectors[V_BIAS]
    grad_proj_bias, grad_fc2_bias = vectors[PROJ_BIAS], vectors[FC2_BIAS]
    grad_ln2_gain, grad_ln2_shift = vectors[LN2_GAIN], vectors[LN2_SHIFT]
    return (
        output,
        grad_tokens,
        grad_ln1_gain,
        grad_ln1_shift,
        grad_w_qkv,
        grad_q_bias,
        grad_v_bias,
        grad_table,
        grad_w_proj,
        grad_proj_bias,
        grad_ln2_gain,
        grad_ln2_shift,
        grad_w_fc1,
        grad_fc1_bias,
        grad_w_fc2,
        grad_fc2_bias,
    )


def solution(mesh):
    return jax.shard_map(
        shards,
        mesh=mesh,
        in_specs=(
            P("rep", "shard", None, None),
            P("shard", None),
            P(),
            P("shard"),
            P("shard"),
            P("shard", None),
            P("shard"),
            P("shard"),
            P(None, "shard"),
            P("shard", None),
            P("shard"),
            P("shard"),
            P("shard"),
            P("shard", None),
            P("shard"),
            P("shard", None),
            P("shard"),
            P("rep", "shard", None, None),
        ),
        out_specs=(
            P("rep", "shard", None, None),
            P("rep", "shard", None, None),
            P("shard"),
            P("shard"),
            P("shard", None),
            P("shard"),
            P("shard"),
            P(None, "shard"),
            P("shard", None),
            P("shard"),
            P("shard"),
            P("shard"),
            P("shard", None),
            P("shard"),
            P("shard", None),
            P("shard"),
        ),
        check_vma=False,
    )
```

```python
import functools

import jax
import jax.numpy as jnp
import numpy as np
from jax import lax
from jax.experimental import pallas as pl
from jax.experimental.pallas import tpu as pltpu
from jax.sharding import PartitionSpec as P

D = 512
HEADS = 16
HD = 32
WT = 8
WH = 7
WW = 7
WIN = 392
TABLE = 2535
FF = 2048
FF_TILE = 256
PAD = 416
LANES = 512
GROUP = 4
CHUNKS = 20
SCALE = HD ** (-0.5)
NN = (((1,), (0,)), ((), ()))
NT = (((1,), (1,)), ((), ()))
TN = (((0,), (0,)), ((), ()))
VMEM_LIMIT = 60 * 2**20
f32 = jnp.float32
bf16 = jnp.bfloat16

PIECES = (
    ((0, 4), (0, 4), 112, 0),
    ((4, 8), (0, 4), 112, 112),
    ((0, 4), (4, 7), 96, 224),
    ((4, 8), (4, 7), 96, 320),
)


def send_matrix():
    matrix = np.zeros((2 * PAD, WT * WH * 2 * WW), np.float32)
    for window in range(2):
        for (t0, t1), (h0, h1), _, first in PIECES:
            row = window * PAD + first
            for t in range(t0, t1):
                for h in range(h0, h1):
                    for w in range(WW):
                        column = (window * WW + w + WW // 2) % (2 * WW)
                        source = ((t + 4) % WT * WH + (h + 3) % WH) * 2 * WW + column
                        matrix[row, source] = 1.0
                        row += 1
    return matrix


def spread_matrix():
    source = np.arange(WIN).reshape(WT, WH, WW)
    matrix = np.zeros((PAD, WIN), np.float32)
    for (t0, t1), (h0, h1), _, first in PIECES:
        tokens = source[t0:t1, h0:h1].reshape(-1)
        matrix[first + np.arange(tokens.size), tokens] = 1.0
    return matrix


def pieces_of(array, axis, fill):
    shape = array.shape
    split = array.reshape(shape[:axis] + (WT, WH, WW) + shape[axis + 1 :])
    parts = []
    for (t0, t1), (h0, h1), padded, _ in PIECES:
        part = lax.slice_in_dim(lax.slice_in_dim(split, t0, t1, axis=axis), h0, h1, axis=axis + 1)
        length = (t1 - t0) * (h1 - h0) * WW
        part = part.reshape(shape[:axis] + (length,) + shape[axis + 1 :])
        widths = [(0, 0, 0)] * len(shape)
        widths[axis] = (0, padded - length, 0)
        parts.append(lax.pad(part, jnp.asarray(fill, array.dtype), widths))
    return jnp.concatenate(parts, axis)


def dot(a, b, dims=NN):
    return lax.dot_general(a, b, dims, preferred_element_type=f32)


MESH = pl.DeviceIdType.MESH
PARTS = 8
FIRST_ROWS = tuple(first for _, _, _, first in PIECES)
LENGTHS = tuple(padded for _, _, padded, _ in PIECES)
ACROSS = (0, 2, 1, 3)
LN1_GAIN, LN1_SHIFT, Q_BIAS, V_BIAS, PROJ_BIAS, LN2_GAIN, LN2_SHIFT, FC2_BIAS, FC1_BIAS = range(9)
SMALL = 16


def place():
    rep, shard = lax.axis_index("rep"), lax.axis_index("shard")
    return rep, shard, lax.rem(rep, 2), lax.rem(rep // 2, 2), lax.rem(rep // 4, 2)


def flip(rep, bit):
    low = lax.rem(rep // (1 << bit), 2)
    return rep + (1 - 2 * low) * (1 << bit)


def remote(src, dst, send, recv, rep, shard):
    return pltpu.make_async_remote_copy(
        src_ref=src,
        dst_ref=dst,
        send_sem=send,
        recv_sem=recv,
        device_id={"rep": rep, "shard": shard},
        device_id_type=MESH,
    )


def greet(peers):
    barrier = pltpu.get_barrier_semaphore()
    for rep, shard in peers:
        pl.semaphore_signal(
            barrier, inc=1, device_id={"rep": rep, "shard": shard}, device_id_type=MESH
        )
    pl.semaphore_wait(barrier, len(peers))


def peers_of(rep, shard):
    return [(rep, lax.rem(shard + k, 4)) for k in (1, 2, 3)] + [
        (flip(rep, bit), shard) for bit in (0, 1, 2)
    ]


def quarter_across(shard, bits):
    low, high = lax.rem(shard, 2), shard // 2
    if bits & 1:
        low = 1 - low
    if bits & 2:
        high = 1 - high
    return high * 2 + low


def pieces_to(source, target, send, recv, rep, shard, window, columns=None, which=(3, 1, 2)):
    copies = []
    for piece in which:
        rows = pl.ds(
            pl.multiple_of(window * PAD + FIRST_ROWS[piece], 16), LENGTHS[piece]
        )
        at = (rows,) if columns is None else (rows, columns)
        copies.append(
            remote(
                source.at[at],
                target.at[at],
                send(piece - 1),
                recv(piece - 1),
                rep,
                quarter_across(shard, ACROSS[piece]),
            )
        )
    return copies


def norm_rows(rows):
    centre = rows - jnp.mean(rows, -1, keepdims=True)
    inverse = lax.rsqrt(jnp.mean(centre * centre, -1, keepdims=True) + 1e-05)
    return centre * inverse, inverse


def small_row(ref, row):
    return jnp.concatenate([ref[s, row : row + 1, :] for s in range(4)], 1)


FIXED = 4096.0
TAIL = 112
Z_PHASE, NEXT_PHASE, FIRST_PHASE, SECOND_PHASE, CORE_PHASE = range(5)
X_FIRST = (True, False, True, False, True)
HALF_QKV = 3 * D // 2


def front_kernel(
    tokens,
    order,
    spread,
    small,
    table,
    row_ids,
    rel,
    qkv_part,
    proj_part,
    fc1_part,
    fc2_part,
    qkv_whole_a,
    qkv_whole_b,
    proj_whole,
    fc1_whole,
    fc2_whole,
    small_out,
    rolled_out,
    mixed_out,
    attend_out,
    inverse_out,
    context_out,
    back_out,
    rel_out,
    small_all,
    table_all,
    table_wide,
    outgoing,
    arriving,
    rolled,
    weights_a,
    weights_b,
    mixed,
    index,
    index_tail,
    bias_tail,
    bias,
    mask,
    attend,
    inverse,
    contexts,
    gather_send,
    gather_recv,
    small_send,
    small_recv,
    bias_send,
    bias_recv,
    piece_send,
    piece_recv,
    back_send,
    back_recv,
    local,
    attend_sem,
):
    rep, shard, core, x_bit, y_bit = place()
    greet(peers_of(rep, shard))
    first_half, second_half = pl.ds(0, HALF_QKV), pl.ds(HALF_QKV, HALF_QKV)
    parts = (
        qkv_part.at[:, :, :, :, first_half],
        qkv_part.at[:, :, :, :, second_half],
        proj_part,
        fc1_part,
        fc2_part,
    )
    wholes = (weights_a, weights_b, proj_whole, fc1_whole, fc2_whole)
    feed_forward = (2, 3, 4)

    def gather(matrix, phase):
        copies = []
        whole = wholes[matrix]
        here = (y_bit, x_bit, core)

        def along_z(n, source, at, bits):
            return remote(
                source,
                whole.at[(at,) + here],
                gather_send.at[matrix, phase, n],
                gather_recv.at[matrix, phase, n],
                rep,
                quarter_across(shard, bits),
            )

        if phase == Z_PHASE:
            own_part = parts[matrix].at[here]
            return [along_z(0, own_part, shard, 2), along_z(1, own_part, shard, 1)]
        if phase == NEXT_PHASE:
            across = quarter_across(shard, 2)
            return [along_z(0, whole.at[(across,) + here], across, 1)]
        for k in (1, 2, 3):
            at = lax.rem(shard + k, 4)
            x_first = X_FIRST[matrix]
            if phase == FIRST_PHASE:
                block, partner = whole.at[at, y_bit, x_bit, core], flip(rep, 1 if x_first else 2)
            elif phase == SECOND_PHASE and x_first:
                block, partner = whole.at[at, y_bit, :, core], flip(rep, 2)
            elif phase == SECOND_PHASE:
                block, partner = whole.at[at, :, x_bit, core], flip(rep, 1)
            else:
                block, partner = whole.at[at, :, :, core], flip(rep, 0)
            copies.append(
                remote(
                    block,
                    block,
                    gather_send.at[matrix, phase, k - 1],
                    gather_recv.at[matrix, phase, k - 1],
                    partner,
                    shard,
                )
            )
        return copies

    def start(matrix, phase):
        for copy in gather(matrix, phase):
            copy.start()

    def arrived(matrix, phase):
        for copy in gather(matrix, phase):
            copy.wait_recv()

    def small_copies():
        return [
            remote(
                small_all.at[shard],
                small_all.at[shard],
                small_send.at[0, k - 1],
                small_recv.at[0, 3 - k],
                rep,
                lax.rem(shard + k, 4),
            )
            for k in (1, 2, 3)
        ]

    def table_copy(k):
        return remote(
            table_all.at[shard],
            table_all.at[shard],
            small_send.at[1, k - 1],
            small_recv.at[1, 3 - k],
            rep,
            lax.rem(shard + k, 4),
        )

    def table_copies(action):
        for k in (1, 2, 3):
            if action == "recv":
                wanted = lax.rem(shard + 4 - k, 4) // 2 == core
            else:
                wanted = shard // 2 == core

            @pl.when(wanted)
            def _():
                if action == "start":
                    table_copy(k).start()
                elif action == "recv":
                    table_copy(k).wait_recv()
                else:
                    table_copy(k).wait_send()

    small_all[shard] = small[...]
    columns = table[...].astype(f32)
    spare = jnp.zeros((GROUP, CHUNKS * 128 - TABLE), f32)
    for chunk in range(CHUNKS):
        piece = columns[:, chunk * 128 : (chunk + 1) * 128]
        if chunk == CHUNKS - 1:
            piece = jnp.concatenate([piece, spare], 1)
        table_all[shard, chunk * GROUP : (chunk + 1) * GROUP, :] = piece
    table_copies("start")
    for copy in small_copies():
        copy.start()
    start(0, Z_PHASE)
    start(1, Z_PHASE)
    own = [
        pltpu.make_async_copy(parts[m], wholes[m].at[shard], local.at[m]) for m in feed_forward
    ]
    for copy in own:
        copy.start()
    weights_a[shard] = qkv_part[..., :HALF_QKV]
    weights_b[shard] = qkv_part[..., HALF_QKV:]

    outgoing[...] = dot(order[...], tokens[...]).astype(bf16)

    def roll_copies(window):
        return pieces_to(
            outgoing,
            arriving,
            lambda n: piece_send.at[window, n],
            lambda n: piece_recv.at[window, n],
            rep,
            shard,
            window,
        )

    for copy in roll_copies(0):
        copy.start()
    for window in range(2):
        rows = slice(window * PAD, window * PAD + LENGTHS[0])
        arriving[rows, :] = outgoing[rows, :]

    rel_index = rel[...]
    digits = (rel_index // 256).astype(f32).astype(bf16), (rel_index & 255).astype(f32).astype(bf16)
    moved = []
    for digit in digits:
        half = dot(spread[...], digit).astype(bf16)
        moved.append(dot(half, spread[...], NT).astype(jnp.int32))
    index[:, :PAD] = moved[0] * 256 + moved[1]
    index[:, PAD:] = jnp.zeros((PAD, LANES - PAD), jnp.int32)

    ids = lax.broadcasted_iota(jnp.int32, (8, LANES), 0)
    for window in range(2):
        kinds = jnp.where(row_ids[window] + 1 == ids, 1.0, 0.0).astype(bf16)[:, :PAD]
        mask[window] = (dot(kinds, kinds, TN) - 1.0) * 1e30

    for copy in small_copies():
        copy.wait_recv()
    table_copies("recv")

    for block in range(4):
        count = min(TAIL, PAD - block * TAIL)
        lanes = slice(block * 32, block * 32 + 32)
        index_tail[:count, lanes] = index[block * TAIL : block * TAIL + count, PAD - 32 : PAD]
        if count < TAIL:
            index_tail[count:, lanes] = jnp.zeros((TAIL - count, 32), jnp.int32)

    upper, lower = (
        jnp.floor(table_all[2 * core + n] * FIXED + 0.5).astype(jnp.int32) for n in range(2)
    )
    words = upper * 65536 + (lower + 32768)
    for chunk in range(CHUNKS):
        for head in range(GROUP):
            row = chunk * GROUP + head
            table_wide[chunk, head] = jnp.broadcast_to(words[row : row + 1, :], (8, 128))
    mine = core * (HEADS // 2)

    def bias_copy(rows, step):
        block = bias.at[pl.ds(mine, HEADS // 2), rows]
        return remote(block, block, bias_send.at[step], bias_recv.at[step], flip(rep, 0), shard)

    def on_the_way(step, table_of_steps):
        for when, actions in table_of_steps.items():

            @pl.when(step == when)
            def _():
                for action, matrix, phase in actions:
                    action(matrix, phase)

    def advance(matrix, phase):
        arrived(matrix, phase)
        if phase < CORE_PHASE:
            start(matrix, phase + 1)

    schedule = {
        4: [(advance, 0, Z_PHASE), (advance, 1, Z_PHASE), *[(start, m, Z_PHASE) for m in feed_forward]],
        11: [(advance, 0, NEXT_PHASE), (advance, 1, NEXT_PHASE)],
        18: [(advance, 0, FIRST_PHASE), (advance, 1, FIRST_PHASE)],
        20: [*[(advance, m, Z_PHASE) for m in feed_forward]],
    }
    later = {
        1: [*[(advance, m, NEXT_PHASE) for m in feed_forward]],
        6: [*[(advance, m, FIRST_PHASE) for m in feed_forward]],
    }

    def look_up(here):
        found = [[] for _ in range(GROUP)]
        for s in (0, 8):
            low, high = here[s : s + 8] & 127, here[s : s + 8] >> 7
            values = [None] * GROUP
            for chunk in range(CHUNKS):
                hit = high == chunk
                for head in range(GROUP):
                    value = jnp.take_along_axis(table_wide[chunk, head], low, axis=1)
                    values[head] = jnp.where(hit, value, values[head]) if chunk else value
            for head in range(GROUP):
                found[head].append(values[head])
        joined = [jnp.concatenate(pair, 0) for pair in found]
        uppers = [(word >> 16).astype(f32) for word in joined]
        lowers = [((word & 65535) - 32768).astype(f32) for word in joined]
        return [(value * (1 / FIXED)).astype(bf16) for value in uppers + lowers]

    def tail_step(step, carry):
        rows = pl.ds(pl.multiple_of(step * 16, 16), 16)
        for head, value in enumerate(look_up(index_tail[rows, :])):
            bias_tail[head, rows, :] = value
        return carry

    lax.fori_loop(0, TAIL // 16, tail_step, 0)

    def untail_step(head, carry):
        for block in range(4):
            count = min(TAIL, PAD - block * TAIL)
            value = bias_tail[head, :count, block * 32 : block * 32 + 32]
            bias[mine + head, block * TAIL : block * TAIL + count, PAD - 32 : PAD] = value
        return carry

    lax.fori_loop(0, HEADS // 2, untail_step, 0)

    def bias_step(step, carry):
        on_the_way(step, schedule)
        rows = pl.ds(pl.multiple_of(step * 16, 16), 16)
        for tile in range(3):
            lanes = slice(tile * 128, (tile + 1) * 128)
            for head, value in enumerate(look_up(index[rows, lanes])):
                bias[mine + head, rows, lanes] = value
        bias_copy(rows, step).start()
        return carry

    lax.fori_loop(0, PAD // 16, bias_step, 0)
    for copy in roll_copies(1):
        copy.start()
    for n in range(2):
        advance(n, SECOND_PHASE)

    for n in range(2):
        arrived(n, CORE_PHASE)
    q_bias, v_bias = small_row(small_all, Q_BIAS), small_row(small_all, V_BIAS)
    mixed_bias = jnp.concatenate([q_bias, jnp.zeros_like(q_bias), v_bias], 1).astype(f32)
    gain, shift = small_row(small_all, LN1_GAIN), small_row(small_all, LN1_SHIFT)

    def norm_step(step, carry):
        rows = pl.ds(pl.multiple_of(step * 208, 16), 208)
        normal, _ = norm_rows(arriving[rows, :].astype(f32))
        rolled[rows, :] = (normal * gain.astype(f32) + shift.astype(f32)).astype(bf16)
        return carry

    def mix(window):
        for copy in roll_copies(window):
            copy.wait_recv()
        lax.fori_loop(2 * window, 2 * window + 2, norm_step, 0)
        span = slice(window * PAD, (window + 1) * PAD)
        for n, weight in enumerate((weights_a, weights_b)):
            lanes = slice(n * HALF_QKV, (n + 1) * HALF_QKV)
            got = dot(rolled[span, :], weight[...].reshape(D, HALF_QKV))
            mixed[span, lanes] = (got + mixed_bias[:, lanes]).astype(bf16)

    mix(0)
    keep = [
        pltpu.make_async_copy(rolled, rolled_out, local.at[5]),
        pltpu.make_async_copy(mixed, mixed_out, local.at[6]),
        pltpu.make_async_copy(index, rel_out, local.at[7]),
        pltpu.make_async_copy(small_all, small_out, local.at[8]),
        pltpu.make_async_copy(inverse, inverse_out, local.at[9]),
        pltpu.make_async_copy(contexts, context_out, local.at[12]),
        pltpu.make_async_copy(weights_a, qkv_whole_a, local.at[0]),
        pltpu.make_async_copy(weights_b, qkv_whole_b, local.at[1]),
    ]

    def bias_wait(step, carry):
        bias_copy(pl.ds(pl.multiple_of(step * 16, 16), 16), step).wait_recv()
        return carry

    lax.fori_loop(0, PAD // 16, bias_wait, 0)

    head_of = lax.broadcasted_iota(jnp.int32, (1, 128), 1) // HD
    none = jnp.zeros((), bf16)
    ones = jnp.ones((PAD, 128), bf16)

    def attend_copy(step):
        window, pair, slot = step // (HEADS // 2), lax.rem(step, HEADS // 2), lax.rem(step, 2)
        return pltpu.make_async_copy(
            attend.at[slot], attend_out.at[window, pl.ds(2 * pair, 2)], attend_sem.at[slot]
        )

    def back_copies(step):
        window, group = step // (HEADS // 2), lax.rem(step // 2, HEADS // GROUP)
        lanes = pl.ds(pl.multiple_of(group * 128, 128), 128)
        return pieces_to(
            contexts,
            back_out,
            lambda n: back_send.at[window, group, n],
            lambda n: back_recv.at[window, group, n],
            rep,
            shard,
            window,
            lanes,
        )

    def attend_step(step, carry):
        on_the_way(step, later)

        @pl.when(step == HEADS // 2)
        def _():
            mix(1)

        @pl.when(step >= 2)
        def _():
            attend_copy(step - 2).wait()

        window, slot = step // (HEADS // 2), lax.rem(step, 2)
        rows = pl.ds(pl.multiple_of(window * PAD, 16), PAD)
        for n in range(2):
            head = 2 * lax.rem(step, HEADS // 2) + n
            group, member = head // GROUP, lax.rem(head, GROUP)

            def lanes(part):
                return pl.ds(pl.multiple_of(part * D + group * 128, 128), 128)

            own_lanes = head_of == member
            query = jnp.where(own_lanes, mixed[rows, lanes(0)], none)
            value = jnp.where(own_lanes, mixed[rows, lanes(2)], none)
            scores = dot(query, mixed[rows, lanes(1)], NT) * SCALE
            scores = scores + bias[head, :, :PAD].astype(f32) + mask[window]
            expo = jnp.exp(scores - jnp.max(scores, -1, keepdims=True)).astype(bf16)
            attend[slot, n, :, :PAD] = expo
            result = dot(expo, jnp.concatenate([value, ones], 1))
            over = 1.0 / result[:, 128:]
            context = (result[:, :128] * over).astype(bf16)
            contexts[rows, lanes(0)] = jnp.where(own_lanes, context, contexts[rows, lanes(0)])
            inverse[rows, lanes(0)] = jnp.where(own_lanes, over, inverse[rows, lanes(0)])
        attend_copy(step).start()

        @pl.when(lax.rem(step, 2) == 1)
        def _():
            for copy in back_copies(step):
                copy.start()

        return carry

    lax.fori_loop(0, HEADS, attend_step, 0)
    for copy in keep:
        copy.start()
    for matrix in feed_forward:
        advance(matrix, SECOND_PHASE)
    stay = [
        pltpu.make_async_copy(
            contexts.at[pl.ds(w * PAD, LENGTHS[0])],
            back_out.at[pl.ds(w * PAD, LENGTHS[0])],
            local.at[10 + w],
        )
        for w in range(2)
    ]
    for copy in stay:
        copy.start()
    for matrix in feed_forward:
        arrived(matrix, CORE_PHASE)
    attend_copy(HEADS - 2).wait()
    attend_copy(HEADS - 1).wait()

    def back_wait(step, carry):
        for copy in back_copies(step * 2):
            copy.wait()
        return carry

    lax.fori_loop(0, 2 * HEADS // GROUP, back_wait, 0)

    def bias_sent(step, carry):
        bias_copy(pl.ds(pl.multiple_of(step * 16, 16), 16), step).wait_send()
        return carry

    lax.fori_loop(0, PAD // 16, bias_sent, 0)
    for copy in small_copies():
        copy.wait_send()
    table_copies("send")
    for window in range(2):
        for copy in roll_copies(window):
            copy.wait_send()
    for matrix in range(5):
        for phase in range(CORE_PHASE + 1):
            for copy in gather(matrix, phase):
                copy.wait_send()
    for copy in own + keep + stay:
        copy.wait()


def front(tokens, small, table, row_ids, rel_index, w_qkv, w_proj, w_fc1, w_fc2):
    anywhere, inside = pl.BlockSpec(memory_space=pl.ANY), pl.BlockSpec(memory_space=pltpu.VMEM)
    cut = (2, 2, 2)
    weights = [
        w.reshape(cut + (w.shape[0] // PARTS, w.shape[1])) for w in (w_qkv, w_proj, w_fc1, w_fc2)
    ]
    half = (4,) + weights[0].shape[:-1] + (HALF_QKV,)
    wholes = [jax.ShapeDtypeStruct(half, bf16)] * 2
    wholes += [jax.ShapeDtypeStruct((4,) + w.shape, bf16) for w in weights[1:]]
    dma = pltpu.SemaphoreType.DMA
    results = pl.pallas_call(
        front_kernel,
        out_shape=(
            *wholes,
            jax.ShapeDtypeStruct((4, SMALL, 128), bf16),
            jax.ShapeDtypeStruct((2 * PAD, D), bf16),
            jax.ShapeDtypeStruct((2 * PAD, 3 * D), bf16),
            jax.ShapeDtypeStruct((2, HEADS, PAD, LANES), bf16),
            jax.ShapeDtypeStruct((2 * PAD, D), f32),
            jax.ShapeDtypeStruct((2 * PAD, D), bf16),
            jax.ShapeDtypeStruct((2 * PAD, D), bf16),
            jax.ShapeDtypeStruct((PAD, LANES), jnp.int32),
        ),
        in_specs=[inside] * 11,
        out_specs=(anywhere,) * 13,
        scratch_shapes=[
            pltpu.VMEM((4, SMALL, 128), bf16),
            pltpu.VMEM((4, GROUP * CHUNKS, 128), f32),
            pltpu.VMEM((CHUNKS, GROUP, 8, 128), jnp.int32),
            pltpu.VMEM((2 * PAD, D), bf16),
            pltpu.VMEM((2 * PAD, D), bf16),
            pltpu.VMEM((2 * PAD, D), bf16),
            pltpu.VMEM(half, bf16),
            pltpu.VMEM(half, bf16),
            pltpu.VMEM((2 * PAD, 3 * D), bf16),
            pltpu.VMEM((PAD, LANES), jnp.int32),
            pltpu.VMEM((TAIL, 128), jnp.int32),
            pltpu.VMEM((HEADS // 2, TAIL, 128), bf16),
            pltpu.VMEM((HEADS, PAD, LANES), bf16),
            pltpu.VMEM((2, PAD, PAD), f32),
            pltpu.VMEM((2, 2, PAD, LANES), bf16),
            pltpu.VMEM((2 * PAD, D), f32),
            pltpu.VMEM((2 * PAD, D), bf16),
            dma((5, CORE_PHASE + 1, 3)),
            dma((5, CORE_PHASE + 1, 3)),
            dma((2, 3)),
            dma((2, 3)),
            dma((PAD // 16,)),
            dma((PAD // 16,)),
            dma((2, 3)),
            dma((2, 3)),
            dma((2, HEADS // GROUP, 3)),
            dma((2, HEADS // GROUP, 3)),
            dma((13,)),
            dma((2,)),
        ],
        compiler_params=pltpu.CompilerParams(
            vmem_limit_bytes=VMEM_LIMIT, collective_id=0, has_side_effects=True
        ),
        name="front",
    )(
        tokens,
        jnp.asarray(send_matrix(), bf16),
        jnp.asarray(spread_matrix(), bf16),
        small,
        table,
        row_ids,
        rel_index,
        *weights,
    )
    whole = [w.reshape(-1, w.shape[-1]) for w in results[:5]]
    return (*whole, *results[5:])


CORE_SUM, FIRST_SUM, SECOND_SUM, NEXT_SUM, Z_SUM, SHARE, CORE_SHARE = range(7)
SUMMED = ((16, 2048, True), (64, 512, False), (16, 512, True))
SUMMED += tuple((16, 3 * 128, group % 2 == 0) for group in range(HEADS // GROUP))
FC1, FC2, PROJ, QKV = range(4)
STRIDE = HEADS + 1
CHUNK_ROWS = ((0, 400, (3, 1)), (400, 384, (2, 0)))
SPAN = 256
SPANS = -(-TABLE // SPAN)
BATCH = 16
HALF = PAD // 2
TILES = LANES // 128
TABLE_ROWS = 2 * SPANS * GROUP
SLAB = TABLE_ROWS + SMALL


def rear_kernel(
    order_back,
    tokens,
    small_all,
    returned_in,
    order_in,
    cotangent_in,
    proj_in,
    fc1_in,
    fc2_in,
    weights_a_in,
    weights_b_in,
    rolled_in,
    mixed_in,
    inverse_in,
    contexts_in,
    rel_in,
    attend_in,
    output,
    grad_tokens,
    fc1_out,
    fc2_out,
    proj_out,
    qkv_out_0,
    qkv_out_1,
    qkv_out_2,
    qkv_out_3,
    slab_out,
    weights_a,
    weights_b,
    rolled,
    mixed,
    inverse,
    contexts,
    rel,
    outgoing,
    grad_context,
    grad_middle,
    returned,
    pairs_in,
    fc1_grad,
    fc2_grad,
    proj_grad,
    qkv_grads,
    sums,
    fc1_sum,
    table_sum,
    slab,
    slab_z,
    slab_rep,
    *rest,
):
    count = len(SUMMED)
    held = [rest[6 * m : 6 * m + 6] for m in range(count)]
    (
        sum_send,
        sum_recv,
        extra_send,
        extra_recv,
        piece_send,
        piece_recv,
        back_send,
        back_recv,
        attend_sem,
        pairs_send,
        pairs_recv,
        slab_send,
        slab_recv,
        local,
        load,
    ) = rest[6 * count :]
    rep, shard, core, x_bit, y_bit = place()
    reps = lax.axis_size("rep")
    barrier = pltpu.get_barrier_semaphore()

    def hello(k, carry):
        pl.semaphore_signal(
            barrier,
            inc=1,
            device_id={"rep": lax.rem(rep + k, reps), "shard": shard},
            device_id_type=MESH,
        )
        return carry

    lax.fori_loop(1, reps, hello, 0)
    for k in (1, 2, 3):
        pl.semaphore_signal(
            barrier,
            inc=1,
            device_id={"rep": rep, "shard": lax.rem(shard + k, 4)},
            device_id_type=MESH,
        )
    pl.semaphore_wait(barrier, reps + 2)

    sources = (fc1_grad, fc2_grad, proj_grad) + tuple(qkv_grads.at[g] for g in range(4))

    def axis_of(matrix, first):
        x_first = SUMMED[matrix][2]
        use_x = x_first == first
        return (1, x_bit) if use_x else (2, y_bit)

    def sum_copies(matrix, phase):
        from_core, from_first, summed, from_next, from_z, shared = held[matrix]
        source = sources[matrix]
        x_first = SUMMED[matrix][2]
        first_bit, first = axis_of(matrix, True)
        second_bit, second = axis_of(matrix, False)

        def one(src, dst, bit, n=0):
            return remote(
                src,
                dst,
                sum_send.at[matrix, phase, n],
                sum_recv.at[matrix, phase, n],
                flip(rep, bit),
                shard,
            )

        if phase == CORE_SUM:
            return [one(source.at[:, :, :, 1 - core], from_core, 0)]
        if phase == FIRST_SUM:
            cut = source.at[:, :, 1 - x_bit, core] if x_first else source.at[:, 1 - y_bit, :, core]
            return [one(cut, from_first, first_bit)]
        if phase == SECOND_SUM:
            return [one(from_first.at[:, 1 - second], summed, second_bit)]
        if phase in (NEXT_SUM, Z_SUM):
            low, high = lax.rem(shard, 2), shard // 2
            if phase == NEXT_SUM:
                moves = [(2 * n + 1 - low, from_next.at[n]) for n in range(2)]
            else:
                moves = [(2 * (1 - high) + low, from_z.at[0])]
            return [
                remote(
                    summed.at[owner],
                    target,
                    sum_send.at[matrix, phase, n],
                    sum_recv.at[matrix, phase, n],
                    rep,
                    quarter_across(shard, 1 if phase == NEXT_SUM else 2),
                )
                for n, (owner, target) in enumerate(moves)
            ]
        if phase == CORE_SHARE:
            block = shared.at[:, :, core]
            return [one(block, block, 0)]
        block = shared.at[y_bit, x_bit, core]
        across = flip(flip(rep, 1), 2)
        return [
            remote(
                block,
                block,
                sum_send.at[matrix, phase, n],
                sum_recv.at[matrix, phase, n],
                partner,
                shard,
            )
            for n, partner in enumerate((flip(rep, 1), flip(rep, 2), across))
        ]

    def extra_copy(matrix, bit):
        shared, from_z = held[matrix][5], held[matrix][4]
        return remote(
            shared.at[y_bit, x_bit, core],
            from_z.at[bit - 2],
            extra_send.at[matrix, bit - 3],
            extra_recv.at[matrix, bit - 3],
            flip(rep, bit),
            shard,
        )

    def add(into, at, other, other_at):
        into[at] = into[at] + other[other_at]

    def begin(matrix):
        for copy in sum_copies(matrix, CORE_SUM):
            copy.start()

    def advance(matrix, phase):
        from_core, from_first, summed, from_next, from_z, shared = held[matrix]
        source = sources[matrix]
        x_first = SUMMED[matrix][2]
        _, second = axis_of(matrix, False)
        for copy in sum_copies(matrix, phase):
            copy.wait_recv()
        if phase == CORE_SUM:

            def step(n, carry):
                at = (n // 4, lax.rem(n // 2, 2), lax.rem(n, 2))
                add(source, at + (core,), from_core, at)
                return carry

            lax.fori_loop(0, 16, step, 0)
        elif phase == FIRST_SUM:

            def step(n, carry):
                owner, other = n // 2, lax.rem(n, 2)
                at = (owner, other, x_bit) if x_first else (owner, y_bit, other)
                add(from_first, (owner, other), source, at + (core,))
                return carry

            lax.fori_loop(0, 8, step, 0)
        elif phase == SECOND_SUM:

            def step(owner, carry):
                add(summed, (owner,), from_first, (owner, second))
                return carry

            lax.fori_loop(0, 4, step, 0)
        elif phase == NEXT_SUM:
            low = lax.rem(shard, 2)
            for high in range(2):
                add(summed, (2 * high + low,), from_next, (high,))
        elif phase == Z_SUM:
            total = summed[shard].astype(f32) + from_z[0].astype(f32)
            shared[y_bit, x_bit, core] = total.astype(bf16)
            bit = 3
            while (1 << bit) < reps:
                copy = extra_copy(matrix, bit)
                copy.start()
                copy.wait()
                at = (y_bit, x_bit, core)
                add(shared, at, from_z, (bit - 2,))
                bit += 1
        if phase < CORE_SHARE:
            for copy in sum_copies(matrix, phase + 1):
                copy.start()

    def on_the_way(step, table_of_steps):
        for when, actions in table_of_steps.items():

            @pl.when(step == when)
            def _():
                for matrix, phase in actions:
                    advance(matrix, phase)

    fetched = (
        (weights_a_in, weights_a),
        (weights_b_in, weights_b),
        (rolled_in, rolled),
        (mixed_in, mixed),
        (inverse_in, inverse),
        (contexts_in, contexts),
        (rel_in, rel),
    )
    fetches = [
        pltpu.make_async_copy(src, dst, load.at[n]) for n, (src, dst) in enumerate(fetched)
    ]

    def roll_copies(window, which=(3, 1, 2)):
        return pieces_to(
            outgoing,
            grad_context,
            lambda n: piece_send.at[window, n],
            lambda n: piece_recv.at[window, n],
            rep,
            shard,
            window,
            which=which,
        )

    def feed_forward(
        proj,
        fc1,
        fc2,
        middle,
        normed,
        normed_back,
        active,
        grad_hidden,
        grad_normed,
        branch,
        unrolled,
        grad_unrolled,
        final,
        fc1_bias,
        returned_context,
        order,
        cotangent,
    ):
        loads = [
            pltpu.make_async_copy(src, dst, load.at[len(fetched) + n])
            for n, (src, dst) in enumerate(
                (
                    (returned_in, returned_context),
                    (proj_in, proj),
                    (cotangent_in, cotangent),
                    (fc1_in, fc1),
                    (fc2_in, fc2),
                    (order_in, order),
                )
            )
        ]
        for copy in loads:
            copy.start()
        proj_bias = small_row(small_all, PROJ_BIAS).astype(f32)
        gain, shift = (small_row(small_all, row).astype(f32) for row in (LN2_GAIN, LN2_SHIFT))
        fc2_bias = small_row(small_all, FC2_BIAS).astype(f32)
        for owner in range(4):
            for k in range(4):
                lanes = slice(owner * D + k * 128, owner * D + (k + 1) * 128)
                fc1_bias[:, lanes] = small_all[owner, FC1_BIAS + k : FC1_BIAS + k + 1, :].astype(f32)
        sums[...] = jnp.zeros_like(sums)
        fc1_sum[...] = jnp.zeros_like(fc1_sum)
        for copy in loads[:2]:
            copy.wait()
        for first, length, _ in CHUNK_ROWS:
            rows = pl.ds(first, length)
            unrolled[rows, :] = dot(order_back[rows, :], returned_context[...]).astype(bf16)
            got = dot(unrolled[rows, :], proj[...]) + proj_bias
            middle[rows, :] = tokens[rows, :].astype(f32) + got
            normal, _ = norm_rows(middle[rows, :])
            normed[rows, :] = (normal * gain + shift).astype(bf16)
        for copy in loads[2:]:
            copy.wait()

        def forward_step(tile, carry):
            for n in range(2):
                lanes = pl.ds(pl.multiple_of((2 * tile + n) * FF_TILE, FF_TILE), FF_TILE)
                hidden = dot(normed[...], fc1[:, lanes]) + fc1_bias[:, lanes]
                share = 0.5 + 0.5 * lax.erf(hidden * 0.7071067811865476)
                active[:, lanes] = (hidden * share).astype(bf16)
                slope = share + hidden * jnp.exp(-0.5 * hidden * hidden) * 0.3989422804014327
                grad_hidden[:, lanes] = slope.astype(bf16)
            return carry

        for copy in fetches:
            copy.start()
        lax.fori_loop(0, FF // FF_TILE // 2, forward_step, 0)

        def fc2_step(tile, carry):
            lanes = pl.ds(pl.multiple_of(tile * 256, 256), 256)
            got = dot(active[:, lanes], cotangent[...], TN).astype(bf16)
            fc2_grad[tile // 2, lax.rem(tile, 2)] = got.reshape(2, 2, 64, D)
            return carry

        lax.fori_loop(0, FF // 256, fc2_step, 0)
        begin(FC2)
        for first, length, pieces in CHUNK_ROWS:
            rows = pl.ds(first, length)

            def backward_step(tile, carry):
                lanes = pl.ds(pl.multiple_of(tile * D, D), D)
                grad_active = dot(cotangent[rows, :], fc2[lanes, :], NT)
                grad = (grad_active * grad_hidden[rows, lanes].astype(f32)).astype(bf16)
                grad_hidden[rows, lanes] = grad
                fc1_sum[:, lanes] += jnp.sum(grad.astype(f32), 0, keepdims=True)
                return carry

            lax.fori_loop(0, FF // D, backward_step, 0)
            grad_normed[rows, :] = dot(grad_hidden[rows, :], fc1[...], NT)
            normal, over = norm_rows(middle[rows, :])
            grad_out = grad_normed[rows, :]
            scaled = grad_out * gain
            inner = (
                scaled
                - jnp.mean(scaled, -1, keepdims=True)
                - normal * jnp.mean(scaled * normal, -1, keepdims=True)
            )
            upper = cotangent[rows, :].astype(f32)
            grad_middle[rows, :] = upper + over * inner
            branch[rows, :] = grad_middle[rows, :].astype(bf16)
            for row, value in (
                (PROJ_BIAS, branch[rows, :].astype(f32)),
                (LN2_GAIN, grad_out * normal),
                (LN2_SHIFT, grad_out),
                (FC2_BIAS, upper),
            ):
                sums[row : row + 1, :] += jnp.sum(value, 0, keepdims=True)
            grad_unrolled[rows, :] = dot(branch[rows, :], proj[...], NT).astype(bf16)
            source = pl.ds(0, 400) if first == 0 else pl.ds(384, 400)
            for window in range(2):
                for piece in pieces:
                    at = pl.ds(window * PAD + FIRST_ROWS[piece], LENGTHS[piece])
                    got = dot(order[at, source], grad_unrolled[source, :]).astype(bf16)
                    if piece:
                        outgoing[at, :] = got
                    else:
                        grad_context[at, :] = got
            for window in range(2):
                for copy in roll_copies(window, [piece for piece in pieces if piece]):
                    copy.start()
        same = lax.broadcasted_iota(jnp.int32, (D, D), 0) == lax.broadcasted_iota(
            jnp.int32, (D, D), 1
        )
        unit = jnp.where(same, jnp.ones((), bf16), jnp.zeros((), bf16))
        normed_back[...] = dot(unit, normed[...], NT).astype(bf16)

        def fc1_step(tile, carry):
            lanes = pl.ds(pl.multiple_of(tile * 512, 512), 512)
            got = dot(normed_back[...], grad_hidden[:, lanes]).astype(bf16)
            fc1_grad[:, :, :, :, :, lanes] = got.reshape(4, 2, 2, 2, 16, 512)
            return carry

        lax.fori_loop(0, FF // 512, fc1_step, 0)
        begin(FC1)

        got = dot(unrolled[...], branch[...], TN).astype(bf16)
        proj_grad[...] = got.reshape(proj_grad.shape)
        begin(PROJ)
        advance(FC2, CORE_SUM)
        final[...] = (middle[...] + dot(active[...], fc2[...]) + fc2_bias).astype(bf16)
        written = pltpu.make_async_copy(final, output, load.at[len(fetched) + 6])
        written.start()
        for matrix in (FC1, PROJ):
            advance(matrix, CORE_SUM)
        written.wait()

    count_rows = tokens.shape[0]
    pl.run_scoped(
        feed_forward,
        pltpu.VMEM((D, D), bf16),
        pltpu.VMEM((D, FF), bf16),
        pltpu.VMEM((FF, D), bf16),
        pltpu.VMEM((count_rows, D), f32),
        pltpu.VMEM((count_rows, D), bf16),
        pltpu.VMEM((D, count_rows), bf16),
        pltpu.VMEM((count_rows, FF), bf16),
        pltpu.VMEM((count_rows, FF), bf16),
        pltpu.VMEM((count_rows, D), f32),
        pltpu.VMEM((count_rows, D), bf16),
        pltpu.VMEM((count_rows, D), bf16),
        pltpu.VMEM((count_rows, D), bf16),
        pltpu.VMEM((count_rows, D), bf16),
        pltpu.VMEM((1, FF), f32),
        pltpu.VMEM((2 * PAD, D), bf16),
        pltpu.VMEM((2 * PAD, count_rows), bf16),
        pltpu.VMEM((count_rows, D), bf16),
    )
    for copy in fetches:
        copy.wait()
    def return_copies(window):
        return pieces_to(
            outgoing,
            returned,
            lambda n: back_send.at[window, n],
            lambda n: back_recv.at[window, n],
            rep,
            shard,
            window,
        )

    def attend_back(attend, grads, rolled_back, pairs, pairs_out):
        head_of = lax.broadcasted_iota(jnp.int32, (1, 128), 1) // HD
        none = jnp.zeros((), bf16)

        def attend_copy(head):
            slot = lax.rem(head, 2)
            return pltpu.make_async_copy(
                attend_in.at[:, head], attend.at[slot], attend_sem.at[slot]
            )

        attend_copy(0).start()
        same = lax.broadcasted_iota(jnp.int32, (D, D), 0) == lax.broadcasted_iota(
            jnp.int32, (D, D), 1
        )
        unit = jnp.where(same, jnp.ones((), bf16), none)
        rolled_back[...] = dot(unit, rolled[...], NT).astype(bf16)

        def qkv_group(group):
            columns = [
                grads[:, part * D + group * 128 : part * D + (group + 1) * 128] for part in range(3)
            ]
            got = dot(rolled_back[...], jnp.concatenate(columns, 1)).astype(bf16)
            qkv_grads[group] = got.reshape(qkv_grads.shape[1:])
            begin(QKV + group)

        slow = (FC1, PROJ)
        first_schedule = {
            1: [(FC2, FIRST_SUM)],
            6: [(QKV + 0, CORE_SUM), *[(m, FIRST_SUM) for m in slow]],
            7: [(FC2, SECOND_SUM)],
            9: [(QKV + 0, FIRST_SUM)],
            10: [(QKV + 1, CORE_SUM), (FC2, NEXT_SUM)],
            12: [(QKV + 0, SECOND_SUM), *[(m, SECOND_SUM) for m in slow]],
            13: [(QKV + 1, FIRST_SUM), (FC2, Z_SUM)],
            14: [(QKV + 2, CORE_SUM)],
            15: [(QKV + 0, NEXT_SUM), *[(m, NEXT_SUM) for m in slow]],
        }
        second_schedule = {
            0: [(QKV + 1, SECOND_SUM)],
            1: [(QKV + 2, FIRST_SUM)],
            2: [(QKV + 3, CORE_SUM), (QKV + 1, NEXT_SUM), (QKV + 0, Z_SUM), (FC2, SHARE), *[(m, Z_SUM) for m in slow]],
            4: [(QKV + 3, FIRST_SUM), (QKV + 2, SECOND_SUM)],
            5: [(QKV + 1, Z_SUM)],
            6: [(QKV + 0, SHARE)],
            7: [(QKV + 3, SECOND_SUM), (QKV + 2, NEXT_SUM)],
            8: [*[(m, SHARE) for m in slow]],
            9: [(QKV + 1, SHARE)],
            10: [(QKV + 3, NEXT_SUM), (QKV + 2, Z_SUM)],
        }

        for window in range(2):
            for copy in roll_copies(window):
                copy.wait_recv()

        def head_step(head, carry):
            on_the_way(head, first_schedule)
            for done in range(1, HEADS // GROUP):

                @pl.when(head == done * GROUP)
                def _():
                    qkv_group(done - 1)

            @pl.when(head + 1 < HEADS)
            def _():
                attend_copy(head + 1).start()

            attend_copy(head).wait()
            slot = lax.rem(head, 2)
            group, member = head // GROUP, lax.rem(head, GROUP)

            def lanes(part):
                return pl.ds(pl.multiple_of(part * D + group * 128, 128), 128)

            mine = head_of == member
            both = []
            for window in range(2):
                rows = pl.ds(window * PAD, PAD)
                query = jnp.where(mine, mixed[rows, lanes(0)], none)
                key = jnp.where(mine, mixed[rows, lanes(1)], none)
                grad = grad_context[rows, lanes(0)].astype(f32) * inverse[rows, lanes(0)]
                grad = jnp.where(mine, grad, 0.0).astype(bf16)
                expo = attend[slot, window, :, :PAD]
                grad_attend = dot(grad, mixed[rows, lanes(2)], NT)
                inner = jnp.sum(
                    grad.astype(f32) * contexts[rows, lanes(0)].astype(f32), -1, keepdims=True
                )
                grad_scores = (expo.astype(f32) * (grad_attend - inner)).astype(bf16)
                both.append(grad_scores)
                for part, value in (
                    (0, dot(grad_scores, key) * SCALE),
                    (1, dot(grad_scores, query, TN) * SCALE),
                    (2, dot(expo, grad, TN)),
                ):
                    grads[rows, lanes(part)] = jnp.where(
                        mine, value.astype(bf16), grads[rows, lanes(part)]
                    )
            total = both[0].astype(f32) + both[1].astype(f32)
            for tile in range(TILES):
                part = total[:, tile * 128 : (tile + 1) * 128]
                if part.shape[1] < 128:
                    part = jnp.concatenate([part, jnp.zeros((PAD, 128 - part.shape[1]), f32)], 1)
                pairs[tile, pl.ds(head, PAD, stride=STRIDE), :] = part
            return carry

        lax.fori_loop(0, HEADS, head_step, 0)

        for window in range(2):
            for copy in roll_copies(window):
                copy.wait_send()

        for window in range(2):
            span = slice(window * PAD, (window + 1) * PAD)
            got = dot(grads[span, :HALF_QKV], weights_a[...], NT)
            got = got + dot(grads[span, HALF_QKV:], weights_b[...], NT)
            outgoing[span, :] = got.astype(bf16)
            for copy in return_copies(window):
                copy.start()
            rows = slice(window * PAD, window * PAD + LENGTHS[0])
            returned[rows, :] = outgoing[rows, :]
        qkv_group(HEADS // GROUP - 1)

        def round_step(step, carry):
            source = pl.ds(((1 - core) * HALF + step) * STRIDE, HEADS)
            at = pl.ds(pl.multiple_of(step * HEADS, HEADS), HEADS)
            for tile in range(TILES):
                pairs_out[tile, at, :] = pairs[tile, source, :].astype(bf16)
            return carry

        def pairs_copy(half):
            block = pl.ds(half * (HALF * HEADS // 2), HALF * HEADS // 2)
            return remote(
                pairs_out.at[:, block],
                pairs_in.at[:, block],
                pairs_send.at[half],
                pairs_recv.at[half],
                flip(rep, 0),
                shard,
            )

        for half in range(2):
            lax.fori_loop(half * (HALF // 2), (half + 1) * (HALF // 2), round_step, 0)
            pairs_copy(half).start()

        low_of = lax.broadcasted_iota(jnp.int32, (SPAN, LANES - 128), 0).astype(f32).astype(bf16)
        table_sum[...] = jnp.zeros_like(table_sum)
        for half in range(2):
            pairs_copy(half).wait_recv()

        def operands(total, index):
            width = index.shape[1]
            low = (index & (SPAN - 1)).astype(f32).astype(bf16)
            high = jnp.broadcast_to((index // SPAN).astype(f32).astype(bf16), (HEADS, width))
            nothing = jnp.zeros_like(total)
            left = jnp.concatenate(
                [jnp.where(high == jnp.asarray(s, bf16), total, nothing) for s in range(SPANS)], 0
            )
            hit = low_of[:, :width] == jnp.broadcast_to(low, (SPAN, width))
            return left, jnp.where(hit, jnp.ones((), bf16), jnp.zeros((), bf16))

        lane_of = lax.broadcasted_iota(jnp.int32, (1, 128), 1)

        def table_step(step, carry):
            on_the_way(step, second_schedule)
            factors = []
            for k in range(BATCH):
                row = step * BATCH + k
                there = core * HALF + row
                at = pl.ds(there * STRIDE, HEADS)
                near = pl.ds(pl.multiple_of(row * HEADS, HEADS), HEADS)
                index = rel[pl.ds(there, 1), :]
                sums_of = [pairs[t, at, :] + pairs_in[t, near, :].astype(f32) for t in range(TILES)]
                total = jnp.concatenate(sums_of[:-1], 1).astype(bf16)
                factors.append(operands(total, index[:, : LANES - 128]))
                last, places, turn = sums_of[-1], index[:, LANES - 128 :], 32 * (k % 4)
                if turn:
                    last = tail + pltpu.roll(last, turn, 1)
                    places = jnp.where(lane_of >= turn, pltpu.roll(places, turn, 1), tail_places)
                tail, tail_places = last, places
                if k % 4 == 3:
                    factors.append(operands(tail.astype(bf16), tail_places))
            left, right = zip(*factors)
            table_sum[...] += dot(jnp.concatenate(left, 1), jnp.concatenate(right, 1), NT)
            return carry

        lax.fori_loop(0, HALF // BATCH, table_step, 0)
        for half in range(2):
            pairs_copy(half).wait_send()
        sums[Q_BIAS : Q_BIAS + 1, :] = jnp.sum(grads[:, :D].astype(f32), 0, keepdims=True)
        sums[V_BIAS : V_BIAS + 1, :] = jnp.sum(grads[:, 2 * D :].astype(f32), 0, keepdims=True)

    pl.run_scoped(
        attend_back,
        pltpu.VMEM((2, 2, PAD, LANES), bf16),
        pltpu.VMEM((2 * PAD, 3 * D), bf16),
        pltpu.VMEM((D, 2 * PAD), bf16),
        pltpu.VMEM((TILES, PAD * STRIDE, 128), f32),
        pltpu.VMEM((TILES, HALF * HEADS, 128), bf16),
    )

    slab_rows = (pl.ds(0, TABLE_ROWS), pl.ds(TABLE_ROWS, SMALL))

    def slab_copies(part):
        return [
            remote(
                slab.at[lax.rem(shard + k, 4), slab_rows[part]],
                slab_z.at[3 - k, slab_rows[part]],
                slab_send.at[part, k - 1],
                slab_recv.at[part, 3 - k],
                rep,
                lax.rem(shard + k, 4),
            )
            for k in (1, 2, 3)
        ]

    def slab_share(part, k):
        block = slab_rep.at[rep, slab_rows[part]]
        return remote(
            block,
            block,
            slab_send.at[part, 2 + k],
            slab_recv.at[part, 2 + reps - k],
            lax.rem(rep + k, reps),
            shard,
        )

    def slab_onward(part):
        for copy in slab_copies(part):
            copy.wait_recv()
        rows = slab_rows[part]
        slab_rep[rep, rows] = slab[shard, rows] + (
            slab_z[0, rows] + slab_z[1, rows] + slab_z[2, rows]
        )

        def share_start(k, carry):
            slab_share(part, k).start()
            return carry

        lax.fori_loop(1, reps, share_start, 0)

    for owner in range(4):
        entries = jnp.concatenate(
            [table_sum[pl.ds(s * HEADS + GROUP * owner, GROUP), :] for s in range(SPANS)], 0
        )
        slab[owner, : SPANS * GROUP, :] = entries[:, :128]
        slab[owner, SPANS * GROUP : TABLE_ROWS, :] = entries[:, 128:]
    for copy in slab_copies(0):
        copy.start()

    for window in range(2):
        for copy in return_copies(window):
            copy.wait_recv()
    gain = small_row(small_all, LN1_GAIN).astype(f32)

    def norm_step(step, carry):
        gain_sum, shift_sum = carry
        rows = pl.ds(pl.multiple_of(step * 112, 16), 112)
        grad_out = dot(order_back[rows, :], returned[...])
        normal, over = norm_rows(tokens[rows, :].astype(f32))
        scaled = grad_out * gain
        inner = (
            scaled
            - jnp.mean(scaled, -1, keepdims=True)
            - normal * jnp.mean(scaled * normal, -1, keepdims=True)
        )
        grad_middle[rows, :] += over * inner
        return (
            gain_sum + jnp.sum(grad_out * normal, 0, keepdims=True),
            shift_sum + jnp.sum(grad_out, 0, keepdims=True),
        )

    nought = jnp.zeros((1, D), f32)
    some = lax.fori_loop(0, 4, norm_step, (nought, nought))
    slab_onward(0)
    gain_sum, shift_sum = lax.fori_loop(4, 7, norm_step, some)
    sums[LN1_GAIN : LN1_GAIN + 1, :] = gain_sum
    sums[LN1_SHIFT : LN1_SHIFT + 1, :] = shift_sum
    for owner in range(4):
        lanes = slice(owner * 128, (owner + 1) * 128)
        slab[owner, TABLE_ROWS:, :] = jnp.concatenate(
            [sums[:, lanes]]
            + [fc1_sum[:, owner * D + k * 128 : owner * D + (k + 1) * 128] for k in range(4)]
            + [jnp.zeros((4, 128), f32)],
            0,
        )
    for copy in slab_copies(1):
        copy.start()
    tokens_copy = pltpu.make_async_copy(grad_middle, grad_tokens, load.at[0])
    tokens_copy.start()

    slow = (FC1, PROJ)
    for matrix, phase in [(QKV + 3, Z_SUM), (QKV + 3, SHARE), (QKV + 2, SHARE)]:
        advance(matrix, phase)

    for matrix in range(count):
        advance(matrix, CORE_SHARE)
    outs = (fc1_out, fc2_out, proj_out, qkv_out_0, qkv_out_1, qkv_out_2, qkv_out_3)
    results = [
        pltpu.make_async_copy(held[matrix][5], outs[matrix], local.at[count + matrix])
        for matrix in range(count)
    ]
    for copy in results:
        copy.start()
    slab_onward(1)

    def share_wait(k, carry):
        for part in range(2):
            slab_share(part, k).wait()
        return carry

    lax.fori_loop(1, reps, share_wait, 0)

    def slab_step(k, total):
        return total + slab_rep[k]

    slab_out[...] = lax.fori_loop(1, reps, slab_step, slab_rep[0])

    for part in range(2):
        for copy in slab_copies(part):
            copy.wait_send()
    for window in range(2):
        for copy in return_copies(window):
            copy.wait_send()
    for matrix in range(count):
        for phase in range(CORE_SHARE + 1):
            for copy in sum_copies(matrix, phase):
                copy.wait_send()
    for copy in results + [tokens_copy]:
        copy.wait()


def rear(
    returned_context,
    tokens,
    cotangent,
    small_all,
    whole_proj,
    whole_fc1,
    whole_fc2,
    weights_a,
    weights_b,
    rolled,
    mixed,
    inverse,
    contexts,
    rel,
    attend,
):
    anywhere, inside = pl.BlockSpec(memory_space=pl.ANY), pl.BlockSpec(memory_space=pltpu.VMEM)
    reps = lax.axis_size("rep")
    dma = pltpu.SemaphoreType.DMA
    order = send_matrix()
    extra = max(1, reps.bit_length() - 4)
    held = []
    for rows, columns, _ in SUMMED:
        held += [
            pltpu.VMEM((4, 2, 2, rows, columns), bf16),
            pltpu.VMEM((4, 2, rows, columns), bf16),
            pltpu.VMEM((4, rows, columns), bf16),
            pltpu.VMEM((2, rows, columns), bf16),
            pltpu.VMEM((1 + extra, rows, columns), bf16),
            pltpu.VMEM((2, 2, 2, rows, columns), bf16),
        ]
    return pl.pallas_call(
        rear_kernel,
        out_shape=(
            jax.ShapeDtypeStruct(tokens.shape, bf16),
            jax.ShapeDtypeStruct(tokens.shape, f32),
            *[jax.ShapeDtypeStruct((2, 2, 2) + shape[:2], bf16) for shape in SUMMED],
            jax.ShapeDtypeStruct((SLAB, 128), f32),
        ),
        in_specs=[inside] * 3 + [anywhere] * 14,
        out_specs=(*[anywhere] * (2 + len(SUMMED)), inside),
        scratch_shapes=[
            pltpu.VMEM(weights_a.shape, bf16),
            pltpu.VMEM(weights_b.shape, bf16),
            pltpu.VMEM(rolled.shape, bf16),
            pltpu.VMEM(mixed.shape, bf16),
            pltpu.VMEM(inverse.shape, f32),
            pltpu.VMEM(contexts.shape, bf16),
            pltpu.VMEM(rel.shape, jnp.int32),
            pltpu.VMEM((2 * PAD, D), bf16),
            pltpu.VMEM((2 * PAD, D), bf16),
            pltpu.VMEM(tokens.shape, f32),
            pltpu.VMEM((2 * PAD, D), bf16),
            pltpu.VMEM((TILES, HALF * HEADS, 128), bf16),
            pltpu.VMEM((4, 2, 2, 2, 16, 2048), bf16),
            pltpu.VMEM((4, 2, 2, 2, 64, 512), bf16),
            pltpu.VMEM((4, 2, 2, 2, 16, 512), bf16),
            pltpu.VMEM((HEADS // GROUP, 4, 2, 2, 2, 16, 3 * 128), bf16),
            pltpu.VMEM((8, D), f32),
            pltpu.VMEM((1, FF), f32),
            pltpu.VMEM((SPANS * HEADS, SPAN), f32),
            pltpu.VMEM((4, SLAB, 128), f32),
            pltpu.VMEM((3, SLAB, 128), f32),
            pltpu.VMEM((reps, SLAB, 128), f32),
            *held,
            dma((len(SUMMED), CORE_SHARE + 1, 3)),
            dma((len(SUMMED), CORE_SHARE + 1, 3)),
            dma((len(SUMMED), extra)),
            dma((len(SUMMED), extra)),
            dma((2, 3)),
            dma((2, 3)),
            dma((2, 3)),
            dma((2, 3)),
            dma((2,)),
            dma((2,)),
            dma((2,)),
            dma((2, 3 + reps)),
            dma((2, 3 + reps)),
            dma((2 * len(SUMMED),)),
            dma((14,)),
        ],
        compiler_params=pltpu.CompilerParams(
            vmem_limit_bytes=VMEM_LIMIT, collective_id=1, has_side_effects=True
        ),
        name="rear",
    )(
        jnp.asarray(order.T, bf16),
        tokens,
        small_all,
        returned_context,
        jnp.asarray(order, bf16),
        cotangent,
        whole_proj,
        whole_fc1,
        whole_fc2,
        weights_a,
        weights_b,
        rolled,
        mixed,
        inverse,
        contexts,
        rel,
        attend,
    )


def finish_kernel(
    output_in,
    tokens_in,
    fc1_in,
    fc2_in,
    proj_in,
    qkv_0,
    qkv_1,
    qkv_2,
    qkv_3,
    slab,
    output,
    tokens,
    fc1,
    fc2,
    proj,
    qkv,
    table,
    fc1_bias,
    *vectors,
):
    output[...] = output_in[...]
    tokens[...] = tokens_in[...]
    for part, whole in ((fc1_in, fc1), (fc2_in, fc2), (proj_in, proj)):
        whole[...] = part[...].astype(f32).reshape(whole.shape)
    for group, part in enumerate((qkv_0, qkv_1, qkv_2, qkv_3)):
        got = part[...].astype(f32).reshape(qkv.shape[0], 3 * 128)
        for n in range(3):
            first = n * D + group * 128
            qkv[:, first : first + 128] = got[:, n * 128 : (n + 1) * 128]
    entries = [
        slab[pl.ds((half * SPANS + span) * GROUP, GROUP), :]
        for span in range(SPANS)
        for half in range(2)
    ]
    table[...] = jnp.concatenate(entries, 1)[:, :TABLE]
    for row, vector in enumerate(vectors):
        vector[...] = slab[TABLE_ROWS + row : TABLE_ROWS + row + 1, :]
    first = TABLE_ROWS + FC1_BIAS
    fc1_bias[...] = jnp.concatenate([slab[first + k : first + k + 1, :] for k in range(4)], 1)


def finish(output, grad_tokens, fc1, fc2, proj, qkv, slab):
    inside = pl.BlockSpec(memory_space=pltpu.VMEM)
    shapes = [(128, FF), (FF // 4, D), (128, D), (128, 3 * D), (GROUP, TABLE), (1, D)]
    shapes += [(1, 128)] * FC1_BIAS
    return pl.pallas_call(
        finish_kernel,
        out_shape=(
            jax.ShapeDtypeStruct(output.shape, bf16),
            jax.ShapeDtypeStruct(grad_tokens.shape, f32),
            *[jax.ShapeDtypeStruct(shape, f32) for shape in shapes],
        ),
        in_specs=[inside] * 10,
        out_specs=(inside,) * (2 + len(shapes)),
        compiler_params=pltpu.CompilerParams(vmem_limit_bytes=VMEM_LIMIT),
        name="finish",
    )(output, grad_tokens, fc1, fc2, proj, *qkv, slab)


def shards(
    tokens,
    region,
    rel_index,
    ln1_gain,
    ln1_shift,
    w_qkv,
    q_bias,
    v_bias,
    table,
    w_proj,
    proj_bias,
    ln2_gain,
    ln2_shift,
    w_fc1,
    fc1_bias,
    w_fc2,
    fc2_bias,
    cotangent,
):
    small = jnp.zeros((SMALL, 128), f32)
    vectors = (ln1_gain, ln1_shift, q_bias, v_bias, proj_bias, ln2_gain, ln2_shift, fc2_bias, fc1_bias)
    for row, vector in enumerate(vectors):
        block = vector.reshape(-1, 128).astype(f32)
        small += jnp.pad(block, ((row, SMALL - row - block.shape[0]), (0, 0)))
    small = small.astype(bf16)
    labels = region.reshape(WT, WH, 2, WW).transpose(2, 0, 1, 3).reshape(2, WIN)
    labels = pieces_of(labels, 1, -1)
    row_ids = jnp.pad(labels, ((0, 0), (0, LANES - PAD)), constant_values=-1)[:, None]
    (
        whole_qkv_a,
        whole_qkv_b,
        whole_proj,
        whole_fc1,
        whole_fc2,
        small,
        rolled,
        qkv,
        attend,
        inverse,
        contexts,
        returned,
        rel,
    ) = front(
        tokens.reshape(-1, D),
        small,
        table.T,
        row_ids,
        rel_index,
        w_qkv,
        w_proj,
        w_fc1,
        w_fc2,
    )
    output, grad_tokens, grad_w_fc1, grad_w_fc2, grad_w_proj, *grads_qkv, slab = rear(
        returned,
        tokens.reshape(-1, D),
        cotangent.reshape(-1, D),
        small,
        whole_proj,
        whole_fc1,
        whole_fc2,
        whole_qkv_a,
        whole_qkv_b,
        rolled,
        qkv,
        inverse,
        contexts,
        rel,
        attend,
    )
    (
        output,
        grad_tokens,
        grad_w_fc1,
        grad_w_fc2,
        grad_w_proj,
        grad_w_qkv,
        grad_table,
        grad_fc1_bias,
        *vectors,
    ) = finish(output, grad_tokens, grad_w_fc1, grad_w_fc2, grad_w_proj, grads_qkv, slab)
    output = output.reshape(tokens.shape)
    grad_tokens = grad_tokens.reshape(tokens.shape)
    grad_table = grad_table.T
    grad_fc1_bias = grad_fc1_bias.reshape(-1)
    vectors = [vector.reshape(-1) for vector in vectors]
    grad_ln1_gain, grad_ln1_shift = vectors[LN1_GAIN], vectors[LN1_SHIFT]
    grad_q_bias, grad_v_bias = vectors[Q_BIAS], vectors[V_BIAS]
    grad_proj_bias, grad_fc2_bias = vectors[PROJ_BIAS], vectors[FC2_BIAS]
    grad_ln2_gain, grad_ln2_shift = vectors[LN2_GAIN], vectors[LN2_SHIFT]
    return (
        output,
        grad_tokens,
        grad_ln1_gain,
        grad_ln1_shift,
        grad_w_qkv,
        grad_q_bias,
        grad_v_bias,
        grad_table,
        grad_w_proj,
        grad_proj_bias,
        grad_ln2_gain,
        grad_ln2_shift,
        grad_w_fc1,
        grad_fc1_bias,
        grad_w_fc2,
        grad_fc2_bias,
    )


def solution(mesh):
    return jax.shard_map(
        shards,
        mesh=mesh,
        in_specs=(
            P("rep", "shard", None, None),
            P("shard", None),
            P(),
            P("shard"),
            P("shard"),
            P("shard", None),
            P("shard"),
            P("shard"),
            P(None, "shard"),
            P("shard", None),
            P("shard"),
            P("shard"),
            P("shard"),
            P("shard", None),
            P("shard"),
            P("shard", None),
            P("shard"),
            P("rep", "shard", None, None),
        ),
        out_specs=(
            P("rep", "shard", None, None),
            P("rep", "shard", None, None),
            P("shard"),
            P("shard"),
            P("shard", None),
            P("shard"),
            P("shard"),
            P(None, "shard"),
            P("shard", None),
            P("shard"),
            P("shard"),
            P("shard"),
            P("shard", None),
            P("shard"),
            P("shard", None),
            P("shard"),
        ),
        check_vma=False,
    )
```
